32 devices in a mesh: grp: 2 (over x), rows: 16 (over z, y, core).
Axes of the slice: x: 2, y: 2, z: 4, core: 2. Of those that a mesh axis runs over, the one named last changes fastest.
Arguments:
- probes: float32 [64, 262144], P(None, ('grp', 'rows')), parts along dimension 1, may hold values from -6 to 6
- worker_len: int32 [32768], P(('grp', 'rows')), parts along dimension 0, may hold values from 1 to 8, as said below
- spell_to_slot: int32 [262144], P(('grp', 'rows')), parts along dimension 0, may hold values from 0 to 255, as said below
- slot_to_firm: int32 [8192], P(('grp', 'rows')), parts along dimension 0, may hold values from 0 to 1023, as said below
Outputs:
- demeaned: float32 [64, 262144], P(None, ('grp', 'rows')), parts along dimension 1
The draws below stay inside these ranges and needn't reach their ends.
There are 2 independent parts, one for each index of `grp`. The reference program is written for one: setup_inputs(seed, part) draws one part's arguments, and reference() takes and returns one part's arrays. A program takes and returns all parts, laid end to end along the dimension named above; each array names one. Nothing has to cross between parts.
Inputs may be any that keep to these rules, and one draw needn't show every extreme that they name: `worker_len`: at least one worker of every device has 8 spells and one has a single spell. `spell_to_slot`: every device has a row of slot 0 and a row of slot 255. `slot_to_firm`: firms may repeat across slots and devices.
All inputs are finite; a program needn't handle non-finite values.
Results may differ from the reference program's by a relative error of at most 0.0001.
Values sent between devices are 32-bit elements; how exact they have to be, the bound alone decides.
No kernel may reach another device: no remote copies, remote signals or barrier semaphores. Data moves between devices by JAX's collectives and lax.ppermute only.
A program may use at most 64 MiB of HBM per device.

```python
import jax
import jax.numpy as jnp
from jax import lax

C = 64
PAD = 8
W_DEV = 1024
CAP = 16
FIRMS_PER_SHARD = 1024
SWEEPS = 2
SPELLS_PER_SHARD = 8192
TOTAL_SPELLS = 131072
WORKERS = 16384
SLOTS_PER_SHARD = 256
FIRMS = 16384
N_ROWS = 16


def draw_worker_len(key, part):
    key = jax.random.fold_in(key, 3)
    lengths = jax.random.randint(key, (WORKERS,), 1, PAD + 1)
    lengths = lengths.reshape(-1, W_DEV).at[:, 0].set(PAD).at[:, 1].set(1)
    return lengths.reshape(-1).astype(jnp.int32)


def draw_spell_to_slot(key, part):
    key = jax.random.fold_in(key, 5)
    shard_slots = jax.random.randint(key, (TOTAL_SPELLS,), 0, SLOTS_PER_SHARD)
    shard_slots = shard_slots.reshape(-1, SPELLS_PER_SHARD).at[:, 0].set(0).at[:, 1].set(SLOTS_PER_SHARD - 1)
    return shard_slots.reshape(-1).astype(jnp.int32)


def draw_slot_to_firm(key, part):
    key = jax.random.fold_in(key, 7)
    employer_ids = jax.random.randint(key, (SLOTS_PER_SHARD * N_ROWS,), 0, FIRMS_PER_SHARD)
    employer_ids = employer_ids.at[0].set(0).at[1].set(FIRMS_PER_SHARD - 1)
    return employer_ids.astype(jnp.int32)


def steps_of(key, dims, cuts, least, largest):
    def one(axis_at, parts):
        heights = jax.random.uniform(jax.random.fold_in(jax.random.fold_in(key, 6), axis_at), (parts,), jnp.float32, least / len(cuts), largest / len(cuts))
        return jnp.repeat(jnp.exp(heights), dims[axis_at] // parts).reshape((-1,) + (1,) * (len(dims) - axis_at - 1))

    level = one(*cuts[0])
    for cut in cuts[1:]:
        level = level * one(*cut)
    return level


def gaussian(key, dims, deviation, most, cuts=(), held_as=jnp.bfloat16):
    loudness = steps_of(key, dims, cuts, -0.22, 0.18) if cuts else 1.0
    result = jax.random.normal(key, dims, jnp.float32) * deviation * loudness
    return jnp.minimum(jnp.maximum(result, -most), most).astype(held_as)


def setup_inputs(seed: int = 0, part: int = 0) -> dict:
    streams_of = jax.random.split(jax.random.key(seed), 5)
    part_keys = jax.random.split(jax.random.fold_in(streams_of[4], part), 5)
    return {
        "probes": gaussian(part_keys[0], (C, TOTAL_SPELLS), 1.0, 6.0, ((1, 16),), jnp.float32),
        "worker_len": draw_worker_len(jax.random.fold_in(jax.random.fold_in(streams_of[4], part), 71), part),
        "spell_to_slot": draw_spell_to_slot(jax.random.fold_in(jax.random.fold_in(streams_of[4], part), 71), part),
        "slot_to_firm": draw_slot_to_firm(jax.random.fold_in(jax.random.fold_in(streams_of[4], part), 71), part),
    }


def reference(probes, worker_len, spell_to_slot, slot_to_firm):
    rows_all = probes.shape[1]
    inside = lax.broadcasted_iota(jnp.int32, (WORKERS, PAD), 1) < worker_len[:, None]
    valid_mask = inside.astype(jnp.float32).reshape(rows_all)
    shard_owner = (jnp.arange(rows_all, dtype=jnp.int32) // SPELLS_PER_SHARD).astype(jnp.int32)
    shard_local_firm = slot_to_firm[(shard_owner * SLOTS_PER_SHARD + spell_to_slot).astype(jnp.int32)]
    firm = ((spell_to_slot // CAP) * FIRMS_PER_SHARD + shard_local_firm).astype(jnp.int32)
    count = jax.ops.segment_sum(valid_mask, firm, FIRMS)
    denom = jnp.maximum(count, 1.0)
    lengths = worker_len.astype(jnp.float32)
    demeaned = probes * valid_mask[None, :]
    for sweep in range(SWEEPS):
        shaped = demeaned.reshape(C, WORKERS, PAD)
        worker_mean = jnp.sum(shaped, axis=2) / lengths[None, :]
        demeaned = (shaped - worker_mean[:, :, None]).reshape(C, rows_all) * valid_mask[None, :]
        sums = jax.vmap(lambda probe_column: jax.ops.segment_sum(probe_column, firm, FIRMS))(demeaned)
        means = sums / denom[None, :]
        demeaned = (demeaned - jnp.take(means, firm, axis=1)) * valid_mask[None, :]
    return demeaned
```

```python
import functools

import jax
import jax.numpy as jnp
from jax import lax
from jax.experimental import pallas as pl
from jax.experimental.pallas import tpu as pltpu
from jax.sharding import PartitionSpec as P

FIRMS_PER_SHARD = 1024
LANES = 128
BLOCK = 1024
VMEM_BYTES = 48 * 1024 * 1024
F32, BF16 = jnp.float32, jnp.bfloat16
NT = (((1,), (1,)), ((), ()))
NN = (((1,), (0,)), ((), ()))


def dot(a, b, dims=NN):
    return lax.dot_general(a, b, dims, preferred_element_type=F32)


def iota(shape, dim):
    return lax.broadcasted_iota(jnp.int32, shape, dim)


def split(x):
    hi = x.astype(BF16)
    return hi, (x - hi.astype(F32)).astype(BF16)


def row(ref, block, size):
    per = size // LANES
    return jnp.concatenate([ref[block * per + k : block * per + k + 1, :] for k in range(per)], axis=1)


def one_hot(ids, slots):
    return (iota((slots, ids.shape[1]), 0) == ids).astype(F32).astype(BF16)


def same_worker(pad, width):
    return (iota((width, width), 0) // pad == iota((width, width), 1) // pad).astype(F32).astype(BF16)


def by_worker(x, table):
    rows, width = x.shape
    hi, lo = split(x)
    both = jnp.concatenate([hi, lo], axis=0)
    step = table.shape[0]
    total = jnp.concatenate([dot(both[:, k : k + step], table) for k in range(0, width, step)], axis=1)
    return total[:rows] + total[rows:]


def fold(x):
    return x + pltpu.roll(x, x.shape[1] // 2, axis=1)


def halves(x):
    hi, lo = split(x)
    return jnp.where(iota(x.shape, 1) < x.shape[1] // 2, hi.astype(F32), lo.astype(F32))


def sums_kernel(pad, cap, probes, lengths, ids, firms, send, own, own_count, mask_ids, weight, valid, x, acc, sems):
    blocks = x.shape[1] // BLOCK
    slots = own.shape[0]
    copies = [
        pltpu.make_async_copy(probes.at[:, pl.ds(b * BLOCK, BLOCK)], x.at[:, pl.ds(b * BLOCK, BLOCK)], sems.at[b])
        for b in range(blocks)
    ]
    for copy in copies:
        copy.start()
    total_rows = ids.shape[0]
    here = iota((total_rows, LANES), 0)
    lane = iota((total_rows, LANES), 1)
    wide = jnp.broadcast_to(
        lengths[...].astype(F32)[:, None, :], (lengths.shape[0], total_rows // lengths.shape[0], LANES)
    ).reshape(total_rows, LANES)
    per = LANES // pad
    wide = jnp.where(lane // per == here % pad, wide, 0.0).astype(BF16)
    spread = (iota((LANES, LANES), 0) % per == iota((LANES, LANES), 1) // pad).astype(F32).astype(BF16)
    row_len = dot(wide, spread)
    inside = (lane % pad).astype(F32) < row_len
    valid[...] = jnp.where(inside, 1.0, 0.0)
    weight[...] = jnp.where(inside, 1.0 / row_len, 0.0)
    mask_ids[...] = jnp.where(inside, ids[...], -1)

    table = same_worker(pad, 256)
    for b in range(blocks):
        copies[b].wait()
        ok = row(valid, b, BLOCK)
        x0 = x[:, b * BLOCK : (b + 1) * BLOCK] * ok
        x1 = x0 - by_worker(x0, table) * row(weight, b, BLOCK)
        hi, lo = split(x1)
        counted = jnp.broadcast_to(ok, (16, BLOCK)).astype(BF16)
        data = jnp.concatenate([hi, lo, counted], axis=0)
        part = dot(one_hot(row(mask_ids, b, BLOCK), slots), data, NT)
        if b == 0:
            acc[...] = part
        else:
            acc[...] += part
    both = fold(acc[:, :LANES])
    own[...] = both
    count = jnp.broadcast_to(acc[:, LANES : LANES + 1], (slots, LANES))
    own_count[...] = count
    half = slots // 2
    send[:half] = jnp.where(iota((half, LANES), 1) < LANES // 2, both[:half], both[half:])
    tiles = slots // LANES
    slot = iota((tiles, LANES), 0) * LANES + iota((tiles, LANES), 1)
    keys = ((slot // cap) * FIRMS_PER_SHARD + firms[...]).astype(F32)
    send[half : half + tiles] = keys
    for k in range(tiles):
        send[half + tiles + k : half + tiles + k + 1] = count[k * LANES : (k + 1) * LANES].T[:1]


def worker_kernel(pad, lengths, mask_ids, out):
    slots = out.shape[1]
    workers = lengths.shape[0] * LANES
    group = 256
    rows_group = group * pad
    pick = (iota((rows_group, group), 0) // pad == iota((rows_group, group), 1)).astype(F32).astype(BF16)
    total = jnp.zeros((2 * slots, slots), F32)
    for g in range(workers // group):
        counts = dot(one_hot(row(mask_ids, g, rows_group), slots), pick)
        inverse = 1.0 / row(lengths, g, group).astype(F32)
        hi, lo = split(counts * inverse)
        total += dot(jnp.concatenate([hi, lo], axis=0), counts.astype(BF16), NT)
    hi, lo = split(total[:slots] + total[slots:])
    out[:slots] = hi
    out[slots:] = lo


def column(ref, tiles):
    return jnp.concatenate([jnp.broadcast_to(ref[k : k + 1, :], (LANES, LANES)).T for k in range(tiles)], axis=0)


def own_keys(firms, cap):
    tiles = firms.shape[0]
    slots = tiles * LANES
    return (iota((slots, LANES), 0) // cap * FIRMS_PER_SHARD).astype(F32) + column(firms[...].astype(F32), tiles)


def firm_sums(n, received, info, mine, tiles, count=None):
    slots = tiles * LANES
    half = slots // 2
    rows, info_rows = received.shape[0] // n, info.shape[0] // n
    left = iota((half, LANES), 1) < LANES // 2

    def from_device(d, carry):
        total, count = carry
        start = pl.multiple_of(d * rows, 8)
        about = info[pl.ds(pl.multiple_of(d * info_rows, 8), info_rows), :]
        match = []
        for k in range(tiles):
            same = mine == about[k : k + 1]
            if count is not None:
                count += jnp.where(same, about[tiles + k : tiles + k + 1], 0.0)
            match.append(same.astype(F32).astype(BF16))
        block = received[pl.ds(start, half), :]
        turned = pltpu.roll(block, LANES // 2, axis=1)
        data = jnp.concatenate(
            [halves(jnp.where(left, block, turned)), halves(jnp.where(left, turned, block))], axis=0
        ).astype(BF16)
        return total + dot(jnp.concatenate(match, axis=1), data), count

    total, count = lax.fori_loop(0, n, from_device, (jnp.zeros((slots, LANES), F32), count), unroll=4)
    return fold(total), count


def means_kernel(n, cap, received, firms, own, own_count, pairs, mean, send, inverse, info):
    tiles = firms.shape[0]
    slots = tiles * LANES
    half = slots // 2
    rows, info_rows = received.shape[0] // n, info.shape[0] // n
    for d in range(n):
        info[d * info_rows : (d + 1) * info_rows] = received[d * rows + half : (d + 1) * rows]
    total, count = firm_sums(n, received, info, own_keys(firms, cap), tiles, jnp.zeros((slots, LANES), F32))
    scale = 1.0 / jnp.maximum(jnp.sum(count, axis=1, keepdims=True), 1.0)
    inverse[...] = jnp.broadcast_to(scale, (slots, LANES))
    found = total * scale
    mean[...] = found
    change = dot(pairs[...], halves(found).astype(BF16))
    new = own[...] - own_count[...] * found + fold(change[:slots] + change[slots:])
    left = iota((half, LANES), 1) < LANES // 2
    send[...] = jnp.where(left, new[:half], new[half:])


def column_copies(source, target, sems):
    width = source.shape[1]
    cuts = [pl.ds(start, BLOCK) for start in range(0, width, BLOCK)]
    return [pltpu.make_async_copy(source.at[:, cut], target.at[:, cut], sems.at[b]) for b, cut in enumerate(cuts)]


def take(parts, ids, slots):
    spread = dot(parts, one_hot(ids, slots))
    columns = parts.shape[0] // 2
    return spread[:columns] + spread[columns:]


def first_kernel(pad, probes, mean, mask_ids, weight, out, x, y, in_sems, out_sems):
    ins, outs = column_copies(probes, x, in_sems), column_copies(y, out, out_sems)
    for copy in ins:
        copy.start()
    slots = mean.shape[0]
    parts = halves(mean[...]).T.astype(BF16)
    table = same_worker(pad, 256)
    for b in range(len(ins)):
        ids = row(mask_ids, b, BLOCK)
        spread = take(parts, ids, slots)
        ins[b].wait()
        rest = jnp.where(ids >= 0, x[:, b * BLOCK : (b + 1) * BLOCK] - spread, 0.0)
        y[:, b * BLOCK : (b + 1) * BLOCK] = rest - by_worker(rest, table) * row(weight, b, BLOCK)
        outs[b].start()
    for copy in outs:
        copy.wait()


def last_kernel(n, cap, received, before, firms, info, inverse, mask_ids, out, x, y, in_sems, out_sems):
    ins, outs = column_copies(before, x, in_sems), column_copies(y, out, out_sems)
    for copy in ins:
        copy.start()
    tiles = firms.shape[0]
    slots = tiles * LANES
    total, _ = firm_sums(n, received, info, own_keys(firms, cap), tiles)
    parts = halves(total * inverse[...]).T.astype(BF16)
    for b in range(len(ins)):
        spread = take(parts, row(mask_ids, b, BLOCK), slots)
        ins[b].wait()
        y[:, b * BLOCK : (b + 1) * BLOCK] = x[:, b * BLOCK : (b + 1) * BLOCK] - spread
        outs[b].start()
    for copy in outs:
        copy.wait()


def call(kernel, out_shape, in_specs, out_specs, scratch, flops, moved):
    return pl.pallas_call(
        kernel,
        out_shape=out_shape,
        in_specs=in_specs,
        out_specs=out_specs,
        scratch_shapes=scratch,
        compiler_params=pltpu.CompilerParams(vmem_limit_bytes=VMEM_BYTES),
        cost_estimate=pl.CostEstimate(flops=flops, bytes_accessed=moved, transcendentals=0),
    )


def body(probes, worker_len, spell_to_slot, slot_to_firm, *, n):
    columns, rows_dev = probes.shape
    workers = worker_len.shape[0]
    pad = rows_dev // workers
    slots = slot_to_firm.shape[0]
    cap = slots // n
    half = slots // 2
    tiles = slots // LANES
    info_rows = -(-2 * tiles // 8) * 8
    blocks = rows_dev // BLOCK
    vmem, anywhere = pl.BlockSpec(memory_space=pltpu.VMEM), pl.BlockSpec(memory_space=pl.ANY)
    lengths = worker_len.reshape(workers // LANES, LANES)
    ids = spell_to_slot.reshape(rows_dev // LANES, LANES)
    firms = slot_to_firm.reshape(tiles, LANES)
    array = jax.ShapeDtypeStruct
    of_rows = (rows_dev // LANES, LANES)
    work = 2 * rows_dev * slots * 2 * columns
    sems = pltpu.SemaphoreType.DMA((blocks,))
    whole = pltpu.VMEM((columns, rows_dev), F32)

    send, own, own_count, mask_ids, weight = call(
        functools.partial(sums_kernel, pad, cap),
        [
            array((half + info_rows, LANES), F32),
            array((slots, LANES), F32),
            array((slots, LANES), F32),
            array(of_rows, jnp.int32),
            array(of_rows, F32),
        ],
        [anywhere, vmem, vmem, vmem],
        [vmem] * 5,
        [pltpu.VMEM(of_rows, F32), whole, pltpu.VMEM((slots, 2 * columns + 16), F32), sems],
        2 * work,
        4 * columns * rows_dev,
    )(probes, lengths, ids, firms)
    received = lax.all_gather(send, "rows", axis=0, tiled=True)
    pairs = call(
        functools.partial(worker_kernel, pad),
        array((2 * slots, slots), BF16),
        [vmem, vmem],
        vmem,
        [],
        2 * work,
        4 * slots * slots,
    )(lengths, mask_ids)
    mean, again, inverse, info = call(
        functools.partial(means_kernel, n, cap),
        [
            array((slots, LANES), F32),
            array((half, LANES), F32),
            array((slots, LANES), F32),
            array((n * info_rows, LANES), F32),
        ],
        [vmem] * 5,
        [vmem] * 4,
        [],
        work // 4,
        received.size * 4,
    )(received, firms, own, own_count, pairs)
    second = lax.all_gather(again, "rows", axis=0, tiled=True)
    before = call(
        functools.partial(first_kernel, pad),
        array((columns, rows_dev), F32),
        [anywhere, vmem, vmem, vmem],
        anywhere,
        [whole, whole, sems, sems],
        2 * work,
        8 * columns * rows_dev,
    )(probes, mean, mask_ids, weight)
    return call(
        functools.partial(last_kernel, n, cap),
        array((columns, rows_dev), F32),
        [vmem, anywhere, vmem, vmem, vmem, vmem],
        anywhere,
        [whole, whole, sems, sems],
        work,
        8 * columns * rows_dev,
    )(second, before, firms, info, inverse, mask_ids)


def solution(mesh):
    placed = (P(None, ("grp", "rows")), P(("grp", "rows")), P(("grp", "rows")), P(("grp", "rows")))
    return jax.shard_map(
        functools.partial(body, n=mesh.shape["rows"]),
        mesh=mesh,
        in_specs=placed,
        out_specs=P(None, ("grp", "rows")),
        check_vma=False,
    )
```

```python
import functools

import jax
import jax.numpy as jnp
from jax import lax
from jax.experimental import pallas as pl
from jax.experimental.pallas import tpu as pltpu
from jax.sharding import PartitionSpec as P

FIRMS_PER_SHARD = 1024
LANES = 128
BLOCK = 1024
VMEM_BYTES = 60 * 1024 * 1024
F32, BF16 = jnp.float32, jnp.bfloat16
NT = (((1,), (1,)), ((), ()))
NN = (((1,), (0,)), ((), ()))


def dot(a, b, dims=NN):
    return lax.dot_general(a, b, dims, preferred_element_type=F32)


def iota(shape, dim):
    return lax.broadcasted_iota(jnp.int32, shape, dim)


def split(x):
    hi = x.astype(BF16)
    return hi, (x - hi.astype(F32)).astype(BF16)


def row(ref, block, size):
    per = size // LANES
    return jnp.concatenate([ref[block * per + k : block * per + k + 1, :] for k in range(per)], axis=1)


def one_hot(ids, slots):
    return (iota((slots, ids.shape[1]), 0) == ids).astype(F32).astype(BF16)


def same_worker(pad, width):
    return (iota((width, width), 0) // pad == iota((width, width), 1) // pad).astype(F32).astype(BF16)


def by_worker(x, table):
    rows, width = x.shape
    hi, lo = split(x)
    both = jnp.concatenate([hi, lo], axis=0)
    step = table.shape[0]
    total = jnp.concatenate([dot(both[:, k : k + step], table) for k in range(0, width, step)], axis=1)
    return total[:rows] + total[rows:]


def fold(x):
    return x + pltpu.roll(x, x.shape[1] // 2, axis=1)


def halves(x):
    hi, lo = split(x)
    return jnp.where(iota(x.shape, 1) < x.shape[1] // 2, hi.astype(F32), lo.astype(F32))


def column(firms):
    return jnp.concatenate(
        [jnp.broadcast_to(firms[k : k + 1, :], (LANES, LANES)).T for k in range(firms.shape[0])], axis=0
    )


def along(x):
    return jnp.concatenate([x[k : k + LANES].T[:1] for k in range(0, x.shape[0], LANES)], axis=1)


def left_of(shape):
    return iota(shape, len(shape) - 1) < LANES // 2


def to_tiles(x, n):
    x = x.reshape(n, 2, 8, LANES)
    return jnp.where(left_of((n, 8, LANES)), x[:, 0], x[:, 1])


def apart(tiles):
    turned = pltpu.roll(tiles, LANES // 2, axis=tiles.ndim - 1)
    left = left_of(tiles.shape)
    return jnp.where(left, tiles, turned), jnp.where(left, turned, tiles)


def from_tiles(tiles):
    n = tiles.shape[0]
    return jnp.stack(apart(tiles), axis=1).reshape(2 * 8 * n, LANES)


def start_all(copies):
    for copy in copies:
        copy.start()


def wait_all(copies):
    for copy in copies:
        copy.wait()


def tiles_out(n, buffer, outs, sem):
    me = lax.axis_index("rows")
    return [pltpu.make_async_copy(buffer.at[me ^ k], outs[k], sem.at[k]) for k in range(n)]


def tiles_in(n, ins, buffer, sem, by_device):
    me = lax.axis_index("rows")
    return [
        pltpu.make_async_copy(ins[k], buffer.at[me ^ k] if by_device else buffer.at[k], sem.at[k]) for k in range(n)
    ]


def column_copies(source, target, sems):
    width = source.shape[1]
    cuts = [pl.ds(start, BLOCK) for start in range(0, width, BLOCK)]
    return [pltpu.make_async_copy(source.at[:, cut], target.at[:, cut], sems.at[b]) for b, cut in enumerate(cuts)]


def sums_kernel(n, pad, probes, lengths_in, ids_in, firms_in, *refs):
    outs, (own, own_count, mask_ids, weight) = refs[:n], refs[n : n + 4]
    valid, x, acc, lengths, ids, firms, buffer, sems, small, sem = refs[n + 4 :]
    copies = column_copies(probes, x, sems)
    first = [
        pltpu.make_async_copy(source, target, small.at[k])
        for k, (source, target) in enumerate(((lengths_in, lengths), (ids_in, ids), (firms_in, firms)))
    ]
    start_all(first)
    start_all(copies)
    slots = own.shape[0]
    total_rows = ids.shape[0]
    here = iota((total_rows, LANES), 0)
    lane = iota((total_rows, LANES), 1)
    wait_all(first)
    wide = jnp.broadcast_to(
        lengths[...].astype(F32)[:, None, :], (lengths.shape[0], total_rows // lengths.shape[0], LANES)
    ).reshape(total_rows, LANES)
    per = LANES // pad
    wide = jnp.where(lane // per == here % pad, wide, 0.0).astype(BF16)
    spread = (iota((LANES, LANES), 0) % per == iota((LANES, LANES), 1) // pad).astype(F32).astype(BF16)
    row_len = dot(wide, spread)
    inside = (lane % pad).astype(F32) < row_len
    valid[...] = jnp.where(inside, 1.0, 0.0)
    weight[...] = jnp.where(inside, 1.0 / row_len, 0.0)
    mask_ids[...] = jnp.where(inside, ids[...], -1)

    table = same_worker(pad, 256)
    for b in range(len(copies)):
        copies[b].wait()
        ok = row(valid, b, BLOCK)
        x0 = x[:, b * BLOCK : (b + 1) * BLOCK] * ok
        x1 = x0 - by_worker(x0, table) * row(weight, b, BLOCK)
        hi, lo = split(x1)
        counted = jnp.broadcast_to(ok, (16, BLOCK)).astype(BF16)
        data = jnp.concatenate([hi, lo, counted], axis=0)
        part = dot(one_hot(row(mask_ids, b, BLOCK), slots), data, NT)
        if b == 0:
            acc[...] = part
        else:
            acc[...] += part
    both = fold(acc[:, :LANES])
    own[...] = both
    count = jnp.broadcast_to(acc[:, LANES : LANES + 1], (slots, LANES))
    own_count[...] = count
    buffer[:, :8] = to_tiles(both, n)
    about = jnp.where(left_of((slots, LANES)), column(firms[...].astype(F32)), count).reshape(n, 2, 8, LANES)
    even = iota((n, 8, LANES), 2) // (LANES // 4) % 2 == 0
    buffer[:, 8:] = jnp.where(even, about[:, 0], about[:, 1])
    copies = tiles_out(n, buffer, outs, sem)
    start_all(copies)
    wait_all(copies)


def worker_kernel(pad, lengths, mask_ids, out):
    slots = out.shape[1]
    workers = lengths.shape[0] * LANES
    group = 256
    rows_group = group * pad
    pick = (iota((rows_group, group), 0) // pad == iota((rows_group, group), 1)).astype(F32).astype(BF16)
    total = jnp.zeros((2 * slots, slots), F32)
    for g in range(workers // group):
        counts = dot(one_hot(row(mask_ids, g, rows_group), slots), pick)
        inverse = 1.0 / row(lengths, g, group).astype(F32)
        hi, lo = split(counts * inverse)
        total += dot(jnp.concatenate([hi, lo], axis=0), counts.astype(BF16), NT)
    hi, lo = split(total[:slots] + total[slots:])
    out[:slots] = hi
    out[slots:] = lo


def owner_means(tiles, table, scale):
    n = tiles.shape[0]
    left, right = apart(tiles.reshape(8 * n, LANES))
    data = jnp.concatenate([halves(left), halves(right)], axis=0).astype(BF16)
    total = fold(dot(table, data)) * scale
    return jnp.where(left_of((8 * n, LANES)), total[: 8 * n], total[8 * n :]).reshape(n, 8, LANES)


def owner_first_kernel(n, *refs):
    ins, outs, (table, scale) = refs[:n], refs[n : 2 * n], refs[2 * n : 2 * n + 2]
    buffer, back, in_sem, sem = refs[2 * n + 2 :]
    copies = tiles_in(n, ins, buffer, in_sem, False)
    start_all(copies)
    wait_all(copies)
    about = buffer[:, 8:].reshape(8 * n, LANES)
    quarter = LANES // 4

    def both(at):
        return jnp.concatenate(
            [jnp.broadcast_to(about[:, k : k + 1], (8 * n, LANES)) for k in (at, at + quarter)], axis=0
        )

    keys, counts = both(0), both(2 * quarter)
    same = keys[:, :1] == along(keys)
    table[...] = same.astype(F32).astype(BF16)
    count = jnp.sum(jnp.where(same, along(counts), 0.0), axis=1, keepdims=True)
    scale[...] = jnp.broadcast_to(1.0 / jnp.maximum(count, 1.0), scale.shape)
    back[...] = owner_means(buffer[:, :8], table[...], scale[...])
    copies = tiles_out_in_place(n, back, outs, sem)
    start_all(copies)
    wait_all(copies)


def owner_second_kernel(n, *refs):
    ins, (table, scale), outs = refs[:n], refs[n : n + 2], refs[n + 2 : 2 * n + 2]
    buffer, back, in_sem, sem = refs[2 * n + 2 :]
    copies = tiles_in(n, ins, buffer, in_sem, False)
    start_all(copies)
    wait_all(copies)
    back[...] = owner_means(buffer[...], table[...], scale[...])
    copies = tiles_out_in_place(n, back, outs, sem)
    start_all(copies)
    wait_all(copies)


def tiles_out_in_place(n, buffer, outs, sem):
    return [pltpu.make_async_copy(buffer.at[k], outs[k], sem.at[k]) for k in range(n)]


def change_kernel(n, *refs):
    ins, (own, own_count, pairs), outs, mean = refs[:n], refs[n : n + 3], refs[n + 3 : 2 * n + 3], refs[2 * n + 3]
    buffer, back, in_sem, sem = refs[2 * n + 4 :]
    copies = tiles_in(n, ins, buffer, in_sem, True)
    start_all(copies)
    wait_all(copies)
    slots = own.shape[0]
    found = from_tiles(buffer[...])
    mean[...] = found
    change = dot(pairs[...], halves(found).astype(BF16))
    new = own[...] - own_count[...] * found + fold(change[:slots] + change[slots:])
    back[...] = to_tiles(new, n)
    copies = tiles_out(n, back, outs, sem)
    start_all(copies)
    wait_all(copies)


def take(parts, ids, slots):
    spread = dot(parts, one_hot(ids, slots))
    columns = parts.shape[0] // 2
    return spread[:columns] + spread[columns:]


def first_kernel(pad, probes, mean, mask_ids, weight, out, x, y, in_sems, out_sems):
    ins, outs = column_copies(probes, x, in_sems), column_copies(y, out, out_sems)
    start_all(ins)
    slots = mean.shape[0]
    parts = halves(mean[...]).T.astype(BF16)
    table = same_worker(pad, 256)
    for b in range(len(ins)):
        ids = row(mask_ids, b, BLOCK)
        spread = take(parts, ids, slots)
        ins[b].wait()
        rest = jnp.where(ids >= 0, x[:, b * BLOCK : (b + 1) * BLOCK] - spread, 0.0)
        y[:, b * BLOCK : (b + 1) * BLOCK] = rest - by_worker(rest, table) * row(weight, b, BLOCK)
        outs[b].start()
    wait_all(outs)


def last_kernel(n, *refs):
    arrived, (before, mask_ids, out) = refs[:n], refs[n : n + 3]
    buffer, x, y, tile_sem, in_sems, out_sems = refs[n + 3 :]
    ins, outs = column_copies(before, x, in_sems), column_copies(y, out, out_sems)
    copies = tiles_in(n, arrived, buffer, tile_sem, True)
    start_all(copies)
    start_all(ins)
    wait_all(copies)
    mean = from_tiles(buffer[...])
    parts = halves(mean).T.astype(BF16)
    for b in range(len(ins)):
        spread = take(parts, row(mask_ids, b, BLOCK), mean.shape[0])
        ins[b].wait()
        y[:, b * BLOCK : (b + 1) * BLOCK] = x[:, b * BLOCK : (b + 1) * BLOCK] - spread
        outs[b].start()
    wait_all(outs)


def exchange(tiles):
    n = len(tiles)
    return [tiles[0]] + [lax.ppermute(tiles[k], "rows", [(i, i ^ k) for i in range(n)]) for k in range(1, n)]


def call(kernel, out_shape, in_specs, out_specs, scratch, flops, moved):
    return pl.pallas_call(
        kernel,
        out_shape=out_shape,
        in_specs=in_specs,
        out_specs=out_specs,
        scratch_shapes=scratch,
        compiler_params=pltpu.CompilerParams(vmem_limit_bytes=VMEM_BYTES),
        cost_estimate=pl.CostEstimate(flops=flops, bytes_accessed=moved, transcendentals=0),
    )


def body(probes, worker_len, spell_to_slot, slot_to_firm, *, n):
    columns, rows_dev = probes.shape
    workers = worker_len.shape[0]
    pad = rows_dev // workers
    slots = slot_to_firm.shape[0]
    firm_tiles = slots // LANES
    blocks = rows_dev // BLOCK
    vmem, anywhere = pl.BlockSpec(memory_space=pltpu.VMEM), pl.BlockSpec(memory_space=pl.ANY)
    lengths = worker_len.reshape(workers // LANES, LANES)
    ids = spell_to_slot.reshape(rows_dev // LANES, LANES)
    firms = slot_to_firm.reshape(firm_tiles, LANES)
    array = jax.ShapeDtypeStruct
    of_rows = (rows_dev // LANES, LANES)
    work = 2 * rows_dev * slots * 2 * columns
    sems = pltpu.SemaphoreType.DMA((blocks,))
    sem = pltpu.SemaphoreType.DMA((n,))
    whole = pltpu.VMEM((columns, rows_dev), F32)
    of_slots = array((slots, LANES), F32)
    tile, tall = array((8, LANES), F32), array((16, LANES), F32)
    tiles, talls = pltpu.VMEM((n, 8, LANES), F32), pltpu.VMEM((n, 16, LANES), F32)

    *send, own, own_count, mask_ids, weight = call(
        functools.partial(sums_kernel, n, pad),
        [tall] * n + [of_slots, of_slots, array(of_rows, jnp.int32), array(of_rows, F32)],
        [anywhere] * 4,
        [anywhere] * n + [vmem] * 4,
        [
            pltpu.VMEM(of_rows, F32),
            whole,
            pltpu.VMEM((slots, 2 * columns + 16), F32),
            pltpu.VMEM(lengths.shape, jnp.int32),
            pltpu.VMEM(ids.shape, jnp.int32),
            pltpu.VMEM(firms.shape, jnp.int32),
            talls,
            sems,
            pltpu.SemaphoreType.DMA((3,)),
            sem,
        ],
        2 * work,
        4 * columns * rows_dev,
    )(probes, lengths, ids, firms)
    received = exchange(send)
    pairs = call(
        functools.partial(worker_kernel, pad),
        array((2 * slots, slots), BF16),
        [vmem, vmem],
        vmem,
        [],
        2 * work,
        4 * slots * slots,
    )(lengths, mask_ids)
    *send, table, scale = call(
        functools.partial(owner_first_kernel, n),
        [tile] * n + [array((slots, slots), BF16), of_slots],
        [anywhere] * n,
        [anywhere] * n + [vmem] * 2,
        [talls, tiles, sem, sem],
        work // 16,
        slots * slots * 4,
    )(*received)
    received = exchange(send)
    *send, mean = call(
        functools.partial(change_kernel, n),
        [tile] * n + [of_slots],
        [anywhere] * n + [vmem] * 3,
        [anywhere] * n + [vmem],
        [tiles, tiles, sem, sem],
        work // 16,
        slots * slots * 4,
    )(*received, own, own_count, pairs)
    received = exchange(send)
    before = call(
        functools.partial(first_kernel, pad),
        array((columns, rows_dev), F32),
        [anywhere, vmem, vmem, vmem],
        anywhere,
        [whole, whole, sems, sems],
        2 * work,
        8 * columns * rows_dev,
    )(probes, mean, mask_ids, weight)
    send = call(
        functools.partial(owner_second_kernel, n),
        [tile] * n,
        [anywhere] * n + [vmem] * 2,
        [anywhere] * n,
        [tiles, tiles, sem, sem],
        work // 16,
        slots * slots * 4,
    )(*received, table, scale)
    received = exchange(send)
    return call(
        functools.partial(last_kernel, n),
        array((columns, rows_dev), F32),
        [anywhere] * n + [anywhere, vmem],
        anywhere,
        [tiles, whole, whole, sem, sems, sems],
        work,
        8 * columns * rows_dev,
    )(*received, before, mask_ids)


def solution(mesh):
    placed = (P(None, ("grp", "rows")), P(("grp", "rows")), P(("grp", "rows")), P(("grp", "rows")))
    return jax.shard_map(
        functools.partial(body, n=mesh.shape["rows"]),
        mesh=mesh,
        in_specs=placed,
        out_specs=P(None, ("grp", "rows")),
        check_vma=False,
    )
```

```python
import functools

import jax
import jax.numpy as jnp
from jax import lax
from jax.experimental import pallas as pl
from jax.experimental.pallas import tpu as pltpu
from jax.sharding import PartitionSpec as P

FIRMS_PER_SHARD = 1024
LANES = 128
BLOCK = 1024
VMEM_BYTES = 60 * 1024 * 1024
F32, BF16 = jnp.float32, jnp.bfloat16
NT = (((1,), (1,)), ((), ()))
NN = (((1,), (0,)), ((), ()))


def dot(a, b, dims=NN):
    return lax.dot_general(a, b, dims, preferred_element_type=F32)


def iota(shape, dim):
    return lax.broadcasted_iota(jnp.int32, shape, dim)


def split(x):
    hi = x.astype(BF16)
    return hi, (x - hi.astype(F32)).astype(BF16)


def row(ref, block, size):
    per = size // LANES
    return jnp.concatenate([ref[block * per + k : block * per + k + 1, :] for k in range(per)], axis=1)


def one_hot(ids, slots):
    return (iota((slots, ids.shape[1]), 0) == ids).astype(F32).astype(BF16)


def same_worker(pad, width):
    return (iota((width, width), 0) // pad == iota((width, width), 1) // pad).astype(F32).astype(BF16)


def by_worker(x, table):
    rows, width = x.shape
    hi, lo = split(x)
    both = jnp.concatenate([hi, lo], axis=0)
    step = table.shape[0]
    total = jnp.concatenate([dot(both[:, k : k + step], table) for k in range(0, width, step)], axis=1)
    return total[:rows] + total[rows:]


def fold(x):
    return x + pltpu.roll(x, x.shape[1] // 2, axis=1)


def halves(x):
    hi, lo = split(x)
    return jnp.where(iota(x.shape, 1) < x.shape[1] // 2, hi.astype(F32), lo.astype(F32))


def column(firms):
    return jnp.concatenate(
        [jnp.broadcast_to(firms[k : k + 1, :], (LANES, LANES)).T for k in range(firms.shape[0])], axis=0
    )


def along(x):
    return jnp.concatenate([x[k : k + LANES].T[:1] for k in range(0, x.shape[0], LANES)], axis=1)


def left_of(shape):
    return iota(shape, len(shape) - 1) < LANES // 2


def to_tiles(x, n):
    x = x.reshape(n, 2, 8, LANES)
    return jnp.where(left_of((n, 8, LANES)), x[:, 0], x[:, 1])


def apart(tiles):
    turned = pltpu.roll(tiles, LANES // 2, axis=tiles.ndim - 1)
    left = left_of(tiles.shape)
    return jnp.where(left, tiles, turned), jnp.where(left, turned, tiles)


def from_tiles(tiles):
    n = tiles.shape[0]
    return jnp.stack(apart(tiles), axis=1).reshape(2 * 8 * n, LANES)


def start_all(copies):
    for copy in copies:
        copy.start()


def wait_all(copies):
    for copy in copies:
        copy.wait()


def move(source, target, sem):
    copy = pltpu.make_async_copy(source, target, sem)
    copy.start()
    copy.wait()


def column_copies(source, target, sems):
    width = source.shape[1]
    cuts = [pl.ds(start, BLOCK) for start in range(0, width, BLOCK)]
    return [pltpu.make_async_copy(source.at[:, cut], target.at[:, cut], sems.at[b]) for b, cut in enumerate(cuts)]


def sums_kernel(n, pad, *refs):
    probes, lengths_in, ids_in, firms_in, send, own, own_count, mask_ids, weight = refs[:9]
    valid, x, acc, lengths, ids, firms, buffer, sems, small, sem = refs[9:]
    copies = column_copies(probes, x, sems)
    first = [
        pltpu.make_async_copy(source, target, small.at[k])
        for k, (source, target) in enumerate(((lengths_in, lengths), (ids_in, ids), (firms_in, firms)))
    ]
    start_all(first)
    start_all(copies)
    slots = own.shape[0]
    total_rows = ids.shape[0]
    here = iota((total_rows, LANES), 0)
    lane = iota((total_rows, LANES), 1)
    wait_all(first)
    wide = jnp.broadcast_to(
        lengths[...].astype(F32)[:, None, :], (lengths.shape[0], total_rows // lengths.shape[0], LANES)
    ).reshape(total_rows, LANES)
    per = LANES // pad
    wide = jnp.where(lane // per == here % pad, wide, 0.0).astype(BF16)
    spread = (iota((LANES, LANES), 0) % per == iota((LANES, LANES), 1) // pad).astype(F32).astype(BF16)
    row_len = dot(wide, spread)
    inside = (lane % pad).astype(F32) < row_len
    valid[...] = jnp.where(inside, 1.0, 0.0)
    weight[...] = jnp.where(inside, 1.0 / row_len, 0.0)
    mask_ids[...] = jnp.where(inside, ids[...], -1)

    table = same_worker(pad, 256)
    for b in range(len(copies)):
        copies[b].wait()
        ok = row(valid, b, BLOCK)
        x0 = x[:, b * BLOCK : (b + 1) * BLOCK] * ok
        x1 = x0 - by_worker(x0, table) * row(weight, b, BLOCK)
        hi, lo = split(x1)
        counted = jnp.broadcast_to(ok, (16, BLOCK)).astype(BF16)
        data = jnp.concatenate([hi, lo, counted], axis=0)
        part = dot(one_hot(row(mask_ids, b, BLOCK), slots), data, NT)
        if b == 0:
            acc[...] = part
        else:
            acc[...] += part
    both = fold(acc[:, :LANES])
    own[...] = both
    count = jnp.broadcast_to(acc[:, LANES : LANES + 1], (slots, LANES))
    own_count[...] = count
    buffer[:, :8] = to_tiles(both, n)
    about = jnp.where(left_of((slots, LANES)), column(firms[...].astype(F32)), count).reshape(n, 2, 8, LANES)
    even = iota((n, 8, LANES), 2) // (LANES // 4) % 2 == 0
    buffer[:, 8:] = jnp.where(even, about[:, 0], about[:, 1])
    move(buffer, send, sem)


def worker_kernel(pad, lengths, mask_ids, out):
    slots = out.shape[1]
    workers = lengths.shape[0] * LANES
    group = 256
    rows_group = group * pad
    pick = (iota((rows_group, group), 0) // pad == iota((rows_group, group), 1)).astype(F32).astype(BF16)
    total = jnp.zeros((2 * slots, slots), F32)
    for g in range(workers // group):
        counts = dot(one_hot(row(mask_ids, g, rows_group), slots), pick)
        inverse = 1.0 / row(lengths, g, group).astype(F32)
        hi, lo = split(counts * inverse)
        total += dot(jnp.concatenate([hi, lo], axis=0), counts.astype(BF16), NT)
    hi, lo = split(total[:slots] + total[slots:])
    out[:slots] = hi
    out[slots:] = lo


def owner_means(tiles, table, scale):
    n = tiles.shape[0]
    left, right = apart(tiles.reshape(8 * n, LANES))
    data = jnp.concatenate([halves(left), halves(right)], axis=0).astype(BF16)
    total = fold(dot(table, data)) * scale
    return jnp.where(left_of((8 * n, LANES)), total[: 8 * n], total[8 * n :]).reshape(n, 8, LANES)


def owner_first_kernel(received, send, table, scale, buffer, back, in_sem, sem):
    n = buffer.shape[0]
    move(received, buffer, in_sem)
    about = buffer[:, 8:].reshape(8 * n, LANES)
    quarter = LANES // 4

    def both(at):
        return jnp.concatenate(
            [jnp.broadcast_to(about[:, k : k + 1], (8 * n, LANES)) for k in (at, at + quarter)], axis=0
        )

    keys, counts = both(0), both(2 * quarter)
    same = keys[:, :1] == along(keys)
    table[...] = same.astype(F32).astype(BF16)
    count = jnp.sum(jnp.where(same, along(counts), 0.0), axis=1, keepdims=True)
    scale[...] = jnp.broadcast_to(1.0 / jnp.maximum(count, 1.0), scale.shape)
    back[...] = owner_means(buffer[:, :8], table[...], scale[...])
    move(back, send, sem)


def owner_second_kernel(received, table, scale, send, buffer, back, in_sem, sem):
    move(received, buffer, in_sem)
    back[...] = owner_means(buffer[...], table[...], scale[...])
    move(back, send, sem)


def change_kernel(received, own, own_count, pairs, send, mean, buffer, back, in_sem, sem):
    move(received, buffer, in_sem)
    slots = own.shape[0]
    found = from_tiles(buffer[...])
    mean[...] = found
    change = dot(pairs[...], halves(found).astype(BF16))
    new = own[...] - own_count[...] * found + fold(change[:slots] + change[slots:])
    back[...] = to_tiles(new, buffer.shape[0])
    move(back, send, sem)


def take(parts, ids, slots):
    spread = dot(parts, one_hot(ids, slots))
    columns = parts.shape[0] // 2
    return spread[:columns] + spread[columns:]


def first_kernel(pad, probes, mean, mask_ids, weight, out, x, y, in_sems, out_sems):
    ins, outs = column_copies(probes, x, in_sems), column_copies(y, out, out_sems)
    start_all(ins)
    slots = mean.shape[0]
    parts = halves(mean[...]).T.astype(BF16)
    table = same_worker(pad, 256)
    for b in range(len(ins)):
        ids = row(mask_ids, b, BLOCK)
        spread = take(parts, ids, slots)
        ins[b].wait()
        rest = jnp.where(ids >= 0, x[:, b * BLOCK : (b + 1) * BLOCK] - spread, 0.0)
        y[:, b * BLOCK : (b + 1) * BLOCK] = rest - by_worker(rest, table) * row(weight, b, BLOCK)
        outs[b].start()
    wait_all(outs)


def last_kernel(received, before, mask_ids, out, buffer, x, y, tile_sem, in_sems, out_sems):
    ins, outs = column_copies(before, x, in_sems), column_copies(y, out, out_sems)
    copy = pltpu.make_async_copy(received, buffer, tile_sem)
    copy.start()
    start_all(ins)
    copy.wait()
    mean = from_tiles(buffer[...])
    parts = halves(mean).T.astype(BF16)
    for b in range(len(ins)):
        spread = take(parts, row(mask_ids, b, BLOCK), mean.shape[0])
        ins[b].wait()
        y[:, b * BLOCK : (b + 1) * BLOCK] = x[:, b * BLOCK : (b + 1) * BLOCK] - spread
        outs[b].start()
    wait_all(outs)


def exchange(tiles):
    return lax.all_to_all(tiles, "rows", split_axis=0, concat_axis=0, tiled=True)


def call(kernel, out_shape, in_specs, out_specs, scratch, flops, moved):
    return pl.pallas_call(
        kernel,
        out_shape=out_shape,
        in_specs=in_specs,
        out_specs=out_specs,
        scratch_shapes=scratch,
        compiler_params=pltpu.CompilerParams(vmem_limit_bytes=VMEM_BYTES),
        cost_estimate=pl.CostEstimate(flops=flops, bytes_accessed=moved, transcendentals=0),
    )


def body(probes, worker_len, spell_to_slot, slot_to_firm, *, n):
    columns, rows_dev = probes.shape
    workers = worker_len.shape[0]
    pad = rows_dev // workers
    slots = slot_to_firm.shape[0]
    firm_tiles = slots // LANES
    blocks = rows_dev // BLOCK
    vmem, anywhere = pl.BlockSpec(memory_space=pltpu.VMEM), pl.BlockSpec(memory_space=pl.ANY)
    lengths = worker_len.reshape(workers // LANES, LANES)
    ids = spell_to_slot.reshape(rows_dev // LANES, LANES)
    firms = slot_to_firm.reshape(firm_tiles, LANES)
    array = jax.ShapeDtypeStruct
    of_rows = (rows_dev // LANES, LANES)
    work = 2 * rows_dev * slots * 2 * columns
    sems = pltpu.SemaphoreType.DMA((blocks,))
    sem = pltpu.SemaphoreType.DMA
    whole = pltpu.VMEM((columns, rows_dev), F32)
    of_slots = array((slots, LANES), F32)
    all_tiles, all_talls = array((n, 8, LANES), F32), array((n, 16, LANES), F32)
    tiles, talls = pltpu.VMEM((n, 8, LANES), F32), pltpu.VMEM((n, 16, LANES), F32)

    send, own, own_count, mask_ids, weight = call(
        functools.partial(sums_kernel, n, pad),
        [all_talls, of_slots, of_slots, array(of_rows, jnp.int32), array(of_rows, F32)],
        [anywhere] * 4,
        [anywhere] + [vmem] * 4,
        [
            pltpu.VMEM(of_rows, F32),
            whole,
            pltpu.VMEM((slots, 2 * columns + 16), F32),
            pltpu.VMEM(lengths.shape, jnp.int32),
            pltpu.VMEM(ids.shape, jnp.int32),
            pltpu.VMEM(firms.shape, jnp.int32),
            talls,
            sems,
            pltpu.SemaphoreType.DMA((3,)),
            sem,
        ],
        2 * work,
        4 * columns * rows_dev,
    )(probes, lengths, ids, firms)
    received = exchange(send)
    pairs = call(
        functools.partial(worker_kernel, pad),
        array((2 * slots, slots), BF16),
        [vmem, vmem],
        vmem,
        [],
        2 * work,
        4 * slots * slots,
    )(lengths, mask_ids)
    send, table, scale = call(
        owner_first_kernel,
        [all_tiles, array((slots, slots), BF16), of_slots],
        [anywhere],
        [anywhere] + [vmem] * 2,
        [talls, tiles, sem, sem],
        work // 16,
        slots * slots * 4,
    )(received)
    received = exchange(send)
    send, mean = call(
        change_kernel,
        [all_tiles, of_slots],
        [anywhere] + [vmem] * 3,
        [anywhere, vmem],
        [tiles, tiles, sem, sem],
        work // 16,
        slots * slots * 4,
    )(received, own, own_count, pairs)
    received = exchange(send)
    before = call(
        functools.partial(first_kernel, pad),
        array((columns, rows_dev), F32),
        [anywhere, vmem, vmem, vmem],
        anywhere,
        [whole, whole, sems, sems],
        2 * work,
        8 * columns * rows_dev,
    )(probes, mean, mask_ids, weight)
    send = call(
        owner_second_kernel,
        all_tiles,
        [anywhere] + [vmem] * 2,
        anywhere,
        [tiles, tiles, sem, sem],
        work // 16,
        slots * slots * 4,
    )(received, table, scale)
    received = exchange(send)
    return call(
        last_kernel,
        array((columns, rows_dev), F32),
        [anywhere, anywhere, vmem],
        anywhere,
        [tiles, whole, whole, sem, sems, sems],
        work,
        8 * columns * rows_dev,
    )(received, before, mask_ids)


def solution(mesh):
    placed = (P(None, ("grp", "rows")), P(("grp", "rows")), P(("grp", "rows")), P(("grp", "rows")))
    return jax.shard_map(
        functools.partial(body, n=mesh.shape["rows"]),
        mesh=mesh,
        in_specs=placed,
        out_specs=P(None, ("grp", "rows")),
        check_vma=False,
    )
```

```python
import functools

import jax
import jax.numpy as jnp
from jax import lax
from jax.experimental import pallas as pl
from jax.experimental.pallas import tpu as pltpu
from jax.sharding import PartitionSpec as P

FIRMS_PER_SHARD = 1024
LANES = 128
BLOCK = 1024
VMEM_BYTES = 40 * 1024 * 1024
NEAR = 4
F32, BF16 = jnp.float32, jnp.bfloat16
NT = (((1,), (1,)), ((), ()))
NN = (((1,), (0,)), ((), ()))


def dot(a, b, dims=NN):
    return lax.dot_general(a, b, dims, preferred_element_type=F32)


def iota(shape, dim):
    return lax.broadcasted_iota(jnp.int32, shape, dim)


def split(x):
    hi = x.astype(BF16)
    return hi, (x - hi.astype(F32)).astype(BF16)


def row(ref, block, size):
    per = size // LANES
    return jnp.concatenate([ref[block * per + k : block * per + k + 1, :] for k in range(per)], axis=1)


def one_hot(ids, slots):
    return (iota((slots, ids.shape[1]), 0) == ids).astype(F32).astype(BF16)


def same_worker(pad, width):
    return (iota((width, width), 0) // pad == iota((width, width), 1) // pad).astype(F32).astype(BF16)


def by_worker(x, table):
    rows, width = x.shape
    hi, lo = split(x)
    both = jnp.concatenate([hi, lo], axis=0)
    step = table.shape[0]
    total = jnp.concatenate([dot(both[:, k : k + step], table) for k in range(0, width, step)], axis=1)
    return total[:rows] + total[rows:]


def fold(x):
    return x + pltpu.roll(x, x.shape[1] // 2, axis=1)


def halves(x):
    hi, lo = split(x)
    return jnp.where(iota(x.shape, 1) < x.shape[1] // 2, hi.astype(F32), lo.astype(F32))


def column(firms):
    return jnp.concatenate(
        [jnp.broadcast_to(firms[k : k + 1, :], (LANES, LANES)).T for k in range(firms.shape[0])], axis=0
    )


def along(x):
    return jnp.concatenate([x[k : k + LANES].T[:1] for k in range(0, x.shape[0], LANES)], axis=1)


def left_of(shape):
    return iota(shape, len(shape) - 1) < LANES // 2


def to_tiles(x, n):
    x = x.reshape(n, 2, 8, LANES)
    return jnp.where(left_of((n, 8, LANES)), x[:, 0], x[:, 1])


def apart(tiles):
    turned = pltpu.roll(tiles, LANES // 2, axis=tiles.ndim - 1)
    left = left_of(tiles.shape)
    return jnp.where(left, tiles, turned), jnp.where(left, turned, tiles)


def from_tiles(tiles):
    n = tiles.shape[0]
    return jnp.stack(apart(tiles), axis=1).reshape(2 * 8 * n, LANES)


def start_all(copies):
    for copy in copies:
        copy.start()


def wait_all(copies):
    for copy in copies:
        copy.wait()


def column_copies(source, target, sems):
    width = source.shape[1]
    cuts = [pl.ds(start, BLOCK) for start in range(0, width, BLOCK)]
    return [pltpu.make_async_copy(source.at[:, cut], target.at[:, cut], sems.at[b]) for b, cut in enumerate(cuts)]


def sums_kernel(n, pad, *refs):
    probes, lengths_in, ids_in, firms_in, send, own, own_count, mask_ids, weight = refs[:9]
    valid, x, acc, lengths, ids, firms, sems, small = refs[9:]
    copies = column_copies(probes, x, sems)
    first = [
        pltpu.make_async_copy(source, target, small.at[k])
        for k, (source, target) in enumerate(((lengths_in, lengths), (ids_in, ids), (firms_in, firms)))
    ]
    start_all(first)
    start_all(copies)
    slots = own.shape[0]
    total_rows = ids.shape[0]
    here = iota((total_rows, LANES), 0)
    lane = iota((total_rows, LANES), 1)
    wait_all(first)
    wide = jnp.broadcast_to(
        lengths[...].astype(F32)[:, None, :], (lengths.shape[0], total_rows // lengths.shape[0], LANES)
    ).reshape(total_rows, LANES)
    per = LANES // pad
    wide = jnp.where(lane // per == here % pad, wide, 0.0).astype(BF16)
    spread = (iota((LANES, LANES), 0) % per == iota((LANES, LANES), 1) // pad).astype(F32).astype(BF16)
    row_len = dot(wide, spread)
    inside = (lane % pad).astype(F32) < row_len
    valid[...] = jnp.where(inside, 1.0, 0.0)
    weight[...] = jnp.where(inside, 1.0 / row_len, 0.0)
    mask_ids[...] = jnp.where(inside, ids[...], -1)

    table = same_worker(pad, 256)
    for b in range(len(copies)):
        copies[b].wait()
        ok = row(valid, b, BLOCK)
        x0 = x[:, b * BLOCK : (b + 1) * BLOCK] * ok
        x1 = x0 - by_worker(x0, table) * row(weight, b, BLOCK)
        hi, lo = split(x1)
        counted = jnp.broadcast_to(ok, (16, BLOCK)).astype(BF16)
        data = jnp.concatenate([hi, lo, counted], axis=0)
        part = dot(one_hot(row(mask_ids, b, BLOCK), slots), data, NT)
        if b == 0:
            acc[...] = part
        else:
            acc[...] += part
    both = fold(acc[:, :LANES])
    own[...] = both
    count = jnp.broadcast_to(acc[:, LANES : LANES + 1], (slots, LANES))
    own_count[...] = count
    far = n // NEAR
    send[:, : 8 * NEAR] = to_tiles(both, n).reshape(far, 8 * NEAR, LANES)
    about = jnp.where(iota((slots, LANES), 1) % 16 < 8, column(firms[...].astype(F32)), count)
    about = about.reshape(far, NEAR, 2, 8, LANES)
    eighth = iota((far, 8, LANES), 2) // 8
    packed = about[:, 0, 0]
    for owner in range(NEAR):
        for side in range(2):
            packed = jnp.where(eighth // 2 == 2 * owner + side, about[:, owner, side], packed)
    send[:, 8 * NEAR :] = packed


def worker_kernel(pad, lengths, mask_ids, out):
    slots = out.shape[1]
    workers = lengths.shape[0] * LANES
    group = 256
    rows_group = group * pad
    pick = (iota((rows_group, group), 0) // pad == iota((rows_group, group), 1)).astype(F32).astype(BF16)
    total = jnp.zeros((2 * slots, slots), F32)
    for g in range(workers // group):
        counts = dot(one_hot(row(mask_ids, g, rows_group), slots), pick)
        inverse = 1.0 / row(lengths, g, group).astype(F32)
        hi, lo = split(counts * inverse)
        total += dot(jnp.concatenate([hi, lo], axis=0), counts.astype(BF16), NT)
    hi, lo = split(total[:slots] + total[slots:])
    out[:slots] = hi
    out[slots:] = lo


def owner_means(parts, table, scale):
    rows = 8 * NEAR * parts[0].shape[0]
    data = [apart(part.reshape(rows, LANES)) for part in parts]
    data = [halves(side) for sides in data for side in sides]
    total = fold(dot(table, jnp.concatenate(data, axis=0).astype(BF16))) * scale
    return jnp.where(left_of((rows, LANES)), total[:rows], total[rows:]).reshape(parts[0].shape)


def owner_first_kernel(*refs):
    parts, (send, table, scale) = refs[:NEAR], refs[NEAR:]
    far = send.shape[0]

    def sides(part, kind):
        about = part[:, 8 * NEAR :].reshape(8 * far, LANES)
        found = []
        for side in range(2):
            one = [
                jnp.broadcast_to(about[:, at : at + 1], (8 * far, LANES)).reshape(far, 1, 8, LANES)
                for at in (16 * (2 * owner + side) + 8 * kind for owner in range(NEAR))
            ]
            found.append(jnp.concatenate(one, axis=1).reshape(8 * NEAR * far, LANES))
        return found

    keys = [sides(part, 0) for part in parts]
    counts = [along(side) for part in parts for side in sides(part, 1)]
    rows = 8 * NEAR * far
    owner = iota((rows, LANES), 0) // 8 % NEAR * FIRMS_PER_SHARD
    keys = [[side + owner.astype(F32) for side in part] for part in keys]
    mine = jnp.concatenate(keys[0], axis=0)
    same = [mine[:, :1] == along(side) for part in keys for side in part]
    total = jnp.zeros((2 * rows, rows), F32)
    for k, (hit, count) in enumerate(zip(same, counts)):
        table[:, k * rows : (k + 1) * rows] = hit.astype(F32).astype(BF16)
        total += jnp.where(hit, count, 0.0)
    total = jnp.sum(total, axis=1, keepdims=True)
    scale[...] = jnp.broadcast_to(1.0 / jnp.maximum(total, 1.0), scale.shape)
    send[...] = owner_means([part[:, : 8 * NEAR] for part in parts], table[...], scale[...])


def owner_second_kernel(*refs):
    parts, (table, scale, send) = refs[:NEAR], refs[NEAR:]
    send[...] = owner_means([part[...] for part in parts], table[...], scale[...])


def change_kernel(received, own, own_count, pairs, send, mean):
    slots = own.shape[0]
    n = slots // 16
    found = from_tiles(received[...].reshape(n, 8, LANES))
    mean[...] = found
    change = dot(pairs[...], halves(found).astype(BF16))
    new = own[...] - own_count[...] * found + fold(change[:slots] + change[slots:])
    send[...] = to_tiles(new, n).reshape(send.shape)


def take(parts, ids, slots):
    spread = dot(parts, one_hot(ids, slots))
    columns = parts.shape[0] // 2
    return spread[:columns] + spread[columns:]


def first_kernel(pad, probes, mean, mask_ids, weight, out, x, y, in_sems, out_sems):
    ins, outs = column_copies(probes, x, in_sems), column_copies(y, out, out_sems)
    start_all(ins)
    slots = mean.shape[0]
    parts = halves(mean[...]).T.astype(BF16)
    table = same_worker(pad, 256)
    for b in range(len(ins)):
        ids = row(mask_ids, b, BLOCK)
        spread = take(parts, ids, slots)
        ins[b].wait()
        rest = jnp.where(ids >= 0, x[:, b * BLOCK : (b + 1) * BLOCK] - spread, 0.0)
        y[:, b * BLOCK : (b + 1) * BLOCK] = rest - by_worker(rest, table) * row(weight, b, BLOCK)
        outs[b].start()
    wait_all(outs)


def last_kernel(received, before, mask_ids, out, x, y, in_sems, out_sems):
    ins, outs = column_copies(before, x, in_sems), column_copies(y, out, out_sems)
    start_all(ins)
    mean = from_tiles(received[...].reshape(-1, 8, LANES))
    parts = halves(mean).T.astype(BF16)
    for b in range(len(ins)):
        spread = take(parts, row(mask_ids, b, BLOCK), mean.shape[0])
        ins[b].wait()
        y[:, b * BLOCK : (b + 1) * BLOCK] = x[:, b * BLOCK : (b + 1) * BLOCK] - spread
        outs[b].start()
    wait_all(outs)


def exchange(tiles, n):
    groups = [list(range(k, n, NEAR)) for k in range(NEAR)]
    return lax.all_to_all(tiles, "rows", split_axis=0, concat_axis=0, axis_index_groups=groups, tiled=True)


def share(part, n):
    return [part] + [lax.ppermute(part, "rows", [(i, i ^ k) for i in range(n)]) for k in range(1, NEAR)]


def call(kernel, out_shape, in_specs, out_specs, scratch, flops, moved):
    return pl.pallas_call(
        kernel,
        out_shape=out_shape,
        in_specs=in_specs,
        out_specs=out_specs,
        scratch_shapes=scratch,
        compiler_params=pltpu.CompilerParams(vmem_limit_bytes=VMEM_BYTES),
        cost_estimate=pl.CostEstimate(flops=flops, bytes_accessed=moved, transcendentals=0),
    )


def body(probes, worker_len, spell_to_slot, slot_to_firm, *, n):
    columns, rows_dev = probes.shape
    workers = worker_len.shape[0]
    pad = rows_dev // workers
    slots = slot_to_firm.shape[0]
    firm_tiles = slots // LANES
    blocks = rows_dev // BLOCK
    vmem, hbm = pl.BlockSpec(memory_space=pltpu.VMEM), pl.BlockSpec(memory_space=pltpu.HBM)
    lengths = worker_len.reshape(workers // LANES, LANES)
    ids = spell_to_slot.reshape(rows_dev // LANES, LANES)
    firms = slot_to_firm.reshape(firm_tiles, LANES)
    array = jax.ShapeDtypeStruct
    of_rows = (rows_dev // LANES, LANES)
    work = 2 * rows_dev * slots * 2 * columns
    sems = pltpu.SemaphoreType.DMA((blocks,))
    whole = pltpu.VMEM((columns, rows_dev), F32)
    of_slots = array((slots, LANES), F32)
    far = n // NEAR
    tiles, tiles_about = array((far, 8 * NEAR, LANES), F32), array((far, 8 * NEAR + 8, LANES), F32)
    mine = 16 * NEAR * far

    send, own, own_count, mask_ids, weight = call(
        functools.partial(sums_kernel, n, pad),
        [tiles_about, of_slots, of_slots, array(of_rows, jnp.int32), array(of_rows, F32)],
        [hbm] * 4,
        [vmem] * 5,
        [
            pltpu.VMEM(of_rows, F32),
            whole,
            pltpu.VMEM((slots, 2 * columns + 16), F32),
            pltpu.VMEM(lengths.shape, jnp.int32),
            pltpu.VMEM(ids.shape, jnp.int32),
            pltpu.VMEM(firms.shape, jnp.int32),
            sems,
            pltpu.SemaphoreType.DMA((3,)),
        ],
        2 * work,
        4 * columns * rows_dev,
    )(probes, lengths, ids, firms)
    received = share(exchange(send, n), n)
    pairs = call(
        functools.partial(worker_kernel, pad),
        array((2 * slots, slots), BF16),
        [vmem, vmem],
        vmem,
        [],
        2 * work,
        4 * slots * slots,
    )(lengths, mask_ids)
    send, table, scale = call(
        owner_first_kernel,
        [tiles, array((mine, NEAR * mine), BF16), array((mine, LANES), F32)],
        [vmem] * NEAR,
        [vmem] * 3,
        [],
        work // 16,
        slots * slots * 4,
    )(*received)
    received = exchange(send, n)
    send, mean = call(
        change_kernel,
        [tiles, of_slots],
        [vmem] * 4,
        [vmem] * 2,
        [],
        work // 16,
        slots * slots * 4,
    )(received, own, own_count, pairs)
    received = share(exchange(send, n), n)
    before = call(
        functools.partial(first_kernel, pad),
        array((columns, rows_dev), F32),
        [hbm, vmem, vmem, vmem],
        hbm,
        [whole, whole, sems, sems],
        2 * work,
        8 * columns * rows_dev,
    )(probes, mean, mask_ids, weight)
    send = call(
        owner_second_kernel,
        tiles,
        [vmem] * (NEAR + 2),
        vmem,
        [],
        work // 16,
        slots * slots * 4,
    )(*received, table, scale)
    received = exchange(send, n)
    return call(
        last_kernel,
        array((columns, rows_dev), F32),
        [vmem, hbm, vmem],
        hbm,
        [whole, whole, sems, sems],
        work,
        8 * columns * rows_dev,
    )(received, before, mask_ids)


def solution(mesh):
    placed = (P(None, ("grp", "rows")), P(("grp", "rows")), P(("grp", "rows")), P(("grp", "rows")))
    return jax.shard_map(
        functools.partial(body, n=mesh.shape["rows"]),
        mesh=mesh,
        in_specs=placed,
        out_specs=P(None, ("grp", "rows")),
        check_vma=False,
    )
```

```python
import functools

import jax
import jax.numpy as jnp
from jax import lax
from jax.experimental import pallas as pl
from jax.experimental.pallas import tpu as pltpu
from jax.sharding import PartitionSpec as P

FIRMS_PER_SHARD = 1024
LANES = 128
BLOCK = 1024
VMEM_BYTES = 40 * 1024 * 1024
NEAR = 4
F32, BF16 = jnp.float32, jnp.bfloat16
NT = (((1,), (1,)), ((), ()))
NN = (((1,), (0,)), ((), ()))


def dot(a, b, dims=NN):
    return lax.dot_general(a, b, dims, preferred_element_type=F32)


def iota(shape, dim):
    return lax.broadcasted_iota(jnp.int32, shape, dim)


def split(x):
    hi = x.astype(BF16)
    return hi, (x - hi.astype(F32)).astype(BF16)


def row(ref, block, size):
    per = size // LANES
    return jnp.concatenate([ref[block * per + k : block * per + k + 1, :] for k in range(per)], axis=1)


def one_hot(ids, slots):
    return (iota((slots, ids.shape[1]), 0) == ids).astype(F32).astype(BF16)


def same_worker(pad, width):
    return (iota((width, width), 0) // pad == iota((width, width), 1) // pad).astype(F32).astype(BF16)


def by_worker(x, table):
    rows, width = x.shape
    hi, lo = split(x)
    both = jnp.concatenate([hi, lo], axis=0)
    step = table.shape[0]
    total = jnp.concatenate([dot(both[:, k : k + step], table) for k in range(0, width, step)], axis=1)
    return total[:rows] + total[rows:]


def fold(x):
    return x + pltpu.roll(x, x.shape[1] // 2, axis=1)


def halves(x):
    hi, lo = split(x)
    return jnp.where(iota(x.shape, 1) < x.shape[1] // 2, hi.astype(F32), lo.astype(F32))


def column(firms):
    return jnp.concatenate(
        [jnp.broadcast_to(firms[k : k + 1, :], (LANES, LANES)).T for k in range(firms.shape[0])], axis=0
    )


def along(x):
    return jnp.concatenate([x[k : k + LANES].T[:1] for k in range(0, x.shape[0], LANES)], axis=1)


def left_of(shape):
    return iota(shape, len(shape) - 1) < LANES // 2


def to_tiles(x, n):
    x = x.reshape(n, 2, 8, LANES)
    return jnp.where(left_of((n, 8, LANES)), x[:, 0], x[:, 1])


def apart(tiles):
    turned = pltpu.roll(tiles, LANES // 2, axis=tiles.ndim - 1)
    left = left_of(tiles.shape)
    return jnp.where(left, tiles, turned), jnp.where(left, turned, tiles)


def from_tiles(tiles):
    n = tiles.shape[0]
    return jnp.stack(apart(tiles), axis=1).reshape(2 * 8 * n, LANES)


def start_all(copies):
    for copy in copies:
        copy.start()


def wait_all(copies):
    for copy in copies:
        copy.wait()


def place(tiles, sends):
    me = lax.axis_index("rows") // NEAR
    for k, send in enumerate(sends):
        send[...] = tiles[me ^ k]


def column_copies(source, target, sems):
    width = source.shape[1]
    cuts = [pl.ds(start, BLOCK) for start in range(0, width, BLOCK)]
    return [pltpu.make_async_copy(source.at[:, cut], target.at[:, cut], sems.at[b]) for b, cut in enumerate(cuts)]


def sums_kernel(n, pad, *refs):
    far = n // NEAR
    (probes, lengths_in, ids_in, firms_in), sends = refs[:4], refs[4 : 4 + far]
    own, own_count, mask_ids, weight, valid, x, acc, lengths, ids, firms, tiles, sems, small = refs[4 + far :]
    copies = column_copies(probes, x, sems)
    first = [
        pltpu.make_async_copy(source, target, small.at[k])
        for k, (source, target) in enumerate(((lengths_in, lengths), (ids_in, ids), (firms_in, firms)))
    ]
    start_all(first)
    start_all(copies)
    slots = own.shape[0]
    total_rows = ids.shape[0]
    here = iota((total_rows, LANES), 0)
    lane = iota((total_rows, LANES), 1)
    wait_all(first)
    wide = jnp.broadcast_to(
        lengths[...].astype(F32)[:, None, :], (lengths.shape[0], total_rows // lengths.shape[0], LANES)
    ).reshape(total_rows, LANES)
    per = LANES // pad
    wide = jnp.where(lane // per == here % pad, wide, 0.0).astype(BF16)
    spread = (iota((LANES, LANES), 0) % per == iota((LANES, LANES), 1) // pad).astype(F32).astype(BF16)
    row_len = dot(wide, spread)
    inside = (lane % pad).astype(F32) < row_len
    valid[...] = jnp.where(inside, 1.0, 0.0)
    weight[...] = jnp.where(inside, 1.0 / row_len, 0.0)
    mask_ids[...] = jnp.where(inside, ids[...], -1)

    table = same_worker(pad, 256)
    for b in range(len(copies)):
        copies[b].wait()
        ok = row(valid, b, BLOCK)
        x0 = x[:, b * BLOCK : (b + 1) * BLOCK] * ok
        x1 = x0 - by_worker(x0, table) * row(weight, b, BLOCK)
        hi, lo = split(x1)
        counted = jnp.broadcast_to(ok, (16, BLOCK)).astype(BF16)
        data = jnp.concatenate([hi, lo, counted], axis=0)
        part = dot(one_hot(row(mask_ids, b, BLOCK), slots), data, NT)
        if b == 0:
            acc[...] = part
        else:
            acc[...] += part
    both = fold(acc[:, :LANES])
    own[...] = both
    count = jnp.broadcast_to(acc[:, LANES : LANES + 1], (slots, LANES))
    own_count[...] = count
    tiles[:, : 8 * NEAR] = to_tiles(both, n).reshape(far, 8 * NEAR, LANES)
    about = jnp.where(iota((slots, LANES), 1) % 16 < 8, column(firms[...].astype(F32)), count)
    about = about.reshape(far, NEAR, 2, 8, LANES)
    eighth = iota((far, 8, LANES), 2) // 8
    packed = about[:, 0, 0]
    for owner in range(NEAR):
        for side in range(2):
            packed = jnp.where(eighth // 2 == 2 * owner + side, about[:, owner, side], packed)
    tiles[:, 8 * NEAR :] = packed
    place(tiles, sends)


def join_kernel(*refs):
    for k, part in enumerate(refs[:-1]):
        refs[-1][k] = part[...]


def worker_kernel(pad, lengths, mask_ids, out):
    slots = out.shape[1]
    workers = lengths.shape[0] * LANES
    group = 256
    rows_group = group * pad
    pick = (iota((rows_group, group), 0) // pad == iota((rows_group, group), 1)).astype(F32).astype(BF16)
    total = jnp.zeros((2 * slots, slots), F32)
    for g in range(workers // group):
        counts = dot(one_hot(row(mask_ids, g, rows_group), slots), pick)
        inverse = 1.0 / row(lengths, g, group).astype(F32)
        hi, lo = split(counts * inverse)
        total += dot(jnp.concatenate([hi, lo], axis=0), counts.astype(BF16), NT)
    hi, lo = split(total[:slots] + total[slots:])
    out[:slots] = hi
    out[slots:] = lo


def owner_means(parts, table, scale):
    rows = 8 * NEAR * parts[0].shape[0]
    data = [apart(part.reshape(rows, LANES)) for part in parts]
    data = [halves(side) for sides in data for side in sides]
    total = fold(dot(table, jnp.concatenate(data, axis=0).astype(BF16))) * scale
    return jnp.where(left_of((rows, LANES)), total[:rows], total[rows:]).reshape(parts[0].shape)


def owner_first_kernel(*refs):
    parts, sends, (table, scale) = refs[:NEAR], refs[NEAR:-2], refs[-2:]
    far = len(sends)

    def sides(part, kind):
        about = part[:, 8 * NEAR :].reshape(8 * far, LANES)
        found = []
        for side in range(2):
            one = [
                jnp.broadcast_to(about[:, at : at + 1], (8 * far, LANES)).reshape(far, 1, 8, LANES)
                for at in (16 * (2 * owner + side) + 8 * kind for owner in range(NEAR))
            ]
            found.append(jnp.concatenate(one, axis=1).reshape(8 * NEAR * far, LANES))
        return found

    keys = [sides(part, 0) for part in parts]
    counts = [along(side) for part in parts for side in sides(part, 1)]
    rows = 8 * NEAR * far
    owner = iota((rows, LANES), 0) // 8 % NEAR * FIRMS_PER_SHARD
    keys = [[side + owner.astype(F32) for side in part] for part in keys]
    mine = jnp.concatenate(keys[0], axis=0)
    same = [mine[:, :1] == along(side) for part in keys for side in part]
    total = jnp.zeros((2 * rows, rows), F32)
    for k, (hit, count) in enumerate(zip(same, counts)):
        table[:, k * rows : (k + 1) * rows] = hit.astype(F32).astype(BF16)
        total += jnp.where(hit, count, 0.0)
    total = jnp.sum(total, axis=1, keepdims=True)
    scale[...] = jnp.broadcast_to(1.0 / jnp.maximum(total, 1.0), scale.shape)
    means = owner_means([part[:, : 8 * NEAR] for part in parts], table[...], scale[...])
    for k, send in enumerate(sends):
        send[...] = means[k]


def owner_second_kernel(*refs):
    parts, (table, scale), sends = refs[:NEAR], refs[NEAR : NEAR + 2], refs[NEAR + 2 :]
    means = owner_means([part[...] for part in parts], table[...], scale[...])
    for k, send in enumerate(sends):
        send[...] = means[k]


def own_means(parts, tiles):
    me = lax.axis_index("rows") // NEAR
    for k, part in enumerate(parts):
        tiles[me ^ k] = part[...]
    return from_tiles(tiles[...].reshape(len(parts) * NEAR, 8, LANES))


def change_kernel(far, *refs):
    parts, (own, own_count, pairs), sends, (mean, tiles) = (
        refs[:far], refs[far : far + 3], refs[far + 3 : 2 * far + 3], refs[2 * far + 3 :]
    )
    slots = own.shape[0]
    found = own_means(parts, tiles)
    mean[...] = found
    change = dot(pairs[...], halves(found).astype(BF16))
    new = own[...] - own_count[...] * found + fold(change[:slots] + change[slots:])
    tiles[...] = to_tiles(new, far * NEAR).reshape(tiles.shape)
    place(tiles, sends)


def take(parts, ids, slots):
    spread = dot(parts, one_hot(ids, slots))
    columns = parts.shape[0] // 2
    return spread[:columns] + spread[columns:]


def first_kernel(pad, probes, mean, mask_ids, weight, y, x, sems):
    ins = column_copies(probes, x, sems)
    start_all(ins)
    slots = mean.shape[0]
    parts = halves(mean[...]).T.astype(BF16)
    table = same_worker(pad, 256)
    for b in range(len(ins)):
        ids = row(mask_ids, b, BLOCK)
        spread = take(parts, ids, slots)
        ins[b].wait()
        rest = jnp.where(ids >= 0, x[:, b * BLOCK : (b + 1) * BLOCK] - spread, 0.0)
        y[:, b * BLOCK : (b + 1) * BLOCK] = rest - by_worker(rest, table) * row(weight, b, BLOCK)


def last_kernel(far, *refs):
    parts, (before, mask_ids, out, tiles, y, sems) = refs[:far], refs[far:]
    outs = column_copies(y, out, sems)
    mean = own_means(parts, tiles)
    split_mean = halves(mean).T.astype(BF16)
    for b in range(len(outs)):
        spread = take(split_mean, row(mask_ids, b, BLOCK), mean.shape[0])
        y[:, b * BLOCK : (b + 1) * BLOCK] = before[:, b * BLOCK : (b + 1) * BLOCK] - spread
        outs[b].start()
    wait_all(outs)


def exchange(parts, n):
    steps = [[(i, i ^ (k * NEAR)) for i in range(n)] for k in range(len(parts))]
    return [parts[0]] + [lax.ppermute(part, "rows", step) for part, step in zip(parts[1:], steps[1:])]


def share(part, n):
    return [part] + [lax.ppermute(part, "rows", [(i, i ^ k) for i in range(n)]) for k in range(1, NEAR)]


def in_hbm(x):
    return pltpu.with_memory_space_constraint(x, pltpu.HBM)


def call(kernel, out_shape, in_specs, out_specs, scratch, flops, moved):
    return pl.pallas_call(
        kernel,
        out_shape=out_shape,
        in_specs=in_specs,
        out_specs=out_specs,
        scratch_shapes=scratch,
        compiler_params=pltpu.CompilerParams(vmem_limit_bytes=VMEM_BYTES),
        cost_estimate=pl.CostEstimate(flops=flops, bytes_accessed=moved, transcendentals=0),
    )


def body(probes, worker_len, spell_to_slot, slot_to_firm, *, n):
    columns, rows_dev = probes.shape
    workers = worker_len.shape[0]
    pad = rows_dev // workers
    slots = slot_to_firm.shape[0]
    firm_tiles = slots // LANES
    blocks = rows_dev // BLOCK
    vmem, hbm = pl.BlockSpec(memory_space=pltpu.VMEM), pl.BlockSpec(memory_space=pltpu.HBM)
    lengths = worker_len.reshape(workers // LANES, LANES)
    ids = spell_to_slot.reshape(rows_dev // LANES, LANES)
    firms = slot_to_firm.reshape(firm_tiles, LANES)
    array = jax.ShapeDtypeStruct
    of_rows = (rows_dev // LANES, LANES)
    work = 2 * rows_dev * slots * 2 * columns
    sems = pltpu.SemaphoreType.DMA((blocks,))
    whole = pltpu.VMEM((columns, rows_dev), F32)
    of_slots = array((slots, LANES), F32)
    far = n // NEAR
    tile, tile_about = array((8 * NEAR, LANES), F32), array((8 * NEAR + 8, LANES), F32)
    tiles = pltpu.VMEM((far, 8 * NEAR, LANES), F32)
    mine = 16 * NEAR * far

    *sends, own, own_count, mask_ids, weight = call(
        functools.partial(sums_kernel, n, pad),
        [tile_about] * far + [of_slots, of_slots, array(of_rows, jnp.int32), array(of_rows, F32)],
        [hbm] * 4,
        [vmem] * (far + 4),
        [
            pltpu.VMEM(of_rows, F32),
            whole,
            pltpu.VMEM((slots, 2 * columns + 16), F32),
            pltpu.VMEM(lengths.shape, jnp.int32),
            pltpu.VMEM(ids.shape, jnp.int32),
            pltpu.VMEM(firms.shape, jnp.int32),
            pltpu.VMEM((far, 8 * NEAR + 8, LANES), F32),
            sems,
            pltpu.SemaphoreType.DMA((3,)),
        ],
        2 * work,
        4 * columns * rows_dev,
    )(in_hbm(probes), in_hbm(lengths), in_hbm(ids), in_hbm(firms))

    def join(parts):
        shape = array((far, *parts[0].shape), F32)
        return call(join_kernel, shape, [vmem] * far, vmem, [], 0, shape.size * 8)(*parts)

    received = share(join(exchange(sends, n)), n)
    pairs = call(
        functools.partial(worker_kernel, pad),
        array((2 * slots, slots), BF16),
        [vmem, vmem],
        vmem,
        [],
        2 * work,
        4 * slots * slots,
    )(lengths, mask_ids)
    *sends, table, scale = call(
        owner_first_kernel,
        [tile] * far + [array((mine, NEAR * mine), BF16), array((mine, LANES), F32)],
        [vmem] * NEAR,
        [vmem] * (far + 2),
        [],
        work // 16,
        slots * slots * 4,
    )(*received)
    received = exchange(sends, n)
    *sends, mean = call(
        functools.partial(change_kernel, far),
        [tile] * far + [of_slots],
        [vmem] * (far + 3),
        [vmem] * (far + 1),
        [tiles],
        work // 16,
        slots * slots * 4,
    )(*received, own, own_count, pairs)
    received = share(join(exchange(sends, n)), n)
    before = call(
        functools.partial(first_kernel, pad),
        array((columns, rows_dev), F32),
        [hbm, vmem, vmem, vmem],
        vmem,
        [whole, sems],
        2 * work,
        8 * columns * rows_dev,
    )(in_hbm(probes), mean, mask_ids, weight)
    sends = call(
        owner_second_kernel,
        [tile] * far,
        [vmem] * (NEAR + 2),
        [vmem] * far,
        [],
        work // 16,
        slots * slots * 4,
    )(*received, table, scale)
    received = exchange(sends, n)
    return call(
        functools.partial(last_kernel, far),
        array((columns, rows_dev), F32),
        [vmem] * (far + 2),
        hbm,
        [tiles, whole, sems],
        work,
        8 * columns * rows_dev,
    )(*received, before, mask_ids)


def solution(mesh):
    placed = (P(None, ("grp", "rows")), P(("grp", "rows")), P(("grp", "rows")), P(("grp", "rows")))
    return jax.shard_map(
        functools.partial(body, n=mesh.shape["rows"]),
        mesh=mesh,
        in_specs=placed,
        out_specs=P(None, ("grp", "rows")),
        check_vma=False,
    )
```

```python
import functools

import jax
import jax.numpy as jnp
from jax import lax
from jax.experimental import pallas as pl
from jax.experimental.pallas import tpu as pltpu
from jax.sharding import PartitionSpec as P

FIRMS_PER_SHARD = 1024
LANES = 128
BLOCK = 1024
VMEM_BYTES = 40 * 1024 * 1024
NEAR = 4
F32, BF16 = jnp.float32, jnp.bfloat16
NT = (((1,), (1,)), ((), ()))
NN = (((1,), (0,)), ((), ()))


def dot(a, b, dims=NN):
    return lax.dot_general(a, b, dims, preferred_element_type=F32)


def iota(shape, dim):
    return lax.broadcasted_iota(jnp.int32, shape, dim)


def split(x):
    hi = x.astype(BF16)
    return hi, (x - hi.astype(F32)).astype(BF16)


def row(ref, block, size):
    per = size // LANES
    return jnp.concatenate([ref[block * per + k : block * per + k + 1, :] for k in range(per)], axis=1)


def one_hot(ids, slots):
    kind = BF16 if slots <= 256 else F32
    slot = iota((slots, LANES), 0).astype(F32).astype(kind)
    ids = ids.astype(F32).astype(kind)
    one, zero = jnp.ones((slots, LANES), kind), jnp.zeros((slots, LANES), kind)
    parts = [jnp.where(slot == ids[:, k : k + LANES], one, zero) for k in range(0, ids.shape[1], LANES)]
    return jnp.concatenate(parts, axis=1).astype(BF16)


def same_worker(pad, width):
    return (iota((width, width), 0) // pad == iota((width, width), 1) // pad).astype(F32).astype(BF16)


def by_worker(x, table):
    rows, width = x.shape
    hi, lo = split(x)
    both = jnp.concatenate([hi, lo], axis=0)
    step = table.shape[0]
    total = jnp.concatenate([dot(both[:, k : k + step], table) for k in range(0, width, step)], axis=1)
    return total[:rows] + total[rows:]


def fold(x):
    return x + pltpu.roll(x, x.shape[1] // 2, axis=1)


def halves(x):
    hi, lo = split(x)
    return jnp.where(iota(x.shape, 1) < x.shape[1] // 2, hi.astype(F32), lo.astype(F32))


def column(firms):
    return jnp.concatenate(
        [jnp.broadcast_to(firms[k : k + 1, :], (LANES, LANES)).T for k in range(firms.shape[0])], axis=0
    )


def along(x):
    return jnp.concatenate([x[k : k + LANES].T[:1] for k in range(0, x.shape[0], LANES)], axis=1)


def left_of(shape):
    return iota(shape, len(shape) - 1) < LANES // 2


def to_tiles(x, n):
    x = x.reshape(n, 2, 8, LANES)
    return jnp.where(left_of((n, 8, LANES)), x[:, 0], x[:, 1])


def apart(tiles):
    turned = pltpu.roll(tiles, LANES // 2, axis=tiles.ndim - 1)
    left = left_of(tiles.shape)
    return jnp.where(left, tiles, turned), jnp.where(left, turned, tiles)


def from_tiles(tiles):
    n = tiles.shape[0]
    return jnp.stack(apart(tiles), axis=1).reshape(2 * 8 * n, LANES)


def start_all(copies):
    for copy in copies:
        copy.start()


def wait_all(copies):
    for copy in copies:
        copy.wait()


def place(tiles, sends):
    me = lax.axis_index("rows") // NEAR
    for k, send in enumerate(sends):
        send[...] = tiles[me ^ k]


def column_copies(source, target, sems):
    width = source.shape[1]
    cuts = [pl.ds(start, BLOCK) for start in range(0, width, BLOCK)]
    return [pltpu.make_async_copy(source.at[:, cut], target.at[:, cut], sems.at[b]) for b, cut in enumerate(cuts)]


def sums_kernel(n, pad, *refs):
    far = n // NEAR
    (probes, lengths_in, ids_in, firms_in), sends = refs[:4], refs[4 : 4 + far]
    own, own_count, mask_ids, weight, valid, x, acc, lengths, ids, firms, tiles, sems, small = refs[4 + far :]
    copies = column_copies(probes, x, sems)
    first = [
        pltpu.make_async_copy(source, target, small.at[k])
        for k, (source, target) in enumerate(((lengths_in, lengths), (ids_in, ids), (firms_in, firms)))
    ]
    start_all(first)
    start_all(copies)
    slots = own.shape[0]
    total_rows = ids.shape[0]
    here = iota((total_rows, LANES), 0)
    lane = iota((total_rows, LANES), 1)
    wait_all(first)
    wide = jnp.broadcast_to(
        lengths[...].astype(F32)[:, None, :], (lengths.shape[0], total_rows // lengths.shape[0], LANES)
    ).reshape(total_rows, LANES)
    per = LANES // pad
    wide = jnp.where(lane // per == here % pad, wide, 0.0).astype(BF16)
    spread = (iota((LANES, LANES), 0) % per == iota((LANES, LANES), 1) // pad).astype(F32).astype(BF16)
    row_len = dot(wide, spread)
    inside = (lane % pad).astype(F32) < row_len
    valid[...] = jnp.where(inside, 1.0, 0.0)
    weight[...] = jnp.where(inside, 1.0 / row_len, 0.0)
    mask_ids[...] = jnp.where(inside, ids[...], -1)

    table = same_worker(pad, 256)
    for b in range(len(copies)):
        copies[b].wait()
        ok = row(valid, b, BLOCK)
        x0 = x[:, b * BLOCK : (b + 1) * BLOCK] * ok
        x1 = x0 - by_worker(x0, table) * row(weight, b, BLOCK)
        hi, lo = split(x1)
        counted = jnp.broadcast_to(ok, (16, BLOCK)).astype(BF16)
        data = jnp.concatenate([hi, lo, counted], axis=0)
        part = dot(one_hot(row(mask_ids, b, BLOCK), slots), data, NT)
        if b == 0:
            acc[...] = part
        else:
            acc[...] += part
    both = fold(acc[:, :LANES])
    own[...] = both
    count = jnp.broadcast_to(acc[:, LANES : LANES + 1], (slots, LANES))
    own_count[...] = count
    tiles[:, : 8 * NEAR] = to_tiles(both, n).reshape(far, 8 * NEAR, LANES)
    about = jnp.where(iota((slots, LANES), 1) % 16 < 8, column(firms[...].astype(F32)), count)
    about = about.reshape(far, NEAR, 2, 8, LANES)
    eighth = iota((far, 8, LANES), 2) // 8
    packed = about[:, 0, 0]
    for owner in range(NEAR):
        for side in range(2):
            packed = jnp.where(eighth // 2 == 2 * owner + side, about[:, owner, side], packed)
    tiles[:, 8 * NEAR :] = packed
    place(tiles, sends)


def join_kernel(*refs):
    for k, part in enumerate(refs[:-1]):
        refs[-1][k] = part[...]


def worker_kernel(pad, lengths, mask_ids, out):
    slots = out.shape[1]
    workers = lengths.shape[0] * LANES
    group = 256
    rows_group = group * pad
    pick = (iota((rows_group, group), 0) // pad == iota((rows_group, group), 1)).astype(F32).astype(BF16)
    total = jnp.zeros((2 * slots, slots), F32)
    for g in range(workers // group):
        counts = dot(one_hot(row(mask_ids, g, rows_group), slots), pick)
        inverse = 1.0 / row(lengths, g, group).astype(F32)
        hi, lo = split(counts * inverse)
        total += dot(jnp.concatenate([hi, lo], axis=0), counts.astype(BF16), NT)
    hi, lo = split(total[:slots] + total[slots:])
    out[:slots] = hi
    out[slots:] = lo


def owner_means(parts, table, scale):
    rows = 8 * NEAR * parts[0].shape[0]
    data = [apart(part.reshape(rows, LANES)) for part in parts]
    data = [halves(side) for sides in data for side in sides]
    total = fold(dot(table, jnp.concatenate(data, axis=0).astype(BF16))) * scale
    return jnp.where(left_of((rows, LANES)), total[:rows], total[rows:]).reshape(parts[0].shape)


def owner_first_kernel(*refs):
    parts, sends, (table, scale) = refs[:NEAR], refs[NEAR + 1 : -2], refs[-2:]
    far = len(sends)

    def sides(part, kind):
        about = part[:, 8 * NEAR :].reshape(8 * far, LANES)
        found = []
        for side in range(2):
            one = [
                jnp.broadcast_to(about[:, at : at + 1], (8 * far, LANES)).reshape(far, 1, 8, LANES)
                for at in (16 * (2 * owner + side) + 8 * kind for owner in range(NEAR))
            ]
            found.append(jnp.concatenate(one, axis=1).reshape(8 * NEAR * far, LANES))
        return found

    keys = [sides(part, 0) for part in parts]
    counts = [along(side) for part in parts for side in sides(part, 1)]
    rows = 8 * NEAR * far
    owner = iota((rows, LANES), 0) // 8 % NEAR * FIRMS_PER_SHARD
    keys = [[side + owner.astype(F32) for side in part] for part in keys]
    mine = jnp.concatenate(keys[0], axis=0)
    same = [mine[:, :1] == along(side) for part in keys for side in part]
    total = jnp.zeros((2 * rows, rows), F32)
    for k, (hit, count) in enumerate(zip(same, counts)):
        table[:, k * rows : (k + 1) * rows] = hit.astype(F32).astype(BF16)
        total += jnp.where(hit, count, 0.0)
    total = jnp.sum(total, axis=1, keepdims=True)
    scale[...] = jnp.broadcast_to(1.0 / jnp.maximum(total, 1.0), scale.shape)
    means = owner_means([part[:, : 8 * NEAR] for part in parts], table[...], scale[...])
    for k, send in enumerate(sends):
        send[...] = means[k]


def owner_second_kernel(*refs):
    parts, (table, scale), sends = refs[:NEAR], refs[NEAR : NEAR + 2], refs[NEAR + 3 :]
    means = owner_means([part[...] for part in parts], table[...], scale[...])
    for k, send in enumerate(sends):
        send[...] = means[k]


def own_means(parts, tiles):
    me = lax.axis_index("rows") // NEAR
    for k, part in enumerate(parts):
        tiles[me ^ k] = part[...]
    return from_tiles(tiles[...].reshape(len(parts) * NEAR, 8, LANES))


def change_kernel(far, *refs):
    parts, (own, own_count, pairs), sends, (mean, tiles) = (
        refs[:far], refs[far : far + 3], refs[far + 3 : 2 * far + 3], refs[2 * far + 3 :]
    )
    slots = own.shape[0]
    found = own_means(parts, tiles)
    mean[...] = found
    change = dot(pairs[...], halves(found).astype(BF16))
    new = own[...] - own_count[...] * found + fold(change[:slots] + change[slots:])
    tiles[...] = to_tiles(new, far * NEAR).reshape(tiles.shape)
    place(tiles, sends)


def take(parts, ids, slots):
    spread = dot(parts, one_hot(ids, slots))
    columns = parts.shape[0] // 2
    return spread[:columns] + spread[columns:]


def first_kernel(pad, start, probes, mean, mask_ids, weight, y, x, sems):
    ins = column_copies(probes.at[:, pl.ds(start * BLOCK, y.shape[1])], x, sems)
    start_all(ins)
    slots = mean.shape[0]
    parts = halves(mean[...]).T.astype(BF16)
    table = same_worker(pad, 256)
    for b in range(len(ins)):
        ids = row(mask_ids, start + b, BLOCK)
        spread = take(parts, ids, slots)
        ins[b].wait()
        rest = jnp.where(ids >= 0, x[:, b * BLOCK : (b + 1) * BLOCK] - spread, 0.0)
        y[:, b * BLOCK : (b + 1) * BLOCK] = rest - by_worker(rest, table) * row(weight, start + b, BLOCK)


def last_kernel(far, *refs):
    parts, (before, after, mask_ids, out, tiles, y, sems) = refs[:far], refs[far:]
    cut = before.shape[1] // BLOCK
    outs = column_copies(y, out, sems)
    mean = own_means(parts, tiles)
    split_mean = halves(mean).T.astype(BF16)
    for b in range(len(outs)):
        spread = take(split_mean, row(mask_ids, b, BLOCK), mean.shape[0])
        source, at = (before, b) if b < cut else (after, b - cut)
        y[:, b * BLOCK : (b + 1) * BLOCK] = source[:, at * BLOCK : (at + 1) * BLOCK] - spread
        outs[b].start()
    wait_all(outs)


def exchange(parts, n):
    steps = [[(i, i ^ (k * NEAR)) for i in range(n)] for k in range(len(parts))]
    return [parts[0]] + [lax.ppermute(part, "rows", step) for part, step in zip(parts[1:], steps[1:])]


def share(part, n):
    return [part] + [lax.ppermute(part, "rows", [(i, i ^ k) for i in range(n)]) for k in range(1, NEAR)]


def in_hbm(x):
    return pltpu.with_memory_space_constraint(x, pltpu.HBM)


def call(kernel, out_shape, in_specs, out_specs, scratch, flops, moved):
    return pl.pallas_call(
        kernel,
        out_shape=out_shape,
        in_specs=in_specs,
        out_specs=out_specs,
        scratch_shapes=scratch,
        compiler_params=pltpu.CompilerParams(vmem_limit_bytes=VMEM_BYTES),
        cost_estimate=pl.CostEstimate(flops=flops, bytes_accessed=moved, transcendentals=0),
    )


def body(probes, worker_len, spell_to_slot, slot_to_firm, *, n):
    columns, rows_dev = probes.shape
    workers = worker_len.shape[0]
    pad = rows_dev // workers
    slots = slot_to_firm.shape[0]
    firm_tiles = slots // LANES
    blocks = rows_dev // BLOCK
    vmem, hbm = pl.BlockSpec(memory_space=pltpu.VMEM), pl.BlockSpec(memory_space=pltpu.HBM)
    lengths = worker_len.reshape(workers // LANES, LANES)
    ids = spell_to_slot.reshape(rows_dev // LANES, LANES)
    firms = slot_to_firm.reshape(firm_tiles, LANES)
    array = jax.ShapeDtypeStruct
    of_rows = (rows_dev // LANES, LANES)
    work = 2 * rows_dev * slots * 2 * columns
    sems = pltpu.SemaphoreType.DMA((blocks,))
    whole = pltpu.VMEM((columns, rows_dev), F32)
    of_slots = array((slots, LANES), F32)
    far = n // NEAR
    tile, tile_about = array((8 * NEAR, LANES), F32), array((8 * NEAR + 8, LANES), F32)
    tiles = pltpu.VMEM((far, 8 * NEAR, LANES), F32)
    mine = 16 * NEAR * far

    *sends, own, own_count, mask_ids, weight = call(
        functools.partial(sums_kernel, n, pad),
        [tile_about] * far + [of_slots, of_slots, array(of_rows, jnp.int32), array(of_rows, F32)],
        [hbm] * 4,
        [vmem] * (far + 4),
        [
            pltpu.VMEM(of_rows, F32),
            whole,
            pltpu.VMEM((slots, 2 * columns + 16), F32),
            pltpu.VMEM(lengths.shape, jnp.int32),
            pltpu.VMEM(ids.shape, jnp.int32),
            pltpu.VMEM(firms.shape, jnp.int32),
            pltpu.VMEM((far, 8 * NEAR + 8, LANES), F32),
            sems,
            pltpu.SemaphoreType.DMA((3,)),
        ],
        2 * work,
        4 * columns * rows_dev,
    )(in_hbm(probes), in_hbm(lengths), in_hbm(ids), in_hbm(firms))

    def join(parts):
        shape = array((far, *parts[0].shape), F32)
        return call(join_kernel, shape, [vmem] * far, vmem, [], 0, shape.size * 8)(*parts)

    received = share(join(exchange(sends, n)), n)
    pairs = call(
        functools.partial(worker_kernel, pad),
        array((2 * slots, slots), BF16),
        [vmem, vmem],
        vmem,
        [],
        2 * work,
        4 * slots * slots,
    )(lengths, mask_ids)
    *sends, table, scale = call(
        owner_first_kernel,
        [tile] * far + [array((mine, NEAR * mine), BF16), array((mine, LANES), F32)],
        [vmem] * (NEAR + 1),
        [vmem] * (far + 2),
        [],
        work // 16,
        slots * slots * 4,
    )(*received, pairs)
    received = exchange(sends, n)
    *sends, mean = call(
        functools.partial(change_kernel, far),
        [tile] * far + [of_slots],
        [vmem] * (far + 3),
        [vmem] * (far + 1),
        [tiles],
        work // 16,
        slots * slots * 4,
    )(*received, own, own_count, pairs)
    received = share(join(exchange(sends, n)), n)

    def first(start, stop):
        width = (stop - start) * BLOCK
        return call(
            functools.partial(first_kernel, pad, start),
            array((columns, width), F32),
            [hbm, vmem, vmem, vmem],
            vmem,
            [pltpu.VMEM((columns, width), F32), sems],
            2 * work * (stop - start) // blocks,
            8 * columns * width,
        )(in_hbm(probes), mean, mask_ids, weight)

    before, after = first(0, 5 * blocks // 8), first(5 * blocks // 8, blocks)
    sends = call(
        owner_second_kernel,
        [tile] * far,
        [vmem] * (NEAR + 3),
        [vmem] * far,
        [],
        work // 16,
        slots * slots * 4,
    )(*received, table, scale, before)
    received = exchange(sends, n)
    return call(
        functools.partial(last_kernel, far),
        array((columns, rows_dev), F32),
        [vmem] * (far + 3),
        hbm,
        [tiles, whole, sems],
        work,
        8 * columns * rows_dev,
    )(*received, before, after, mask_ids)


def solution(mesh):
    placed = (P(None, ("grp", "rows")), P(("grp", "rows")), P(("grp", "rows")), P(("grp", "rows")))
    return jax.shard_map(
        functools.partial(body, n=mesh.shape["rows"]),
        mesh=mesh,
        in_specs=placed,
        out_specs=P(None, ("grp", "rows")),
        check_vma=False,
    )
```

```python
import functools

import jax
import jax.numpy as jnp
from jax import lax
from jax.experimental import pallas as pl
from jax.experimental.pallas import tpu as pltpu
from jax.sharding import PartitionSpec as P

FIRMS_PER_SHARD = 1024
LANES = 128
BLOCK = 1024
VMEM_BYTES = 40 * 1024 * 1024
NEAR = 4
F32, BF16 = jnp.float32, jnp.bfloat16
NT = (((1,), (1,)), ((), ()))
NN = (((1,), (0,)), ((), ()))


def dot(a, b, dims=NN):
    return lax.dot_general(a, b, dims, preferred_element_type=F32)


def iota(shape, dim):
    return lax.broadcasted_iota(jnp.int32, shape, dim)


def split(x):
    hi = x.astype(BF16)
    return hi, (x - hi.astype(F32)).astype(BF16)


def row(ref, block, size):
    per = size // LANES
    return jnp.concatenate([ref[block * per + k : block * per + k + 1, :] for k in range(per)], axis=1)


def one_hot(ids, slots):
    kind = BF16 if slots <= 256 else F32
    slot = iota((slots, LANES), 0).astype(F32).astype(kind)
    ids = ids.astype(F32).astype(kind)
    one, zero = jnp.ones((slots, LANES), kind), jnp.zeros((slots, LANES), kind)
    parts = [jnp.where(slot == ids[:, k : k + LANES], one, zero) for k in range(0, ids.shape[1], LANES)]
    return jnp.concatenate(parts, axis=1).astype(BF16)


def same_worker(pad, width):
    return (iota((width, width), 0) // pad == iota((width, width), 1) // pad).astype(F32).astype(BF16)


def by_worker(x, table):
    rows, width = x.shape
    hi, lo = split(x)
    both = jnp.concatenate([hi, lo], axis=0)
    step = table.shape[0]
    total = jnp.concatenate([dot(both[:, k : k + step], table) for k in range(0, width, step)], axis=1)
    return total[:rows] + total[rows:]


def fold(x):
    return x + pltpu.roll(x, x.shape[1] // 2, axis=1)


def halves(x):
    hi, lo = split(x)
    return jnp.where(iota(x.shape, 1) < x.shape[1] // 2, hi.astype(F32), lo.astype(F32))


def column(firms):
    return jnp.concatenate(
        [jnp.broadcast_to(firms[k : k + 1, :], (LANES, LANES)).T for k in range(firms.shape[0])], axis=0
    )


def along(x):
    return jnp.concatenate([x[k : k + LANES].T[:1] for k in range(0, x.shape[0], LANES)], axis=1)


def left_of(shape):
    return iota(shape, len(shape) - 1) < LANES // 2


def to_tiles(x, n):
    x = x.reshape(n, 2, 8, LANES)
    return jnp.where(left_of((n, 8, LANES)), x[:, 0], x[:, 1])


def apart(tiles):
    turned = pltpu.roll(tiles, LANES // 2, axis=tiles.ndim - 1)
    left = left_of(tiles.shape)
    return jnp.where(left, tiles, turned), jnp.where(left, turned, tiles)


def from_tiles(tiles):
    n = tiles.shape[0]
    return jnp.stack(apart(tiles), axis=1).reshape(2 * 8 * n, LANES)


def start_all(copies):
    for copy in copies:
        copy.start()


def wait_all(copies):
    for copy in copies:
        copy.wait()


def senders(far):
    left = [group for group in range(far) if group != far // 2 - 1]
    return left, [far - 1 - group for group in left]


def place(halves_of, sends):
    far = len(sends)
    me = lax.axis_index("rows") // NEAR
    for send, group in zip(sends, [far // 2 - 1] + senders(far)[0]):
        send[...] = halves_of[jnp.where(me == group, 0, 1)]


def own_means(parts, tiles):
    far = len(parts)
    me = lax.axis_index("rows") // NEAR
    for k, part in enumerate(parts):
        tiles[k] = part[...]
    found = []
    for steps in senders(far):
        at = 0
        for k, group in enumerate(steps):
            at += jnp.where(me == group, k + 1, 0)
        found.append(tiles[at])
    return from_tiles(jnp.concatenate(found, axis=0).reshape(-1, 8, LANES))


def column_copies(source, target, sems):
    width = source.shape[1]
    cuts = [pl.ds(start, BLOCK) for start in range(0, width, BLOCK)]
    return [pltpu.make_async_copy(source.at[:, cut], target.at[:, cut], sems.at[b]) for b, cut in enumerate(cuts)]


def sums_kernel(n, pad, *refs):
    far = n // NEAR
    (probes, lengths_in, ids_in, firms_in), sends = refs[:4], refs[4 : 4 + far]
    own, own_count, mask_ids, weight, valid, x, acc, lengths, ids, firms, tiles, sems, small = refs[4 + far :]
    copies = column_copies(probes, x, sems)
    first = [
        pltpu.make_async_copy(source, target, small.at[k])
        for k, (source, target) in enumerate(((lengths_in, lengths), (ids_in, ids), (firms_in, firms)))
    ]
    start_all(first)
    start_all(copies)
    slots = own.shape[0]
    total_rows = ids.shape[0]
    here = iota((total_rows, LANES), 0)
    lane = iota((total_rows, LANES), 1)
    wait_all(first)
    wide = jnp.broadcast_to(
        lengths[...].astype(F32)[:, None, :], (lengths.shape[0], total_rows // lengths.shape[0], LANES)
    ).reshape(total_rows, LANES)
    per = LANES // pad
    wide = jnp.where(lane // per == here % pad, wide, 0.0).astype(BF16)
    spread = (iota((LANES, LANES), 0) % per == iota((LANES, LANES), 1) // pad).astype(F32).astype(BF16)
    row_len = dot(wide, spread)
    inside = (lane % pad).astype(F32) < row_len
    valid[...] = jnp.where(inside, 1.0, 0.0)
    weight[...] = jnp.where(inside, 1.0 / row_len, 0.0)
    mask_ids[...] = jnp.where(inside, ids[...], -1)

    table = same_worker(pad, 256)
    for b in range(len(copies)):
        copies[b].wait()
        ok = row(valid, b, BLOCK)
        x0 = x[:, b * BLOCK : (b + 1) * BLOCK] * ok
        x1 = x0 - by_worker(x0, table) * row(weight, b, BLOCK)
        hi, lo = split(x1)
        counted = jnp.broadcast_to(ok, (16, BLOCK)).astype(BF16)
        data = jnp.concatenate([hi, lo, counted], axis=0)
        part = dot(one_hot(row(mask_ids, b, BLOCK), slots), data, NT)
        if b == 0:
            acc[...] = part
        else:
            acc[...] += part
    both = fold(acc[:, :LANES])
    own[...] = both
    count = jnp.broadcast_to(acc[:, LANES : LANES + 1], (slots, LANES))
    own_count[...] = count
    data = 4 * n
    tiles[:, :data] = to_tiles(both, n).reshape(2, data, LANES)
    about = jnp.where(iota((slots, LANES), 1) % 16 < 8, column(firms[...].astype(F32)), count)
    about = about.reshape(n // 4, 4, 2, 8, LANES)
    sixteenth = iota((n // 4, 8, LANES), 2) // 16
    packed = about[:, 0, 0]
    for owner in range(4):
        for side in range(2):
            packed = jnp.where(sixteenth == 2 * owner + side, about[:, owner, side], packed)
    tiles[:, data:] = packed.reshape(2, n, LANES)
    place(tiles, sends)


def join_kernel(*refs):
    for k, part in enumerate(refs[:-1]):
        refs[-1][k] = part[...]


def worker_kernel(pad, lengths, mask_ids, out):
    slots = out.shape[1]
    workers = lengths.shape[0] * LANES
    group = 256
    rows_group = group * pad
    pick = (iota((rows_group, group), 0) // pad == iota((rows_group, group), 1)).astype(F32).astype(BF16)
    total = jnp.zeros((2 * slots, slots), F32)
    for g in range(workers // group):
        counts = dot(one_hot(row(mask_ids, g, rows_group), slots), pick)
        inverse = 1.0 / row(lengths, g, group).astype(F32)
        hi, lo = split(counts * inverse)
        total += dot(jnp.concatenate([hi, lo], axis=0), counts.astype(BF16), NT)
    hi, lo = split(total[:slots] + total[slots:])
    out[:slots] = hi
    out[slots:] = lo


def owner_means(parts, table, scale, sends):
    far = len(sends)
    rows = 8 * far
    for owner in range(table.shape[0]):
        at = slice(8 * owner, 8 * owner + 8)
        block = jnp.concatenate([part[:, at].reshape(rows, LANES) for part in parts], axis=0)
        data = jnp.concatenate([halves(side) for side in apart(block)], axis=0).astype(BF16)
        means = fold(dot(table[owner], data)) * scale[owner]
        means = jnp.where(left_of((rows, LANES)), means[:rows], means[rows:])
        for k, send in enumerate(sends):
            send[at] = means[8 * k : 8 * k + 8]


def owner_first_kernel(*refs):
    parts, sends, (table, scale) = refs[:NEAR], refs[NEAR + 1 : -2], refs[-2:]
    far = len(sends)
    rows = 8 * far
    owners = table.shape[0]
    for four in range(owners // 4):
        start = 8 * owners + 8 * four
        about = [part[:, start : start + 8].reshape(rows, LANES) for part in parts]
        turned = jnp.concatenate(about, axis=0).T
        for k in range(4):
            at = [32 * k, 32 * k + 16]
            mine = jnp.concatenate([jnp.broadcast_to(about[0][:, i : i + 1], (rows, LANES)) for i in at], axis=0)
            keys = jnp.concatenate([turned[i : i + 1] for i in at], axis=1)
            counts = jnp.concatenate([turned[i + 8 : i + 9] for i in at], axis=1)
            same = mine[:, :1] == keys
            total = jnp.sum(jnp.where(same, counts, 0.0), axis=1, keepdims=True)
            table[4 * four + k] = same.astype(F32).astype(BF16)
            scale[4 * four + k] = jnp.broadcast_to(1.0 / jnp.maximum(total, 1.0), (2 * rows, LANES))
    owner_means(parts, table, scale, sends)


def owner_second_kernel(*refs):
    parts, (table, scale), sends = refs[:NEAR], refs[NEAR : NEAR + 2], refs[NEAR + 3 :]
    owner_means(parts, table, scale, sends)


def change_kernel(far, *refs):
    parts, (own, own_count, pairs), sends, (mean, tiles) = (
        refs[:far], refs[far : far + 3], refs[far + 3 : 2 * far + 3], refs[2 * far + 3 :]
    )
    slots = own.shape[0]
    found = own_means(parts, tiles)
    mean[...] = found
    change = dot(pairs[...], halves(found).astype(BF16))
    new = own[...] - own_count[...] * found + fold(change[:slots] + change[slots:])
    for half in range(2):
        tiles[half] = to_tiles(new, far * NEAR).reshape(2, -1, LANES)[half]
    place(tiles, sends)


def take(parts, ids, slots):
    spread = dot(parts, one_hot(ids, slots))
    columns = parts.shape[0] // 2
    return spread[:columns] + spread[columns:]


def first_kernel(pad, start, probes, mean, mask_ids, weight, y, x, sems):
    ins = column_copies(probes.at[:, pl.ds(start * BLOCK, y.shape[1])], x, sems)
    start_all(ins)
    slots = mean.shape[0]
    parts = halves(mean[...]).T.astype(BF16)
    table = same_worker(pad, 256)
    for b in range(len(ins)):
        ids = row(mask_ids, start + b, BLOCK)
        spread = take(parts, ids, slots)
        ins[b].wait()
        rest = jnp.where(ids >= 0, x[:, b * BLOCK : (b + 1) * BLOCK] - spread, 0.0)
        y[:, b * BLOCK : (b + 1) * BLOCK] = rest - by_worker(rest, table) * row(weight, start + b, BLOCK)


def last_kernel(far, *refs):
    parts, (before, after, mask_ids, out, tiles, y, sems) = refs[:far], refs[far:]
    cut = before.shape[1] // BLOCK
    outs = column_copies(y, out, sems)
    mean = own_means(parts, tiles)
    split_mean = halves(mean).T.astype(BF16)
    for b in range(len(outs)):
        spread = take(split_mean, row(mask_ids, b, BLOCK), mean.shape[0])
        source, at = (before, b) if b < cut else (after, b - cut)
        y[:, b * BLOCK : (b + 1) * BLOCK] = source[:, at * BLOCK : (at + 1) * BLOCK] - spread
        outs[b].start()
    wait_all(outs)


def steps_to_hubs(n):
    far = n // NEAR
    left, right = far // 2 - 1, far // 2
    return [
        [(NEAR * group + k, NEAR * hub + k) for group, hub in ((one, left), (other, right)) for k in range(NEAR)]
        for one, other in zip(*senders(far))
    ]


def to_hubs(parts, n):
    return [parts[0]] + [lax.ppermute(part, "rows", step) for part, step in zip(parts[1:], steps_to_hubs(n))]


def from_hubs(parts, n):
    steps = [[(hub, group) for group, hub in step] for step in steps_to_hubs(n)]
    return [parts[0]] + [lax.ppermute(part, "rows", step) for part, step in zip(parts[1:], steps)]


def share(part, n):
    hubs = range(n // 2 - NEAR, n // 2 + NEAR)

    def swap(part, k):
        return lax.ppermute(part, "rows", [(i, i ^ k) for i in hubs])

    far_side = swap(part, 2)
    return [part, swap(part, 1), far_side, swap(far_side, 1)]


def in_hbm(x):
    return pltpu.with_memory_space_constraint(x, pltpu.HBM)


def call(kernel, out_shape, in_specs, out_specs, scratch, flops, moved):
    return pl.pallas_call(
        kernel,
        out_shape=out_shape,
        in_specs=in_specs,
        out_specs=out_specs,
        scratch_shapes=scratch,
        compiler_params=pltpu.CompilerParams(vmem_limit_bytes=VMEM_BYTES),
        cost_estimate=pl.CostEstimate(flops=flops, bytes_accessed=moved, transcendentals=0),
    )


def body(probes, worker_len, spell_to_slot, slot_to_firm, *, n):
    columns, rows_dev = probes.shape
    workers = worker_len.shape[0]
    pad = rows_dev // workers
    slots = slot_to_firm.shape[0]
    firm_tiles = slots // LANES
    blocks = rows_dev // BLOCK
    vmem, hbm = pl.BlockSpec(memory_space=pltpu.VMEM), pl.BlockSpec(memory_space=pltpu.HBM)
    lengths = worker_len.reshape(workers // LANES, LANES)
    ids = spell_to_slot.reshape(rows_dev // LANES, LANES)
    firms = slot_to_firm.reshape(firm_tiles, LANES)
    array = jax.ShapeDtypeStruct
    of_rows = (rows_dev // LANES, LANES)
    work = 2 * rows_dev * slots * 2 * columns
    sems = pltpu.SemaphoreType.DMA((blocks,))
    whole = pltpu.VMEM((columns, rows_dev), F32)
    of_slots = array((slots, LANES), F32)
    far = n // NEAR
    tile, tile_about = array((4 * n, LANES), F32), array((5 * n, LANES), F32)
    tiles = pltpu.VMEM((far, 4 * n, LANES), F32)
    mine = 16 * far

    *sends, own, own_count, mask_ids, weight = call(
        functools.partial(sums_kernel, n, pad),
        [tile_about] * far + [of_slots, of_slots, array(of_rows, jnp.int32), array(of_rows, F32)],
        [hbm] * 4,
        [vmem] * (far + 4),
        [
            pltpu.VMEM(of_rows, F32),
            whole,
            pltpu.VMEM((slots, 2 * columns + 16), F32),
            pltpu.VMEM(lengths.shape, jnp.int32),
            pltpu.VMEM(ids.shape, jnp.int32),
            pltpu.VMEM(firms.shape, jnp.int32),
            pltpu.VMEM((2, 5 * n, LANES), F32),
            sems,
            pltpu.SemaphoreType.DMA((3,)),
        ],
        2 * work,
        4 * columns * rows_dev,
    )(in_hbm(probes), in_hbm(lengths), in_hbm(ids), in_hbm(firms))

    def join(parts):
        shape = array((far, *parts[0].shape), F32)
        return call(join_kernel, shape, [vmem] * far, vmem, [], 0, shape.size * 8)(*parts)

    received = share(join(to_hubs(sends, n)), n)
    pairs = call(
        functools.partial(worker_kernel, pad),
        array((2 * slots, slots), BF16),
        [vmem, vmem],
        vmem,
        [],
        2 * work,
        4 * slots * slots,
    )(lengths, mask_ids)
    *sends, table, scale = call(
        owner_first_kernel,
        [tile] * far + [array((n // 2, mine, NEAR * mine), BF16), array((n // 2, mine, LANES), F32)],
        [vmem] * (NEAR + 1),
        [vmem] * (far + 2),
        [],
        work // 16,
        slots * slots * 4,
    )(*received, pairs)
    received = from_hubs(sends, n)
    *sends, mean = call(
        functools.partial(change_kernel, far),
        [tile] * far + [of_slots],
        [vmem] * (far + 3),
        [vmem] * (far + 1),
        [tiles],
        work // 16,
        slots * slots * 4,
    )(*received, own, own_count, pairs)
    received = share(join(to_hubs(sends, n)), n)

    def first(start, stop):
        width = (stop - start) * BLOCK
        return call(
            functools.partial(first_kernel, pad, start),
            array((columns, width), F32),
            [hbm, vmem, vmem, vmem],
            vmem,
            [pltpu.VMEM((columns, width), F32), sems],
            2 * work * (stop - start) // blocks,
            8 * columns * width,
        )(in_hbm(probes), mean, mask_ids, weight)

    before, after = first(0, 5 * blocks // 8), first(5 * blocks // 8, blocks)
    sends = call(
        owner_second_kernel,
        [tile] * far,
        [vmem] * (NEAR + 3),
        [vmem] * far,
        [],
        work // 16,
        slots * slots * 4,
    )(*received, table, scale, before)
    received = from_hubs(sends, n)
    return call(
        functools.partial(last_kernel, far),
        array((columns, rows_dev), F32),
        [vmem] * (far + 3),
        hbm,
        [tiles, whole, sems],
        work,
        8 * columns * rows_dev,
    )(*received, before, after, mask_ids)


def solution(mesh):
    placed = (P(None, ("grp", "rows")), P(("grp", "rows")), P(("grp", "rows")), P(("grp", "rows")))
    return jax.shard_map(
        functools.partial(body, n=mesh.shape["rows"]),
        mesh=mesh,
        in_specs=placed,
        out_specs=P(None, ("grp", "rows")),
        check_vma=False,
    )
```

```python
import functools

import jax
import jax.numpy as jnp
from jax import lax
from jax.experimental import pallas as pl
from jax.experimental.pallas import tpu as pltpu
from jax.sharding import PartitionSpec as P

FIRMS_PER_SHARD = 1024
LANES = 128
BLOCK = 1024
VMEM_BYTES = 40 * 1024 * 1024
NEAR = 4
F32, BF16 = jnp.float32, jnp.bfloat16
NT = (((1,), (1,)), ((), ()))
NN = (((1,), (0,)), ((), ()))


def dot(a, b, dims=NN):
    return lax.dot_general(a, b, dims, preferred_element_type=F32)


def iota(shape, dim):
    return lax.broadcasted_iota(jnp.int32, shape, dim)


def split(x):
    hi = x.astype(BF16)
    return hi, (x - hi.astype(F32)).astype(BF16)


def row(ref, block, size):
    per = size // LANES
    return jnp.concatenate([ref[block * per + k : block * per + k + 1, :] for k in range(per)], axis=1)


def one_hot(ids, slots):
    kind = BF16 if slots <= 256 else F32
    slot = iota((slots, LANES), 0).astype(F32).astype(kind)
    ids = ids.astype(F32).astype(kind)
    one, zero = jnp.ones((slots, LANES), kind), jnp.zeros((slots, LANES), kind)
    parts = [jnp.where(slot == ids[:, k : k + LANES], one, zero) for k in range(0, ids.shape[1], LANES)]
    return jnp.concatenate(parts, axis=1).astype(BF16)


def same_worker(pad, width):
    return (iota((width, width), 0) // pad == iota((width, width), 1) // pad).astype(F32).astype(BF16)


def by_worker(x, table):
    rows, width = x.shape
    hi, lo = split(x)
    both = jnp.concatenate([hi, lo], axis=0)
    step = table.shape[0]
    total = jnp.concatenate([dot(both[:, k : k + step], table) for k in range(0, width, step)], axis=1)
    return total[:rows] + total[rows:]


def fold(x):
    return x + pltpu.roll(x, x.shape[1] // 2, axis=1)


def halves(x):
    hi, lo = split(x)
    return jnp.where(iota(x.shape, 1) < x.shape[1] // 2, hi.astype(F32), lo.astype(F32))


def column(firms):
    return jnp.concatenate(
        [jnp.broadcast_to(firms[k : k + 1, :], (LANES, LANES)).T for k in range(firms.shape[0])], axis=0
    )


def along(x):
    return jnp.concatenate([x[k : k + LANES].T[:1] for k in range(0, x.shape[0], LANES)], axis=1)


def left_of(shape):
    return iota(shape, len(shape) - 1) < LANES // 2


def to_tiles(x, n):
    x = x.reshape(n, 2, 8, LANES)
    return jnp.where(left_of((n, 8, LANES)), x[:, 0], x[:, 1])


def apart(tiles):
    turned = pltpu.roll(tiles, LANES // 2, axis=tiles.ndim - 1)
    left = left_of(tiles.shape)
    return jnp.where(left, tiles, turned), jnp.where(left, turned, tiles)


def from_tiles(tiles):
    n = tiles.shape[0]
    return jnp.stack(apart(tiles), axis=1).reshape(2 * 8 * n, LANES)


def start_all(copies):
    for copy in copies:
        copy.start()


def wait_all(copies):
    for copy in copies:
        copy.wait()


def place(tiles, sends):
    me = lax.axis_index("rows") // NEAR
    for k, send in enumerate(sends):
        send[...] = tiles[me ^ k]


def column_copies(source, target, sems):
    width = source.shape[1]
    cuts = [pl.ds(start, BLOCK) for start in range(0, width, BLOCK)]
    return [pltpu.make_async_copy(source.at[:, cut], target.at[:, cut], sems.at[b]) for b, cut in enumerate(cuts)]


def sums_kernel(n, pad, *refs):
    far = n // NEAR
    (probes, lengths_in, ids_in, firms_in), sends = refs[:4], refs[4 : 4 + far]
    own, own_count, mask_ids, weight, valid, x, acc, lengths, ids, firms, tiles, sems, small = refs[4 + far :]
    copies = column_copies(probes, x, sems)
    first = [
        pltpu.make_async_copy(source, target, small.at[k])
        for k, (source, target) in enumerate(((lengths_in, lengths), (ids_in, ids), (firms_in, firms)))
    ]
    start_all(first)
    start_all(copies)
    slots = own.shape[0]
    total_rows = ids.shape[0]
    here = iota((total_rows, LANES), 0)
    lane = iota((total_rows, LANES), 1)
    wait_all(first)
    wide = jnp.broadcast_to(
        lengths[...].astype(F32)[:, None, :], (lengths.shape[0], total_rows // lengths.shape[0], LANES)
    ).reshape(total_rows, LANES)
    per = LANES // pad
    wide = jnp.where(lane // per == here % pad, wide, 0.0).astype(BF16)
    spread = (iota((LANES, LANES), 0) % per == iota((LANES, LANES), 1) // pad).astype(F32).astype(BF16)
    row_len = dot(wide, spread)
    inside = (lane % pad).astype(F32) < row_len
    valid[...] = jnp.where(inside, 1.0, 0.0)
    weight[...] = jnp.where(inside, 1.0 / row_len, 0.0)
    mask_ids[...] = jnp.where(inside, ids[...], -1)

    table = same_worker(pad, 256)
    for b in range(len(copies)):
        copies[b].wait()
        ok = row(valid, b, BLOCK)
        x0 = x[:, b * BLOCK : (b + 1) * BLOCK] * ok
        x1 = x0 - by_worker(x0, table) * row(weight, b, BLOCK)
        hi, lo = split(x1)
        counted = jnp.broadcast_to(ok, (16, BLOCK)).astype(BF16)
        data = jnp.concatenate([hi, lo, counted], axis=0)
        part = dot(data, one_hot(row(mask_ids, b, BLOCK), slots), NT)
        if b == 0:
            acc[...] = part
        else:
            acc[...] += part
    columns = x.shape[0]
    sums = acc[:columns] + acc[columns : 2 * columns]
    both = jnp.concatenate([sums, sums], axis=0).T
    own[...] = both
    count = jnp.broadcast_to(acc[2 * columns : 2 * columns + 1], (LANES, slots)).T
    own_count[...] = count
    tiles[:, : 8 * NEAR] = to_tiles(both, n).reshape(far, 8 * NEAR, LANES)
    about = jnp.where(iota((slots, LANES), 1) % 16 < 8, column(firms[...].astype(F32)), count)
    about = about.reshape(far, NEAR, 2, 8, LANES)
    eighth = iota((far, 8, LANES), 2) // 8
    packed = about[:, 0, 0]
    for owner in range(NEAR):
        for side in range(2):
            packed = jnp.where(eighth // 2 == 2 * owner + side, about[:, owner, side], packed)
    tiles[:, 8 * NEAR :] = packed
    place(tiles, sends)


def join_kernel(*refs):
    for k, part in enumerate(refs[:-1]):
        refs[-1][k] = part[...]


def worker_kernel(pad, lengths, mask_ids, out):
    slots = out.shape[1]
    workers = lengths.shape[0] * LANES
    group = 256
    rows_group = group * pad
    pick = (iota((rows_group, group), 0) // pad == iota((rows_group, group), 1)).astype(F32).astype(BF16)
    total = jnp.zeros((2 * slots, slots), F32)
    for g in range(workers // group):
        counts = dot(one_hot(row(mask_ids, g, rows_group), slots), pick)
        inverse = 1.0 / row(lengths, g, group).astype(F32)
        hi, lo = split(counts * inverse)
        total += dot(jnp.concatenate([hi, lo], axis=0), counts.astype(BF16), NT)
    hi, lo = split(total[:slots] + total[slots:])
    out[:slots] = hi
    out[slots:] = lo


def owner_means(parts, table, scale):
    rows = 8 * NEAR * parts[0].shape[0]
    data = [apart(part.reshape(rows, LANES)) for part in parts]
    data = [halves(side) for sides in data for side in sides]
    total = fold(dot(table, jnp.concatenate(data, axis=0).astype(BF16))) * scale
    return jnp.where(left_of((rows, LANES)), total[:rows], total[rows:]).reshape(parts[0].shape)


def owner_first_kernel(*refs):
    parts, sends, (table, scale) = refs[:NEAR], refs[NEAR + 1 : -2], refs[-2:]
    far = len(sends)

    def sides(part, kind):
        about = part[:, 8 * NEAR :].reshape(8 * far, LANES)
        found = []
        for side in range(2):
            one = [
                jnp.broadcast_to(about[:, at : at + 1], (8 * far, LANES)).reshape(far, 1, 8, LANES)
                for at in (16 * (2 * owner + side) + 8 * kind for owner in range(NEAR))
            ]
            found.append(jnp.concatenate(one, axis=1).reshape(8 * NEAR * far, LANES))
        return found

    keys = [sides(part, 0) for part in parts]
    counts = [along(side) for part in parts for side in sides(part, 1)]
    rows = 8 * NEAR * far
    owner = iota((rows, LANES), 0) // 8 % NEAR * FIRMS_PER_SHARD
    keys = [[side + owner.astype(F32) for side in part] for part in keys]
    mine = jnp.concatenate(keys[0], axis=0)
    same = [mine[:, :1] == along(side) for part in keys for side in part]
    total = jnp.zeros((2 * rows, rows), F32)
    for k, (hit, count) in enumerate(zip(same, counts)):
        table[:, k * rows : (k + 1) * rows] = hit.astype(F32).astype(BF16)
        total += jnp.where(hit, count, 0.0)
    total = jnp.sum(total, axis=1, keepdims=True)
    scale[...] = jnp.broadcast_to(1.0 / jnp.maximum(total, 1.0), scale.shape)
    means = owner_means([part[:, : 8 * NEAR] for part in parts], table[...], scale[...])
    for k, send in enumerate(sends):
        send[...] = means[k]


def owner_second_kernel(*refs):
    parts, (table, scale), sends = refs[:NEAR], refs[NEAR : NEAR + 2], refs[NEAR + 3 :]
    means = owner_means([part[...] for part in parts], table[...], scale[...])
    for k, send in enumerate(sends):
        send[...] = means[k]


def own_means(parts, tiles):
    me = lax.axis_index("rows") // NEAR
    for k, part in enumerate(parts):
        tiles[me ^ k] = part[...]
    return from_tiles(tiles[...].reshape(len(parts) * NEAR, 8, LANES))


def change_kernel(far, *refs):
    parts, (own, own_count, pairs), sends, (mean, tiles) = (
        refs[:far], refs[far : far + 3], refs[far + 3 : 2 * far + 3], refs[2 * far + 3 :]
    )
    slots = own.shape[0]
    found = own_means(parts, tiles)
    mean[...] = found
    change = dot(pairs[...], halves(found).astype(BF16))
    new = own[...] - own_count[...] * found + fold(change[:slots] + change[slots:])
    tiles[...] = to_tiles(new, far * NEAR).reshape(tiles.shape)
    place(tiles, sends)


def take(parts, ids, slots):
    spread = dot(parts, one_hot(ids, slots))
    columns = parts.shape[0] // 2
    return spread[:columns] + spread[columns:]


def first_kernel(pad, start, probes, mean, mask_ids, weight, y, x, sems):
    ins = column_copies(probes.at[:, pl.ds(start * BLOCK, y.shape[1])], x, sems)
    start_all(ins)
    slots = mean.shape[0]
    parts = halves(mean[...]).T.astype(BF16)
    table = same_worker(pad, 256)
    for b in range(len(ins)):
        ids = row(mask_ids, start + b, BLOCK)
        spread = take(parts, ids, slots)
        ins[b].wait()
        rest = jnp.where(ids >= 0, x[:, b * BLOCK : (b + 1) * BLOCK] - spread, 0.0)
        y[:, b * BLOCK : (b + 1) * BLOCK] = rest - by_worker(rest, table) * row(weight, start + b, BLOCK)


def last_kernel(far, *refs):
    parts, (before, after, mask_ids, out, tiles, y, sems) = refs[:far], refs[far:]
    cut = before.shape[1] // BLOCK
    outs = column_copies(y, out, sems)
    mean = own_means(parts, tiles)
    split_mean = halves(mean).T.astype(BF16)
    for b in range(len(outs)):
        spread = take(split_mean, row(mask_ids, b, BLOCK), mean.shape[0])
        source, at = (before, b) if b < cut else (after, b - cut)
        y[:, b * BLOCK : (b + 1) * BLOCK] = source[:, at * BLOCK : (at + 1) * BLOCK] - spread
        outs[b].start()
    wait_all(outs)


def exchange(parts, n):
    steps = [[(i, i ^ (k * NEAR)) for i in range(n)] for k in range(len(parts))]
    return [parts[0]] + [lax.ppermute(part, "rows", step) for part, step in zip(parts[1:], steps[1:])]


def share(part, n):
    return [part] + [lax.ppermute(part, "rows", [(i, i ^ k) for i in range(n)]) for k in range(1, NEAR)]


def in_hbm(x):
    return pltpu.with_memory_space_constraint(x, pltpu.HBM)


def call(kernel, out_shape, in_specs, out_specs, scratch, flops, moved):
    return pl.pallas_call(
        kernel,
        out_shape=out_shape,
        in_specs=in_specs,
        out_specs=out_specs,
        scratch_shapes=scratch,
        compiler_params=pltpu.CompilerParams(vmem_limit_bytes=VMEM_BYTES),
        cost_estimate=pl.CostEstimate(flops=flops, bytes_accessed=moved, transcendentals=0),
    )


def body(probes, worker_len, spell_to_slot, slot_to_firm, *, n):
    columns, rows_dev = probes.shape
    workers = worker_len.shape[0]
    pad = rows_dev // workers
    slots = slot_to_firm.shape[0]
    firm_tiles = slots // LANES
    blocks = rows_dev // BLOCK
    vmem, hbm = pl.BlockSpec(memory_space=pltpu.VMEM), pl.BlockSpec(memory_space=pltpu.HBM)
    lengths = worker_len.reshape(workers // LANES, LANES)
    ids = spell_to_slot.reshape(rows_dev // LANES, LANES)
    firms = slot_to_firm.reshape(firm_tiles, LANES)
    array = jax.ShapeDtypeStruct
    of_rows = (rows_dev // LANES, LANES)
    work = 2 * rows_dev * slots * 2 * columns
    sems = pltpu.SemaphoreType.DMA((blocks,))
    whole = pltpu.VMEM((columns, rows_dev), F32)
    of_slots = array((slots, LANES), F32)
    far = n // NEAR
    tile, tile_about = array((8 * NEAR, LANES), F32), array((8 * NEAR + 8, LANES), F32)
    tiles = pltpu.VMEM((far, 8 * NEAR, LANES), F32)
    mine = 16 * NEAR * far

    *sends, own, own_count, mask_ids, weight = call(
        functools.partial(sums_kernel, n, pad),
        [tile_about] * far + [of_slots, of_slots, array(of_rows, jnp.int32), array(of_rows, F32)],
        [hbm] * 4,
        [vmem] * (far + 4),
        [
            pltpu.VMEM(of_rows, F32),
            whole,
            pltpu.VMEM((2 * columns + 16, slots), F32),
            pltpu.VMEM(lengths.shape, jnp.int32),
            pltpu.VMEM(ids.shape, jnp.int32),
            pltpu.VMEM(firms.shape, jnp.int32),
            pltpu.VMEM((far, 8 * NEAR + 8, LANES), F32),
            sems,
            pltpu.SemaphoreType.DMA((3,)),
        ],
        2 * work,
        4 * columns * rows_dev,
    )(in_hbm(probes), in_hbm(lengths), in_hbm(ids), in_hbm(firms))

    def join(parts):
        shape = array((far, *parts[0].shape), F32)
        return call(join_kernel, shape, [vmem] * far, vmem, [], 0, shape.size * 8)(*parts)

    received = share(join(exchange(sends, n)), n)
    pairs = call(
        functools.partial(worker_kernel, pad),
        array((2 * slots, slots), BF16),
        [vmem, vmem],
        vmem,
        [],
        2 * work,
        4 * slots * slots,
    )(lengths, mask_ids)
    *sends, table, scale = call(
        owner_first_kernel,
        [tile] * far + [array((mine, NEAR * mine), BF16), array((mine, LANES), F32)],
        [vmem] * (NEAR + 1),
        [vmem] * (far + 2),
        [],
        work // 16,
        slots * slots * 4,
    )(*received, pairs)
    received = exchange(sends, n)
    *sends, mean = call(
        functools.partial(change_kernel, far),
        [tile] * far + [of_slots],
        [vmem] * (far + 3),
        [vmem] * (far + 1),
        [tiles],
        work // 16,
        slots * slots * 4,
    )(*received, own, own_count, pairs)
    received = share(join(exchange(sends, n)), n)

    def first(start, stop):
        width = (stop - start) * BLOCK
        return call(
            functools.partial(first_kernel, pad, start),
            array((columns, width), F32),
            [hbm, vmem, vmem, vmem],
            vmem,
            [pltpu.VMEM((columns, width), F32), sems],
            2 * work * (stop - start) // blocks,
            8 * columns * width,
        )(in_hbm(probes), mean, mask_ids, weight)

    before, after = first(0, 5 * blocks // 8), first(5 * blocks // 8, blocks)
    sends = call(
        owner_second_kernel,
        [tile] * far,
        [vmem] * (NEAR + 3),
        [vmem] * far,
        [],
        work // 16,
        slots * slots * 4,
    )(*received, table, scale, before)
    received = exchange(sends, n)
    return call(
        functools.partial(last_kernel, far),
        array((columns, rows_dev), F32),
        [vmem] * (far + 3),
        hbm,
        [tiles, whole, sems],
        work,
        8 * columns * rows_dev,
    )(*received, before, after, mask_ids)


def solution(mesh):
    placed = (P(None, ("grp", "rows")), P(("grp", "rows")), P(("grp", "rows")), P(("grp", "rows")))
    return jax.shard_map(
        functools.partial(body, n=mesh.shape["rows"]),
        mesh=mesh,
        in_specs=placed,
        out_specs=P(None, ("grp", "rows")),
        check_vma=False,
    )
```

```python
import functools

import jax
import jax.numpy as jnp
from jax import lax
from jax.experimental import pallas as pl
from jax.experimental.pallas import tpu as pltpu
from jax.sharding import PartitionSpec as P

FIRMS_PER_SHARD = 1024
LANES = 128
BLOCK = 1024
VMEM_BYTES = 40 * 1024 * 1024
NEAR = 4
F32, BF16 = jnp.float32, jnp.bfloat16
NT = (((1,), (1,)), ((), ()))
NN = (((1,), (0,)), ((), ()))


def dot(a, b, dims=NN):
    return lax.dot_general(a, b, dims, preferred_element_type=F32)


def iota(shape, dim):
    return lax.broadcasted_iota(jnp.int32, shape, dim)


def split(x):
    hi = x.astype(BF16)
    return hi, (x - hi.astype(F32)).astype(BF16)


def row(ref, block, size):
    per = size // LANES
    return jnp.concatenate([ref[block * per + k : block * per + k + 1, :] for k in range(per)], axis=1)


def one_hot(ids, slots):
    kind = BF16 if slots <= 256 else F32
    slot = iota((slots, LANES), 0).astype(F32).astype(kind)
    ids = ids.astype(F32).astype(kind)
    one, zero = jnp.ones((slots, LANES), kind), jnp.zeros((slots, LANES), kind)
    parts = [jnp.where(slot == ids[:, k : k + LANES], one, zero) for k in range(0, ids.shape[1], LANES)]
    return jnp.concatenate(parts, axis=1).astype(BF16)


def same_worker(pad, width):
    return (iota((width, width), 0) // pad == iota((width, width), 1) // pad).astype(F32).astype(BF16)


def by_worker(x, table):
    rows, width = x.shape
    hi, lo = split(x)
    both = jnp.concatenate([hi, lo], axis=0)
    step = table.shape[0]
    total = jnp.concatenate([dot(both[:, k : k + step], table) for k in range(0, width, step)], axis=1)
    return total[:rows] + total[rows:]


def fold(x):
    return x + pltpu.roll(x, x.shape[1] // 2, axis=1)


def halves(x):
    hi, lo = split(x)
    return jnp.where(iota(x.shape, 1) < x.shape[1] // 2, hi.astype(F32), lo.astype(F32))


def column(firms):
    return jnp.concatenate(
        [jnp.broadcast_to(firms[k : k + 1, :], (LANES, LANES)).T for k in range(firms.shape[0])], axis=0
    )


def along(x):
    return jnp.concatenate([x[k : k + LANES].T[:1] for k in range(0, x.shape[0], LANES)], axis=1)


def left_of(shape):
    return iota(shape, len(shape) - 1) < LANES // 2


def to_tiles(x, n):
    x = x.reshape(n, 2, 8, LANES)
    return jnp.where(left_of((n, 8, LANES)), x[:, 0], x[:, 1])


def apart(tiles):
    turned = pltpu.roll(tiles, LANES // 2, axis=tiles.ndim - 1)
    left = left_of(tiles.shape)
    return jnp.where(left, tiles, turned), jnp.where(left, turned, tiles)


def from_tiles(tiles):
    n = tiles.shape[0]
    return jnp.stack(apart(tiles), axis=1).reshape(2 * 8 * n, LANES)


def start_all(copies):
    for copy in copies:
        copy.start()


def wait_all(copies):
    for copy in copies:
        copy.wait()


def place(tiles, keep, send):
    me = lax.axis_index("rows") // NEAR
    half = keep.shape[1]
    for k in range(half):
        keep[0, k] = tiles[me ^ k]
        send[0, k] = tiles[me ^ (half + k)]


def column_copies(source, target, sems):
    width = source.shape[1]
    cuts = [pl.ds(start, BLOCK) for start in range(0, width, BLOCK)]
    return [pltpu.make_async_copy(source.at[:, cut], target.at[:, cut], sems.at[b]) for b, cut in enumerate(cuts)]


def sums_kernel(n, pad, *refs):
    far = n // NEAR
    probes, lengths_in, ids_in, firms_in, keep, send, own, own_count, mask_ids, weight = refs[:10]
    valid, x, acc, lengths, ids, firms, tiles, sems, small = refs[10:]
    copies = column_copies(probes, x, sems)
    first = [
        pltpu.make_async_copy(source, target, small.at[k])
        for k, (source, target) in enumerate(((lengths_in, lengths), (ids_in, ids), (firms_in, firms)))
    ]
    start_all(first)
    start_all(copies)
    slots = own.shape[0]
    total_rows = ids.shape[0]
    here = iota((total_rows, LANES), 0)
    lane = iota((total_rows, LANES), 1)
    wait_all(first)
    wide = jnp.broadcast_to(
        lengths[...].astype(F32)[:, None, :], (lengths.shape[0], total_rows // lengths.shape[0], LANES)
    ).reshape(total_rows, LANES)
    per = LANES // pad
    wide = jnp.where(lane // per == here % pad, wide, 0.0).astype(BF16)
    spread = (iota((LANES, LANES), 0) % per == iota((LANES, LANES), 1) // pad).astype(F32).astype(BF16)
    row_len = dot(wide, spread)
    inside = (lane % pad).astype(F32) < row_len
    valid[...] = jnp.where(inside, 1.0, 0.0)
    weight[...] = jnp.where(inside, 1.0 / row_len, 0.0)
    mask_ids[...] = jnp.where(inside, ids[...], -1)

    table = same_worker(pad, 256)
    for b in range(len(copies)):
        copies[b].wait()
        ok = row(valid, b, BLOCK)
        x0 = x[:, b * BLOCK : (b + 1) * BLOCK] * ok
        x1 = x0 - by_worker(x0, table) * row(weight, b, BLOCK)
        hi, lo = split(x1)
        counted = jnp.broadcast_to(ok, (16, BLOCK)).astype(BF16)
        data = jnp.concatenate([hi, lo, counted], axis=0)
        part = dot(data, one_hot(row(mask_ids, b, BLOCK), slots), NT)
        if b == 0:
            acc[...] = part
        else:
            acc[...] += part
    columns = x.shape[0]
    sums = acc[:columns] + acc[columns : 2 * columns]
    both = jnp.concatenate([sums, sums], axis=0).T
    own[...] = both
    count = jnp.broadcast_to(acc[2 * columns : 2 * columns + 1], (LANES, slots)).T
    own_count[...] = count
    tiles[:, : 8 * NEAR] = to_tiles(both, n).reshape(far, 8 * NEAR, LANES)
    about = jnp.where(iota((slots, LANES), 1) % 16 < 8, column(firms[...].astype(F32)), count)
    about = about.reshape(far, NEAR, 2, 8, LANES)
    eighth = iota((far, 8, LANES), 2) // 8
    packed = about[:, 0, 0]
    for owner in range(NEAR):
        for side in range(2):
            packed = jnp.where(eighth // 2 == 2 * owner + side, about[:, owner, side], packed)
    tiles[:, 8 * NEAR :] = packed
    place(tiles, keep, send)


def halve_kernel(kept, received, keep, send):
    count, half = kept.shape[0], keep.shape[1]
    for at, part in ((0, kept), (count, received)):
        keep[at : at + count] = part[:, :half]
        send[at : at + count] = part[:, half:]


def double_kernel(kept, received, keep, send):
    half, count = keep.shape[0], kept.shape[1]
    for at, part in ((0, kept), (count, received)):
        keep[:, at : at + count] = part[:half]
        send[:, at : at + count] = part[half:]


def join_kernel(kept, received, out):
    count = kept.shape[0]
    out[:count] = kept[:, 0]
    out[count:] = received[:, 0]


def worker_kernel(pad, lengths, mask_ids, out):
    slots = out.shape[1]
    workers = lengths.shape[0] * LANES
    group = 256
    rows_group = group * pad
    pick = (iota((rows_group, group), 0) // pad == iota((rows_group, group), 1)).astype(F32).astype(BF16)
    total = jnp.zeros((2 * slots, slots), F32)
    for g in range(workers // group):
        counts = dot(one_hot(row(mask_ids, g, rows_group), slots), pick)
        inverse = 1.0 / row(lengths, g, group).astype(F32)
        hi, lo = split(counts * inverse)
        total += dot(jnp.concatenate([hi, lo], axis=0), counts.astype(BF16), NT)
    hi, lo = split(total[:slots] + total[slots:])
    out[:slots] = hi
    out[slots:] = lo


def owner_means(parts, table, scale):
    rows = 8 * NEAR * parts[0].shape[0]
    data = [apart(part.reshape(rows, LANES)) for part in parts]
    data = [halves(side) for sides in data for side in sides]
    total = fold(dot(table, jnp.concatenate(data, axis=0).astype(BF16))) * scale
    return jnp.where(left_of((rows, LANES)), total[:rows], total[rows:]).reshape(parts[0].shape)


def owner_first_kernel(*refs):
    parts, (keep, send, table, scale) = refs[:NEAR], refs[NEAR + 1 :]
    far = 2 * keep.shape[0]

    def sides(part, kind):
        about = part[:, 8 * NEAR :].reshape(8 * far, LANES)
        found = []
        for side in range(2):
            one = [
                jnp.broadcast_to(about[:, at : at + 1], (8 * far, LANES)).reshape(far, 1, 8, LANES)
                for at in (16 * (2 * owner + side) + 8 * kind for owner in range(NEAR))
            ]
            found.append(jnp.concatenate(one, axis=1).reshape(8 * NEAR * far, LANES))
        return found

    keys = [sides(part, 0) for part in parts]
    counts = [along(side) for part in parts for side in sides(part, 1)]
    rows = 8 * NEAR * far
    owner = iota((rows, LANES), 0) // 8 % NEAR * FIRMS_PER_SHARD
    keys = [[side + owner.astype(F32) for side in part] for part in keys]
    mine = jnp.concatenate(keys[0], axis=0)
    same = [mine[:, :1] == along(side) for part in keys for side in part]
    total = jnp.zeros((2 * rows, rows), F32)
    for k, (hit, count) in enumerate(zip(same, counts)):
        table[:, k * rows : (k + 1) * rows] = hit.astype(F32).astype(BF16)
        total += jnp.where(hit, count, 0.0)
    total = jnp.sum(total, axis=1, keepdims=True)
    scale[...] = jnp.broadcast_to(1.0 / jnp.maximum(total, 1.0), scale.shape)
    means = owner_means([part[:, : 8 * NEAR] for part in parts], table[...], scale[...])
    keep[:, 0] = means[: far // 2]
    send[:, 0] = means[far // 2 :]


def owner_second_kernel(*refs):
    parts, (table, scale), (keep, send) = refs[:NEAR], refs[NEAR : NEAR + 2], refs[NEAR + 3 :]
    far = 2 * keep.shape[0]
    means = owner_means([part[...] for part in parts], table[...], scale[...])
    keep[:, 0] = means[: far // 2]
    send[:, 0] = means[far // 2 :]


def own_means(kept, received, tiles):
    me = lax.axis_index("rows") // NEAR
    half = kept.shape[1]
    for k in range(half):
        tiles[me ^ k] = kept[0, k]
        tiles[me ^ (half + k)] = received[0, k]
    return from_tiles(tiles[...].reshape(2 * half * NEAR, 8, LANES))


def change_kernel(kept, received, own, own_count, pairs, keep, send, mean, tiles):
    slots = own.shape[0]
    found = own_means(kept, received, tiles)
    mean[...] = found
    change = dot(pairs[...], halves(found).astype(BF16))
    new = own[...] - own_count[...] * found + fold(change[:slots] + change[slots:])
    tiles[...] = to_tiles(new, slots // 16).reshape(tiles.shape)
    place(tiles, keep, send)


def take(parts, ids, slots):
    spread = dot(parts, one_hot(ids, slots))
    columns = parts.shape[0] // 2
    return spread[:columns] + spread[columns:]


def first_kernel(pad, start, probes, mean, mask_ids, weight, y, x, sems):
    ins = column_copies(probes.at[:, pl.ds(start * BLOCK, y.shape[1])], x, sems)
    start_all(ins)
    slots = mean.shape[0]
    parts = halves(mean[...]).T.astype(BF16)
    table = same_worker(pad, 256)
    for b in range(len(ins)):
        ids = row(mask_ids, start + b, BLOCK)
        spread = take(parts, ids, slots)
        ins[b].wait()
        rest = jnp.where(ids >= 0, x[:, b * BLOCK : (b + 1) * BLOCK] - spread, 0.0)
        y[:, b * BLOCK : (b + 1) * BLOCK] = rest - by_worker(rest, table) * row(weight, start + b, BLOCK)


def last_kernel(kept, received, before, after, mask_ids, out, tiles, y, sems):
    cut = before.shape[1] // BLOCK
    outs = column_copies(y, out, sems)
    mean = own_means(kept, received, tiles)
    split_mean = halves(mean).T.astype(BF16)
    for b in range(len(outs)):
        spread = take(split_mean, row(mask_ids, b, BLOCK), mean.shape[0])
        source, at = (before, b) if b < cut else (after, b - cut)
        y[:, b * BLOCK : (b + 1) * BLOCK] = source[:, at * BLOCK : (at + 1) * BLOCK] - spread
        outs[b].start()
    wait_all(outs)


def share(part, n):
    return [part] + [lax.ppermute(part, "rows", [(i, i ^ k) for i in range(n)]) for k in range(1, NEAR)]


def in_hbm(x):
    return pltpu.with_memory_space_constraint(x, pltpu.HBM)


def call(kernel, out_shape, in_specs, out_specs, scratch, flops, moved):
    return pl.pallas_call(
        kernel,
        out_shape=out_shape,
        in_specs=in_specs,
        out_specs=out_specs,
        scratch_shapes=scratch,
        compiler_params=pltpu.CompilerParams(vmem_limit_bytes=VMEM_BYTES),
        cost_estimate=pl.CostEstimate(flops=flops, bytes_accessed=moved, transcendentals=0),
    )


def body(probes, worker_len, spell_to_slot, slot_to_firm, *, n):
    columns, rows_dev = probes.shape
    workers = worker_len.shape[0]
    pad = rows_dev // workers
    slots = slot_to_firm.shape[0]
    firm_tiles = slots // LANES
    blocks = rows_dev // BLOCK
    vmem, hbm = pl.BlockSpec(memory_space=pltpu.VMEM), pl.BlockSpec(memory_space=pltpu.HBM)
    lengths = worker_len.reshape(workers // LANES, LANES)
    ids = spell_to_slot.reshape(rows_dev // LANES, LANES)
    firms = slot_to_firm.reshape(firm_tiles, LANES)
    array = jax.ShapeDtypeStruct
    of_rows = (rows_dev // LANES, LANES)
    work = 2 * rows_dev * slots * 2 * columns
    sems = pltpu.SemaphoreType.DMA((blocks,))
    whole = pltpu.VMEM((columns, rows_dev), F32)
    of_slots = array((slots, LANES), F32)
    far = n // NEAR
    tile, tile_about = array((8 * NEAR, LANES), F32), array((8 * NEAR + 8, LANES), F32)
    tiles = pltpu.VMEM((far, 8 * NEAR, LANES), F32)
    mine = 16 * NEAR * far

    def swap(part, step):
        return lax.ppermute(part, "rows", [(i, i ^ (step * NEAR)) for i in range(n)])

    def sort(kernel, kept, received, sources, places):
        shape = array((sources, places, *kept.shape[2:]), F32)
        return call(kernel, [shape] * 2, [vmem] * 2, [vmem] * 2, [], 0, shape.size * 16)(kept, received)

    def to_owners(kept, send):
        places, sources = far // 2, 1
        while places > 1:
            kept, send = sort(halve_kernel, kept, swap(send, places), 2 * sources, places // 2)
            places, sources = places // 2, 2 * sources
        shape = array((far, *kept.shape[2:]), F32)
        return call(join_kernel, shape, [vmem] * 2, vmem, [], 0, shape.size * 8)(kept, swap(send, 1))

    def from_owners(kept, send):
        places = 1
        while places < far // 2:
            kept, send = sort(double_kernel, kept, swap(send, places), far // 4 // places, 2 * places)
            places *= 2
        return kept, swap(send, places)

    keep, send, own, own_count, mask_ids, weight = call(
        functools.partial(sums_kernel, n, pad),
        [array((1, far // 2, *tile_about.shape), F32)] * 2 + [of_slots, of_slots, array(of_rows, jnp.int32), array(of_rows, F32)],
        [hbm] * 4,
        [vmem] * 6,
        [
            pltpu.VMEM(of_rows, F32),
            whole,
            pltpu.VMEM((2 * columns + 16, slots), F32),
            pltpu.VMEM(lengths.shape, jnp.int32),
            pltpu.VMEM(ids.shape, jnp.int32),
            pltpu.VMEM(firms.shape, jnp.int32),
            pltpu.VMEM((far, 8 * NEAR + 8, LANES), F32),
            sems,
            pltpu.SemaphoreType.DMA((3,)),
        ],
        2 * work,
        4 * columns * rows_dev,
    )(in_hbm(probes), in_hbm(lengths), in_hbm(ids), in_hbm(firms))

    received = share(to_owners(keep, send), n)
    pairs = call(
        functools.partial(worker_kernel, pad),
        array((2 * slots, slots), BF16),
        [vmem, vmem],
        vmem,
        [],
        2 * work,
        4 * slots * slots,
    )(lengths, mask_ids)
    keep, send, table, scale = call(
        owner_first_kernel,
        [array((far // 2, 1, *tile.shape), F32)] * 2 + [array((mine, NEAR * mine), BF16), array((mine, LANES), F32)],
        [vmem] * (NEAR + 1),
        [vmem] * 4,
        [],
        work // 16,
        slots * slots * 4,
    )(*received, pairs)
    kept, received = from_owners(keep, send)
    keep, send, mean = call(
        change_kernel,
        [array((1, far // 2, *tile.shape), F32)] * 2 + [of_slots],
        [vmem] * 5,
        [vmem] * 3,
        [tiles],
        work // 16,
        slots * slots * 4,
    )(kept, received, own, own_count, pairs)
    received = share(to_owners(keep, send), n)

    def first(start, stop):
        width = (stop - start) * BLOCK
        return call(
            functools.partial(first_kernel, pad, start),
            array((columns, width), F32),
            [hbm, vmem, vmem, vmem],
            vmem,
            [pltpu.VMEM((columns, width), F32), sems],
            2 * work * (stop - start) // blocks,
            8 * columns * width,
        )(in_hbm(probes), mean, mask_ids, weight)

    before, after = first(0, 5 * blocks // 8), first(5 * blocks // 8, blocks)
    keep, send = call(
        owner_second_kernel,
        [array((far // 2, 1, *tile.shape), F32)] * 2,
        [vmem] * (NEAR + 3),
        [vmem] * 2,
        [],
        work // 16,
        slots * slots * 4,
    )(*received, table, scale, before)
    kept, received = from_owners(keep, send)
    return call(
        last_kernel,
        array((columns, rows_dev), F32),
        [vmem] * 5,
        hbm,
        [tiles, whole, sems],
        work,
        8 * columns * rows_dev,
    )(kept, received, before, after, mask_ids)


def solution(mesh):
    placed = (P(None, ("grp", "rows")), P(("grp", "rows")), P(("grp", "rows")), P(("grp", "rows")))
    return jax.shard_map(
        functools.partial(body, n=mesh.shape["rows"]),
        mesh=mesh,
        in_specs=placed,
        out_specs=P(None, ("grp", "rows")),
        check_vma=False,
    )
```

```python
import functools

import jax
import jax.numpy as jnp
from jax import lax
from jax.experimental import pallas as pl
from jax.experimental.pallas import tpu as pltpu
from jax.sharding import PartitionSpec as P

FIRMS_PER_SHARD = 1024
LANES = 128
BLOCK = 1024
VMEM_BYTES = 40 * 1024 * 1024
NEAR = 4
F32, BF16 = jnp.float32, jnp.bfloat16
NT = (((1,), (1,)), ((), ()))
NN = (((1,), (0,)), ((), ()))


def dot(a, b, dims=NN):
    return lax.dot_general(a, b, dims, preferred_element_type=F32)


def iota(shape, dim):
    return lax.broadcasted_iota(jnp.int32, shape, dim)


def split(x):
    hi = x.astype(BF16)
    return hi, (x - hi.astype(F32)).astype(BF16)


def row(ref, block, size):
    per = size // LANES
    return jnp.concatenate([ref[block * per + k : block * per + k + 1, :] for k in range(per)], axis=1)


def one_hot(ids, slots):
    kind = BF16 if slots <= 256 else F32
    slot = iota((slots, LANES), 0).astype(F32).astype(kind)
    ids = ids.astype(F32).astype(kind)
    one, zero = jnp.ones((slots, LANES), kind), jnp.zeros((slots, LANES), kind)
    parts = [jnp.where(slot == ids[:, k : k + LANES], one, zero) for k in range(0, ids.shape[1], LANES)]
    return jnp.concatenate(parts, axis=1).astype(BF16)


def same_worker(pad, width):
    return (iota((width, width), 0) // pad == iota((width, width), 1) // pad).astype(F32).astype(BF16)


def by_worker(x, table):
    rows, width = x.shape
    hi, lo = split(x)
    both = jnp.concatenate([hi, lo], axis=0)
    step = table.shape[0]
    total = jnp.concatenate([dot(both[:, k : k + step], table) for k in range(0, width, step)], axis=1)
    return total[:rows] + total[rows:]


def fold(x):
    return x + pltpu.roll(x, x.shape[1] // 2, axis=1)


def halves(x):
    hi, lo = split(x)
    return jnp.where(iota(x.shape, 1) < x.shape[1] // 2, hi.astype(F32), lo.astype(F32))


def column(firms):
    return jnp.concatenate(
        [jnp.broadcast_to(firms[k : k + 1, :], (LANES, LANES)).T for k in range(firms.shape[0])], axis=0
    )


def along(x):
    return jnp.concatenate([x[k : k + LANES].T[:1] for k in range(0, x.shape[0], LANES)], axis=1)


def left_of(shape):
    return iota(shape, len(shape) - 1) < LANES // 2


def to_tiles(x, n):
    x = x.reshape(n, 2, 8, LANES)
    return jnp.where(left_of((n, 8, LANES)), x[:, 0], x[:, 1])


def apart(tiles):
    turned = pltpu.roll(tiles, LANES // 2, axis=tiles.ndim - 1)
    left = left_of(tiles.shape)
    return jnp.where(left, tiles, turned), jnp.where(left, turned, tiles)


def from_tiles(tiles):
    n = tiles.shape[0]
    return jnp.stack(apart(tiles), axis=1).reshape(2 * 8 * n, LANES)


def start_all(copies):
    for copy in copies:
        copy.start()


def wait_all(copies):
    for copy in copies:
        copy.wait()


def place(tiles, sends):
    me = lax.axis_index("rows") // NEAR
    for k, send in enumerate(sends):
        send[...] = tiles[me ^ k]


def column_copies(source, target, sems):
    width = source.shape[1]
    cuts = [pl.ds(start, BLOCK) for start in range(0, width, BLOCK)]
    return [pltpu.make_async_copy(source.at[:, cut], target.at[:, cut], sems.at[b]) for b, cut in enumerate(cuts)]


def row_lengths(lengths, pad):
    total_rows = lengths.shape[0] * pad
    here = iota((total_rows, LANES), 0)
    lane = iota((total_rows, LANES), 1)
    wide = jnp.broadcast_to(lengths.astype(F32)[:, None, :], (lengths.shape[0], pad, LANES)).reshape(total_rows, LANES)
    per = LANES // pad
    wide = jnp.where(lane // per == here % pad, wide, 0.0).astype(BF16)
    spread = (iota((LANES, LANES), 0) % per == iota((LANES, LANES), 1) // pad).astype(F32).astype(BF16)
    row_len = dot(wide, spread)
    return row_len, (lane % pad).astype(F32) < row_len


def sums_kernel(n, pad, *refs):
    far = n // NEAR
    (probes, lengths_in, ids_in, firms_in), sends = refs[:4], refs[4 : 4 + far]
    mask_ids, weight, valid, x, acc, lengths, ids, firms, tiles, sems, small = refs[4 + far :]
    copies = column_copies(probes, x, sems)
    first = [
        pltpu.make_async_copy(source, target, small.at[k])
        for k, (source, target) in enumerate(((lengths_in, lengths), (ids_in, ids), (firms_in, firms)))
    ]
    start_all(first)
    start_all(copies)
    slots = acc.shape[1]
    wait_all(first)
    row_len, inside = row_lengths(lengths[...], pad)
    valid[...] = jnp.where(inside, 1.0, 0.0)
    weight[...] = jnp.where(inside, 1.0 / row_len, 0.0)
    mask_ids[...] = jnp.where(inside, ids[...], -1)

    table = same_worker(pad, 256)
    for b in range(len(copies)):
        copies[b].wait()
        ok = row(valid, b, BLOCK)
        x0 = x[:, b * BLOCK : (b + 1) * BLOCK] * ok
        x1 = x0 - by_worker(x0, table) * row(weight, b, BLOCK)
        hi, lo = split(x1)
        counted = jnp.broadcast_to(ok, (16, BLOCK)).astype(BF16)
        data = jnp.concatenate([hi, lo, counted], axis=0)
        part = dot(data, one_hot(row(mask_ids, b, BLOCK), slots), NT)
        if b == 0:
            acc[...] = part
        else:
            acc[...] += part
    columns = x.shape[0]
    sums = acc[:columns] + acc[columns : 2 * columns]
    both = jnp.concatenate([sums, sums], axis=0).T
    count = jnp.broadcast_to(acc[2 * columns : 2 * columns + 1], (LANES, slots)).T
    tiles[:, : 8 * NEAR] = to_tiles(both, n).reshape(far, 8 * NEAR, LANES)
    about = jnp.where(iota((slots, LANES), 1) % 16 < 8, column(firms[...].astype(F32)), count)
    about = about.reshape(far, NEAR, 2, 8, LANES)
    eighth = iota((far, 8, LANES), 2) // 8
    packed = about[:, 0, 0]
    for owner in range(NEAR):
        for side in range(2):
            packed = jnp.where(eighth // 2 == 2 * owner + side, about[:, owner, side], packed)
    tiles[:, 8 * NEAR :] = packed
    place(tiles, sends)


def join_kernel(*refs):
    for k, part in enumerate(refs[:-1]):
        refs[-1][k] = part[...]


def pairs_kernel(pad, far, all_lengths, all_ids, out, counts):
    me = lax.axis_index("rows") // NEAR
    own, slots = out.shape[1] // 2, out.shape[2]
    kind = BF16 if slots <= 256 else F32
    per = LANES // pad
    total_rows = all_ids.shape[1]
    at = iota((LANES, pad * LANES), 1)
    deal = (iota((LANES, pad * LANES), 0) == at % per * pad + at // LANES).astype(F32).astype(BF16)
    mine = iota((total_rows, pad * LANES), 1) % LANES // per == iota((total_rows, pad * LANES), 0) % pad
    slot = iota((slots, LANES), 0).astype(F32).astype(kind)
    one, zero = jnp.ones((slots, LANES), kind), jnp.zeros((slots, LANES), kind)
    diagonal = iota((own, slots), 1) == me * own + iota((own, slots), 0)
    for k in range(far):
        lengths = all_lengths[me ^ k]
        _, inside = row_lengths(lengths, pad)
        ids = jnp.where(inside, all_ids[me ^ k], -1).astype(F32)
        dealt = dot(jnp.concatenate(split(ids), axis=0), deal)
        dealt = jnp.where(mine, dealt[:total_rows] + dealt[total_rows:], 0.0)
        spells = jnp.sum(dealt.reshape(total_rows // pad, pad, pad * LANES), axis=1).astype(kind)
        for g in range(total_rows // pad):
            total = zero
            for j in range(pad):
                total += jnp.where(slot == spells[g : g + 1, j * LANES : (j + 1) * LANES], one, zero)
            counts[:, g * LANES : (g + 1) * LANES] = total.astype(BF16)
        here = counts[pl.ds(pl.multiple_of(me * own, own), own), :].astype(F32)
        inverse = 1.0 / lengths.astype(F32)
        inverse = jnp.concatenate([inverse[g : g + 1] for g in range(total_rows // pad)], axis=1)
        total = dot(jnp.concatenate(split(here * inverse), axis=0), counts[...], NT)
        total = total[:own] + total[own:] - jnp.where(diagonal, jnp.sum(here, axis=1, keepdims=True), 0.0)
        hi, lo = split(total)
        out[k, :own] = hi
        out[k, own:] = lo


def owner_means(parts, table, scale):
    rows = 8 * NEAR * parts[0].shape[0]
    data = [apart(part.reshape(rows, LANES)) for part in parts]
    data = [halves(side) for sides in data for side in sides]
    total = fold(dot(table, jnp.concatenate(data, axis=0).astype(BF16))) * scale
    return jnp.where(left_of((rows, LANES)), total[:rows], total[rows:]).reshape(parts[0].shape)


def owner_first_kernel(*refs):
    parts, (send, table, scale) = refs[:NEAR], refs[NEAR:]
    far = send.shape[0]

    def sides(part, kind):
        about = part[:, 8 * NEAR :].reshape(8 * far, LANES)
        found = []
        for side in range(2):
            one = [
                jnp.broadcast_to(about[:, at : at + 1], (8 * far, LANES)).reshape(far, 1, 8, LANES)
                for at in (16 * (2 * owner + side) + 8 * kind for owner in range(NEAR))
            ]
            found.append(jnp.concatenate(one, axis=1).reshape(8 * NEAR * far, LANES))
        return found

    keys = [sides(part, 0) for part in parts]
    counts = [along(side) for part in parts for side in sides(part, 1)]
    rows = 8 * NEAR * far
    owner = iota((rows, LANES), 0) // 8 % NEAR * FIRMS_PER_SHARD
    keys = [[side + owner.astype(F32) for side in part] for part in keys]
    mine = jnp.concatenate(keys[0], axis=0)
    same = [mine[:, :1] == along(side) for part in keys for side in part]
    total = jnp.zeros((2 * rows, rows), F32)
    for k, (hit, count) in enumerate(zip(same, counts)):
        table[:, k * rows : (k + 1) * rows] = hit.astype(F32).astype(BF16)
        total += jnp.where(hit, count, 0.0)
    total = jnp.sum(total, axis=1, keepdims=True)
    scale[...] = jnp.broadcast_to(1.0 / jnp.maximum(total, 1.0), scale.shape)
    send[...] = owner_means([part[:, : 8 * NEAR] for part in parts], table[...], scale[...])


def owner_second_kernel(*refs):
    parts, (table, scale), sends = refs[:NEAR], refs[NEAR : NEAR + 2], refs[NEAR + 3 :]
    means = owner_means([part[...] for part in parts], table[...], scale[...])
    for k, send in enumerate(sends):
        send[...] = means[k]


def own_means(parts, tiles):
    me = lax.axis_index("rows") // NEAR
    for k, part in enumerate(parts):
        tiles[me ^ k] = part[...]
    return from_tiles(tiles[...].reshape(len(parts) * NEAR, 8, LANES))


def change_kernel(far, *refs):
    parts, (sums, pairs, send, mean, tiles) = refs[:far], refs[far:]
    me = lax.axis_index("rows") // NEAR
    own = pairs.shape[1] // 2
    for i in range(far):
        for k, part in enumerate(parts):
            tiles[i, me ^ k] = part[k ^ i]
        found = from_tiles(tiles[i].reshape(far * NEAR, 8, LANES))
        if i == 0:
            mean[...] = found
        change = dot(pairs[i], halves(found).astype(BF16))
        change = to_tiles(fold(change[:own] + change[own:]), NEAR).reshape(8 * NEAR, LANES)
        send[i] = sums[i, : 8 * NEAR] + change


def take(parts, ids, slots):
    spread = dot(parts, one_hot(ids, slots))
    columns = parts.shape[0] // 2
    return spread[:columns] + spread[columns:]


def first_kernel(pad, start, probes, mean, mask_ids, weight, y, x, sems):
    ins = column_copies(probes.at[:, pl.ds(start * BLOCK, y.shape[1])], x, sems)
    start_all(ins)
    slots = mean.shape[0]
    parts = halves(mean[...]).T.astype(BF16)
    table = same_worker(pad, 256)
    for b in range(len(ins)):
        ids = row(mask_ids, start + b, BLOCK)
        spread = take(parts, ids, slots)
        ins[b].wait()
        rest = jnp.where(ids >= 0, x[:, b * BLOCK : (b + 1) * BLOCK] - spread, 0.0)
        y[:, b * BLOCK : (b + 1) * BLOCK] = rest - by_worker(rest, table) * row(weight, start + b, BLOCK)


def last_kernel(far, *refs):
    parts, (before, after, mask_ids, out, tiles, y, sems) = refs[:far], refs[far:]
    cut = before.shape[1] // BLOCK
    outs = column_copies(y, out, sems)
    mean = own_means(parts, tiles)
    split_mean = halves(mean).T.astype(BF16)
    for b in range(len(outs)):
        spread = take(split_mean, row(mask_ids, b, BLOCK), mean.shape[0])
        source, at = (before, b) if b < cut else (after, b - cut)
        y[:, b * BLOCK : (b + 1) * BLOCK] = source[:, at * BLOCK : (at + 1) * BLOCK] - spread
        outs[b].start()
    wait_all(outs)


def all_far(part, n):
    steps = [[(i, i ^ (k * NEAR)) for i in range(n)] for k in range(1, part.shape[0])]
    return [part] + [lax.ppermute(part, "rows", step) for step in steps]


def exchange(parts, n):
    steps = [[(i, i ^ (k * NEAR)) for i in range(n)] for k in range(len(parts))]
    return [parts[0]] + [lax.ppermute(part, "rows", step) for part, step in zip(parts[1:], steps[1:])]


def share(part, n):
    return [part] + [lax.ppermute(part, "rows", [(i, i ^ k) for i in range(n)]) for k in range(1, NEAR)]


def in_hbm(x):
    return pltpu.with_memory_space_constraint(x, pltpu.HBM)


def call(kernel, out_shape, in_specs, out_specs, scratch, flops, moved):
    return pl.pallas_call(
        kernel,
        out_shape=out_shape,
        in_specs=in_specs,
        out_specs=out_specs,
        scratch_shapes=scratch,
        compiler_params=pltpu.CompilerParams(vmem_limit_bytes=VMEM_BYTES),
        cost_estimate=pl.CostEstimate(flops=flops, bytes_accessed=moved, transcendentals=0),
    )


def body(probes, worker_len, spell_to_slot, slot_to_firm, *, n):
    columns, rows_dev = probes.shape
    workers = worker_len.shape[0]
    pad = rows_dev // workers
    slots = slot_to_firm.shape[0]
    firm_tiles = slots // LANES
    blocks = rows_dev // BLOCK
    vmem, hbm = pl.BlockSpec(memory_space=pltpu.VMEM), pl.BlockSpec(memory_space=pltpu.HBM)
    lengths = worker_len.reshape(workers // LANES, LANES)
    ids = spell_to_slot.reshape(rows_dev // LANES, LANES)
    firms = slot_to_firm.reshape(firm_tiles, LANES)
    array = jax.ShapeDtypeStruct
    of_rows = (rows_dev // LANES, LANES)
    work = 2 * rows_dev * slots * 2 * columns
    sems = pltpu.SemaphoreType.DMA((blocks,))
    whole = pltpu.VMEM((columns, rows_dev), F32)
    of_slots = array((slots, LANES), F32)
    far = n // NEAR
    tile, tile_about = array((8 * NEAR, LANES), F32), array((8 * NEAR + 8, LANES), F32)
    tiles = pltpu.VMEM((far, 8 * NEAR, LANES), F32)
    mine = 16 * NEAR * far

    groups = [list(range(k, n, NEAR)) for k in range(NEAR)]
    all_ids = lax.all_gather(ids, "rows", axis_index_groups=groups)
    all_lengths = lax.all_gather(lengths, "rows", axis_index_groups=groups)
    *sends, mask_ids, weight = call(
        functools.partial(sums_kernel, n, pad),
        [tile_about] * far + [array(of_rows, jnp.int32), array(of_rows, F32)],
        [hbm] * 4,
        [vmem] * (far + 2),
        [
            pltpu.VMEM(of_rows, F32),
            whole,
            pltpu.VMEM((2 * columns + 16, slots), F32),
            pltpu.VMEM(lengths.shape, jnp.int32),
            pltpu.VMEM(ids.shape, jnp.int32),
            pltpu.VMEM(firms.shape, jnp.int32),
            pltpu.VMEM((far, 8 * NEAR + 8, LANES), F32),
            sems,
            pltpu.SemaphoreType.DMA((3,)),
        ],
        2 * work,
        4 * columns * rows_dev,
    )(in_hbm(probes), in_hbm(lengths), in_hbm(ids), in_hbm(firms))

    def join(parts):
        shape = array((far, *parts[0].shape), F32)
        return call(join_kernel, shape, [vmem] * far, vmem, [], 0, shape.size * 8)(*parts)

    received = share(join(exchange(sends, n)), n)
    means, table, scale = call(
        owner_first_kernel,
        [array((far, *tile.shape), F32), array((mine, NEAR * mine), BF16), array((mine, LANES), F32)],
        [vmem] * NEAR,
        [vmem] * 3,
        [],
        work // 16,
        slots * slots * 4,
    )(*received)
    own = 16 * NEAR
    pairs = call(
        functools.partial(pairs_kernel, pad, far),
        array((far, 2 * own, slots), BF16),
        [vmem] * 2,
        vmem,
        [pltpu.VMEM((slots, workers), BF16)],
        work,
        4 * slots * slots,
    )(all_lengths, all_ids)
    sums, mean = call(
        functools.partial(change_kernel, far),
        [array((far, *tile.shape), F32), of_slots],
        [vmem] * (far + 2),
        [vmem] * 2,
        [pltpu.VMEM((far, far, *tile.shape), F32)],
        work // 16,
        slots * slots * 4,
    )(*all_far(means, n), received[0], pairs)
    received = share(sums, n)

    def first(start, stop):
        width = (stop - start) * BLOCK
        return call(
            functools.partial(first_kernel, pad, start),
            array((columns, width), F32),
            [hbm, vmem, vmem, vmem],
            vmem,
            [pltpu.VMEM((columns, width), F32), sems],
            2 * work * (stop - start) // blocks,
            8 * columns * width,
        )(in_hbm(probes), mean, mask_ids, weight)

    before, after = first(0, 5 * blocks // 8), first(5 * blocks // 8, blocks)
    sends = call(
        owner_second_kernel,
        [tile] * far,
        [vmem] * (NEAR + 3),
        [vmem] * far,
        [],
        work // 16,
        slots * slots * 4,
    )(*received, table, scale, before)
    received = exchange(sends, n)
    return call(
        functools.partial(last_kernel, far),
        array((columns, rows_dev), F32),
        [vmem] * (far + 3),
        hbm,
        [tiles, whole, sems],
        work,
        8 * columns * rows_dev,
    )(*received, before, after, mask_ids)


def solution(mesh):
    placed = (P(None, ("grp", "rows")), P(("grp", "rows")), P(("grp", "rows")), P(("grp", "rows")))
    return jax.shard_map(
        functools.partial(body, n=mesh.shape["rows"]),
        mesh=mesh,
        in_specs=placed,
        out_specs=P(None, ("grp", "rows")),
        check_vma=False,
    )
```

```python
import functools

import jax
import jax.numpy as jnp
from jax import lax
from jax.experimental import pallas as pl
from jax.experimental.pallas import tpu as pltpu
from jax.sharding import PartitionSpec as P

FIRMS_PER_SHARD = 1024
LANES = 128
BLOCK = 1024
VMEM_BYTES = 40 * 1024 * 1024
NEAR = 4
F32, BF16 = jnp.float32, jnp.bfloat16
NT = (((1,), (1,)), ((), ()))
NN = (((1,), (0,)), ((), ()))


def dot(a, b, dims=NN):
    return lax.dot_general(a, b, dims, preferred_element_type=F32)


def iota(shape, dim):
    return lax.broadcasted_iota(jnp.int32, shape, dim)


def split(x):
    hi = x.astype(BF16)
    return hi, (x - hi.astype(F32)).astype(BF16)


def row(ref, block, size):
    per = size // LANES
    return jnp.concatenate([ref[block * per + k : block * per + k + 1, :] for k in range(per)], axis=1)


def one_hot(ids, slots):
    kind = BF16 if slots <= 256 else F32
    slot = iota((slots, LANES), 0).astype(F32).astype(kind)
    ids = ids.astype(F32).astype(kind)
    one, zero = jnp.ones((slots, LANES), kind), jnp.zeros((slots, LANES), kind)
    parts = [jnp.where(slot == ids[:, k : k + LANES], one, zero) for k in range(0, ids.shape[1], LANES)]
    return jnp.concatenate(parts, axis=1).astype(BF16)


def same_worker(pad, width):
    return (iota((width, width), 0) // pad == iota((width, width), 1) // pad).astype(F32).astype(BF16)


def by_worker(x, table):
    rows, width = x.shape
    hi, lo = split(x)
    both = jnp.concatenate([hi, lo], axis=0)
    step = table.shape[0]
    total = jnp.concatenate([dot(both[:, k : k + step], table) for k in range(0, width, step)], axis=1)
    return total[:rows] + total[rows:]


def fold(x):
    return x + pltpu.roll(x, x.shape[1] // 2, axis=1)


def halves(x):
    hi, lo = split(x)
    return jnp.where(iota(x.shape, 1) < x.shape[1] // 2, hi.astype(F32), lo.astype(F32))


def column(firms):
    return jnp.concatenate(
        [jnp.broadcast_to(firms[k : k + 1, :], (LANES, LANES)).T for k in range(firms.shape[0])], axis=0
    )


def along(x):
    return jnp.concatenate([x[k : k + LANES].T[:1] for k in range(0, x.shape[0], LANES)], axis=1)


def left_of(shape):
    return iota(shape, len(shape) - 1) < LANES // 2


def to_tiles(x, n):
    x = x.reshape(n, 2, 8, LANES)
    return jnp.where(left_of((n, 8, LANES)), x[:, 0], x[:, 1])


def apart(tiles):
    turned = pltpu.roll(tiles, LANES // 2, axis=tiles.ndim - 1)
    left = left_of(tiles.shape)
    return jnp.where(left, tiles, turned), jnp.where(left, turned, tiles)


def from_tiles(tiles):
    n = tiles.shape[0]
    return jnp.stack(apart(tiles), axis=1).reshape(2 * 8 * n, LANES)


def start_all(copies):
    for copy in copies:
        copy.start()


def wait_all(copies):
    for copy in copies:
        copy.wait()


def place(tiles, sends):
    me = lax.axis_index("rows") // NEAR
    for k, send in enumerate(sends):
        send[: tiles.shape[1]] = tiles[me ^ k]


def column_copies(source, target, sems):
    width = source.shape[1]
    cuts = [pl.ds(start, BLOCK) for start in range(0, width, BLOCK)]
    return [pltpu.make_async_copy(source.at[:, cut], target.at[:, cut], sems.at[b]) for b, cut in enumerate(cuts)]


def row_lengths(lengths, pad):
    total_rows = lengths.shape[0] * pad
    here = iota((total_rows, LANES), 0)
    lane = iota((total_rows, LANES), 1)
    wide = jnp.broadcast_to(lengths.astype(F32)[:, None, :], (lengths.shape[0], pad, LANES)).reshape(total_rows, LANES)
    per = LANES // pad
    wide = jnp.where(lane // per == here % pad, wide, 0.0).astype(BF16)
    spread = (iota((LANES, LANES), 0) % per == iota((LANES, LANES), 1) // pad).astype(F32).astype(BF16)
    row_len = dot(wide, spread)
    return row_len, (lane % pad).astype(F32) < row_len


def sums_kernel(n, pad, *refs):
    far = n // NEAR
    (probes, lengths_in, ids_in, firms_in), sends = refs[:4], refs[4 : 4 + far]
    mask_ids, weight, valid, x, acc, lengths, ids, firms, tiles, sems, small = refs[4 + far :]
    copies = column_copies(probes, x, sems)
    first = [
        pltpu.make_async_copy(source, target, small.at[k])
        for k, (source, target) in enumerate(((lengths_in, lengths), (ids_in, ids), (firms_in, firms)))
    ]
    start_all(first)
    start_all(copies)
    slots = acc.shape[1]
    wait_all(first)
    row_len, inside = row_lengths(lengths[...], pad)
    valid[...] = jnp.where(inside, 1.0, 0.0)
    weight[...] = jnp.where(inside, 1.0 / row_len, 0.0)
    mask_ids[...] = jnp.where(inside, ids[...], -1)
    for send in sends:
        send[tiles.shape[1] :] = mask_ids[...].astype(F32)

    table = same_worker(pad, 256)
    for b in range(len(copies)):
        copies[b].wait()
        ok = row(valid, b, BLOCK)
        x0 = x[:, b * BLOCK : (b + 1) * BLOCK] * ok
        x1 = x0 - by_worker(x0, table) * row(weight, b, BLOCK)
        hi, lo = split(x1)
        counted = jnp.broadcast_to(ok, (16, BLOCK)).astype(BF16)
        data = jnp.concatenate([hi, lo, counted], axis=0)
        part = dot(data, one_hot(row(mask_ids, b, BLOCK), slots), NT)
        if b == 0:
            acc[...] = part
        else:
            acc[...] += part
    columns = x.shape[0]
    sums = acc[:columns] + acc[columns : 2 * columns]
    both = jnp.concatenate([sums, sums], axis=0).T
    count = jnp.broadcast_to(acc[2 * columns : 2 * columns + 1], (LANES, slots)).T
    tiles[:, : 8 * NEAR] = to_tiles(both, n).reshape(far, 8 * NEAR, LANES)
    about = jnp.where(iota((slots, LANES), 1) % 16 < 8, column(firms[...].astype(F32)), count)
    about = about.reshape(far, NEAR, 2, 8, LANES)
    eighth = iota((far, 8, LANES), 2) // 8
    packed = about[:, 0, 0]
    for owner in range(NEAR):
        for side in range(2):
            packed = jnp.where(eighth // 2 == 2 * owner + side, about[:, owner, side], packed)
    tiles[:, 8 * NEAR :] = packed
    place(tiles, sends)


def join_kernel(*refs):
    for k, part in enumerate(refs[:-1]):
        refs[-1][k] = part[: refs[-1].shape[1]]


def pairs_kernel(pad, *refs):
    parts, (out, ids, counts) = refs[:-3], refs[-3:]
    me = lax.axis_index("rows") // NEAR
    far, own, slots = len(parts), out.shape[1] // 2, out.shape[2]
    kind = BF16 if slots <= 256 else F32
    per = LANES // pad
    total_rows = ids.shape[1]
    for k, part in enumerate(parts):
        ids[k] = part[part.shape[0] - total_rows :]
    at = iota((LANES, pad * LANES), 1)
    deal = (iota((LANES, pad * LANES), 0) == at % per * pad + at // LANES).astype(F32).astype(BF16)
    mine = iota((total_rows, pad * LANES), 1) % LANES // per == iota((total_rows, pad * LANES), 0) % pad
    slot = iota((slots, LANES), 0).astype(F32).astype(kind)
    one, zero = jnp.ones((slots, LANES), kind), jnp.zeros((slots, LANES), kind)
    diagonal = iota((own, slots), 1) == me * own + iota((own, slots), 0)

    def device(k, carry):
        dealt = dot(jnp.concatenate(split(ids[k]), axis=0), deal)
        dealt = jnp.where(mine, dealt[:total_rows] + dealt[total_rows:], 0.0)
        dealt = jnp.sum(dealt.reshape(total_rows // pad, pad, pad * LANES), axis=1)
        spells = dealt.astype(kind)
        for g in range(total_rows // pad):
            total = zero
            for j in range(pad):
                total += jnp.where(slot == spells[g : g + 1, j * LANES : (j + 1) * LANES], one, zero)
            counts[:, g * LANES : (g + 1) * LANES] = total.astype(BF16)
        valid = jnp.where(dealt >= 0.0, 1.0, 0.0)
        length = valid[:, :LANES]
        for j in range(1, pad):
            length += valid[:, j * LANES : (j + 1) * LANES]
        inverse = 1.0 / length
        inverse = jnp.concatenate([inverse[g : g + 1] for g in range(total_rows // pad)], axis=1)
        here = counts[pl.ds(pl.multiple_of(me * own, own), own), :].astype(F32)
        total = dot(jnp.concatenate(split(here * inverse), axis=0), counts[...], NT)
        total = total[:own] + total[own:] - jnp.where(diagonal, jnp.sum(here, axis=1, keepdims=True), 0.0)
        hi, lo = split(total)
        out[k, :own] = hi
        out[k, own:] = lo
        return carry

    lax.fori_loop(0, far, device, 0, unroll=far if far <= 4 else 1)


def owner_means(parts, table, scale):
    rows = 8 * NEAR * parts[0].shape[0]
    data = [apart(part.reshape(rows, LANES)) for part in parts]
    data = [halves(side) for sides in data for side in sides]
    total = fold(dot(table, jnp.concatenate(data, axis=0).astype(BF16))) * scale
    return jnp.where(left_of((rows, LANES)), total[:rows], total[rows:]).reshape(parts[0].shape)


def owner_first_kernel(*refs):
    parts, (send, table, scale) = refs[:NEAR], refs[NEAR:]
    far = send.shape[0]

    def sides(part, kind):
        about = part[:, 8 * NEAR :].reshape(8 * far, LANES)
        found = []
        for side in range(2):
            one = [
                jnp.broadcast_to(about[:, at : at + 1], (8 * far, LANES)).reshape(far, 1, 8, LANES)
                for at in (16 * (2 * owner + side) + 8 * kind for owner in range(NEAR))
            ]
            found.append(jnp.concatenate(one, axis=1).reshape(8 * NEAR * far, LANES))
        return found

    keys = [sides(part, 0) for part in parts]
    counts = [along(side) for part in parts for side in sides(part, 1)]
    rows = 8 * NEAR * far
    owner = iota((rows, LANES), 0) // 8 % NEAR * FIRMS_PER_SHARD
    keys = [[side + owner.astype(F32) for side in part] for part in keys]
    mine = jnp.concatenate(keys[0], axis=0)
    same = [mine[:, :1] == along(side) for part in keys for side in part]
    total = jnp.zeros((2 * rows, rows), F32)
    for k, (hit, count) in enumerate(zip(same, counts)):
        table[:, k * rows : (k + 1) * rows] = hit.astype(F32).astype(BF16)
        total += jnp.where(hit, count, 0.0)
    total = jnp.sum(total, axis=1, keepdims=True)
    scale[...] = jnp.broadcast_to(1.0 / jnp.maximum(total, 1.0), scale.shape)
    send[...] = owner_means([part[:, : 8 * NEAR] for part in parts], table[...], scale[...])


def owner_second_kernel(*refs):
    parts, (table, scale), sends = refs[:NEAR], refs[NEAR : NEAR + 2], refs[NEAR + 3 :]
    means = owner_means([part[...] for part in parts], table[...], scale[...])
    for k, send in enumerate(sends):
        send[...] = means[k]


def own_means(parts, tiles):
    me = lax.axis_index("rows") // NEAR
    for k, part in enumerate(parts):
        tiles[me ^ k] = part[...]
    return from_tiles(tiles[...].reshape(len(parts) * NEAR, 8, LANES))


def change_kernel(far, *refs):
    parts, (sums, pairs, send, mean, tiles) = refs[:far], refs[far:]
    me = lax.axis_index("rows") // NEAR
    own = pairs.shape[1] // 2
    for i in range(far):
        for k, part in enumerate(parts):
            tiles[i, me ^ k] = part[k ^ i]
        found = from_tiles(tiles[i].reshape(far * NEAR, 8, LANES))
        if i == 0:
            mean[...] = found
        change = dot(pairs[i], halves(found).astype(BF16))
        change = to_tiles(fold(change[:own] + change[own:]), NEAR).reshape(8 * NEAR, LANES)
        send[i] = sums[i, : 8 * NEAR] + change


def take(parts, ids, slots):
    spread = dot(parts, one_hot(ids, slots))
    columns = parts.shape[0] // 2
    return spread[:columns] + spread[columns:]


def first_kernel(pad, start, probes, mean, mask_ids, weight, y, x, sems):
    ins = column_copies(probes.at[:, pl.ds(start * BLOCK, y.shape[1])], x, sems)
    start_all(ins)
    slots = mean.shape[0]
    parts = halves(mean[...]).T.astype(BF16)
    table = same_worker(pad, 256)
    for b in range(len(ins)):
        ids = row(mask_ids, start + b, BLOCK)
        spread = take(parts, ids, slots)
        ins[b].wait()
        rest = jnp.where(ids >= 0, x[:, b * BLOCK : (b + 1) * BLOCK] - spread, 0.0)
        y[:, b * BLOCK : (b + 1) * BLOCK] = rest - by_worker(rest, table) * row(weight, start + b, BLOCK)


def last_kernel(far, *refs):
    parts, (before, after, mask_ids, out, tiles, y, sems) = refs[:far], refs[far:]
    cut = before.shape[1] // BLOCK
    outs = column_copies(y, out, sems)
    mean = own_means(parts, tiles)
    split_mean = halves(mean).T.astype(BF16)
    for b in range(len(outs)):
        spread = take(split_mean, row(mask_ids, b, BLOCK), mean.shape[0])
        source, at = (before, b) if b < cut else (after, b - cut)
        y[:, b * BLOCK : (b + 1) * BLOCK] = source[:, at * BLOCK : (at + 1) * BLOCK] - spread
        outs[b].start()
    wait_all(outs)


def all_far(part, n):
    steps = [[(i, i ^ (k * NEAR)) for i in range(n)] for k in range(1, part.shape[0])]
    return [part] + [lax.ppermute(part, "rows", step) for step in steps]


def exchange(parts, n):
    steps = [[(i, i ^ (k * NEAR)) for i in range(n)] for k in range(len(parts))]
    return [parts[0]] + [lax.ppermute(part, "rows", step) for part, step in zip(parts[1:], steps[1:])]


def share(part, n):
    return [part] + [lax.ppermute(part, "rows", [(i, i ^ k) for i in range(n)]) for k in range(1, NEAR)]


def in_hbm(x):
    return pltpu.with_memory_space_constraint(x, pltpu.HBM)


def call(kernel, out_shape, in_specs, out_specs, scratch, flops, moved):
    return pl.pallas_call(
        kernel,
        out_shape=out_shape,
        in_specs=in_specs,
        out_specs=out_specs,
        scratch_shapes=scratch,
        compiler_params=pltpu.CompilerParams(vmem_limit_bytes=VMEM_BYTES),
        cost_estimate=pl.CostEstimate(flops=flops, bytes_accessed=moved, transcendentals=0),
    )


def body(probes, worker_len, spell_to_slot, slot_to_firm, *, n):
    columns, rows_dev = probes.shape
    workers = worker_len.shape[0]
    pad = rows_dev // workers
    slots = slot_to_firm.shape[0]
    firm_tiles = slots // LANES
    blocks = rows_dev // BLOCK
    vmem, hbm = pl.BlockSpec(memory_space=pltpu.VMEM), pl.BlockSpec(memory_space=pltpu.HBM)
    lengths = worker_len.reshape(workers // LANES, LANES)
    ids = spell_to_slot.reshape(rows_dev // LANES, LANES)
    firms = slot_to_firm.reshape(firm_tiles, LANES)
    array = jax.ShapeDtypeStruct
    of_rows = (rows_dev // LANES, LANES)
    work = 2 * rows_dev * slots * 2 * columns
    sems = pltpu.SemaphoreType.DMA((blocks,))
    whole = pltpu.VMEM((columns, rows_dev), F32)
    of_slots = array((slots, LANES), F32)
    far = n // NEAR
    tile, tile_about = array((8 * NEAR, LANES), F32), array((8 * NEAR + 8, LANES), F32)
    tiles = pltpu.VMEM((far, 8 * NEAR, LANES), F32)
    mine = 16 * NEAR * far

    *sends, mask_ids, weight = call(
        functools.partial(sums_kernel, n, pad),
        [array((tile_about.shape[0] + of_rows[0], LANES), F32)] * far
        + [array(of_rows, jnp.int32), array(of_rows, F32)],
        [hbm] * 4,
        [vmem] * (far + 2),
        [
            pltpu.VMEM(of_rows, F32),
            whole,
            pltpu.VMEM((2 * columns + 16, slots), F32),
            pltpu.VMEM(lengths.shape, jnp.int32),
            pltpu.VMEM(ids.shape, jnp.int32),
            pltpu.VMEM(firms.shape, jnp.int32),
            pltpu.VMEM((far, 8 * NEAR + 8, LANES), F32),
            sems,
            pltpu.SemaphoreType.DMA((3,)),
        ],
        2 * work,
        4 * columns * rows_dev,
    )(in_hbm(probes), in_hbm(lengths), in_hbm(ids), in_hbm(firms))

    def join(parts):
        shape = array((far, *tile_about.shape), F32)
        return call(join_kernel, shape, [vmem] * far, vmem, [], 0, shape.size * 8)(*parts)

    arrived = exchange(sends, n)
    received = share(join(arrived), n)
    means, table, scale = call(
        owner_first_kernel,
        [array((far, *tile.shape), F32), array((mine, NEAR * mine), BF16), array((mine, LANES), F32)],
        [vmem] * NEAR,
        [vmem] * 3,
        [],
        work // 16,
        slots * slots * 4,
    )(*received)
    own = 16 * NEAR
    pairs = call(
        functools.partial(pairs_kernel, pad),
        array((far, 2 * own, slots), BF16),
        [vmem] * far,
        vmem,
        [pltpu.VMEM((far, *of_rows), F32), pltpu.VMEM((slots, workers), BF16)],
        work,
        4 * slots * slots,
    )(*arrived)
    sums, mean = call(
        functools.partial(change_kernel, far),
        [array((far, *tile.shape), F32), of_slots],
        [vmem] * (far + 2),
        [vmem] * 2,
        [pltpu.VMEM((far, far, *tile.shape), F32)],
        work // 16,
        slots * slots * 4,
    )(*all_far(means, n), received[0], pairs)
    received = share(sums, n)

    def first(start, stop):
        width = (stop - start) * BLOCK
        return call(
            functools.partial(first_kernel, pad, start),
            array((columns, width), F32),
            [hbm, vmem, vmem, vmem],
            vmem,
            [pltpu.VMEM((columns, width), F32), sems],
            2 * work * (stop - start) // blocks,
            8 * columns * width,
        )(in_hbm(probes), mean, mask_ids, weight)

    before, after = first(0, 5 * blocks // 8), first(5 * blocks // 8, blocks)
    sends = call(
        owner_second_kernel,
        [tile] * far,
        [vmem] * (NEAR + 3),
        [vmem] * far,
        [],
        work // 16,
        slots * slots * 4,
    )(*received, table, scale, before)
    received = exchange(sends, n)
    return call(
        functools.partial(last_kernel, far),
        array((columns, rows_dev), F32),
        [vmem] * (far + 3),
        hbm,
        [tiles, whole, sems],
        work,
        8 * columns * rows_dev,
    )(*received, before, after, mask_ids)


def solution(mesh):
    placed = (P(None, ("grp", "rows")), P(("grp", "rows")), P(("grp", "rows")), P(("grp", "rows")))
    return jax.shard_map(
        functools.partial(body, n=mesh.shape["rows"]),
        mesh=mesh,
        in_specs=placed,
        out_specs=P(None, ("grp", "rows")),
        check_vma=False,
    )
```

```python
import functools

import jax
import jax.numpy as jnp
from jax import lax
from jax.experimental import pallas as pl
from jax.experimental.pallas import tpu as pltpu
from jax.sharding import PartitionSpec as P

FIRMS_PER_SHARD = 1024
LANES = 128
BLOCK = 1024
VMEM_BYTES = 32 * 1024 * 1024
NEAR = 4
F32, BF16 = jnp.float32, jnp.bfloat16
NT = (((1,), (1,)), ((), ()))
NN = (((1,), (0,)), ((), ()))


def dot(a, b, dims=NN):
    return lax.dot_general(a, b, dims, preferred_element_type=F32)


def iota(shape, dim):
    return lax.broadcasted_iota(jnp.int32, shape, dim)


def split(x):
    hi = x.astype(BF16)
    return hi, (x - hi.astype(F32)).astype(BF16)


def row(ref, block, size):
    per = size // LANES
    return jnp.concatenate([ref[block * per + k : block * per + k + 1, :] for k in range(per)], axis=1)


def one_hot(ids, slots):
    kind = BF16 if slots <= 256 else F32
    slot = iota((slots, LANES), 0).astype(F32).astype(kind)
    ids = ids.astype(F32).astype(kind)
    one, zero = jnp.ones((slots, LANES), kind), jnp.zeros((slots, LANES), kind)
    parts = [jnp.where(slot == ids[:, k : k + LANES], one, zero) for k in range(0, ids.shape[1], LANES)]
    return jnp.concatenate(parts, axis=1).astype(BF16)


def same_worker(pad, width):
    return (iota((width, width), 0) // pad == iota((width, width), 1) // pad).astype(F32).astype(BF16)


def by_worker(x, table):
    rows, width = x.shape
    hi, lo = split(x)
    both = jnp.concatenate([hi, lo], axis=0)
    step = table.shape[0]
    total = jnp.concatenate([dot(both[:, k : k + step], table) for k in range(0, width, step)], axis=1)
    return total[:rows] + total[rows:]


def start_all(copies):
    for copy in copies:
        copy.start()


def wait_all(copies):
    for copy in copies:
        copy.wait()


def column_copies(source, target, sems):
    width = source.shape[1]
    cuts = [pl.ds(start, BLOCK) for start in range(0, width, BLOCK)]
    return [pltpu.make_async_copy(source.at[:, cut], target.at[:, cut], sems.at[b]) for b, cut in enumerate(cuts)]


def row_lengths(lengths, pad):
    total_rows = lengths.shape[0] * pad
    here = iota((total_rows, LANES), 0)
    lane = iota((total_rows, LANES), 1)
    wide = jnp.broadcast_to(lengths.astype(F32)[:, None, :], (lengths.shape[0], pad, LANES)).reshape(total_rows, LANES)
    per = LANES // pad
    wide = jnp.where(lane // per == here % pad, wide, 0.0).astype(BF16)
    spread = (iota((LANES, LANES), 0) % per == iota((LANES, LANES), 1) // pad).astype(F32).astype(BF16)
    row_len = dot(wide, spread)
    return row_len, (lane % pad).astype(F32) < row_len


def along(ref):
    return jnp.concatenate([ref[k : k + 1, :] for k in range(ref.shape[0])], axis=1)


def sums_kernel(pad, cap, *refs):
    (probes, lengths_in, ids_in, firms_in), sends, refs = refs[:4], refs[4 : 4 + NEAR], refs[4 + NEAR :]
    x1, mask_ids, weight, valid, x, acc, sums, lengths, ids, firms, sems, small = refs
    copies = column_copies(probes, x, sems)
    first = [
        pltpu.make_async_copy(source, target, small.at[k])
        for k, (source, target) in enumerate(((lengths_in, lengths), (ids_in, ids), (firms_in, firms)))
    ]
    start_all(first)
    start_all(copies)
    columns, slots = sums.shape
    part = columns // NEAR
    me = lax.axis_index("rows") % NEAR
    wait_all(first)
    row_len, inside = row_lengths(lengths[...], pad)
    valid[...] = jnp.where(inside, 1.0, 0.0)
    weight[...] = jnp.where(inside, 1.0 / row_len, 0.0)
    masked = jnp.where(inside, ids[...], -1)
    mask_ids[...] = masked
    keys = (iota((1, slots), 1) // cap * FIRMS_PER_SHARD + along(firms)).astype(F32)
    across = slots // LANES
    rows = ids.shape[0] // across
    masked = jnp.concatenate([masked[k * rows : (k + 1) * rows] for k in range(across)], axis=1).astype(F32)
    for send in sends:
        send[part + 8 :] = masked

    table = same_worker(pad, 256)
    for b in range(len(copies)):
        copies[b].wait()
        ok = row(valid, b, BLOCK)
        x0 = x[:, b * BLOCK : (b + 1) * BLOCK] * ok
        rest = x0 - by_worker(x0, table) * row(weight, b, BLOCK)
        x1[:, b * BLOCK : (b + 1) * BLOCK] = rest
        counted = jnp.broadcast_to(ok, (16, BLOCK)).astype(BF16)
        data = jnp.concatenate([*split(rest), counted], axis=0)
        block = dot(data, one_hot(row(mask_ids, b, BLOCK), slots), NT)
        if b == 0:
            acc[...] = block
        else:
            acc[...] += block
    sums[...] = acc[:columns] + acc[columns : 2 * columns]
    about = jnp.where(iota((8, slots), 0) == 0, keys, acc[2 * columns : 2 * columns + 1])
    for k, send in enumerate(sends):
        send[:part] = sums[pl.ds(pl.multiple_of((me ^ k) * part, part), part), :]
        send[part : part + 8] = about


def join_kernel(part, *refs):
    parts, out = refs[:NEAR], refs[-1]
    for k, one in enumerate(parts):
        out[part * k : part * (k + 1)] = one[:part]
        out[part * NEAR + 2 * k : part * NEAR + 2 * k + 2] = one[part : part + 2]


def pairs_kernel(pad, start, *refs):
    parts, (out, ids, counts) = refs[:-3], refs[-3:]
    slots = out.shape[1]
    kind = BF16 if slots <= 256 else F32
    per = LANES // pad
    total_rows = ids.shape[1]
    across = slots // LANES
    rows = total_rows // across
    for k, part in enumerate(parts):
        for at in range(across):
            ids[k, at * rows : (at + 1) * rows] = part[start:, at * LANES : (at + 1) * LANES]
    at = iota((LANES, pad * LANES), 1)
    deal = (iota((LANES, pad * LANES), 0) == at % per * pad + at // LANES).astype(F32).astype(BF16)
    mine = iota((total_rows, pad * LANES), 1) % LANES // per == iota((total_rows, pad * LANES), 0) % pad
    slot = iota((slots, LANES), 0).astype(F32).astype(kind)
    one, zero = jnp.ones((slots, LANES), kind), jnp.zeros((slots, LANES), kind)
    diagonal = iota((slots, slots), 1) == iota((slots, slots), 0)

    def device(k, carry):
        dealt = dot(jnp.concatenate(split(ids[k]), axis=0), deal)
        dealt = jnp.where(mine, dealt[:total_rows] + dealt[total_rows:], 0.0)
        dealt = jnp.sum(dealt.reshape(total_rows // pad, pad, pad * LANES), axis=1)
        spells = dealt.astype(kind)
        for g in range(total_rows // pad):
            total = zero
            for j in range(pad):
                total += jnp.where(slot == spells[g : g + 1, j * LANES : (j + 1) * LANES], one, zero)
            counts[:, g * LANES : (g + 1) * LANES] = total.astype(BF16)
        valid = jnp.where(dealt >= 0.0, 1.0, 0.0)
        length = valid[:, :LANES]
        for j in range(1, pad):
            length += valid[:, j * LANES : (j + 1) * LANES]
        inverse = 1.0 / length
        inverse = jnp.concatenate([inverse[g : g + 1] for g in range(total_rows // pad)], axis=1)
        here = counts[...].astype(F32)
        total = dot(jnp.concatenate(split(here * inverse), axis=0), counts[...], NT)
        total = total[:slots] + total[slots:] - jnp.where(diagonal, jnp.sum(here, axis=1, keepdims=True), 0.0)
        hi, lo = split(total)
        out[k, :, :slots] = hi
        out[k, :, slots:] = lo
        return carry

    lax.fori_loop(0, len(parts), device, 0, unroll=len(parts) if slots <= 256 else 1)


def same_firm(parts, part, at):
    def keys(one, k):
        return one[part * NEAR + 2 * k : part * NEAR + 2 * k + 1, at]

    down = [jnp.broadcast_to(keys(parts[0], k), (LANES, LANES)).T for k in range(NEAR)]
    down = jnp.concatenate(down, axis=0)
    found = [(down == keys(one, k)).astype(F32).astype(BF16) for one in parts for k in range(NEAR)]
    return jnp.concatenate(found, axis=1)


def gathered(parts, part, at):
    data = [one[part * k : part * (k + 1), at] for one in parts for k in range(NEAR)]
    return jnp.concatenate(split(jnp.concatenate(data, axis=1)), axis=0)


def spread_out(means, out, part, at):
    for k in range(NEAR):
        out[part * k : part * (k + 1), at] = means[:, k * LANES : (k + 1) * LANES]


def each_tile(slots, do):
    tiles = slots // LANES
    if tiles <= 2:
        for t in range(tiles):
            do(t, slice(t * LANES, (t + 1) * LANES))
    else:
        lax.fori_loop(0, tiles, lambda t, c: (do(t, pl.ds(pl.multiple_of(t * LANES, LANES), LANES)), c)[1], 0)


def change_kernel(far, part, *refs):
    parts, (own_pairs, pairs, mean, sums, scale), table = refs[:far], refs[far : far + 5], refs[far + 5 :]
    slots = mean.shape[1]

    def tile(t, at):
        same = same_firm(parts, part, at)
        if table:
            table[0][t] = same
        count = [one[part * NEAR + 2 * k + 1 : part * NEAR + 2 * k + 2, at] for one in parts for k in range(NEAR)]
        count = jnp.concatenate(count, axis=1)
        high = count.astype(BF16).astype(F32)
        counts = jnp.where(iota((16, count.shape[1]), 0) < 8, high, count - high).astype(BF16)
        found = dot(jnp.concatenate([gathered(parts, part, at), counts], axis=0), same, NT)
        size = found[2 * part : 2 * part + 1] + found[2 * part + 8 : 2 * part + 9]
        inverse = 1.0 / jnp.maximum(size, 1.0)
        scale[t] = jnp.broadcast_to(inverse, scale.shape[1:])
        spread_out((found[:part] + found[part : 2 * part]) * inverse, mean, part, at)

    each_tile(slots, tile)
    for k in range(NEAR):
        cut = slice(part * k, part * (k + 1))
        both = jnp.concatenate(split(mean[cut]), axis=0)
        change = dot(both, own_pairs[0] if k == 0 else pairs[k - 1])
        change = change[:part] + change[part:]
        sums[cut] = parts[0][cut] + (change[:, :slots] + change[:, slots:])


def means_kernel(far, part, *refs):
    parts, source, (scale, mean), sends, second = refs[:far], refs[far:-7], refs[-7:-5], refs[-5:-1], refs[-1]

    def tile(t, at):
        same = source[0][t] if len(source) == 1 else same_firm(source, part, at)
        found = dot(gathered(parts, part, at), same, NT)
        spread_out((found[:part] + found[part:]) * scale[t][:1], second, part, at)

    each_tile(mean.shape[1], tile)
    for k, send in enumerate(sends):
        cut = slice(part * k, part * (k + 1))
        send[:part] = mean[cut]
        send[part:] = mean[cut] + second[cut]


def last_kernel(pad, part, *refs):
    parts, (x1, mask_ids, weight, out, means, y, sems) = refs[:NEAR], refs[NEAR:]
    outs = column_copies(y, out, sems)
    me = lax.axis_index("rows") % NEAR
    columns, slots = means.shape[1:]
    for k, one in enumerate(parts):
        at = pl.ds(pl.multiple_of((me ^ k) * part, part), part)
        means[0, at, :] = one[:part]
        means[1, at, :] = one[part:]
    both = jnp.concatenate([*split(means[0]), *split(means[1])], axis=0)
    table = same_worker(pad, 256)
    for b in range(len(outs)):
        at = slice(b * BLOCK, (b + 1) * BLOCK)
        found = dot(both, one_hot(row(mask_ids, b, BLOCK), slots))
        first = found[:columns] + found[columns : 2 * columns]
        total = found[2 * columns : 3 * columns] + found[3 * columns :]
        y[:, at] = x1[:, at] - total + by_worker(first, table) * row(weight, b, BLOCK)
        outs[b].start()
    wait_all(outs)


def near_exchange(parts, n):
    steps = [[(i, i ^ k) for i in range(n)] for k in range(1, NEAR)]
    return [parts[0]] + [lax.ppermute(one, "rows", step) for one, step in zip(parts[1:], steps)]


def far_share(one, n):
    steps = [[(i, i ^ (k * NEAR)) for i in range(n)] for k in range(1, n // NEAR)]
    return [one] + [lax.ppermute(one, "rows", step) for step in steps]


def in_hbm(x):
    return pltpu.with_memory_space_constraint(x, pltpu.HBM)


def call(kernel, out_shape, in_specs, out_specs, scratch, flops, moved):
    return pl.pallas_call(
        kernel,
        out_shape=out_shape,
        in_specs=in_specs,
        out_specs=out_specs,
        scratch_shapes=scratch,
        compiler_params=pltpu.CompilerParams(vmem_limit_bytes=VMEM_BYTES),
        cost_estimate=pl.CostEstimate(flops=flops, bytes_accessed=moved, transcendentals=0),
    )


def body(probes, worker_len, spell_to_slot, slot_to_firm, *, n):
    columns, rows_dev = probes.shape
    workers = worker_len.shape[0]
    pad = rows_dev // workers
    slots = slot_to_firm.shape[0]
    tiles = slots // LANES
    part = columns // NEAR
    far = n // NEAR
    keep = tiles * NEAR * n * LANES * LANES * 2 <= 8 * 1024 * 1024
    blocks = rows_dev // BLOCK
    vmem, hbm = pl.BlockSpec(memory_space=pltpu.VMEM), pl.BlockSpec(memory_space=pltpu.HBM)
    lengths = worker_len.reshape(workers // LANES, LANES)
    ids = spell_to_slot.reshape(rows_dev // LANES, LANES)
    firms = slot_to_firm.reshape(tiles, LANES)
    array = jax.ShapeDtypeStruct
    of_rows = (rows_dev // LANES, LANES)
    work = 2 * rows_dev * slots * 2 * columns
    sems = pltpu.SemaphoreType.DMA((blocks,))
    whole = (columns, rows_dev)
    about = part + 8
    message = array((about + rows_dev // slots, slots), F32)
    of_near = array((columns, slots), F32)

    *sends, x1, mask_ids, weight = call(
        functools.partial(sums_kernel, pad, slots // n),
        [message] * NEAR + [array(whole, F32), array(of_rows, jnp.int32), array(of_rows, F32)],
        [hbm] * 4,
        [vmem] * (NEAR + 3),
        [
            pltpu.VMEM(of_rows, F32),
            pltpu.VMEM(whole, F32),
            pltpu.VMEM((2 * columns + 16, slots), F32),
            pltpu.VMEM((columns, slots), F32),
            pltpu.VMEM(lengths.shape, jnp.int32),
            pltpu.VMEM(ids.shape, jnp.int32),
            pltpu.VMEM(firms.shape, jnp.int32),
            sems,
            pltpu.SemaphoreType.DMA((3,)),
        ],
        2 * work,
        4 * columns * rows_dev,
    )(in_hbm(probes), in_hbm(lengths), in_hbm(ids), in_hbm(firms))

    def pair_counts(parts):
        return call(
            functools.partial(pairs_kernel, pad, about),
            array((len(parts), slots, 2 * slots), BF16),
            [vmem] * len(parts),
            vmem,
            [pltpu.VMEM((len(parts), *of_rows), F32), pltpu.VMEM((slots, workers), BF16)],
            work * len(parts) // 4,
            4 * slots * slots,
        )(*parts)

    arrived = near_exchange(sends, n)
    own_pairs = pair_counts(arrived[:1])
    joined = call(
        functools.partial(join_kernel, part),
        array((columns + 2 * NEAR, slots), F32),
        [vmem] * (NEAR + 1),
        vmem,
        [],
        0,
        message.size * 8,
    )(*arrived, own_pairs)
    shared = far_share(joined, n)
    pairs = pair_counts(arrived[1:])
    table = array((tiles, NEAR * LANES, n * LANES), BF16)
    scale = array((tiles, 8, NEAR * LANES), F32)
    mean, sums, scales, *tables = call(
        functools.partial(change_kernel, far, part),
        [of_near, of_near, scale] + [table] * keep,
        [vmem] * (far + 2),
        [vmem] * (3 + keep),
        [],
        work // 4,
        slots * slots * 4,
    )(*shared, own_pairs, pairs)
    again = far_share(sums, n)
    source = tables if keep else shared
    sends = call(
        functools.partial(means_kernel, far, part),
        [array((2 * part, slots), F32)] * NEAR,
        [vmem] * (far + len(source) + 2),
        [vmem] * NEAR,
        [pltpu.VMEM((columns, slots), F32)],
        work // 4,
        slots * slots * 4,
    )(*again, *source, scales, mean)
    arrived = near_exchange(sends, n)
    return call(
        functools.partial(last_kernel, pad, part),
        array(whole, F32),
        [vmem] * (NEAR + 3),
        hbm,
        [pltpu.VMEM((2, columns, slots), F32), pltpu.VMEM(whole, F32), sems],
        work,
        8 * columns * rows_dev,
    )(*arrived, x1, mask_ids, weight)


def solution(mesh):
    placed = (P(None, ("grp", "rows")), P(("grp", "rows")), P(("grp", "rows")), P(("grp", "rows")))
    return jax.shard_map(
        functools.partial(body, n=mesh.shape["rows"]),
        mesh=mesh,
        in_specs=placed,
        out_specs=P(None, ("grp", "rows")),
        check_vma=False,
    )
```

```python
import functools

import jax
import jax.numpy as jnp
from jax import lax
from jax.experimental import pallas as pl
from jax.experimental.pallas import tpu as pltpu
from jax.sharding import PartitionSpec as P

FIRMS_PER_SHARD = 1024
LANES = 128
BLOCK = 1024
VMEM_BYTES = 32 * 1024 * 1024
NEAR = 4
F32, BF16 = jnp.float32, jnp.bfloat16
NT = (((1,), (1,)), ((), ()))
NN = (((1,), (0,)), ((), ()))


def dot(a, b, dims=NN):
    return lax.dot_general(a, b, dims, preferred_element_type=F32)


def iota(shape, dim):
    return lax.broadcasted_iota(jnp.int32, shape, dim)


def split(x):
    hi = x.astype(BF16)
    return hi, (x - hi.astype(F32)).astype(BF16)


def row(ref, block, size):
    per = size // LANES
    return jnp.concatenate([ref[block * per + k : block * per + k + 1, :] for k in range(per)], axis=1)


def one_hot(ids, slots):
    kind = BF16 if slots <= 256 else F32
    slot = iota((slots, LANES), 0).astype(F32).astype(kind)
    ids = ids.astype(F32).astype(kind)
    one, zero = jnp.ones((slots, LANES), kind), jnp.zeros((slots, LANES), kind)
    parts = [jnp.where(slot == ids[:, k : k + LANES], one, zero) for k in range(0, ids.shape[1], LANES)]
    return jnp.concatenate(parts, axis=1).astype(BF16)


def one_hot_down(columns, slots):
    kind = BF16 if slots <= 256 else F32
    one, zero = jnp.ones((LANES, LANES), kind), jnp.zeros((LANES, LANES), kind)
    along_slots = [(iota((LANES, LANES), 1) + at).astype(F32).astype(kind) for at in range(0, slots, LANES)]
    parts = []
    for k in range(columns.shape[1]):
        ids = jnp.broadcast_to(columns[:, k : k + 1], (LANES, LANES)).astype(kind)
        parts.append(jnp.concatenate([jnp.where(slot == ids, one, zero) for slot in along_slots], axis=1))
    return jnp.concatenate(parts, axis=0).astype(BF16)


def same_worker(pad, width):
    return (iota((width, width), 0) // pad == iota((width, width), 1) // pad).astype(F32).astype(BF16)


def by_worker(x, table):
    rows, width = x.shape
    hi, lo = split(x)
    both = jnp.concatenate([hi, lo], axis=0)
    step = table.shape[0]
    total = jnp.concatenate([dot(both[:, k : k + step], table) for k in range(0, width, step)], axis=1)
    return total[:rows] + total[rows:]


def start_all(copies):
    for copy in copies:
        copy.start()


def wait_all(copies):
    for copy in copies:
        copy.wait()


def column_copies(source, target, sems):
    width = source.shape[1]
    cuts = [pl.ds(start, BLOCK) for start in range(0, width, BLOCK)]
    return [pltpu.make_async_copy(source.at[:, cut], target.at[:, cut], sems.at[b]) for b, cut in enumerate(cuts)]


def row_lengths(lengths, pad):
    total_rows = lengths.shape[0] * pad
    here = iota((total_rows, LANES), 0)
    lane = iota((total_rows, LANES), 1)
    wide = jnp.broadcast_to(lengths.astype(F32)[:, None, :], (lengths.shape[0], pad, LANES)).reshape(total_rows, LANES)
    per = LANES // pad
    wide = jnp.where(lane // per == here % pad, wide, 0.0).astype(BF16)
    spread = (iota((LANES, LANES), 0) % per == iota((LANES, LANES), 1) // pad).astype(F32).astype(BF16)
    row_len = dot(wide, spread)
    return row_len, (lane % pad).astype(F32) < row_len


def along(ref):
    return jnp.concatenate([ref[k : k + 1, :] for k in range(ref.shape[0])], axis=1)


def sums_kernel(pad, cap, *refs):
    (probes, lengths_in, ids_in, firms_in), sends, refs = refs[:4], refs[4 : 4 + NEAR], refs[4 + NEAR :]
    x1, mask_ids, weight, valid, x, acc, sums, lengths, ids, firms, sems, small = refs
    copies = column_copies(probes, x, sems)
    first = [
        pltpu.make_async_copy(source, target, small.at[k])
        for k, (source, target) in enumerate(((lengths_in, lengths), (ids_in, ids), (firms_in, firms)))
    ]
    start_all(first)
    start_all(copies)
    columns, slots = sums.shape
    part = columns // NEAR
    me = lax.axis_index("rows") % NEAR
    wait_all(first)
    row_len, inside = row_lengths(lengths[...], pad)
    valid[...] = jnp.where(inside, 1.0, 0.0)
    weight[...] = jnp.where(inside, 1.0 / row_len, 0.0)
    masked = jnp.where(inside, ids[...], -1)
    mask_ids[...] = masked
    turned = jnp.concatenate([masked.astype(F32)] * (LANES // masked.shape[0]), axis=0).T
    keys = (iota((1, slots), 1) // cap * FIRMS_PER_SHARD + along(firms)).astype(F32)
    across = slots // LANES
    rows = ids.shape[0] // across
    masked = jnp.concatenate([masked[k * rows : (k + 1) * rows] for k in range(across)], axis=1).astype(F32)
    for send in sends:
        send[part + 8 :] = masked

    table = same_worker(pad, 256)
    for b in range(len(copies)):
        copies[b].wait()
        ok = row(valid, b, BLOCK)
        x0 = x[:, b * BLOCK : (b + 1) * BLOCK] * ok
        rest = x0 - by_worker(x0, table) * row(weight, b, BLOCK)
        x1[:, b * BLOCK : (b + 1) * BLOCK] = rest
        counted = jnp.broadcast_to(ok, (16, BLOCK)).astype(BF16)
        data = jnp.concatenate([*split(rest), counted], axis=0)
        per = BLOCK // LANES
        block = dot(data, one_hot_down(turned[:, b * per : (b + 1) * per], slots))
        if b == 0:
            acc[...] = block
        else:
            acc[...] += block
    sums[...] = acc[:columns] + acc[columns : 2 * columns]
    about = jnp.where(iota((8, slots), 0) == 0, keys, acc[2 * columns : 2 * columns + 1])
    for k, send in enumerate(sends):
        send[:part] = sums[pl.ds(pl.multiple_of((me ^ k) * part, part), part), :]
        send[part : part + 8] = about


def join_kernel(part, *refs):
    parts, out = refs[:NEAR], refs[-1]
    for k, one in enumerate(parts):
        out[part * k : part * (k + 1)] = one[:part]
        out[part * NEAR + 2 * k : part * NEAR + 2 * k + 2] = one[part : part + 2]


def pairs_kernel(pad, start, *refs):
    parts, (out, ids, counts) = refs[:-3], refs[-3:]
    slots = out.shape[1]
    kind = BF16 if slots <= 256 else F32
    per = LANES // pad
    total_rows = ids.shape[1]
    across = slots // LANES
    rows = total_rows // across
    for k, part in enumerate(parts):
        for at in range(across):
            ids[k, at * rows : (at + 1) * rows] = part[start:, at * LANES : (at + 1) * LANES]
    at = iota((LANES, pad * LANES), 1)
    deal = (iota((LANES, pad * LANES), 0) == at % per * pad + at // LANES).astype(F32).astype(BF16)
    mine = iota((total_rows, pad * LANES), 1) % LANES // per == iota((total_rows, pad * LANES), 0) % pad
    slot = iota((slots, LANES), 0).astype(F32).astype(kind)
    one, zero = jnp.ones((slots, LANES), kind), jnp.zeros((slots, LANES), kind)
    diagonal = iota((slots, slots), 1) == iota((slots, slots), 0)

    def device(k, carry):
        dealt = dot(jnp.concatenate(split(ids[k]), axis=0), deal)
        dealt = jnp.where(mine, dealt[:total_rows] + dealt[total_rows:], 0.0)
        dealt = jnp.sum(dealt.reshape(total_rows // pad, pad, pad * LANES), axis=1)
        spells = dealt.astype(kind)
        for g in range(total_rows // pad):
            total = zero
            for j in range(pad):
                total += jnp.where(slot == spells[g : g + 1, j * LANES : (j + 1) * LANES], one, zero)
            counts[:, g * LANES : (g + 1) * LANES] = total.astype(BF16)
        valid = jnp.where(dealt >= 0.0, 1.0, 0.0)
        length = valid[:, :LANES]
        for j in range(1, pad):
            length += valid[:, j * LANES : (j + 1) * LANES]
        inverse = 1.0 / length
        inverse = jnp.concatenate([inverse[g : g + 1] for g in range(total_rows // pad)], axis=1)
        here = counts[...].astype(F32)
        total = dot(jnp.concatenate(split(here * inverse), axis=0), counts[...], NT)
        total = total[:slots] + total[slots:] - jnp.where(diagonal, jnp.sum(here, axis=1, keepdims=True), 0.0)
        hi, lo = split(total)
        out[k, :, :slots] = hi
        out[k, :, slots:] = lo
        return carry

    lax.fori_loop(0, len(parts), device, 0, unroll=len(parts) if slots <= 256 else 1)


def same_firm(parts, part, at):
    keys = [one[part * NEAR + 2 * k : part * NEAR + 2 * k + 1, at] for one in parts for k in range(NEAR)]
    mine = jnp.concatenate(keys[:NEAR], axis=1)
    down = jnp.concatenate(keys, axis=0).T
    found = [(down[:, k : k + 1] == mine).astype(F32).astype(BF16) for k in range(len(keys))]
    return jnp.concatenate(found, axis=0)


def gathered(parts, part, at):
    data = [one[part * k : part * (k + 1), at] for one in parts for k in range(NEAR)]
    return jnp.concatenate(split(jnp.concatenate(data, axis=1)), axis=0)


def spread_out(means, out, part, at):
    for k in range(NEAR):
        out[part * k : part * (k + 1), at] = means[:, k * LANES : (k + 1) * LANES]


def each_tile(slots, do):
    tiles = slots // LANES
    if tiles <= 2:
        for t in range(tiles):
            do(t, slice(t * LANES, (t + 1) * LANES))
    else:
        lax.fori_loop(0, tiles, lambda t, c: (do(t, pl.ds(pl.multiple_of(t * LANES, LANES), LANES)), c)[1], 0)


def change_kernel(far, part, *refs):
    parts, (own_pairs, pairs, mean, sums, scale), table = refs[:far], refs[far : far + 5], refs[far + 5 :]
    slots = mean.shape[1]

    def tile(t, at):
        same = same_firm(parts, part, at)
        if table:
            table[0][t] = same
        count = [one[part * NEAR + 2 * k + 1 : part * NEAR + 2 * k + 2, at] for one in parts for k in range(NEAR)]
        count = jnp.concatenate(count, axis=1)
        high = count.astype(BF16).astype(F32)
        counts = jnp.where(iota((16, count.shape[1]), 0) < 8, high, count - high).astype(BF16)
        found = dot(jnp.concatenate([gathered(parts, part, at), counts], axis=0), same)
        size = found[2 * part : 2 * part + 1] + found[2 * part + 8 : 2 * part + 9]
        inverse = 1.0 / jnp.maximum(size, 1.0)
        scale[t] = jnp.broadcast_to(inverse, scale.shape[1:])
        spread_out((found[:part] + found[part : 2 * part]) * inverse, mean, part, at)

    each_tile(slots, tile)
    for k in range(NEAR):
        cut = slice(part * k, part * (k + 1))
        both = jnp.concatenate(split(mean[cut]), axis=0)
        change = dot(both, own_pairs[0] if k == 0 else pairs[k - 1])
        change = change[:part] + change[part:]
        sums[cut] = parts[0][cut] + (change[:, :slots] + change[:, slots:])


def means_kernel(far, part, *refs):
    parts, source, (scale, mean), sends, second = refs[:far], refs[far:-7], refs[-7:-5], refs[-5:-1], refs[-1]

    def tile(t, at):
        same = source[0][t] if len(source) == 1 else same_firm(source, part, at)
        found = dot(gathered(parts, part, at), same)
        spread_out((found[:part] + found[part:]) * scale[t][:1], second, part, at)

    each_tile(mean.shape[1], tile)
    for k, send in enumerate(sends):
        cut = slice(part * k, part * (k + 1))
        send[:part] = mean[cut]
        send[part:] = mean[cut] + second[cut]


def last_kernel(pad, part, *refs):
    parts, (x1, mask_ids, weight, out, means, y, sems) = refs[:NEAR], refs[NEAR:]
    outs = column_copies(y, out, sems)
    me = lax.axis_index("rows") % NEAR
    columns, slots = means.shape[1:]
    for k, one in enumerate(parts):
        at = pl.ds(pl.multiple_of((me ^ k) * part, part), part)
        means[0, at, :] = one[:part]
        means[1, at, :] = one[part:]
    both = jnp.concatenate([*split(means[0]), *split(means[1])], axis=0)
    table = same_worker(pad, 256)
    for b in range(len(outs)):
        at = slice(b * BLOCK, (b + 1) * BLOCK)
        found = dot(both, one_hot(row(mask_ids, b, BLOCK), slots))
        first = found[:columns] + found[columns : 2 * columns]
        total = found[2 * columns : 3 * columns] + found[3 * columns :]
        y[:, at] = x1[:, at] - total + by_worker(first, table) * row(weight, b, BLOCK)
        outs[b].start()
    wait_all(outs)


def near_exchange(parts, n):
    steps = [[(i, i ^ k) for i in range(n)] for k in range(1, NEAR)]
    return [parts[0]] + [lax.ppermute(one, "rows", step) for one, step in zip(parts[1:], steps)]


def far_share(one, n):
    steps = [[(i, i ^ (k * NEAR)) for i in range(n)] for k in range(1, n // NEAR)]
    return [one] + [lax.ppermute(one, "rows", step) for step in steps]


def in_hbm(x):
    return pltpu.with_memory_space_constraint(x, pltpu.HBM)


def call(kernel, out_shape, in_specs, out_specs, scratch, flops, moved):
    return pl.pallas_call(
        kernel,
        out_shape=out_shape,
        in_specs=in_specs,
        out_specs=out_specs,
        scratch_shapes=scratch,
        compiler_params=pltpu.CompilerParams(vmem_limit_bytes=VMEM_BYTES),
        cost_estimate=pl.CostEstimate(flops=flops, bytes_accessed=moved, transcendentals=0),
    )


def body(probes, worker_len, spell_to_slot, slot_to_firm, *, n):
    columns, rows_dev = probes.shape
    workers = worker_len.shape[0]
    pad = rows_dev // workers
    slots = slot_to_firm.shape[0]
    tiles = slots // LANES
    part = columns // NEAR
    far = n // NEAR
    keep = tiles * NEAR * n * LANES * LANES * 2 <= 8 * 1024 * 1024
    blocks = rows_dev // BLOCK
    vmem, hbm = pl.BlockSpec(memory_space=pltpu.VMEM), pl.BlockSpec(memory_space=pltpu.HBM)
    lengths = worker_len.reshape(workers // LANES, LANES)
    ids = spell_to_slot.reshape(rows_dev // LANES, LANES)
    firms = slot_to_firm.reshape(tiles, LANES)
    array = jax.ShapeDtypeStruct
    of_rows = (rows_dev // LANES, LANES)
    work = 2 * rows_dev * slots * 2 * columns
    sems = pltpu.SemaphoreType.DMA((blocks,))
    whole = (columns, rows_dev)
    about = part + 8
    message = array((about + rows_dev // slots, slots), F32)
    of_near = array((columns, slots), F32)

    *sends, x1, mask_ids, weight = call(
        functools.partial(sums_kernel, pad, slots // n),
        [message] * NEAR + [array(whole, F32), array(of_rows, jnp.int32), array(of_rows, F32)],
        [hbm] * 4,
        [vmem] * (NEAR + 3),
        [
            pltpu.VMEM(of_rows, F32),
            pltpu.VMEM(whole, F32),
            pltpu.VMEM((2 * columns + 16, slots), F32),
            pltpu.VMEM((columns, slots), F32),
            pltpu.VMEM(lengths.shape, jnp.int32),
            pltpu.VMEM(ids.shape, jnp.int32),
            pltpu.VMEM(firms.shape, jnp.int32),
            sems,
            pltpu.SemaphoreType.DMA((3,)),
        ],
        2 * work,
        4 * columns * rows_dev,
    )(in_hbm(probes), in_hbm(lengths), in_hbm(ids), in_hbm(firms))

    def pair_counts(parts):
        return call(
            functools.partial(pairs_kernel, pad, about),
            array((len(parts), slots, 2 * slots), BF16),
            [vmem] * len(parts),
            vmem,
            [pltpu.VMEM((len(parts), *of_rows), F32), pltpu.VMEM((slots, workers), BF16)],
            work * len(parts) // 4,
            4 * slots * slots,
        )(*parts)

    arrived = near_exchange(sends, n)
    own_pairs = pair_counts(arrived[:1])
    joined = call(
        functools.partial(join_kernel, part),
        array((columns + 2 * NEAR, slots), F32),
        [vmem] * (NEAR + 1),
        vmem,
        [],
        0,
        message.size * 8,
    )(*arrived, own_pairs)
    shared = far_share(joined, n)
    pairs = pair_counts(arrived[1:])
    table = array((tiles, n * LANES, NEAR * LANES), BF16)
    scale = array((tiles, 8, NEAR * LANES), F32)
    mean, sums, scales, *tables = call(
        functools.partial(change_kernel, far, part),
        [of_near, of_near, scale] + [table] * keep,
        [vmem] * (far + 2),
        [vmem] * (3 + keep),
        [],
        work // 4,
        slots * slots * 4,
    )(*shared, own_pairs, pairs)
    again = far_share(sums, n)
    source = tables if keep else shared
    sends = call(
        functools.partial(means_kernel, far, part),
        [array((2 * part, slots), F32)] * NEAR,
        [vmem] * (far + len(source) + 2),
        [vmem] * NEAR,
        [pltpu.VMEM((columns, slots), F32)],
        work // 4,
        slots * slots * 4,
    )(*again, *source, scales, mean)
    arrived = near_exchange(sends, n)
    return call(
        functools.partial(last_kernel, pad, part),
        array(whole, F32),
        [vmem] * (NEAR + 3),
        hbm,
        [pltpu.VMEM((2, columns, slots), F32), pltpu.VMEM(whole, F32), sems],
        work,
        8 * columns * rows_dev,
    )(*arrived, x1, mask_ids, weight)


def solution(mesh):
    placed = (P(None, ("grp", "rows")), P(("grp", "rows")), P(("grp", "rows")), P(("grp", "rows")))
    return jax.shard_map(
        functools.partial(body, n=mesh.shape["rows"]),
        mesh=mesh,
        in_specs=placed,
        out_specs=P(None, ("grp", "rows")),
        check_vma=False,
    )
```

```python
import functools

import jax
import jax.numpy as jnp
from jax import lax
from jax.experimental import pallas as pl
from jax.experimental.pallas import tpu as pltpu
from jax.sharding import PartitionSpec as P

FIRMS_PER_SHARD = 1024
LANES = 128
BLOCK = 1024
VMEM_BYTES = 32 * 1024 * 1024
NEAR = 4
F32, BF16 = jnp.float32, jnp.bfloat16
NT = (((1,), (1,)), ((), ()))
NN = (((1,), (0,)), ((), ()))


def dot(a, b, dims=NN):
    return lax.dot_general(a, b, dims, preferred_element_type=F32)


def iota(shape, dim):
    return lax.broadcasted_iota(jnp.int32, shape, dim)


def split(x):
    hi = x.astype(BF16)
    return hi, (x - hi.astype(F32)).astype(BF16)


def row(ref, block, size):
    per = size // LANES
    return jnp.concatenate([ref[block * per + k : block * per + k + 1, :] for k in range(per)], axis=1)


def one_hot(ids, slots):
    kind = BF16 if slots <= 256 else F32
    slot = iota((slots, LANES), 0).astype(F32).astype(kind)
    ids = ids.astype(F32).astype(kind)
    one, zero = jnp.ones((slots, LANES), kind), jnp.zeros((slots, LANES), kind)
    parts = [jnp.where(slot == ids[:, k : k + LANES], one, zero) for k in range(0, ids.shape[1], LANES)]
    return jnp.concatenate(parts, axis=1).astype(BF16)


def one_hot_down(columns, slots):
    kind = BF16 if slots <= 256 else F32
    one, zero = jnp.ones((LANES, LANES), kind), jnp.zeros((LANES, LANES), kind)
    along_slots = [(iota((LANES, LANES), 1) + at).astype(F32).astype(kind) for at in range(0, slots, LANES)]
    parts = []
    for k in range(columns.shape[1]):
        ids = jnp.broadcast_to(columns[:, k : k + 1], (LANES, LANES)).astype(kind)
        parts.append(jnp.concatenate([jnp.where(slot == ids, one, zero) for slot in along_slots], axis=1))
    return jnp.concatenate(parts, axis=0).astype(BF16)


def by_worker(x, pad):
    parts = []
    steps = [1 << k for k in range(pad.bit_length() - 1)]
    for at in range(0, x.shape[1], LANES):
        part = x[:, at : at + LANES]
        for step in steps:
            part += pltpu.roll(part, LANES - step, axis=1)
        part = jnp.where(iota(part.shape, 1) % pad == 0, part, 0.0)
        for step in steps:
            part += pltpu.roll(part, step, axis=1)
        parts.append(part)
    return jnp.concatenate(parts, axis=1)


def start_all(copies):
    for copy in copies:
        copy.start()


def wait_all(copies):
    for copy in copies:
        copy.wait()


def column_copies(source, target, sems):
    width = source.shape[1]
    cuts = [pl.ds(start, BLOCK) for start in range(0, width, BLOCK)]
    return [pltpu.make_async_copy(source.at[:, cut], target.at[:, cut], sems.at[b]) for b, cut in enumerate(cuts)]


def row_lengths(lengths, pad):
    total_rows = lengths.shape[0] * pad
    here = iota((total_rows, LANES), 0)
    lane = iota((total_rows, LANES), 1)
    wide = jnp.broadcast_to(lengths.astype(F32)[:, None, :], (lengths.shape[0], pad, LANES)).reshape(total_rows, LANES)
    per = LANES // pad
    wide = jnp.where(lane // per == here % pad, wide, 0.0).astype(BF16)
    spread = (iota((LANES, LANES), 0) % per == iota((LANES, LANES), 1) // pad).astype(F32).astype(BF16)
    row_len = dot(wide, spread)
    return row_len, (lane % pad).astype(F32) < row_len


def along(ref):
    return jnp.concatenate([ref[k : k + 1, :] for k in range(ref.shape[0])], axis=1)


def sums_kernel(pad, cap, *refs):
    (probes, lengths_in, ids_in, firms_in), sends, refs = refs[:4], refs[4 : 4 + NEAR], refs[4 + NEAR :]
    x1, mask_ids, weight, valid, x, acc, sums, lengths, ids, firms, sems, small = refs
    copies = column_copies(probes, x, sems)
    first = [
        pltpu.make_async_copy(source, target, small.at[k])
        for k, (source, target) in enumerate(((lengths_in, lengths), (ids_in, ids), (firms_in, firms)))
    ]
    start_all(first)
    start_all(copies)
    columns, slots = sums.shape
    part = columns // NEAR
    me = lax.axis_index("rows") % NEAR
    wait_all(first)
    row_len, inside = row_lengths(lengths[...], pad)
    valid[...] = jnp.where(inside, 1.0, 0.0)
    weight[...] = jnp.where(inside, 1.0 / row_len, 0.0)
    masked = jnp.where(inside, ids[...], -1)
    mask_ids[...] = masked
    turned = jnp.concatenate([masked.astype(F32)] * (LANES // masked.shape[0]), axis=0).T
    keys = (iota((1, slots), 1) // cap * FIRMS_PER_SHARD + along(firms)).astype(F32)
    across = slots // LANES
    rows = ids.shape[0] // across
    masked = jnp.concatenate([masked[k * rows : (k + 1) * rows] for k in range(across)], axis=1).astype(F32)
    for send in sends:
        send[part + 8 :] = masked

    for b in range(len(copies)):
        copies[b].wait()
        ok = row(valid, b, BLOCK)
        x0 = x[:, b * BLOCK : (b + 1) * BLOCK] * ok
        rest = x0 - by_worker(x0, pad) * row(weight, b, BLOCK)
        x1[:, b * BLOCK : (b + 1) * BLOCK] = rest
        counted = jnp.broadcast_to(ok, (16, BLOCK)).astype(BF16)
        data = jnp.concatenate([*split(rest), counted], axis=0)
        per = BLOCK // LANES
        block = dot(data, one_hot_down(turned[:, b * per : (b + 1) * per], slots))
        if b == 0:
            acc[...] = block
        else:
            acc[...] += block
    sums[...] = acc[:columns] + acc[columns : 2 * columns]
    about = jnp.where(iota((8, slots), 0) == 0, keys, acc[2 * columns : 2 * columns + 1])
    for k, send in enumerate(sends):
        send[:part] = sums[pl.ds(pl.multiple_of((me ^ k) * part, part), part), :]
        send[part : part + 8] = about


def join_kernel(part, *refs):
    parts, out = refs[:NEAR], refs[-1]
    for k, one in enumerate(parts):
        out[part * k : part * (k + 1)] = one[:part]
        out[part * NEAR + 2 * k : part * NEAR + 2 * k + 2] = one[part : part + 2]


def pairs_kernel(pad, start, *refs):
    parts, (out, ids, counts) = refs[:-3], refs[-3:]
    slots = out.shape[1]
    kind = BF16 if slots <= 256 else F32
    per = LANES // pad
    total_rows = ids.shape[1]
    across = slots // LANES
    rows = total_rows // across
    for k, part in enumerate(parts):
        for at in range(across):
            ids[k, at * rows : (at + 1) * rows] = part[start:, at * LANES : (at + 1) * LANES]
    at = iota((LANES, pad * LANES), 1)
    deal = (iota((LANES, pad * LANES), 0) == at % per * pad + at // LANES).astype(F32).astype(BF16)
    mine = iota((total_rows, pad * LANES), 1) % LANES // per == iota((total_rows, pad * LANES), 0) % pad
    slot = iota((slots, LANES), 0).astype(F32).astype(kind)
    one, zero = jnp.ones((slots, LANES), kind), jnp.zeros((slots, LANES), kind)
    diagonal = iota((slots, slots), 1) == iota((slots, slots), 0)

    def device(k, carry):
        dealt = dot(jnp.concatenate(split(ids[k]), axis=0), deal)
        dealt = jnp.where(mine, dealt[:total_rows] + dealt[total_rows:], 0.0)
        dealt = jnp.sum(dealt.reshape(total_rows // pad, pad, pad * LANES), axis=1)
        spells = dealt.astype(kind)
        for g in range(total_rows // pad):
            total = zero
            for j in range(pad):
                total += jnp.where(slot == spells[g : g + 1, j * LANES : (j + 1) * LANES], one, zero)
            counts[:, g * LANES : (g + 1) * LANES] = total.astype(BF16)
        valid = jnp.where(dealt >= 0.0, 1.0, 0.0)
        length = valid[:, :LANES]
        for j in range(1, pad):
            length += valid[:, j * LANES : (j + 1) * LANES]
        inverse = 1.0 / length
        inverse = jnp.concatenate([inverse[g : g + 1] for g in range(total_rows // pad)], axis=1)
        here = counts[...].astype(F32)
        total = dot(jnp.concatenate(split(here * inverse), axis=0), counts[...], NT)
        total = total[:slots] + total[slots:] - jnp.where(diagonal, jnp.sum(here, axis=1, keepdims=True), 0.0)
        hi, lo = split(total)
        out[k, :, :slots] = hi
        out[k, :, slots:] = lo
        return carry

    lax.fori_loop(0, len(parts), device, 0, unroll=len(parts) if slots <= 256 else 1)


def same_firm(parts, part, at):
    keys = [one[part * NEAR + 2 * k : part * NEAR + 2 * k + 1, at] for one in parts for k in range(NEAR)]
    mine = jnp.concatenate(keys[:NEAR], axis=1)
    down = jnp.concatenate(keys, axis=0).T
    found = [(down[:, k : k + 1] == mine).astype(F32).astype(BF16) for k in range(len(keys))]
    return jnp.concatenate(found, axis=0)


def gathered(parts, part, at):
    data = [one[part * k : part * (k + 1), at] for one in parts for k in range(NEAR)]
    return jnp.concatenate(split(jnp.concatenate(data, axis=1)), axis=0)


def spread_out(means, out, part, at):
    for k in range(NEAR):
        out[part * k : part * (k + 1), at] = means[:, k * LANES : (k + 1) * LANES]


def each_tile(slots, do):
    tiles = slots // LANES
    if tiles <= 2:
        for t in range(tiles):
            do(t, slice(t * LANES, (t + 1) * LANES))
    else:
        lax.fori_loop(0, tiles, lambda t, c: (do(t, pl.ds(pl.multiple_of(t * LANES, LANES), LANES)), c)[1], 0)


def change_kernel(far, part, *refs):
    parts, (own_pairs, pairs, mean, sums, scale), table = refs[:far], refs[far : far + 5], refs[far + 5 :]
    slots = mean.shape[1]

    def tile(t, at):
        same = same_firm(parts, part, at)
        if table:
            table[0][t] = same
        count = [one[part * NEAR + 2 * k + 1 : part * NEAR + 2 * k + 2, at] for one in parts for k in range(NEAR)]
        count = jnp.concatenate(count, axis=1)
        high = count.astype(BF16).astype(F32)
        counts = jnp.where(iota((16, count.shape[1]), 0) < 8, high, count - high).astype(BF16)
        found = dot(jnp.concatenate([gathered(parts, part, at), counts], axis=0), same)
        size = found[2 * part : 2 * part + 1] + found[2 * part + 8 : 2 * part + 9]
        inverse = 1.0 / jnp.maximum(size, 1.0)
        scale[t] = jnp.broadcast_to(inverse, scale.shape[1:])
        spread_out((found[:part] + found[part : 2 * part]) * inverse, mean, part, at)

    each_tile(slots, tile)
    for k in range(NEAR):
        cut = slice(part * k, part * (k + 1))
        both = jnp.concatenate(split(mean[cut]), axis=0)
        change = dot(both, own_pairs[0] if k == 0 else pairs[k - 1])
        change = change[:part] + change[part:]
        sums[cut] = parts[0][cut] + (change[:, :slots] + change[:, slots:])


def means_kernel(far, part, *refs):
    parts, source, (scale, mean), sends, second = refs[:far], refs[far:-7], refs[-7:-5], refs[-5:-1], refs[-1]

    def tile(t, at):
        same = source[0][t] if len(source) == 1 else same_firm(source, part, at)
        found = dot(gathered(parts, part, at), same)
        spread_out((found[:part] + found[part:]) * scale[t][:1], second, part, at)

    each_tile(mean.shape[1], tile)
    for k, send in enumerate(sends):
        cut = slice(part * k, part * (k + 1))
        send[:part] = mean[cut]
        send[part:] = mean[cut] + second[cut]


def last_kernel(pad, part, *refs):
    parts, (x1, mask_ids, weight, out, means, y, sems) = refs[:NEAR], refs[NEAR:]
    outs = column_copies(y, out, sems)
    me = lax.axis_index("rows") % NEAR
    columns, slots = means.shape[1:]
    for k, one in enumerate(parts):
        at = pl.ds(pl.multiple_of((me ^ k) * part, part), part)
        means[0, at, :] = one[:part]
        means[1, at, :] = one[part:]
    both = jnp.concatenate([*split(means[0]), *split(means[1])], axis=0)
    for b in range(len(outs)):
        at = slice(b * BLOCK, (b + 1) * BLOCK)
        found = dot(both, one_hot(row(mask_ids, b, BLOCK), slots))
        first = found[:columns] + found[columns : 2 * columns]
        total = found[2 * columns : 3 * columns] + found[3 * columns :]
        y[:, at] = x1[:, at] - total + by_worker(first, pad) * row(weight, b, BLOCK)
        outs[b].start()
    wait_all(outs)


def near_exchange(parts, n):
    steps = [[(i, i ^ k) for i in range(n)] for k in range(1, NEAR)]
    return [parts[0]] + [lax.ppermute(one, "rows", step) for one, step in zip(parts[1:], steps)]


def far_share(one, n):
    steps = [[(i, i ^ (k * NEAR)) for i in range(n)] for k in range(1, n // NEAR)]
    return [one] + [lax.ppermute(one, "rows", step) for step in steps]


def in_hbm(x):
    return pltpu.with_memory_space_constraint(x, pltpu.HBM)


def call(kernel, out_shape, in_specs, out_specs, scratch, flops, moved):
    return pl.pallas_call(
        kernel,
        out_shape=out_shape,
        in_specs=in_specs,
        out_specs=out_specs,
        scratch_shapes=scratch,
        compiler_params=pltpu.CompilerParams(vmem_limit_bytes=VMEM_BYTES),
        cost_estimate=pl.CostEstimate(flops=flops, bytes_accessed=moved, transcendentals=0),
    )


def body(probes, worker_len, spell_to_slot, slot_to_firm, *, n):
    columns, rows_dev = probes.shape
    workers = worker_len.shape[0]
    pad = rows_dev // workers
    slots = slot_to_firm.shape[0]
    tiles = slots // LANES
    part = columns // NEAR
    far = n // NEAR
    keep = tiles * NEAR * n * LANES * LANES * 2 <= 8 * 1024 * 1024
    blocks = rows_dev // BLOCK
    vmem, hbm = pl.BlockSpec(memory_space=pltpu.VMEM), pl.BlockSpec(memory_space=pltpu.HBM)
    lengths = worker_len.reshape(workers // LANES, LANES)
    ids = spell_to_slot.reshape(rows_dev // LANES, LANES)
    firms = slot_to_firm.reshape(tiles, LANES)
    array = jax.ShapeDtypeStruct
    of_rows = (rows_dev // LANES, LANES)
    work = 2 * rows_dev * slots * 2 * columns
    sems = pltpu.SemaphoreType.DMA((blocks,))
    whole = (columns, rows_dev)
    about = part + 8
    message = array((about + rows_dev // slots, slots), F32)
    of_near = array((columns, slots), F32)

    *sends, x1, mask_ids, weight = call(
        functools.partial(sums_kernel, pad, slots // n),
        [message] * NEAR + [array(whole, F32), array(of_rows, jnp.int32), array(of_rows, F32)],
        [hbm] * 4,
        [vmem] * (NEAR + 3),
        [
            pltpu.VMEM(of_rows, F32),
            pltpu.VMEM(whole, F32),
            pltpu.VMEM((2 * columns + 16, slots), F32),
            pltpu.VMEM((columns, slots), F32),
            pltpu.VMEM(lengths.shape, jnp.int32),
            pltpu.VMEM(ids.shape, jnp.int32),
            pltpu.VMEM(firms.shape, jnp.int32),
            sems,
            pltpu.SemaphoreType.DMA((3,)),
        ],
        2 * work,
        4 * columns * rows_dev,
    )(in_hbm(probes), in_hbm(lengths), in_hbm(ids), in_hbm(firms))

    def pair_counts(parts):
        return call(
            functools.partial(pairs_kernel, pad, about),
            array((len(parts), slots, 2 * slots), BF16),
            [vmem] * len(parts),
            vmem,
            [pltpu.VMEM((len(parts), *of_rows), F32), pltpu.VMEM((slots, workers), BF16)],
            work * len(parts) // 4,
            4 * slots * slots,
        )(*parts)

    arrived = near_exchange(sends, n)
    own_pairs = pair_counts(arrived[:1])
    joined = call(
        functools.partial(join_kernel, part),
        array((columns + 2 * NEAR, slots), F32),
        [vmem] * (NEAR + 1),
        vmem,
        [],
        0,
        message.size * 8,
    )(*arrived, own_pairs)
    shared = far_share(joined, n)
    pairs = pair_counts(arrived[1:])
    table = array((tiles, n * LANES, NEAR * LANES), BF16)
    scale = array((tiles, 8, NEAR * LANES), F32)
    mean, sums, scales, *tables = call(
        functools.partial(change_kernel, far, part),
        [of_near, of_near, scale] + [table] * keep,
        [vmem] * (far + 2),
        [vmem] * (3 + keep),
        [],
        work // 4,
        slots * slots * 4,
    )(*shared, own_pairs, pairs)
    again = far_share(sums, n)
    source = tables if keep else shared
    sends = call(
        functools.partial(means_kernel, far, part),
        [array((2 * part, slots), F32)] * NEAR,
        [vmem] * (far + len(source) + 2),
        [vmem] * NEAR,
        [pltpu.VMEM((columns, slots), F32)],
        work // 4,
        slots * slots * 4,
    )(*again, *source, scales, mean)
    arrived = near_exchange(sends, n)
    return call(
        functools.partial(last_kernel, pad, part),
        array(whole, F32),
        [vmem] * (NEAR + 3),
        hbm,
        [pltpu.VMEM((2, columns, slots), F32), pltpu.VMEM(whole, F32), sems],
        work,
        8 * columns * rows_dev,
    )(*arrived, x1, mask_ids, weight)


def solution(mesh):
    placed = (P(None, ("grp", "rows")), P(("grp", "rows")), P(("grp", "rows")), P(("grp", "rows")))
    return jax.shard_map(
        functools.partial(body, n=mesh.shape["rows"]),
        mesh=mesh,
        in_specs=placed,
        out_specs=P(None, ("grp", "rows")),
        check_vma=False,
    )
```

```python
import functools

import jax
import jax.numpy as jnp
from jax import lax
from jax.experimental import pallas as pl
from jax.experimental.pallas import tpu as pltpu
from jax.sharding import PartitionSpec as P

FIRMS_PER_SHARD = 1024
LANES = 128
BLOCK = 1024
VMEM_BYTES = 32 * 1024 * 1024
NEAR = 4
F32, BF16 = jnp.float32, jnp.bfloat16
NT = (((1,), (1,)), ((), ()))
NN = (((1,), (0,)), ((), ()))


def dot(a, b, dims=NN):
    return lax.dot_general(a, b, dims, preferred_element_type=F32)


def iota(shape, dim):
    return lax.broadcasted_iota(jnp.int32, shape, dim)


def split(x):
    hi = x.astype(BF16)
    return hi, (x - hi.astype(F32)).astype(BF16)


def row(ref, block, size):
    per = size // LANES
    return jnp.concatenate([ref[block * per + k : block * per + k + 1, :] for k in range(per)], axis=1)


def one_hot(ids, slots):
    kind = BF16 if slots <= 256 else F32
    slot = iota((slots, LANES), 0).astype(F32).astype(kind)
    ids = ids.astype(F32).astype(kind)
    one, zero = jnp.ones((slots, LANES), kind), jnp.zeros((slots, LANES), kind)
    parts = [jnp.where(slot == ids[:, k : k + LANES], one, zero) for k in range(0, ids.shape[1], LANES)]
    return jnp.concatenate(parts, axis=1).astype(BF16)


def one_hot_down(columns, slots):
    kind = BF16 if slots <= 256 else F32
    one, zero = jnp.ones((LANES, LANES), kind), jnp.zeros((LANES, LANES), kind)
    along_slots = [(iota((LANES, LANES), 1) + at).astype(F32).astype(kind) for at in range(0, slots, LANES)]
    parts = []
    for k in range(columns.shape[1]):
        ids = jnp.broadcast_to(columns[:, k : k + 1], (LANES, LANES)).astype(kind)
        parts.append(jnp.concatenate([jnp.where(slot == ids, one, zero) for slot in along_slots], axis=1))
    return jnp.concatenate(parts, axis=0).astype(BF16)


def same_worker(pad, width):
    return (iota((width, width), 0) // pad == iota((width, width), 1) // pad).astype(F32).astype(BF16)


def by_worker(x, table):
    rows, width = x.shape
    hi, lo = split(x)
    both = jnp.concatenate([hi, lo], axis=0)
    step = table.shape[0]
    total = jnp.concatenate([dot(both[:, k : k + step], table) for k in range(0, width, step)], axis=1)
    return total[:rows] + total[rows:]


def start_all(copies):
    for copy in copies:
        copy.start()


def wait_all(copies):
    for copy in copies:
        copy.wait()


def column_copies(source, target, sems):
    width = source.shape[1]
    cuts = [pl.ds(start, BLOCK) for start in range(0, width, BLOCK)]
    return [pltpu.make_async_copy(source.at[:, cut], target.at[:, cut], sems.at[b]) for b, cut in enumerate(cuts)]


def row_lengths(lengths, pad):
    total_rows = lengths.shape[0] * pad
    here = iota((total_rows, LANES), 0)
    lane = iota((total_rows, LANES), 1)
    wide = jnp.broadcast_to(lengths.astype(F32)[:, None, :], (lengths.shape[0], pad, LANES)).reshape(total_rows, LANES)
    per = LANES // pad
    wide = jnp.where(lane // per == here % pad, wide, 0.0).astype(BF16)
    spread = (iota((LANES, LANES), 0) % per == iota((LANES, LANES), 1) // pad).astype(F32).astype(BF16)
    row_len = dot(wide, spread)
    return row_len, (lane % pad).astype(F32) < row_len


def along(ref):
    return jnp.concatenate([ref[k : k + 1, :] for k in range(ref.shape[0])], axis=1)


def sums_kernel(pad, cap, *refs):
    (probes, lengths_in, ids_in, firms_in), sends, refs = refs[:4], refs[4 : 4 + NEAR], refs[4 + NEAR :]
    x1, mask_ids, weight, valid, x, acc, sums, lengths, ids, firms, sems, small = refs
    copies = column_copies(probes, x, sems)
    first = [
        pltpu.make_async_copy(source, target, small.at[k])
        for k, (source, target) in enumerate(((lengths_in, lengths), (ids_in, ids), (firms_in, firms)))
    ]
    start_all(first)
    start_all(copies)
    columns, slots = sums.shape
    part = columns // NEAR
    me = lax.axis_index("rows") % NEAR
    wait_all(first)
    row_len, inside = row_lengths(lengths[...], pad)
    valid[...] = jnp.where(inside, 1.0, 0.0)
    weight[...] = jnp.where(inside, 1.0 / row_len, 0.0)
    masked = jnp.where(inside, ids[...], -1)
    mask_ids[...] = masked
    turned = jnp.concatenate([masked.astype(F32)] * (LANES // masked.shape[0]), axis=0).T
    keys = (iota((1, slots), 1) // cap * FIRMS_PER_SHARD + along(firms)).astype(F32)
    across = slots // LANES
    rows = ids.shape[0] // across
    masked = jnp.concatenate([masked[k * rows : (k + 1) * rows] for k in range(across)], axis=1).astype(F32)
    for send in sends:
        send[part + 8 :] = masked

    table = same_worker(pad, 256)
    for b in range(len(copies)):
        copies[b].wait()
        ok = row(valid, b, BLOCK)
        x0 = x[:, b * BLOCK : (b + 1) * BLOCK] * ok
        rest = x0 - by_worker(x0, table) * row(weight, b, BLOCK)
        x1[:, b * BLOCK : (b + 1) * BLOCK] = rest
        counted = jnp.broadcast_to(ok, (16, BLOCK)).astype(BF16)
        data = jnp.concatenate([*split(rest), counted], axis=0)
        per = BLOCK // LANES
        block = dot(data, one_hot_down(turned[:, b * per : (b + 1) * per], slots))
        if b == 0:
            acc[...] = block
        else:
            acc[...] += block
    sums[...] = acc[:columns] + acc[columns : 2 * columns]
    about = jnp.where(iota((8, slots), 0) == 0, keys, acc[2 * columns : 2 * columns + 1])
    for k, send in enumerate(sends):
        send[:part] = sums[pl.ds(pl.multiple_of((me ^ k) * part, part), part), :]
        send[part : part + 8] = about


def join_kernel(part, *refs):
    parts, out = refs[:NEAR], refs[-1]
    for k, one in enumerate(parts):
        out[part * k : part * (k + 1)] = one[:part]
        out[part * NEAR + 2 * k : part * NEAR + 2 * k + 2] = one[part : part + 2]


def pairs_kernel(pad, start, *refs):
    parts, (out, ids, counts) = refs[:-3], refs[-3:]
    slots = out.shape[1]
    kind = BF16 if slots <= 256 else F32
    per = LANES // pad
    total_rows = ids.shape[1]
    across = slots // LANES
    rows = total_rows // across
    for k, part in enumerate(parts):
        for at in range(across):
            ids[k, at * rows : (at + 1) * rows] = part[start:, at * LANES : (at + 1) * LANES]
    at = iota((LANES, pad * LANES), 1)
    deal = (iota((LANES, pad * LANES), 0) == at % per * pad + at // LANES).astype(F32).astype(BF16)
    mine = iota((total_rows, pad * LANES), 1) % LANES // per == iota((total_rows, pad * LANES), 0) % pad
    slot = iota((slots, LANES), 0).astype(F32).astype(kind)
    one, zero = jnp.ones((slots, LANES), kind), jnp.zeros((slots, LANES), kind)
    diagonal = iota((slots, slots), 1) == iota((slots, slots), 0)

    def device(k, carry):
        dealt = dot(jnp.concatenate(split(ids[k]), axis=0), deal)
        dealt = jnp.where(mine, dealt[:total_rows] + dealt[total_rows:], 0.0)
        dealt = jnp.sum(dealt.reshape(total_rows // pad, pad, pad * LANES), axis=1)
        spells = dealt.astype(kind)
        for g in range(total_rows // pad):
            total = zero
            for j in range(pad):
                total += jnp.where(slot == spells[g : g + 1, j * LANES : (j + 1) * LANES], one, zero)
            counts[:, g * LANES : (g + 1) * LANES] = total.astype(BF16)
        valid = jnp.where(dealt >= 0.0, 1.0, 0.0)
        length = valid[:, :LANES]
        for j in range(1, pad):
            length += valid[:, j * LANES : (j + 1) * LANES]
        inverse = 1.0 / length
        inverse = jnp.concatenate([inverse[g : g + 1] for g in range(total_rows // pad)], axis=1)
        here = counts[...].astype(F32)
        total = dot(jnp.concatenate(split(here * inverse), axis=0), counts[...], NT)
        total = total[:slots] + total[slots:] - jnp.where(diagonal, jnp.sum(here, axis=1, keepdims=True), 0.0)
        hi, lo = split(total)
        out[k, :, :slots] = hi
        out[k, :, slots:] = lo
        return carry

    lax.fori_loop(0, len(parts), device, 0, unroll=len(parts) if slots <= 256 else 1)


def same_firm(parts, part, at):
    keys = [one[part * NEAR + 2 * k : part * NEAR + 2 * k + 1, at] for one in parts for k in range(NEAR)]
    mine = jnp.concatenate(keys[:NEAR], axis=1)
    down = jnp.concatenate(keys, axis=0).T
    found = [(down[:, k : k + 1] == mine).astype(F32).astype(BF16) for k in range(len(keys))]
    return jnp.concatenate(found, axis=0)


def gathered(parts, part, at):
    data = [one[part * k : part * (k + 1), at] for one in parts for k in range(NEAR)]
    return jnp.concatenate(split(jnp.concatenate(data, axis=1)), axis=0)


def spread_out(means, out, part, at):
    for k in range(NEAR):
        out[part * k : part * (k + 1), at] = means[:, k * LANES : (k + 1) * LANES]


def each_tile(slots, do):
    tiles = slots // LANES
    if tiles <= 2:
        for t in range(tiles):
            do(t, slice(t * LANES, (t + 1) * LANES))
    else:
        lax.fori_loop(0, tiles, lambda t, c: (do(t, pl.ds(pl.multiple_of(t * LANES, LANES), LANES)), c)[1], 0)


def change_kernel(far, part, *refs):
    parts, (own_pairs, pairs, mean, sums, scale), table = refs[:far], refs[far : far + 5], refs[far + 5 :]
    slots = mean.shape[1]

    def tile(t, at):
        same = same_firm(parts, part, at)
        if table:
            table[0][t] = same
        count = [one[part * NEAR + 2 * k + 1 : part * NEAR + 2 * k + 2, at] for one in parts for k in range(NEAR)]
        count = jnp.concatenate(count, axis=1)
        high = count.astype(BF16).astype(F32)
        counts = jnp.where(iota((16, count.shape[1]), 0) < 8, high, count - high).astype(BF16)
        found = dot(jnp.concatenate([gathered(parts, part, at), counts], axis=0), same)
        size = found[2 * part : 2 * part + 1] + found[2 * part + 8 : 2 * part + 9]
        inverse = 1.0 / jnp.maximum(size, 1.0)
        scale[t] = jnp.broadcast_to(inverse, scale.shape[1:])
        spread_out((found[:part] + found[part : 2 * part]) * inverse, mean, part, at)

    each_tile(slots, tile)
    for k in range(NEAR):
        cut = slice(part * k, part * (k + 1))
        both = jnp.concatenate(split(mean[cut]), axis=0)
        change = dot(both, own_pairs[0] if k == 0 else pairs[k - 1])
        change = change[:part] + change[part:]
        sums[cut] = parts[0][cut] + (change[:, :slots] + change[:, slots:])


def means_kernel(far, part, *refs):
    parts, source, (scale, mean), sends, second = refs[:far], refs[far:-8], refs[-8:-6], refs[-5:-1], refs[-1]

    def tile(t, at):
        same = source[0][t] if len(source) == 1 else same_firm(source, part, at)
        found = dot(gathered(parts, part, at), same)
        spread_out((found[:part] + found[part:]) * scale[t][:1], second, part, at)

    each_tile(mean.shape[1], tile)
    for k, send in enumerate(sends):
        cut = slice(part * k, part * (k + 1))
        send[:part] = mean[cut]
        send[part:] = mean[cut] + second[cut]


def tables_kernel(pad, mask_ids, after, spread, workers):
    slots, width = spread.shape
    table = same_worker(pad, 256)
    for b in range(width // BLOCK):
        found = one_hot(row(mask_ids, b, BLOCK), slots)
        spread[:, b * BLOCK : (b + 1) * BLOCK] = found
        for at in range(0, BLOCK, 256):
            count = dot(found[:, at : at + 256], table)
            workers[:, b * BLOCK + at : b * BLOCK + at + 256] = count.astype(BF16)


def last_kernel(pad, part, *refs):
    parts, (x1, mask_ids, weight), tables, (out, means, y, sems) = refs[:NEAR], refs[NEAR : NEAR + 3], refs[NEAR + 3 : -4], refs[-4:]
    outs = column_copies(y, out, sems)
    me = lax.axis_index("rows") % NEAR
    columns, slots = means.shape[1:]
    for k, one in enumerate(parts):
        at = pl.ds(pl.multiple_of((me ^ k) * part, part), part)
        means[0, at, :] = one[:part]
        means[1, at, :] = one[part:]
    first, total = (jnp.concatenate(split(means[k]), axis=0) for k in range(2))
    table = same_worker(pad, 256)
    for b in range(len(outs)):
        at = slice(b * BLOCK, (b + 1) * BLOCK)
        if tables:
            spread = dot(total, tables[0][:, at])
            worker = dot(first, tables[1][:, at])
            worker = worker[:columns] + worker[columns:]
        else:
            found = one_hot(row(mask_ids, b, BLOCK), slots)
            spread, worker = dot(total, found), dot(first, found)
            worker = by_worker(worker[:columns] + worker[columns:], table)
        y[:, at] = x1[:, at] - (spread[:columns] + spread[columns:]) + worker * row(weight, b, BLOCK)
        outs[b].start()
    wait_all(outs)


def near_exchange(parts, n):
    steps = [[(i, i ^ k) for i in range(n)] for k in range(1, NEAR)]
    return [parts[0]] + [lax.ppermute(one, "rows", step) for one, step in zip(parts[1:], steps)]


def far_share(one, n):
    steps = [[(i, i ^ (k * NEAR)) for i in range(n)] for k in range(1, n // NEAR)]
    return [one] + [lax.ppermute(one, "rows", step) for step in steps]


def in_hbm(x):
    return pltpu.with_memory_space_constraint(x, pltpu.HBM)


def call(kernel, out_shape, in_specs, out_specs, scratch, flops, moved):
    return pl.pallas_call(
        kernel,
        out_shape=out_shape,
        in_specs=in_specs,
        out_specs=out_specs,
        scratch_shapes=scratch,
        compiler_params=pltpu.CompilerParams(vmem_limit_bytes=VMEM_BYTES),
        cost_estimate=pl.CostEstimate(flops=flops, bytes_accessed=moved, transcendentals=0),
    )


def body(probes, worker_len, spell_to_slot, slot_to_firm, *, n):
    columns, rows_dev = probes.shape
    workers = worker_len.shape[0]
    pad = rows_dev // workers
    slots = slot_to_firm.shape[0]
    tiles = slots // LANES
    part = columns // NEAR
    far = n // NEAR
    keep = tiles * NEAR * n * LANES * LANES * 2 <= 8 * 1024 * 1024
    blocks = rows_dev // BLOCK
    vmem, hbm = pl.BlockSpec(memory_space=pltpu.VMEM), pl.BlockSpec(memory_space=pltpu.HBM)
    lengths = worker_len.reshape(workers // LANES, LANES)
    ids = spell_to_slot.reshape(rows_dev // LANES, LANES)
    firms = slot_to_firm.reshape(tiles, LANES)
    array = jax.ShapeDtypeStruct
    of_rows = (rows_dev // LANES, LANES)
    work = 2 * rows_dev * slots * 2 * columns
    sems = pltpu.SemaphoreType.DMA((blocks,))
    whole = (columns, rows_dev)
    about = part + 8
    message = array((about + rows_dev // slots, slots), F32)
    of_near = array((columns, slots), F32)

    *sends, x1, mask_ids, weight = call(
        functools.partial(sums_kernel, pad, slots // n),
        [message] * NEAR + [array(whole, F32), array(of_rows, jnp.int32), array(of_rows, F32)],
        [hbm] * 4,
        [vmem] * (NEAR + 3),
        [
            pltpu.VMEM(of_rows, F32),
            pltpu.VMEM(whole, F32),
            pltpu.VMEM((2 * columns + 16, slots), F32),
            pltpu.VMEM((columns, slots), F32),
            pltpu.VMEM(lengths.shape, jnp.int32),
            pltpu.VMEM(ids.shape, jnp.int32),
            pltpu.VMEM(firms.shape, jnp.int32),
            sems,
            pltpu.SemaphoreType.DMA((3,)),
        ],
        2 * work,
        4 * columns * rows_dev,
    )(in_hbm(probes), in_hbm(lengths), in_hbm(ids), in_hbm(firms))

    def pair_counts(parts):
        return call(
            functools.partial(pairs_kernel, pad, about),
            array((len(parts), slots, 2 * slots), BF16),
            [vmem] * len(parts),
            vmem,
            [pltpu.VMEM((len(parts), *of_rows), F32), pltpu.VMEM((slots, workers), BF16)],
            work * len(parts) // 4,
            4 * slots * slots,
        )(*parts)

    arrived = near_exchange(sends, n)
    own_pairs = pair_counts(arrived[:1])
    joined = call(
        functools.partial(join_kernel, part),
        array((columns + 2 * NEAR, slots), F32),
        [vmem] * (NEAR + 1),
        vmem,
        [],
        0,
        message.size * 8,
    )(*arrived, own_pairs)
    shared = far_share(joined, n)
    pairs = pair_counts(arrived[1:])
    table = array((tiles, n * LANES, NEAR * LANES), BF16)
    scale = array((tiles, 8, NEAR * LANES), F32)
    mean, sums, scales, *tables = call(
        functools.partial(change_kernel, far, part),
        [of_near, of_near, scale] + [table] * keep,
        [vmem] * (far + 2),
        [vmem] * (3 + keep),
        [],
        work // 4,
        slots * slots * 4,
    )(*shared, own_pairs, pairs)
    again = far_share(sums, n)
    source = tables if keep else shared
    spreads = []
    if keep:
        spreads = call(
            functools.partial(tables_kernel, pad),
            [array((slots, rows_dev), BF16)] * 2,
            [vmem] * 2,
            [vmem] * 2,
            [],
            work,
            4 * slots * rows_dev,
        )(mask_ids, scales)
    sends = call(
        functools.partial(means_kernel, far, part),
        [array((2 * part, slots), F32)] * NEAR,
        [vmem] * (far + len(source) + 3),
        [vmem] * NEAR,
        [pltpu.VMEM((columns, slots), F32)],
        work // 4,
        slots * slots * 4,
    )(*again, *source, scales, mean, spreads[1] if keep else mean)
    arrived = near_exchange(sends, n)
    return call(
        functools.partial(last_kernel, pad, part),
        array(whole, F32),
        [vmem] * (NEAR + 3 + len(spreads)),
        hbm,
        [pltpu.VMEM((2, columns, slots), F32), pltpu.VMEM(whole, F32), sems],
        work,
        8 * columns * rows_dev,
    )(*arrived, x1, mask_ids, weight, *spreads)


def solution(mesh):
    placed = (P(None, ("grp", "rows")), P(("grp", "rows")), P(("grp", "rows")), P(("grp", "rows")))
    return jax.shard_map(
        functools.partial(body, n=mesh.shape["rows"]),
        mesh=mesh,
        in_specs=placed,
        out_specs=P(None, ("grp", "rows")),
        check_vma=False,
    )
```

```python
import functools

import jax
import jax.numpy as jnp
from jax import lax
from jax.experimental import pallas as pl
from jax.experimental.pallas import tpu as pltpu
from jax.sharding import PartitionSpec as P

FIRMS_PER_SHARD = 1024
LANES = 128
BLOCK = 1024
VMEM_BYTES = 32 * 1024 * 1024
NEAR = 4
F32, BF16 = jnp.float32, jnp.bfloat16
NT = (((1,), (1,)), ((), ()))
NN = (((1,), (0,)), ((), ()))


def dot(a, b, dims=NN):
    return lax.dot_general(a, b, dims, preferred_element_type=F32)


def iota(shape, dim):
    return lax.broadcasted_iota(jnp.int32, shape, dim)


def split(x):
    hi = x.astype(BF16)
    return hi, (x - hi.astype(F32)).astype(BF16)


def row(ref, block, size):
    per = size // LANES
    return jnp.concatenate([ref[block * per + k : block * per + k + 1, :] for k in range(per)], axis=1)


def one_hot(ids, slots):
    kind = BF16 if slots <= 256 else F32
    slot = iota((slots, LANES), 0).astype(F32).astype(kind)
    ids = ids.astype(F32).astype(kind)
    one, zero = jnp.ones((slots, LANES), kind), jnp.zeros((slots, LANES), kind)
    parts = [jnp.where(slot == ids[:, k : k + LANES], one, zero) for k in range(0, ids.shape[1], LANES)]
    return jnp.concatenate(parts, axis=1).astype(BF16)


def one_hot_down(columns, slots):
    kind = BF16 if slots <= 256 else F32
    one, zero = jnp.ones((LANES, LANES), kind), jnp.zeros((LANES, LANES), kind)
    along_slots = [(iota((LANES, LANES), 1) + at).astype(F32).astype(kind) for at in range(0, slots, LANES)]
    parts = []
    for k in range(columns.shape[1]):
        ids = jnp.broadcast_to(columns[:, k : k + 1], (LANES, LANES)).astype(kind)
        parts.append(jnp.concatenate([jnp.where(slot == ids, one, zero) for slot in along_slots], axis=1))
    return jnp.concatenate(parts, axis=0).astype(BF16)


def same_worker(pad, width):
    return (iota((width, width), 0) // pad == iota((width, width), 1) // pad).astype(F32).astype(BF16)


def by_worker(x, table):
    rows, width = x.shape
    hi, lo = split(x)
    both = jnp.concatenate([hi, lo], axis=0)
    step = table.shape[0]
    total = jnp.concatenate([dot(both[:, k : k + step], table) for k in range(0, width, step)], axis=1)
    return total[:rows] + total[rows:]


def start_all(copies):
    for copy in copies:
        copy.start()


def wait_all(copies):
    for copy in copies:
        copy.wait()


def column_copies(source, target, sems, size=BLOCK):
    width = source.shape[1]
    cuts = [pl.ds(start, size) for start in range(0, width, size)]
    return [pltpu.make_async_copy(source.at[:, cut], target.at[:, cut], sems.at[b]) for b, cut in enumerate(cuts)]


def row_lengths(lengths, pad):
    total_rows = lengths.shape[0] * pad
    here = iota((total_rows, LANES), 0)
    lane = iota((total_rows, LANES), 1)
    wide = jnp.broadcast_to(lengths.astype(F32)[:, None, :], (lengths.shape[0], pad, LANES)).reshape(total_rows, LANES)
    per = LANES // pad
    wide = jnp.where(lane // per == here % pad, wide, 0.0).astype(BF16)
    spread = (iota((LANES, LANES), 0) % per == iota((LANES, LANES), 1) // pad).astype(F32).astype(BF16)
    row_len = dot(wide, spread)
    return row_len, (lane % pad).astype(F32) < row_len


def along(ref):
    return jnp.concatenate([ref[k : k + 1, :] for k in range(ref.shape[0])], axis=1)


def sums_kernel(pad, cap, *refs):
    (probes, lengths_in, ids_in, firms_in), sends, refs = refs[:4], refs[4 : 4 + NEAR], refs[4 + NEAR :]
    x1, mask_ids, weight, valid, x, sums, lengths, ids, firms, sems, small = refs
    copies = column_copies(probes, x, sems)
    first = [
        pltpu.make_async_copy(source, target, small.at[k])
        for k, (source, target) in enumerate(((lengths_in, lengths), (ids_in, ids), (firms_in, firms)))
    ]
    start_all(first)
    start_all(copies)
    columns, slots = sums.shape
    part = columns // NEAR
    me = lax.axis_index("rows") % NEAR
    wait_all(first)
    row_len, inside = row_lengths(lengths[...], pad)
    valid[...] = jnp.where(inside, 1.0, 0.0)
    weight[...] = jnp.where(inside, 1.0 / row_len, 0.0)
    masked = jnp.where(inside, ids[...], -1)
    mask_ids[...] = masked
    turned = jnp.concatenate([masked.astype(F32)] * (LANES // masked.shape[0]), axis=0).T
    keys = (iota((1, slots), 1) // cap * FIRMS_PER_SHARD + along(firms)).astype(F32)
    across = slots // LANES
    rows = ids.shape[0] // across
    masked = jnp.concatenate([masked[k * rows : (k + 1) * rows] for k in range(across)], axis=1).astype(F32)
    for send in sends:
        send[part + 8 :] = masked

    table = same_worker(pad, 256)
    wait_all(copies)
    total = None
    for b in range(len(copies)):
        ok = row(valid, b, BLOCK)
        x0 = x[:, b * BLOCK : (b + 1) * BLOCK] * ok
        rest = x0 - by_worker(x0, table) * row(weight, b, BLOCK)
        x1[:, b * BLOCK : (b + 1) * BLOCK] = rest
        counted = jnp.broadcast_to(ok, (16, BLOCK)).astype(BF16)
        data = jnp.concatenate([*split(rest), counted], axis=0)
        per = BLOCK // LANES
        block = dot(data, one_hot_down(turned[:, b * per : (b + 1) * per], slots))
        total = block if total is None else total + block
    sums[...] = total[:columns] + total[columns : 2 * columns]
    about = jnp.where(iota((8, slots), 0) == 0, keys, total[2 * columns : 2 * columns + 1])
    for k, send in enumerate(sends):
        send[:part] = sums[pl.ds(pl.multiple_of((me ^ k) * part, part), part), :]
        send[part : part + 8] = about


def join_kernel(part, *refs):
    parts, out = refs[:NEAR], refs[-1]
    for k, one in enumerate(parts):
        out[part * k : part * (k + 1)] = one[:part]
        out[part * NEAR + 2 * k : part * NEAR + 2 * k + 2] = one[part : part + 2]


def pairs_kernel(pad, start, *refs):
    parts, (out, ids, counts) = refs[:-3], refs[-3:]
    slots = out.shape[1]
    kind = BF16 if slots <= 256 else F32
    per = LANES // pad
    total_rows = ids.shape[1]
    across = slots // LANES
    rows = total_rows // across
    for k, part in enumerate(parts):
        for at in range(across):
            ids[k, at * rows : (at + 1) * rows] = part[start:, at * LANES : (at + 1) * LANES]
    at = iota((LANES, pad * LANES), 1)
    deal = (iota((LANES, pad * LANES), 0) == at % per * pad + at // LANES).astype(F32).astype(BF16)
    mine = iota((total_rows, pad * LANES), 1) % LANES // per == iota((total_rows, pad * LANES), 0) % pad
    slot = iota((slots, LANES), 0).astype(F32).astype(kind)
    one, zero = jnp.ones((slots, LANES), kind), jnp.zeros((slots, LANES), kind)
    diagonal = iota((slots, slots), 1) == iota((slots, slots), 0)

    def device(k, carry):
        dealt = dot(jnp.concatenate(split(ids[k]), axis=0), deal)
        dealt = jnp.where(mine, dealt[:total_rows] + dealt[total_rows:], 0.0)
        dealt = jnp.sum(dealt.reshape(total_rows // pad, pad, pad * LANES), axis=1)
        spells = dealt.astype(kind)
        for g in range(total_rows // pad):
            total = zero
            for j in range(pad):
                total += jnp.where(slot == spells[g : g + 1, j * LANES : (j + 1) * LANES], one, zero)
            counts[:, g * LANES : (g + 1) * LANES] = total.astype(BF16)
        valid = jnp.where(dealt >= 0.0, 1.0, 0.0)
        length = valid[:, :LANES]
        for j in range(1, pad):
            length += valid[:, j * LANES : (j + 1) * LANES]
        inverse = 1.0 / length
        inverse = jnp.concatenate([inverse[g : g + 1] for g in range(total_rows // pad)], axis=1)
        here = counts[...].astype(F32)
        total = dot(jnp.concatenate(split(here * inverse), axis=0), counts[...], NT)
        total = total[:slots] + total[slots:] - jnp.where(diagonal, jnp.sum(here, axis=1, keepdims=True), 0.0)
        hi, lo = split(total)
        out[k, :, :slots] = hi
        out[k, :, slots:] = lo
        return carry

    lax.fori_loop(0, len(parts), device, 0, unroll=len(parts) if slots <= 256 else 1)


def same_firm(own, one, part, at):
    mine, keys = ([ref[part * NEAR + 2 * k : part * NEAR + 2 * k + 1, at] for k in range(NEAR)] for ref in (own, one))
    mine = jnp.concatenate(mine, axis=1)
    down = jnp.concatenate([jnp.broadcast_to(key, (8, LANES)) for key in keys], axis=0).T
    found = [(down[:, 8 * k : 8 * k + 1] == mine).astype(F32).astype(BF16) for k in range(NEAR)]
    return jnp.concatenate(found, axis=0)


def each_tile(slots, do):
    tiles = slots // LANES
    if tiles <= 2:
        for t in range(tiles):
            do(t, slice(t * LANES, (t + 1) * LANES))
    else:
        lax.fori_loop(0, tiles, lambda t, c: (do(t, pl.ds(pl.multiple_of(t * LANES, LANES), LANES)), c)[1], 0)


def firms_kernel(part, own, one, out):
    each_tile(own.shape[1], lambda t, at: out.__setitem__(t, same_firm(own, one, part, at)))


def gathered(parts, part, at):
    data = [one[part * k : part * (k + 1), at] for one in parts for k in range(NEAR)]
    return jnp.concatenate(split(jnp.concatenate(data, axis=1)), axis=0)


def spread_out(means, out, part, at):
    for k in range(NEAR):
        out[part * k : part * (k + 1), at] = means[:, k * LANES : (k + 1) * LANES]


def change_kernel(far, part, *refs):
    parts, tables, (own_pairs, pairs, mean, sums, scale) = refs[:far], refs[far:-5], refs[-5:]
    slots = mean.shape[1]

    def tile(t, at):
        same = [table[t] for table in tables] or [same_firm(parts[0], one, part, at) for one in parts]
        same = jnp.concatenate(same, axis=0)
        count = [one[part * NEAR + 2 * k + 1 : part * NEAR + 2 * k + 2, at] for one in parts for k in range(NEAR)]
        count = jnp.concatenate(count, axis=1)
        high = count.astype(BF16).astype(F32)
        counts = jnp.where(iota((16, count.shape[1]), 0) < 8, high, count - high).astype(BF16)
        found = dot(jnp.concatenate([gathered(parts, part, at), counts], axis=0), same)
        size = found[2 * part : 2 * part + 1] + found[2 * part + 8 : 2 * part + 9]
        inverse = 1.0 / jnp.maximum(size, 1.0)
        scale[t] = jnp.broadcast_to(inverse, scale.shape[1:])
        spread_out((found[:part] + found[part : 2 * part]) * inverse, mean, part, at)

    each_tile(slots, tile)
    for k in range(NEAR):
        cut = slice(part * k, part * (k + 1))
        both = jnp.concatenate(split(mean[cut]), axis=0)
        change = dot(both, own_pairs[0] if k == 0 else pairs[k - 1])
        change = change[:part] + change[part:]
        sums[cut] = parts[0][cut] + (change[:, :slots] + change[:, slots:])


def means_kernel(far, part, kept, *refs):
    parts, source, (scale, mean), sends, second = refs[:far], refs[far:-8], refs[-8:-6], refs[-5:-1], refs[-1]

    def tile(t, at):
        same = [table[t] if kept else same_firm(source[0], table, part, at) for table in source]
        same = jnp.concatenate(same, axis=0)
        found = dot(gathered(parts, part, at), same)
        spread_out((found[:part] + found[part:]) * scale[t][:1], second, part, at)

    each_tile(mean.shape[1], tile)
    for k, send in enumerate(sends):
        cut = slice(part * k, part * (k + 1))
        send[:part] = mean[cut]
        send[part:] = mean[cut] + second[cut]


def tables_kernel(pad, mask_ids, after, spread, workers):
    slots, width = spread.shape
    table = same_worker(pad, 256)
    for b in range(width // BLOCK):
        found = one_hot(row(mask_ids, b, BLOCK), slots)
        spread[:, b * BLOCK : (b + 1) * BLOCK] = found
        for at in range(0, BLOCK, 256):
            count = dot(found[:, at : at + 256], table)
            workers[:, b * BLOCK + at : b * BLOCK + at + 256] = count.astype(BF16)


def last_kernel(pad, part, *refs):
    parts, (x1, mask_ids, weight), tables, (out, means, y, sems) = refs[:NEAR], refs[NEAR : NEAR + 3], refs[NEAR + 3 : -4], refs[-4:]
    outs = column_copies(y, out, sems, 2 * BLOCK)
    me = lax.axis_index("rows") % NEAR
    columns, slots = means.shape[1:]
    for k, one in enumerate(parts):
        at = pl.ds(pl.multiple_of((me ^ k) * part, part), part)
        means[0, at, :] = one[:part]
        means[1, at, :] = one[part:]
    first, total = (jnp.concatenate(split(means[k]), axis=0) for k in range(2))
    table = same_worker(pad, 256)
    for b in range(2 * len(outs)):
        at = slice(b * BLOCK, (b + 1) * BLOCK)
        if tables:
            spread = dot(total, tables[0][:, at])
            worker = dot(first, tables[1][:, at])
            worker = worker[:columns] + worker[columns:]
        else:
            found = one_hot(row(mask_ids, b, BLOCK), slots)
            spread, worker = dot(total, found), dot(first, found)
            worker = by_worker(worker[:columns] + worker[columns:], table)
        y[:, at] = x1[:, at] - (spread[:columns] + spread[columns:]) + worker * row(weight, b, BLOCK)
        if b % 2:
            outs[b // 2].start()
    wait_all(outs)


def near_exchange(parts, n):
    steps = [[(i, i ^ k) for i in range(n)] for k in range(1, NEAR)]
    return [parts[0]] + [lax.ppermute(one, "rows", step) for one, step in zip(parts[1:], steps)]


def far_share(one, n):
    steps = [[(i, i ^ (k * NEAR)) for i in range(n)] for k in range(1, n // NEAR)]
    return [one] + [lax.ppermute(one, "rows", step) for step in steps]


def in_hbm(x):
    return pltpu.with_memory_space_constraint(x, pltpu.HBM)


def call(kernel, out_shape, in_specs, out_specs, scratch, flops, moved):
    return pl.pallas_call(
        kernel,
        out_shape=out_shape,
        in_specs=in_specs,
        out_specs=out_specs,
        scratch_shapes=scratch,
        compiler_params=pltpu.CompilerParams(vmem_limit_bytes=VMEM_BYTES),
        cost_estimate=pl.CostEstimate(flops=flops, bytes_accessed=moved, transcendentals=0),
    )


def body(probes, worker_len, spell_to_slot, slot_to_firm, *, n):
    columns, rows_dev = probes.shape
    workers = worker_len.shape[0]
    pad = rows_dev // workers
    slots = slot_to_firm.shape[0]
    tiles = slots // LANES
    part = columns // NEAR
    far = n // NEAR
    keep = tiles * NEAR * n * LANES * LANES * 2 <= 8 * 1024 * 1024
    blocks = rows_dev // BLOCK
    vmem, hbm = pl.BlockSpec(memory_space=pltpu.VMEM), pl.BlockSpec(memory_space=pltpu.HBM)
    lengths = worker_len.reshape(workers // LANES, LANES)
    ids = spell_to_slot.reshape(rows_dev // LANES, LANES)
    firms = slot_to_firm.reshape(tiles, LANES)
    array = jax.ShapeDtypeStruct
    of_rows = (rows_dev // LANES, LANES)
    work = 2 * rows_dev * slots * 2 * columns
    sems = pltpu.SemaphoreType.DMA((blocks,))
    whole = (columns, rows_dev)
    about = part + 8
    message = array((about + rows_dev // slots, slots), F32)
    of_near = array((columns, slots), F32)

    *sends, x1, mask_ids, weight = call(
        functools.partial(sums_kernel, pad, slots // n),
        [message] * NEAR + [array(whole, F32), array(of_rows, jnp.int32), array(of_rows, F32)],
        [hbm] * 4,
        [vmem] * (NEAR + 3),
        [
            pltpu.VMEM(of_rows, F32),
            pltpu.VMEM(whole, F32),
            pltpu.VMEM((columns, slots), F32),
            pltpu.VMEM(lengths.shape, jnp.int32),
            pltpu.VMEM(ids.shape, jnp.int32),
            pltpu.VMEM(firms.shape, jnp.int32),
            sems,
            pltpu.SemaphoreType.DMA((3,)),
        ],
        2 * work,
        4 * columns * rows_dev,
    )(in_hbm(probes), in_hbm(lengths), in_hbm(ids), in_hbm(firms))

    def pair_counts(parts):
        return call(
            functools.partial(pairs_kernel, pad, about),
            array((len(parts), slots, 2 * slots), BF16),
            [vmem] * len(parts),
            vmem,
            [pltpu.VMEM((len(parts), *of_rows), F32), pltpu.VMEM((slots, workers), BF16)],
            work * len(parts) // 4,
            4 * slots * slots,
        )(*parts)

    arrived = near_exchange(sends, n)
    own_pairs = pair_counts(arrived[:1])
    joined = call(
        functools.partial(join_kernel, part),
        array((columns + 2 * NEAR, slots), F32),
        [vmem] * (NEAR + 1),
        vmem,
        [],
        0,
        message.size * 8,
    )(*arrived, own_pairs)
    shared = far_share(joined, n)
    pairs = pair_counts(arrived[1:])
    tables = []
    if keep:
        tables = [
            call(
                functools.partial(firms_kernel, part),
                array((tiles, NEAR * LANES, NEAR * LANES), BF16),
                [vmem] * 2,
                vmem,
                [],
                work // 64,
                tiles * (NEAR * LANES) ** 2 * 2,
            )(joined, one)
            for one in shared
        ]
    scale = array((tiles, 8, NEAR * LANES), F32)
    mean, sums, scales = call(
        functools.partial(change_kernel, far, part),
        [of_near, of_near, scale],
        [vmem] * (far + len(tables) + 2),
        [vmem] * 3,
        [],
        work // 4,
        slots * slots * 4,
    )(*shared, *tables, own_pairs, pairs)
    again = far_share(sums, n)
    source = tables if keep else shared
    spreads = []
    if keep:
        spreads = call(
            functools.partial(tables_kernel, pad),
            [array((slots, rows_dev), BF16)] * 2,
            [vmem] * 2,
            [vmem] * 2,
            [],
            work,
            4 * slots * rows_dev,
        )(mask_ids, scales)
    sends = call(
        functools.partial(means_kernel, far, part, keep),
        [array((2 * part, slots), F32)] * NEAR,
        [vmem] * (far + len(source) + 3),
        [vmem] * NEAR,
        [pltpu.VMEM((columns, slots), F32)],
        work // 4,
        slots * slots * 4,
    )(*again, *source, scales, mean, spreads[1] if keep else mean)
    arrived = near_exchange(sends, n)
    return call(
        functools.partial(last_kernel, pad, part),
        array(whole, F32),
        [vmem] * (NEAR + 3 + len(spreads)),
        hbm,
        [pltpu.VMEM((2, columns, slots), F32), pltpu.VMEM(whole, F32), sems],
        work,
        8 * columns * rows_dev,
    )(*arrived, x1, mask_ids, weight, *spreads)


def solution(mesh):
    placed = (P(None, ("grp", "rows")), P(("grp", "rows")), P(("grp", "rows")), P(("grp", "rows")))
    return jax.shard_map(
        functools.partial(body, n=mesh.shape["rows"]),
        mesh=mesh,
        in_specs=placed,
        out_specs=P(None, ("grp", "rows")),
        check_vma=False,
    )
```

```python
import functools

import jax
import jax.numpy as jnp
from jax import lax
from jax.experimental import pallas as pl
from jax.experimental.pallas import tpu as pltpu
from jax.sharding import PartitionSpec as P

FIRMS_PER_SHARD = 1024
LANES = 128
BLOCK = 1024
VMEM_BYTES = 32 * 1024 * 1024
NEAR = 4
F32, BF16 = jnp.float32, jnp.bfloat16
NT = (((1,), (1,)), ((), ()))
NN = (((1,), (0,)), ((), ()))


def dot(a, b, dims=NN):
    return lax.dot_general(a, b, dims, preferred_element_type=F32)


def iota(shape, dim):
    return lax.broadcasted_iota(jnp.int32, shape, dim)


def split(x):
    hi = x.astype(BF16)
    return hi, (x - hi.astype(F32)).astype(BF16)


def row(ref, block, size):
    per = size // LANES
    return jnp.concatenate([ref[block * per + k : block * per + k + 1, :] for k in range(per)], axis=1)


def one_hot(ids, slots):
    kind = BF16 if slots <= 256 else F32
    slot = iota((slots, LANES), 0).astype(F32).astype(kind)
    ids = ids.astype(F32).astype(kind)
    one, zero = jnp.ones((slots, LANES), kind), jnp.zeros((slots, LANES), kind)
    parts = [jnp.where(slot == ids[:, k : k + LANES], one, zero) for k in range(0, ids.shape[1], LANES)]
    return jnp.concatenate(parts, axis=1).astype(BF16)


def one_hot_down(columns, slots):
    kind = BF16 if slots <= 256 else F32
    one, zero = jnp.ones((LANES, LANES), kind), jnp.zeros((LANES, LANES), kind)
    along_slots = [(iota((LANES, LANES), 1) + at).astype(F32).astype(kind) for at in range(0, slots, LANES)]
    parts = []
    for k in range(columns.shape[1]):
        ids = jnp.broadcast_to(columns[:, k : k + 1], (LANES, LANES)).astype(kind)
        parts.append(jnp.concatenate([jnp.where(slot == ids, one, zero) for slot in along_slots], axis=1))
    return jnp.concatenate(parts, axis=0).astype(BF16)


def same_worker(pad, width):
    return (iota((width, width), 0) // pad == iota((width, width), 1) // pad).astype(F32).astype(BF16)


def by_worker(x, table):
    rows, width = x.shape
    hi, lo = split(x)
    both = jnp.concatenate([hi, lo], axis=0)
    step = table.shape[0]
    total = jnp.concatenate([dot(both[:, k : k + step], table) for k in range(0, width, step)], axis=1)
    return total[:rows] + total[rows:]


def start_all(copies):
    for copy in copies:
        copy.start()


def wait_all(copies):
    for copy in copies:
        copy.wait()


def column_copies(source, target, sems, size=BLOCK):
    width = source.shape[1]
    cuts = [pl.ds(start, size) for start in range(0, width, size)]
    return [pltpu.make_async_copy(source.at[:, cut], target.at[:, cut], sems.at[b]) for b, cut in enumerate(cuts)]


def row_lengths(lengths, pad):
    total_rows = lengths.shape[0] * pad
    here = iota((total_rows, LANES), 0)
    lane = iota((total_rows, LANES), 1)
    wide = jnp.broadcast_to(lengths.astype(F32)[:, None, :], (lengths.shape[0], pad, LANES)).reshape(total_rows, LANES)
    per = LANES // pad
    wide = jnp.where(lane // per == here % pad, wide, 0.0).astype(BF16)
    spread = (iota((LANES, LANES), 0) % per == iota((LANES, LANES), 1) // pad).astype(F32).astype(BF16)
    row_len = dot(wide, spread)
    return row_len, (lane % pad).astype(F32) < row_len


def along(ref):
    return jnp.concatenate([ref[k : k + 1, :] for k in range(ref.shape[0])], axis=1)


def sums_kernel(pad, cap, *refs):
    (probes, lengths_in, ids_in, firms_in), sends, refs = refs[:4], refs[4 : 4 + NEAR], refs[4 + NEAR :]
    x1, mask_ids, weight, valid, x, sums, lengths, ids, firms, sems, small = refs
    copies = column_copies(probes, x, sems)
    first = [
        pltpu.make_async_copy(source, target, small.at[k])
        for k, (source, target) in enumerate(((lengths_in, lengths), (ids_in, ids), (firms_in, firms)))
    ]
    start_all(first)
    start_all(copies)
    columns, slots = sums.shape
    part = columns // NEAR
    me = lax.axis_index("rows") % NEAR
    wait_all(first)
    row_len, inside = row_lengths(lengths[...], pad)
    valid[...] = jnp.where(inside, 1.0, 0.0)
    weight[...] = jnp.where(inside, 1.0 / row_len, 0.0)
    masked = jnp.where(inside, ids[...], -1)
    mask_ids[...] = masked
    turned = jnp.concatenate([masked.astype(F32)] * (LANES // masked.shape[0]), axis=0).T
    keys = (iota((1, slots), 1) // cap * FIRMS_PER_SHARD + along(firms)).astype(F32)
    across = slots // LANES
    rows = ids.shape[0] // across
    masked = jnp.concatenate([masked[k * rows : (k + 1) * rows] for k in range(across)], axis=1).astype(F32)
    for send in sends:
        send[part + 8 :] = masked

    table = same_worker(pad, 256)
    wait_all(copies)
    total = None
    for b in range(len(copies)):
        ok = row(valid, b, BLOCK)
        x0 = x[:, b * BLOCK : (b + 1) * BLOCK] * ok
        rest = x0 - by_worker(x0, table) * row(weight, b, BLOCK)
        x1[:, b * BLOCK : (b + 1) * BLOCK] = rest
        counted = jnp.broadcast_to(ok, (16, BLOCK)).astype(BF16)
        data = jnp.concatenate([*split(rest), counted], axis=0)
        per = BLOCK // LANES
        block = dot(data, one_hot_down(turned[:, b * per : (b + 1) * per], slots))
        total = block if total is None else total + block
    sums[...] = total[:columns] + total[columns : 2 * columns]
    about = jnp.where(iota((8, slots), 0) == 0, keys, total[2 * columns : 2 * columns + 1])
    for k, send in enumerate(sends):
        send[:part] = sums[pl.ds(pl.multiple_of((me ^ k) * part, part), part), :]
        send[part : part + 8] = about


def join_kernel(part, *refs):
    parts, out = refs[:NEAR], refs[-1]
    for k, one in enumerate(parts):
        out[part * k : part * (k + 1)] = one[:part]
        out[part * NEAR + 2 * k : part * NEAR + 2 * k + 2] = one[part : part + 2]


def pairs_kernel(pad, start, *refs):
    parts, (out, ids, size, counts) = refs[:-4], refs[-4:]
    slots = out.shape[1]
    kind = BF16 if slots <= 256 else F32
    per = LANES // pad
    total_rows = ids.shape[1]
    across = slots // LANES
    rows = total_rows // across
    for k, part in enumerate(parts):
        size[k] = jnp.broadcast_to(part[start - 7 : start - 6], (8, slots))
        for at in range(across):
            ids[k, at * rows : (at + 1) * rows] = part[start:, at * LANES : (at + 1) * LANES]
    at = iota((LANES, pad * LANES), 1)
    deal = (iota((LANES, pad * LANES), 0) == at % per * pad + at // LANES).astype(F32).astype(BF16)
    mine = iota((total_rows, pad * LANES), 1) % LANES // per == iota((total_rows, pad * LANES), 0) % pad
    slot = iota((slots, LANES), 0).astype(F32).astype(kind)
    one, zero = jnp.ones((slots, LANES), kind), jnp.zeros((slots, LANES), kind)
    diagonal = iota((slots, slots), 1) == iota((slots, slots), 0)

    def device(k, carry):
        dealt = dot(jnp.concatenate(split(ids[k]), axis=0), deal)
        dealt = jnp.where(mine, dealt[:total_rows] + dealt[total_rows:], 0.0)
        dealt = jnp.sum(dealt.reshape(total_rows // pad, pad, pad * LANES), axis=1)
        spells = dealt.astype(kind)
        for g in range(total_rows // pad):
            total = zero
            for j in range(pad):
                total += jnp.where(slot == spells[g : g + 1, j * LANES : (j + 1) * LANES], one, zero)
            counts[k, :, g * LANES : (g + 1) * LANES] = total.astype(BF16)
        valid = jnp.where(dealt >= 0.0, 1.0, 0.0)
        length = valid[:, :LANES]
        for j in range(1, pad):
            length += valid[:, j * LANES : (j + 1) * LANES]
        inverse = 1.0 / length
        inverse = jnp.concatenate([inverse[g : g + 1] for g in range(total_rows // pad)], axis=1)
        here = counts[k]
        total = dot(jnp.concatenate(split(here.astype(F32) * inverse), axis=0), here, NT)
        total = total[:slots] + total[slots:] - jnp.where(diagonal, size[k, :1], 0.0)
        hi, lo = split(total)
        out[k, :, :slots] = hi
        out[k, :, slots:] = lo
        return carry

    lax.fori_loop(0, len(parts), device, 0, unroll=len(parts) if slots <= 256 else 1)


def same_firm(own, one, part, at):
    mine, keys = ([ref[part * NEAR + 2 * k : part * NEAR + 2 * k + 1, at] for k in range(NEAR)] for ref in (own, one))
    mine = jnp.concatenate(mine, axis=1)
    down = jnp.concatenate([jnp.broadcast_to(key, (8, LANES)) for key in keys], axis=0).T
    found = [(down[:, 8 * k : 8 * k + 1] == mine).astype(F32).astype(BF16) for k in range(NEAR)]
    return jnp.concatenate(found, axis=0)


def each_tile(slots, do):
    tiles = slots // LANES
    if tiles <= 2:
        for t in range(tiles):
            do(t, slice(t * LANES, (t + 1) * LANES))
    else:
        lax.fori_loop(0, tiles, lambda t, c: (do(t, pl.ds(pl.multiple_of(t * LANES, LANES), LANES)), c)[1], 0)


def firms_kernel(part, own, one, out):
    each_tile(own.shape[1], lambda t, at: out.__setitem__(t, same_firm(own, one, part, at)))


def gathered(parts, part, at):
    data = [one[part * k : part * (k + 1), at] for one in parts for k in range(NEAR)]
    return jnp.concatenate(split(jnp.concatenate(data, axis=1)), axis=0)


def spread_out(means, out, part, at):
    for k in range(NEAR):
        out[part * k : part * (k + 1), at] = means[:, k * LANES : (k + 1) * LANES]


def change_kernel(far, part, *refs):
    parts, tables, (own_pairs, pairs, mean, sums, scale) = refs[:far], refs[far:-5], refs[-5:]
    slots = mean.shape[1]

    def tile(t, at):
        same = [table[t] for table in tables] or [same_firm(parts[0], one, part, at) for one in parts]
        same = jnp.concatenate(same, axis=0)
        count = [one[part * NEAR + 2 * k + 1 : part * NEAR + 2 * k + 2, at] for one in parts for k in range(NEAR)]
        count = jnp.concatenate(count, axis=1)
        high = count.astype(BF16).astype(F32)
        counts = jnp.where(iota((16, count.shape[1]), 0) < 8, high, count - high).astype(BF16)
        found = dot(jnp.concatenate([gathered(parts, part, at), counts], axis=0), same)
        size = found[2 * part : 2 * part + 1] + found[2 * part + 8 : 2 * part + 9]
        inverse = 1.0 / jnp.maximum(size, 1.0)
        scale[t] = jnp.broadcast_to(inverse, scale.shape[1:])
        spread_out((found[:part] + found[part : 2 * part]) * inverse, mean, part, at)

    each_tile(slots, tile)
    for k in range(NEAR):
        cut = slice(part * k, part * (k + 1))
        both = jnp.concatenate(split(mean[cut]), axis=0)
        change = dot(both, own_pairs[0] if k == 0 else pairs[k - 1])
        change = change[:part] + change[part:]
        sums[cut] = parts[0][cut] + (change[:, :slots] + change[:, slots:])


def means_kernel(far, part, kept, *refs):
    parts, source, (scale, mean), sends, second = refs[:far], refs[far:-8], refs[-8:-6], refs[-5:-1], refs[-1]

    def tile(t, at):
        same = [table[t] if kept else same_firm(source[0], table, part, at) for table in source]
        same = jnp.concatenate(same, axis=0)
        found = dot(gathered(parts, part, at), same)
        spread_out((found[:part] + found[part:]) * scale[t][:1], second, part, at)

    each_tile(mean.shape[1], tile)
    for k, send in enumerate(sends):
        cut = slice(part * k, part * (k + 1))
        send[:part] = mean[cut]
        send[part:] = mean[cut] + second[cut]


def tables_kernel(pad, mask_ids, after, spread, workers):
    slots, width = spread.shape
    table = same_worker(pad, 256)
    for b in range(width // BLOCK):
        found = one_hot(row(mask_ids, b, BLOCK), slots)
        spread[:, b * BLOCK : (b + 1) * BLOCK] = found
        for at in range(0, BLOCK, 256):
            count = dot(found[:, at : at + 256], table)
            workers[:, b * BLOCK + at : b * BLOCK + at + 256] = count.astype(BF16)


def last_kernel(pad, part, *refs):
    parts, (x1, mask_ids, weight), tables, (out, means, y, sems) = refs[:NEAR], refs[NEAR : NEAR + 3], refs[NEAR + 3 : -4], refs[-4:]
    outs = column_copies(y, out, sems, 2 * BLOCK)
    me = lax.axis_index("rows") % NEAR
    columns, slots = means.shape[1:]
    for k, one in enumerate(parts):
        at = pl.ds(pl.multiple_of((me ^ k) * part, part), part)
        means[0, at, :] = one[:part]
        means[1, at, :] = one[part:]
    first, total = (jnp.concatenate(split(means[k]), axis=0) for k in range(2))
    table = same_worker(pad, 256)
    for b in range(2 * len(outs)):
        at = slice(b * BLOCK, (b + 1) * BLOCK)
        if tables:
            spread = dot(total, tables[0][:, at])
            worker = dot(first, tables[1][:, at])
            worker = worker[:columns] + worker[columns:]
        else:
            found = one_hot(row(mask_ids, b, BLOCK), slots)
            spread, worker = dot(total, found), dot(first, found)
            worker = by_worker(worker[:columns] + worker[columns:], table)
        y[:, at] = x1[:, at] - (spread[:columns] + spread[columns:]) + worker * row(weight, b, BLOCK)
        if b % 2:
            outs[b // 2].start()
    wait_all(outs)


def near_exchange(parts, n):
    steps = [[(i, i ^ k) for i in range(n)] for k in range(1, NEAR)]
    return [parts[0]] + [lax.ppermute(one, "rows", step) for one, step in zip(parts[1:], steps)]


def far_share(one, n):
    steps = [[(i, i ^ (k * NEAR)) for i in range(n)] for k in range(1, n // NEAR)]
    return [one] + [lax.ppermute(one, "rows", step) for step in steps]


def in_hbm(x):
    return pltpu.with_memory_space_constraint(x, pltpu.HBM)


def call(kernel, out_shape, in_specs, out_specs, scratch, flops, moved):
    return pl.pallas_call(
        kernel,
        out_shape=out_shape,
        in_specs=in_specs,
        out_specs=out_specs,
        scratch_shapes=scratch,
        compiler_params=pltpu.CompilerParams(vmem_limit_bytes=VMEM_BYTES),
        cost_estimate=pl.CostEstimate(flops=flops, bytes_accessed=moved, transcendentals=0),
    )


def body(probes, worker_len, spell_to_slot, slot_to_firm, *, n):
    columns, rows_dev = probes.shape
    workers = worker_len.shape[0]
    pad = rows_dev // workers
    slots = slot_to_firm.shape[0]
    tiles = slots // LANES
    part = columns // NEAR
    far = n // NEAR
    keep = tiles * NEAR * n * LANES * LANES * 2 <= 8 * 1024 * 1024
    blocks = rows_dev // BLOCK
    vmem, hbm = pl.BlockSpec(memory_space=pltpu.VMEM), pl.BlockSpec(memory_space=pltpu.HBM)
    lengths = worker_len.reshape(workers // LANES, LANES)
    ids = spell_to_slot.reshape(rows_dev // LANES, LANES)
    firms = slot_to_firm.reshape(tiles, LANES)
    array = jax.ShapeDtypeStruct
    of_rows = (rows_dev // LANES, LANES)
    work = 2 * rows_dev * slots * 2 * columns
    sems = pltpu.SemaphoreType.DMA((blocks,))
    whole = (columns, rows_dev)
    about = part + 8
    message = array((about + rows_dev // slots, slots), F32)
    of_near = array((columns, slots), F32)

    *sends, x1, mask_ids, weight = call(
        functools.partial(sums_kernel, pad, slots // n),
        [message] * NEAR + [array(whole, F32), array(of_rows, jnp.int32), array(of_rows, F32)],
        [hbm] * 4,
        [vmem] * (NEAR + 3),
        [
            pltpu.VMEM(of_rows, F32),
            pltpu.VMEM(whole, F32),
            pltpu.VMEM((columns, slots), F32),
            pltpu.VMEM(lengths.shape, jnp.int32),
            pltpu.VMEM(ids.shape, jnp.int32),
            pltpu.VMEM(firms.shape, jnp.int32),
            sems,
            pltpu.SemaphoreType.DMA((3,)),
        ],
        2 * work,
        4 * columns * rows_dev,
    )(in_hbm(probes), in_hbm(lengths), in_hbm(ids), in_hbm(firms))

    def pair_counts(parts):
        return call(
            functools.partial(pairs_kernel, pad, about),
            array((len(parts), slots, 2 * slots), BF16),
            [vmem] * len(parts),
            vmem,
            [
                pltpu.VMEM((len(parts), *of_rows), F32),
                pltpu.VMEM((len(parts), 8, slots), F32),
                pltpu.VMEM((len(parts), slots, workers), BF16),
            ],
            work * len(parts) // 4,
            4 * slots * slots,
        )(*parts)

    arrived = near_exchange(sends, n)
    own_pairs = pair_counts(arrived[:1])
    joined = call(
        functools.partial(join_kernel, part),
        array((columns + 2 * NEAR, slots), F32),
        [vmem] * (NEAR + 1),
        vmem,
        [],
        0,
        message.size * 8,
    )(*arrived, own_pairs)
    shared = far_share(joined, n)
    pairs = pair_counts(arrived[1:])
    tables = []
    if keep:
        tables = [
            call(
                functools.partial(firms_kernel, part),
                array((tiles, NEAR * LANES, NEAR * LANES), BF16),
                [vmem] * 2,
                vmem,
                [],
                work // 64,
                tiles * (NEAR * LANES) ** 2 * 2,
            )(joined, one)
            for one in shared
        ]
    scale = array((tiles, 8, NEAR * LANES), F32)
    mean, sums, scales = call(
        functools.partial(change_kernel, far, part),
        [of_near, of_near, scale],
        [vmem] * (far + len(tables) + 2),
        [vmem] * 3,
        [],
        work // 4,
        slots * slots * 4,
    )(*shared, *tables, own_pairs, pairs)
    again = far_share(sums, n)
    source = tables if keep else shared
    spreads = []
    if keep:
        spreads = call(
            functools.partial(tables_kernel, pad),
            [array((slots, rows_dev), BF16)] * 2,
            [vmem] * 2,
            [vmem] * 2,
            [],
            work,
            4 * slots * rows_dev,
        )(mask_ids, scales)
    sends = call(
        functools.partial(means_kernel, far, part, keep),
        [array((2 * part, slots), F32)] * NEAR,
        [vmem] * (far + len(source) + 3),
        [vmem] * NEAR,
        [pltpu.VMEM((columns, slots), F32)],
        work // 4,
        slots * slots * 4,
    )(*again, *source, scales, mean, spreads[1] if keep else mean)
    arrived = near_exchange(sends, n)
    return call(
        functools.partial(last_kernel, pad, part),
        array(whole, F32),
        [vmem] * (NEAR + 3 + len(spreads)),
        hbm,
        [pltpu.VMEM((2, columns, slots), F32), pltpu.VMEM(whole, F32), sems],
        work,
        8 * columns * rows_dev,
    )(*arrived, x1, mask_ids, weight, *spreads)


def solution(mesh):
    placed = (P(None, ("grp", "rows")), P(("grp", "rows")), P(("grp", "rows")), P(("grp", "rows")))
    return jax.shard_map(
        functools.partial(body, n=mesh.shape["rows"]),
        mesh=mesh,
        in_specs=placed,
        out_specs=P(None, ("grp", "rows")),
        check_vma=False,
    )
```

```python
import functools

import jax
import jax.numpy as jnp
from jax import lax
from jax.experimental import pallas as pl
from jax.experimental.pallas import tpu as pltpu
from jax.sharding import PartitionSpec as P

FIRMS_PER_SHARD = 1024
LANES = 128
BLOCK = 1024
VMEM_BYTES = 32 * 1024 * 1024
NEAR = 4
NEAR_STEPS = (0, 2, 3, 1)
F32, BF16 = jnp.float32, jnp.bfloat16
NT = (((1,), (1,)), ((), ()))
NN = (((1,), (0,)), ((), ()))


def dot(a, b, dims=NN):
    return lax.dot_general(a, b, dims, preferred_element_type=F32)


def iota(shape, dim):
    return lax.broadcasted_iota(jnp.int32, shape, dim)


def split(x):
    hi = x.astype(BF16)
    return hi, (x - hi.astype(F32)).astype(BF16)


def row(ref, block, size):
    per = size // LANES
    return jnp.concatenate([ref[block * per + k : block * per + k + 1, :] for k in range(per)], axis=1)


def one_hot(ids, slots):
    kind = BF16 if slots <= 256 else F32
    slot = iota((slots, LANES), 0).astype(F32).astype(kind)
    ids = ids.astype(F32).astype(kind)
    one, zero = jnp.ones((slots, LANES), kind), jnp.zeros((slots, LANES), kind)
    parts = [jnp.where(slot == ids[:, k : k + LANES], one, zero) for k in range(0, ids.shape[1], LANES)]
    return jnp.concatenate(parts, axis=1).astype(BF16)


def one_hot_down(columns, slots):
    kind = BF16 if slots <= 256 else F32
    one, zero = jnp.ones((LANES, LANES), kind), jnp.zeros((LANES, LANES), kind)
    along_slots = [(iota((LANES, LANES), 1) + at).astype(F32).astype(kind) for at in range(0, slots, LANES)]
    parts = []
    for k in range(columns.shape[1]):
        ids = jnp.broadcast_to(columns[:, k : k + 1], (LANES, LANES)).astype(kind)
        parts.append(jnp.concatenate([jnp.where(slot == ids, one, zero) for slot in along_slots], axis=1))
    return jnp.concatenate(parts, axis=0).astype(BF16)


def same_worker(pad, width):
    return (iota((width, width), 0) // pad == iota((width, width), 1) // pad).astype(F32).astype(BF16)


def by_worker(x, table):
    rows, width = x.shape
    hi, lo = split(x)
    both = jnp.concatenate([hi, lo], axis=0)
    step = table.shape[0]
    total = jnp.concatenate([dot(both[:, k : k + step], table) for k in range(0, width, step)], axis=1)
    return total[:rows] + total[rows:]


def start_all(copies):
    for copy in copies:
        copy.start()


def wait_all(copies):
    for copy in copies:
        copy.wait()


def column_copies(source, target, sems, size=BLOCK):
    width = source.shape[1]
    cuts = [pl.ds(start, size) for start in range(0, width, size)]
    return [pltpu.make_async_copy(source.at[:, cut], target.at[:, cut], sems.at[b]) for b, cut in enumerate(cuts)]


def row_lengths(lengths, pad):
    total_rows = lengths.shape[0] * pad
    here = iota((total_rows, LANES), 0)
    lane = iota((total_rows, LANES), 1)
    wide = jnp.broadcast_to(lengths.astype(F32)[:, None, :], (lengths.shape[0], pad, LANES)).reshape(total_rows, LANES)
    per = LANES // pad
    wide = jnp.where(lane // per == here % pad, wide, 0.0).astype(BF16)
    spread = (iota((LANES, LANES), 0) % per == iota((LANES, LANES), 1) // pad).astype(F32).astype(BF16)
    row_len = dot(wide, spread)
    return row_len, (lane % pad).astype(F32) < row_len


def along(ref):
    return jnp.concatenate([ref[k : k + 1, :] for k in range(ref.shape[0])], axis=1)


def sums_kernel(pad, cap, *refs):
    (probes, lengths_in, ids_in, firms_in), sends, refs = refs[:4], refs[4 : 4 + NEAR], refs[4 + NEAR :]
    x1, mask_ids, weight, valid, x, sums, lengths, ids, firms, sems, small = refs
    copies = column_copies(probes, x, sems)
    first = [
        pltpu.make_async_copy(source, target, small.at[k])
        for k, (source, target) in enumerate(((lengths_in, lengths), (ids_in, ids), (firms_in, firms)))
    ]
    start_all(first)
    start_all(copies)
    columns, slots = sums.shape
    part = columns // NEAR
    me = lax.axis_index("rows") % NEAR
    wait_all(first)
    row_len, inside = row_lengths(lengths[...], pad)
    valid[...] = jnp.where(inside, 1.0, 0.0)
    weight[...] = jnp.where(inside, 1.0 / row_len, 0.0)
    masked = jnp.where(inside, ids[...], -1)
    mask_ids[...] = masked
    turned = jnp.concatenate([masked.astype(F32)] * (LANES // masked.shape[0]), axis=0).T
    keys = (iota((1, slots), 1) // cap * FIRMS_PER_SHARD + along(firms)).astype(F32)
    across = slots // LANES
    rows = ids.shape[0] // across
    masked = jnp.concatenate([masked[k * rows : (k + 1) * rows] for k in range(across)], axis=1).astype(F32)
    for send in sends:
        send[part + 8 :] = masked

    table = same_worker(pad, 256)
    wait_all(copies)
    total = None
    for b in range(len(copies)):
        ok = row(valid, b, BLOCK)
        x0 = x[:, b * BLOCK : (b + 1) * BLOCK] * ok
        rest = x0 - by_worker(x0, table) * row(weight, b, BLOCK)
        x1[:, b * BLOCK : (b + 1) * BLOCK] = rest
        counted = jnp.broadcast_to(ok, (16, BLOCK)).astype(BF16)
        data = jnp.concatenate([*split(rest), counted], axis=0)
        per = BLOCK // LANES
        block = dot(data, one_hot_down(turned[:, b * per : (b + 1) * per], slots))
        total = block if total is None else total + block
    sums[...] = total[:columns] + total[columns : 2 * columns]
    about = jnp.where(iota((8, slots), 0) == 0, keys, total[2 * columns : 2 * columns + 1])
    for step, send in zip(NEAR_STEPS, sends):
        send[:part] = sums[pl.ds(pl.multiple_of((me ^ step) * part, part), part), :]
        send[part : part + 8] = about


def join_kernel(part, *refs):
    parts, out = refs[:NEAR], refs[-1]
    for k, one in enumerate(parts):
        out[part * k : part * (k + 1)] = one[:part]
        out[part * NEAR + 2 * k : part * NEAR + 2 * k + 2] = one[part : part + 2]


def pairs_kernel(pad, start, *refs):
    parts, (out, ids, size, counts) = refs[:-4], refs[-4:]
    slots = out.shape[1]
    kind = BF16 if slots <= 256 else F32
    per = LANES // pad
    total_rows = ids.shape[1]
    across = slots // LANES
    rows = total_rows // across
    for k, part in enumerate(parts):
        size[k] = jnp.broadcast_to(part[start - 7 : start - 6], (8, slots))
        for at in range(across):
            ids[k, at * rows : (at + 1) * rows] = part[start:, at * LANES : (at + 1) * LANES]
    at = iota((LANES, pad * LANES), 1)
    deal = (iota((LANES, pad * LANES), 0) == at % per * pad + at // LANES).astype(F32).astype(BF16)
    mine = iota((total_rows, pad * LANES), 1) % LANES // per == iota((total_rows, pad * LANES), 0) % pad
    slot = iota((slots, LANES), 0).astype(F32).astype(kind)
    one, zero = jnp.ones((slots, LANES), kind), jnp.zeros((slots, LANES), kind)
    diagonal = iota((slots, slots), 1) == iota((slots, slots), 0)

    def device(k, carry):
        dealt = dot(jnp.concatenate(split(ids[k]), axis=0), deal)
        dealt = jnp.where(mine, dealt[:total_rows] + dealt[total_rows:], 0.0)
        dealt = jnp.sum(dealt.reshape(total_rows // pad, pad, pad * LANES), axis=1)
        spells = dealt.astype(kind)
        for g in range(total_rows // pad):
            total = zero
            for j in range(pad):
                total += jnp.where(slot == spells[g : g + 1, j * LANES : (j + 1) * LANES], one, zero)
            counts[k, :, g * LANES : (g + 1) * LANES] = total.astype(BF16)
        valid = jnp.where(dealt >= 0.0, 1.0, 0.0)
        length = valid[:, :LANES]
        for j in range(1, pad):
            length += valid[:, j * LANES : (j + 1) * LANES]
        inverse = 1.0 / length
        inverse = jnp.concatenate([inverse[g : g + 1] for g in range(total_rows // pad)], axis=1)
        here = counts[k]
        total = dot(jnp.concatenate(split(here.astype(F32) * inverse), axis=0), here, NT)
        total = total[:slots] + total[slots:] - jnp.where(diagonal, size[k, :1], 0.0)
        hi, lo = split(total)
        out[k, :, :slots] = hi
        out[k, :, slots:] = lo
        return carry

    lax.fori_loop(0, len(parts), device, 0, unroll=len(parts) if slots <= 256 else 1)


def same_firm(own, one, part, at):
    mine, keys = ([ref[part * NEAR + 2 * k : part * NEAR + 2 * k + 1, at] for k in range(NEAR)] for ref in (own, one))
    mine = jnp.concatenate(mine, axis=1)
    down = jnp.concatenate([jnp.broadcast_to(key, (8, LANES)) for key in keys], axis=0).T
    found = [(down[:, 8 * k : 8 * k + 1] == mine).astype(F32).astype(BF16) for k in range(NEAR)]
    return jnp.concatenate(found, axis=0)


def each_tile(slots, do):
    tiles = slots // LANES
    if tiles <= 2:
        for t in range(tiles):
            do(t, slice(t * LANES, (t + 1) * LANES))
    else:
        lax.fori_loop(0, tiles, lambda t, c: (do(t, pl.ds(pl.multiple_of(t * LANES, LANES), LANES)), c)[1], 0)


def firms_kernel(part, own, one, after, out):
    each_tile(own.shape[1], lambda t, at: out.__setitem__(t, same_firm(own, one, part, at)))


def gathered(parts, part, at):
    data = [one[part * k : part * (k + 1), at] for one in parts for k in range(NEAR)]
    return jnp.concatenate(split(jnp.concatenate(data, axis=1)), axis=0)


def spread_out(means, out, part, at):
    for k in range(NEAR):
        out[part * k : part * (k + 1), at] = means[:, k * LANES : (k + 1) * LANES]


def change_kernel(far, part, *refs):
    parts, tables, (own_pairs, pairs, mean, sums, scale) = refs[:far], refs[far:-5], refs[-5:]
    slots = mean.shape[1]

    def tile(t, at):
        same = [table[t] for table in tables] or [same_firm(parts[0], one, part, at) for one in parts]
        same = jnp.concatenate(same, axis=0)
        count = [one[part * NEAR + 2 * k + 1 : part * NEAR + 2 * k + 2, at] for one in parts for k in range(NEAR)]
        count = jnp.concatenate(count, axis=1)
        high = count.astype(BF16).astype(F32)
        counts = jnp.where(iota((16, count.shape[1]), 0) < 8, high, count - high).astype(BF16)
        found = dot(jnp.concatenate([gathered(parts, part, at), counts], axis=0), same)
        size = found[2 * part : 2 * part + 1] + found[2 * part + 8 : 2 * part + 9]
        inverse = 1.0 / jnp.maximum(size, 1.0)
        scale[t] = jnp.broadcast_to(inverse, scale.shape[1:])
        spread_out((found[:part] + found[part : 2 * part]) * inverse, mean, part, at)

    each_tile(slots, tile)
    for k in range(NEAR):
        cut = slice(part * k, part * (k + 1))
        both = jnp.concatenate(split(mean[cut]), axis=0)
        change = dot(both, own_pairs[0] if k == 0 else pairs[k - 1])
        change = change[:part] + change[part:]
        sums[cut] = parts[0][cut] + (change[:, :slots] + change[:, slots:])


def means_kernel(far, part, kept, *refs):
    parts, source, (scale, mean), sends, second = refs[:far], refs[far:-8], refs[-8:-6], refs[-5:-1], refs[-1]

    def tile(t, at):
        same = [table[t] if kept else same_firm(source[0], table, part, at) for table in source]
        same = jnp.concatenate(same, axis=0)
        found = dot(gathered(parts, part, at), same)
        spread_out((found[:part] + found[part:]) * scale[t][:1], second, part, at)

    each_tile(mean.shape[1], tile)
    for k, send in enumerate(sends):
        cut = slice(part * k, part * (k + 1))
        send[:part] = mean[cut]
        send[part:] = mean[cut] + second[cut]


def tables_kernel(pad, mask_ids, after, spread, workers):
    slots, width = spread.shape
    table = same_worker(pad, 256)
    for b in range(width // BLOCK):
        found = one_hot(row(mask_ids, b, BLOCK), slots)
        spread[:, b * BLOCK : (b + 1) * BLOCK] = found
        for at in range(0, BLOCK, 256):
            count = dot(found[:, at : at + 256], table)
            workers[:, b * BLOCK + at : b * BLOCK + at + 256] = count.astype(BF16)


def last_kernel(pad, part, *refs):
    parts, (x1, mask_ids, weight), tables, (out, means, y, sems) = refs[:NEAR], refs[NEAR : NEAR + 3], refs[NEAR + 3 : -4], refs[-4:]
    outs = column_copies(y, out, sems, 2 * BLOCK)
    me = lax.axis_index("rows") % NEAR
    columns, slots = means.shape[1:]
    for step, one in zip(NEAR_STEPS, parts):
        at = pl.ds(pl.multiple_of((me ^ step) * part, part), part)
        means[0, at, :] = one[:part]
        means[1, at, :] = one[part:]
    first, total = (jnp.concatenate(split(means[k]), axis=0) for k in range(2))
    table = same_worker(pad, 256)
    for b in range(2 * len(outs)):
        at = slice(b * BLOCK, (b + 1) * BLOCK)
        if tables:
            spread = dot(total, tables[0][:, at])
            worker = dot(first, tables[1][:, at])
            worker = worker[:columns] + worker[columns:]
        else:
            found = one_hot(row(mask_ids, b, BLOCK), slots)
            spread, worker = dot(total, found), dot(first, found)
            worker = by_worker(worker[:columns] + worker[columns:], table)
        y[:, at] = x1[:, at] - (spread[:columns] + spread[columns:]) + worker * row(weight, b, BLOCK)
        if b % 2:
            outs[b // 2].start()
    wait_all(outs)


def near_exchange(parts, n):
    steps = [[(i, i ^ step) for i in range(n)] for step in NEAR_STEPS[1:]]
    return [parts[0]] + [lax.ppermute(one, "rows", step) for one, step in zip(parts[1:], steps)]


def far_share(one, n):
    steps = [[(i, i ^ (k * NEAR)) for i in range(n)] for k in range(1, n // NEAR)]
    return [one] + [lax.ppermute(one, "rows", step) for step in steps]


def in_hbm(x):
    return pltpu.with_memory_space_constraint(x, pltpu.HBM)


def call(kernel, out_shape, in_specs, out_specs, scratch, flops, moved):
    return pl.pallas_call(
        kernel,
        out_shape=out_shape,
        in_specs=in_specs,
        out_specs=out_specs,
        scratch_shapes=scratch,
        compiler_params=pltpu.CompilerParams(vmem_limit_bytes=VMEM_BYTES),
        cost_estimate=pl.CostEstimate(flops=flops, bytes_accessed=moved, transcendentals=0),
    )


def body(probes, worker_len, spell_to_slot, slot_to_firm, *, n):
    columns, rows_dev = probes.shape
    workers = worker_len.shape[0]
    pad = rows_dev // workers
    slots = slot_to_firm.shape[0]
    tiles = slots // LANES
    part = columns // NEAR
    far = n // NEAR
    keep = tiles * NEAR * n * LANES * LANES * 2 <= 8 * 1024 * 1024
    blocks = rows_dev // BLOCK
    vmem, hbm = pl.BlockSpec(memory_space=pltpu.VMEM), pl.BlockSpec(memory_space=pltpu.HBM)
    lengths = worker_len.reshape(workers // LANES, LANES)
    ids = spell_to_slot.reshape(rows_dev // LANES, LANES)
    firms = slot_to_firm.reshape(tiles, LANES)
    array = jax.ShapeDtypeStruct
    of_rows = (rows_dev // LANES, LANES)
    work = 2 * rows_dev * slots * 2 * columns
    sems = pltpu.SemaphoreType.DMA((blocks,))
    whole = (columns, rows_dev)
    about = part + 8
    message = array((about + rows_dev // slots, slots), F32)
    of_near = array((columns, slots), F32)

    *sends, x1, mask_ids, weight = call(
        functools.partial(sums_kernel, pad, slots // n),
        [message] * NEAR + [array(whole, F32), array(of_rows, jnp.int32), array(of_rows, F32)],
        [hbm] * 4,
        [vmem] * (NEAR + 3),
        [
            pltpu.VMEM(of_rows, F32),
            pltpu.VMEM(whole, F32),
            pltpu.VMEM((columns, slots), F32),
            pltpu.VMEM(lengths.shape, jnp.int32),
            pltpu.VMEM(ids.shape, jnp.int32),
            pltpu.VMEM(firms.shape, jnp.int32),
            sems,
            pltpu.SemaphoreType.DMA((3,)),
        ],
        2 * work,
        4 * columns * rows_dev,
    )(in_hbm(probes), in_hbm(lengths), in_hbm(ids), in_hbm(firms))

    def pair_counts(parts):
        return call(
            functools.partial(pairs_kernel, pad, about),
            array((len(parts), slots, 2 * slots), BF16),
            [vmem] * len(parts),
            vmem,
            [
                pltpu.VMEM((len(parts), *of_rows), F32),
                pltpu.VMEM((len(parts), 8, slots), F32),
                pltpu.VMEM((len(parts), slots, workers), BF16),
            ],
            work * len(parts) // 4,
            4 * slots * slots,
        )(*parts)

    arrived = near_exchange(sends, n)
    own_pairs = pair_counts(arrived[:1])
    joined = call(
        functools.partial(join_kernel, part),
        array((columns + 2 * NEAR, slots), F32),
        [vmem] * (NEAR + 1),
        vmem,
        [],
        0,
        message.size * 8,
    )(*arrived, own_pairs)
    shared = far_share(joined, n)
    pairs = pair_counts(arrived[1:])
    tables = []
    if keep:
        after = joined
        for one in [shared[0]] + shared[:0:-1]:
            after = call(
                functools.partial(firms_kernel, part),
                array((tiles, NEAR * LANES, NEAR * LANES), BF16),
                [vmem] * 3,
                vmem,
                [],
                work // 64,
                tiles * (NEAR * LANES) ** 2 * 2,
            )(joined, one, after)
            tables.append(after)
        tables = tables[:1] + tables[:0:-1]
    scale = array((tiles, 8, NEAR * LANES), F32)
    mean, sums, scales = call(
        functools.partial(change_kernel, far, part),
        [of_near, of_near, scale],
        [vmem] * (far + len(tables) + 2),
        [vmem] * 3,
        [],
        work // 4,
        slots * slots * 4,
    )(*shared, *tables, own_pairs, pairs)
    again = far_share(sums, n)
    source = tables if keep else shared
    spreads = []
    if keep:
        spreads = call(
            functools.partial(tables_kernel, pad),
            [array((slots, rows_dev), BF16)] * 2,
            [vmem] * 2,
            [vmem] * 2,
            [],
            work,
            4 * slots * rows_dev,
        )(mask_ids, scales)
    sends = call(
        functools.partial(means_kernel, far, part, keep),
        [array((2 * part, slots), F32)] * NEAR,
        [vmem] * (far + len(source) + 3),
        [vmem] * NEAR,
        [pltpu.VMEM((columns, slots), F32)],
        work // 4,
        slots * slots * 4,
    )(*again, *source, scales, mean, spreads[1] if keep else mean)
    arrived = near_exchange(sends, n)
    return call(
        functools.partial(last_kernel, pad, part),
        array(whole, F32),
        [vmem] * (NEAR + 3 + len(spreads)),
        hbm,
        [pltpu.VMEM((2, columns, slots), F32), pltpu.VMEM(whole, F32), sems],
        work,
        8 * columns * rows_dev,
    )(*arrived, x1, mask_ids, weight, *spreads)


def solution(mesh):
    placed = (P(None, ("grp", "rows")), P(("grp", "rows")), P(("grp", "rows")), P(("grp", "rows")))
    return jax.shard_map(
        functools.partial(body, n=mesh.shape["rows"]),
        mesh=mesh,
        in_specs=placed,
        out_specs=P(None, ("grp", "rows")),
        check_vma=False,
    )
```

```python
import functools

import jax
import jax.numpy as jnp
from jax import lax
from jax.experimental import pallas as pl
from jax.experimental.pallas import tpu as pltpu
from jax.sharding import PartitionSpec as P

FIRMS_PER_SHARD = 1024
LANES = 128
BLOCK = 1024
VMEM_BYTES = 32 * 1024 * 1024
NEAR = 4
NEAR_STEPS = (0, 1, 2, 3)
F32, BF16 = jnp.float32, jnp.bfloat16
NT = (((1,), (1,)), ((), ()))
NN = (((1,), (0,)), ((), ()))


def dot(a, b, dims=NN):
    return lax.dot_general(a, b, dims, preferred_element_type=F32)


def iota(shape, dim):
    return lax.broadcasted_iota(jnp.int32, shape, dim)


def split(x):
    hi = x.astype(BF16)
    return hi, (x - hi.astype(F32)).astype(BF16)


def row(ref, block, size):
    per = size // LANES
    return jnp.concatenate([ref[block * per + k : block * per + k + 1, :] for k in range(per)], axis=1)


def one_hot(ids, slots):
    kind = BF16 if slots <= 256 else F32
    slot = iota((slots, LANES), 0).astype(F32).astype(kind)
    ids = ids.astype(F32).astype(kind)
    one, zero = jnp.ones((slots, LANES), kind), jnp.zeros((slots, LANES), kind)
    parts = [jnp.where(slot == ids[:, k : k + LANES], one, zero) for k in range(0, ids.shape[1], LANES)]
    return jnp.concatenate(parts, axis=1).astype(BF16)


def one_hot_down(columns, slots):
    kind = BF16 if slots <= 256 else F32
    one, zero = jnp.ones((LANES, LANES), kind), jnp.zeros((LANES, LANES), kind)
    along_slots = [(iota((LANES, LANES), 1) + at).astype(F32).astype(kind) for at in range(0, slots, LANES)]
    parts = []
    for k in range(columns.shape[1]):
        ids = jnp.broadcast_to(columns[:, k : k + 1], (LANES, LANES)).astype(kind)
        parts.append(jnp.concatenate([jnp.where(slot == ids, one, zero) for slot in along_slots], axis=1))
    return jnp.concatenate(parts, axis=0).astype(BF16)


def same_worker(pad, width):
    return (iota((width, width), 0) // pad == iota((width, width), 1) // pad).astype(F32).astype(BF16)


def by_worker(x, table):
    rows, width = x.shape
    hi, lo = split(x)
    both = jnp.concatenate([hi, lo], axis=0)
    step = table.shape[0]
    total = jnp.concatenate([dot(both[:, k : k + step], table) for k in range(0, width, step)], axis=1)
    return total[:rows] + total[rows:]


def start_all(copies):
    for copy in copies:
        copy.start()


def wait_all(copies):
    for copy in copies:
        copy.wait()


def column_copies(source, target, sems, size=BLOCK):
    width = source.shape[1]
    cuts = [pl.ds(start, size) for start in range(0, width, size)]
    return [pltpu.make_async_copy(source.at[:, cut], target.at[:, cut], sems.at[b]) for b, cut in enumerate(cuts)]


def row_lengths(lengths, pad):
    total_rows = lengths.shape[0] * pad
    here = iota((total_rows, LANES), 0)
    lane = iota((total_rows, LANES), 1)
    wide = jnp.broadcast_to(lengths.astype(F32)[:, None, :], (lengths.shape[0], pad, LANES)).reshape(total_rows, LANES)
    per = LANES // pad
    wide = jnp.where(lane // per == here % pad, wide, 0.0).astype(BF16)
    spread = (iota((LANES, LANES), 0) % per == iota((LANES, LANES), 1) // pad).astype(F32).astype(BF16)
    row_len = dot(wide, spread)
    return row_len, (lane % pad).astype(F32) < row_len


def along(ref):
    return jnp.concatenate([ref[k : k + 1, :] for k in range(ref.shape[0])], axis=1)


def sums_kernel(pad, cap, *refs):
    (probes, lengths_in, ids_in, firms_in), sends, refs = refs[:4], refs[4 : 4 + NEAR], refs[4 + NEAR :]
    x1, mask_ids, weight, valid, x, sums, lengths, ids, firms, sems, small = refs
    copies = column_copies(probes, x, sems)
    first = [
        pltpu.make_async_copy(source, target, small.at[k])
        for k, (source, target) in enumerate(((lengths_in, lengths), (ids_in, ids), (firms_in, firms)))
    ]
    start_all(first)
    start_all(copies)
    columns, slots = sums.shape
    part = columns // NEAR
    me = lax.axis_index("rows") % NEAR
    wait_all(first)
    row_len, inside = row_lengths(lengths[...], pad)
    valid[...] = jnp.where(inside, 1.0, 0.0)
    weight[...] = jnp.where(inside, 1.0 / row_len, 0.0)
    masked = jnp.where(inside, ids[...], -1)
    mask_ids[...] = masked
    turned = jnp.concatenate([masked.astype(F32)] * (LANES // masked.shape[0]), axis=0).T
    keys = (iota((1, slots), 1) // cap * FIRMS_PER_SHARD + along(firms)).astype(F32)
    across = slots // LANES
    rows = ids.shape[0] // across
    masked = jnp.concatenate([masked[k * rows : (k + 1) * rows] for k in range(across)], axis=1).astype(F32)
    for send in sends:
        send[part + 8 :] = masked

    table = same_worker(pad, 256)
    wait_all(copies)
    total = None
    for b in range(len(copies)):
        ok = row(valid, b, BLOCK)
        x0 = x[:, b * BLOCK : (b + 1) * BLOCK] * ok
        rest = x0 - by_worker(x0, table) * row(weight, b, BLOCK)
        x1[:, b * BLOCK : (b + 1) * BLOCK] = rest
        counted = jnp.broadcast_to(ok, (16, BLOCK)).astype(BF16)
        data = jnp.concatenate([*split(rest), counted], axis=0)
        per = BLOCK // LANES
        block = dot(data, one_hot_down(turned[:, b * per : (b + 1) * per], slots))
        total = block if total is None else total + block
    sums[...] = total[:columns] + total[columns : 2 * columns]
    about = jnp.where(iota((8, slots), 0) == 0, keys, total[2 * columns : 2 * columns + 1])
    for step, send in zip(NEAR_STEPS, sends):
        send[:part] = sums[pl.ds(pl.multiple_of((me ^ step) * part, part), part), :]
        send[part : part + 8] = about


def join_kernel(part, *refs):
    parts, out = refs[:NEAR], refs[-1]
    for k, one in enumerate(parts):
        out[part * k : part * (k + 1)] = one[:part]
        out[part * NEAR + 2 * k : part * NEAR + 2 * k + 2] = one[part : part + 2]


def pairs_kernel(pad, start, *refs):
    parts, (out, ids, size, counts) = refs[:-4], refs[-4:]
    slots = out.shape[1]
    kind = BF16 if slots <= 256 else F32
    per = LANES // pad
    total_rows = ids.shape[1]
    across = slots // LANES
    rows = total_rows // across
    for k, part in enumerate(parts):
        size[k] = jnp.broadcast_to(part[start - 7 : start - 6], (8, slots))
        for at in range(across):
            ids[k, at * rows : (at + 1) * rows] = part[start:, at * LANES : (at + 1) * LANES]
    at = iota((LANES, pad * LANES), 1)
    deal = (iota((LANES, pad * LANES), 0) == at % per * pad + at // LANES).astype(F32).astype(BF16)
    mine = iota((total_rows, pad * LANES), 1) % LANES // per == iota((total_rows, pad * LANES), 0) % pad
    slot = iota((slots, LANES), 0).astype(F32).astype(kind)
    one, zero = jnp.ones((slots, LANES), kind), jnp.zeros((slots, LANES), kind)
    diagonal = iota((slots, slots), 1) == iota((slots, slots), 0)

    def device(k, carry):
        dealt = dot(jnp.concatenate(split(ids[k]), axis=0), deal)
        dealt = jnp.where(mine, dealt[:total_rows] + dealt[total_rows:], 0.0)
        dealt = jnp.sum(dealt.reshape(total_rows // pad, pad, pad * LANES), axis=1)
        spells = dealt.astype(kind)
        for g in range(total_rows // pad):
            total = zero
            for j in range(pad):
                total += jnp.where(slot == spells[g : g + 1, j * LANES : (j + 1) * LANES], one, zero)
            counts[k, :, g * LANES : (g + 1) * LANES] = total.astype(BF16)
        valid = jnp.where(dealt >= 0.0, 1.0, 0.0)
        length = valid[:, :LANES]
        for j in range(1, pad):
            length += valid[:, j * LANES : (j + 1) * LANES]
        inverse = 1.0 / length
        inverse = jnp.concatenate([inverse[g : g + 1] for g in range(total_rows // pad)], axis=1)
        here = counts[k]
        total = dot(jnp.concatenate(split(here.astype(F32) * inverse), axis=0), here, NT)
        total = total[:slots] + total[slots:] - jnp.where(diagonal, size[k, :1], 0.0)
        hi, lo = split(total)
        out[k, :, :slots] = hi
        out[k, :, slots:] = lo
        return carry

    lax.fori_loop(0, len(parts), device, 0, unroll=len(parts) if slots <= 256 else 1)


def same_firm(own, one, part, at):
    mine, keys = ([ref[part * NEAR + 2 * k : part * NEAR + 2 * k + 1, at] for k in range(NEAR)] for ref in (own, one))
    mine = jnp.concatenate(mine, axis=1)
    down = jnp.concatenate([jnp.broadcast_to(key, (8, LANES)) for key in keys], axis=0).T
    found = [(down[:, 8 * k : 8 * k + 1] == mine).astype(F32).astype(BF16) for k in range(NEAR)]
    return jnp.concatenate(found, axis=0)


def each_tile(slots, do):
    tiles = slots // LANES
    if tiles <= 2:
        for t in range(tiles):
            do(t, slice(t * LANES, (t + 1) * LANES))
    else:
        lax.fori_loop(0, tiles, lambda t, c: (do(t, pl.ds(pl.multiple_of(t * LANES, LANES), LANES)), c)[1], 0)


def firms_kernel(part, own, one, after, out):
    each_tile(own.shape[1], lambda t, at: out.__setitem__(t, same_firm(own, one, part, at)))


def gathered(parts, part, at):
    data = [one[part * k : part * (k + 1), at] for one in parts for k in range(NEAR)]
    return jnp.concatenate(split(jnp.concatenate(data, axis=1)), axis=0)


def spread_out(means, out, part, at):
    for k in range(NEAR):
        out[part * k : part * (k + 1), at] = means[:, k * LANES : (k + 1) * LANES]


def change_kernel(far, part, *refs):
    parts, tables, pairs, (mean, sums, scale) = refs[:far], refs[far:-6], refs[-6:-3], refs[-3:]
    pairs = [(group, k) for group in pairs for k in range(group.shape[0])]
    slots = mean.shape[1]

    def tile(t, at):
        same = [table[t] for table in tables] or [same_firm(parts[0], one, part, at) for one in parts]
        same = jnp.concatenate(same, axis=0)
        count = [one[part * NEAR + 2 * k + 1 : part * NEAR + 2 * k + 2, at] for one in parts for k in range(NEAR)]
        count = jnp.concatenate(count, axis=1)
        high = count.astype(BF16).astype(F32)
        counts = jnp.where(iota((16, count.shape[1]), 0) < 8, high, count - high).astype(BF16)
        found = dot(jnp.concatenate([gathered(parts, part, at), counts], axis=0), same)
        size = found[2 * part : 2 * part + 1] + found[2 * part + 8 : 2 * part + 9]
        inverse = 1.0 / jnp.maximum(size, 1.0)
        scale[t] = jnp.broadcast_to(inverse, scale.shape[1:])
        spread_out((found[:part] + found[part : 2 * part]) * inverse, mean, part, at)

    each_tile(slots, tile)
    for k in range(NEAR):
        cut = slice(part * k, part * (k + 1))
        both = jnp.concatenate(split(mean[cut]), axis=0)
        change = dot(both, pairs[k][0][pairs[k][1]])
        change = change[:part] + change[part:]
        sums[cut] = parts[0][cut] + (change[:, :slots] + change[:, slots:])


def means_kernel(far, part, kept, *refs):
    parts, source, (scale, mean), sends, second = refs[:far], refs[far:-8], refs[-8:-6], refs[-5:-1], refs[-1]

    def tile(t, at):
        same = [table[t] if kept else same_firm(source[0], table, part, at) for table in source]
        same = jnp.concatenate(same, axis=0)
        found = dot(gathered(parts, part, at), same)
        spread_out((found[:part] + found[part:]) * scale[t][:1], second, part, at)

    each_tile(mean.shape[1], tile)
    for k, send in enumerate(sends):
        cut = slice(part * k, part * (k + 1))
        send[:part] = mean[cut]
        send[part:] = mean[cut] + second[cut]


def tables_kernel(pad, mask_ids, after, spread, workers):
    slots, width = spread.shape
    table = same_worker(pad, 256)
    for b in range(width // BLOCK):
        found = one_hot(row(mask_ids, b, BLOCK), slots)
        spread[:, b * BLOCK : (b + 1) * BLOCK] = found
        for at in range(0, BLOCK, 256):
            count = dot(found[:, at : at + 256], table)
            workers[:, b * BLOCK + at : b * BLOCK + at + 256] = count.astype(BF16)


def last_kernel(pad, part, *refs):
    parts, (x1, mask_ids, weight), tables, (out, means, y, sems) = refs[:NEAR], refs[NEAR : NEAR + 3], refs[NEAR + 3 : -4], refs[-4:]
    outs = column_copies(y, out, sems, 2 * BLOCK)
    me = lax.axis_index("rows") % NEAR
    columns, slots = means.shape[1:]
    for step, one in zip(NEAR_STEPS, parts):
        at = pl.ds(pl.multiple_of((me ^ step) * part, part), part)
        means[0, at, :] = one[:part]
        means[1, at, :] = one[part:]
    first, total = (jnp.concatenate(split(means[k]), axis=0) for k in range(2))
    table = same_worker(pad, 256)
    for b in range(2 * len(outs)):
        at = slice(b * BLOCK, (b + 1) * BLOCK)
        if tables:
            spread = dot(total, tables[0][:, at])
            worker = dot(first, tables[1][:, at])
            worker = worker[:columns] + worker[columns:]
        else:
            found = one_hot(row(mask_ids, b, BLOCK), slots)
            spread, worker = dot(total, found), dot(first, found)
            worker = by_worker(worker[:columns] + worker[columns:], table)
        y[:, at] = x1[:, at] - (spread[:columns] + spread[columns:]) + worker * row(weight, b, BLOCK)
        if b % 2:
            outs[b // 2].start()
    wait_all(outs)


def near_exchange(parts, n):
    steps = [[(i, i ^ step) for i in range(n)] for step in NEAR_STEPS[1:]]
    return [parts[0]] + [lax.ppermute(one, "rows", step) for one, step in zip(parts[1:], steps)]


def far_share(one, n):
    steps = [[(i, i ^ (k * NEAR)) for i in range(n)] for k in range(1, n // NEAR)]
    return [one] + [lax.ppermute(one, "rows", step) for step in steps]


def in_hbm(x):
    return pltpu.with_memory_space_constraint(x, pltpu.HBM)


def call(kernel, out_shape, in_specs, out_specs, scratch, flops, moved):
    return pl.pallas_call(
        kernel,
        out_shape=out_shape,
        in_specs=in_specs,
        out_specs=out_specs,
        scratch_shapes=scratch,
        compiler_params=pltpu.CompilerParams(vmem_limit_bytes=VMEM_BYTES),
        cost_estimate=pl.CostEstimate(flops=flops, bytes_accessed=moved, transcendentals=0),
    )


def body(probes, worker_len, spell_to_slot, slot_to_firm, *, n):
    columns, rows_dev = probes.shape
    workers = worker_len.shape[0]
    pad = rows_dev // workers
    slots = slot_to_firm.shape[0]
    tiles = slots // LANES
    part = columns // NEAR
    far = n // NEAR
    keep = tiles * NEAR * n * LANES * LANES * 2 <= 8 * 1024 * 1024
    blocks = rows_dev // BLOCK
    vmem, hbm = pl.BlockSpec(memory_space=pltpu.VMEM), pl.BlockSpec(memory_space=pltpu.HBM)
    lengths = worker_len.reshape(workers // LANES, LANES)
    ids = spell_to_slot.reshape(rows_dev // LANES, LANES)
    firms = slot_to_firm.reshape(tiles, LANES)
    array = jax.ShapeDtypeStruct
    of_rows = (rows_dev // LANES, LANES)
    work = 2 * rows_dev * slots * 2 * columns
    sems = pltpu.SemaphoreType.DMA((blocks,))
    whole = (columns, rows_dev)
    about = part + 8
    message = array((about + rows_dev // slots, slots), F32)
    of_near = array((columns, slots), F32)

    *sends, x1, mask_ids, weight = call(
        functools.partial(sums_kernel, pad, slots // n),
        [message] * NEAR + [array(whole, F32), array(of_rows, jnp.int32), array(of_rows, F32)],
        [hbm] * 4,
        [vmem] * (NEAR + 3),
        [
            pltpu.VMEM(of_rows, F32),
            pltpu.VMEM(whole, F32),
            pltpu.VMEM((columns, slots), F32),
            pltpu.VMEM(lengths.shape, jnp.int32),
            pltpu.VMEM(ids.shape, jnp.int32),
            pltpu.VMEM(firms.shape, jnp.int32),
            sems,
            pltpu.SemaphoreType.DMA((3,)),
        ],
        2 * work,
        4 * columns * rows_dev,
    )(in_hbm(probes), in_hbm(lengths), in_hbm(ids), in_hbm(firms))

    def pair_counts(parts):
        return call(
            functools.partial(pairs_kernel, pad, about),
            array((len(parts), slots, 2 * slots), BF16),
            [vmem] * len(parts),
            vmem,
            [
                pltpu.VMEM((len(parts), *of_rows), F32),
                pltpu.VMEM((len(parts), 8, slots), F32),
                pltpu.VMEM((len(parts), slots, workers), BF16),
            ],
            work * len(parts) // 4,
            4 * slots * slots,
        )(*parts)

    arrived = near_exchange(sends, n)
    pairs = [pair_counts(arrived[:1]), pair_counts(arrived[1:2])]
    joined = call(
        functools.partial(join_kernel, part),
        array((columns + 2 * NEAR, slots), F32),
        [vmem] * (NEAR + 2),
        vmem,
        [],
        0,
        message.size * 8,
    )(*arrived, *pairs)
    shared = far_share(joined, n)
    pairs.append(pair_counts(arrived[2:]))
    tables = []
    if keep:
        after = joined
        for one in [shared[0]] + shared[:0:-1]:
            after = call(
                functools.partial(firms_kernel, part),
                array((tiles, NEAR * LANES, NEAR * LANES), BF16),
                [vmem] * 3,
                vmem,
                [],
                work // 64,
                tiles * (NEAR * LANES) ** 2 * 2,
            )(joined, one, after)
            tables.append(after)
        tables = tables[:1] + tables[:0:-1]
    scale = array((tiles, 8, NEAR * LANES), F32)
    mean, sums, scales = call(
        functools.partial(change_kernel, far, part),
        [of_near, of_near, scale],
        [vmem] * (far + len(tables) + len(pairs)),
        [vmem] * 3,
        [],
        work // 4,
        slots * slots * 4,
    )(*shared, *tables, *pairs)
    again = far_share(sums, n)
    source = tables if keep else shared
    spreads = []
    if keep:
        spreads = call(
            functools.partial(tables_kernel, pad),
            [array((slots, rows_dev), BF16)] * 2,
            [vmem] * 2,
            [vmem] * 2,
            [],
            work,
            4 * slots * rows_dev,
        )(mask_ids, scales)
    sends = call(
        functools.partial(means_kernel, far, part, keep),
        [array((2 * part, slots), F32)] * NEAR,
        [vmem] * (far + len(source) + 3),
        [vmem] * NEAR,
        [pltpu.VMEM((columns, slots), F32)],
        work // 4,
        slots * slots * 4,
    )(*again, *source, scales, mean, spreads[1] if keep else mean)
    arrived = near_exchange(sends, n)
    return call(
        functools.partial(last_kernel, pad, part),
        array(whole, F32),
        [vmem] * (NEAR + 3 + len(spreads)),
        hbm,
        [pltpu.VMEM((2, columns, slots), F32), pltpu.VMEM(whole, F32), sems],
        work,
        8 * columns * rows_dev,
    )(*arrived, x1, mask_ids, weight, *spreads)


def solution(mesh):
    placed = (P(None, ("grp", "rows")), P(("grp", "rows")), P(("grp", "rows")), P(("grp", "rows")))
    return jax.shard_map(
        functools.partial(body, n=mesh.shape["rows"]),
        mesh=mesh,
        in_specs=placed,
        out_specs=P(None, ("grp", "rows")),
        check_vma=False,
    )
```

```python
import functools

import jax
import jax.numpy as jnp
from jax import lax
from jax.experimental import pallas as pl
from jax.experimental.pallas import tpu as pltpu
from jax.sharding import PartitionSpec as P

FIRMS_PER_SHARD = 1024
LANES = 128
BLOCK = 1024
VMEM_BYTES = 32 * 1024 * 1024
NEAR = 4
NEAR_STEPS = (0, 1, 2, 3)
F32, BF16 = jnp.float32, jnp.bfloat16
NT = (((1,), (1,)), ((), ()))
NN = (((1,), (0,)), ((), ()))


def dot(a, b, dims=NN):
    return lax.dot_general(a, b, dims, preferred_element_type=F32)


def iota(shape, dim):
    return lax.broadcasted_iota(jnp.int32, shape, dim)


def split(x):
    hi = x.astype(BF16)
    return hi, (x - hi.astype(F32)).astype(BF16)


def row(ref, block, size):
    per = size // LANES
    return jnp.concatenate([ref[block * per + k : block * per + k + 1, :] for k in range(per)], axis=1)


def one_hot(ids, slots):
    kind = BF16 if slots <= 256 else F32
    slot = iota((slots, LANES), 0).astype(F32).astype(kind)
    ids = ids.astype(F32).astype(kind)
    one, zero = jnp.ones((slots, LANES), kind), jnp.zeros((slots, LANES), kind)
    parts = [jnp.where(slot == ids[:, k : k + LANES], one, zero) for k in range(0, ids.shape[1], LANES)]
    return jnp.concatenate(parts, axis=1).astype(BF16)


def one_hot_down(columns, slots):
    kind = BF16 if slots <= 256 else F32
    one, zero = jnp.ones((LANES, LANES), kind), jnp.zeros((LANES, LANES), kind)
    along_slots = [(iota((LANES, LANES), 1) + at).astype(F32).astype(kind) for at in range(0, slots, LANES)]
    parts = []
    for k in range(columns.shape[1]):
        ids = jnp.broadcast_to(columns[:, k : k + 1], (LANES, LANES)).astype(kind)
        parts.append(jnp.concatenate([jnp.where(slot == ids, one, zero) for slot in along_slots], axis=1))
    return jnp.concatenate(parts, axis=0).astype(BF16)


def same_worker(pad, width):
    return (iota((width, width), 0) // pad == iota((width, width), 1) // pad).astype(F32).astype(BF16)


def by_worker(x, table):
    rows, width = x.shape
    hi, lo = split(x)
    both = jnp.concatenate([hi, lo], axis=0)
    step = table.shape[0]
    total = jnp.concatenate([dot(both[:, k : k + step], table) for k in range(0, width, step)], axis=1)
    return total[:rows] + total[rows:]


def start_all(copies):
    for copy in copies:
        copy.start()


def wait_all(copies):
    for copy in copies:
        copy.wait()


def column_copies(source, target, sems, size=BLOCK):
    width = source.shape[1]
    cuts = [pl.ds(start, size) for start in range(0, width, size)]
    return [pltpu.make_async_copy(source.at[:, cut], target.at[:, cut], sems.at[b]) for b, cut in enumerate(cuts)]


def row_lengths(lengths, pad):
    total_rows = lengths.shape[0] * pad
    here = iota((total_rows, LANES), 0)
    lane = iota((total_rows, LANES), 1)
    wide = jnp.broadcast_to(lengths.astype(F32)[:, None, :], (lengths.shape[0], pad, LANES)).reshape(total_rows, LANES)
    per = LANES // pad
    wide = jnp.where(lane // per == here % pad, wide, 0.0).astype(BF16)
    spread = (iota((LANES, LANES), 0) % per == iota((LANES, LANES), 1) // pad).astype(F32).astype(BF16)
    row_len = dot(wide, spread)
    return row_len, (lane % pad).astype(F32) < row_len


def along(ref):
    return jnp.concatenate([ref[k : k + 1, :] for k in range(ref.shape[0])], axis=1)


def sums_kernel(pad, cap, *refs):
    (probes, lengths_in, ids_in, firms_in), sends, refs = refs[:4], refs[4 : 4 + NEAR], refs[4 + NEAR :]
    x1, mask_ids, weight, valid, x, sums, lengths, ids, firms, sems, small = refs
    copies = column_copies(probes, x, sems)
    first = [
        pltpu.make_async_copy(source, target, small.at[k])
        for k, (source, target) in enumerate(((lengths_in, lengths), (ids_in, ids), (firms_in, firms)))
    ]
    start_all(first)
    start_all(copies)
    columns, slots = sums.shape
    part = columns // NEAR
    me = lax.axis_index("rows") % NEAR
    wait_all(first)
    row_len, inside = row_lengths(lengths[...], pad)
    valid[...] = jnp.where(inside, 1.0, 0.0)
    weight[...] = jnp.where(inside, 1.0 / row_len, 0.0)
    masked = jnp.where(inside, ids[...], -1)
    mask_ids[...] = masked
    turned = jnp.concatenate([masked.astype(F32)] * (LANES // masked.shape[0]), axis=0).T
    keys = (iota((1, slots), 1) // cap * FIRMS_PER_SHARD + along(firms)).astype(F32)
    across = slots // LANES
    rows = ids.shape[0] // across
    masked = jnp.concatenate([masked[k * rows : (k + 1) * rows] for k in range(across)], axis=1).astype(F32)
    for send in sends:
        send[part + 8 :] = masked

    table = same_worker(pad, 256)
    wait_all(copies)
    total = None
    for b in range(len(copies)):
        ok = row(valid, b, BLOCK)
        x0 = x[:, b * BLOCK : (b + 1) * BLOCK] * ok
        rest = x0 - by_worker(x0, table) * row(weight, b, BLOCK)
        x1[:, b * BLOCK : (b + 1) * BLOCK] = rest
        counted = jnp.broadcast_to(ok, (16, BLOCK)).astype(BF16)
        data = jnp.concatenate([*split(rest), counted], axis=0)
        per = BLOCK // LANES
        block = dot(data, one_hot_down(turned[:, b * per : (b + 1) * per], slots))
        total = block if total is None else total + block
    sums[...] = total[:columns] + total[columns : 2 * columns]
    about = jnp.where(iota((8, slots), 0) == 0, keys, total[2 * columns : 2 * columns + 1])
    for step, send in zip(NEAR_STEPS, sends):
        send[:part] = sums[pl.ds(pl.multiple_of((me ^ step) * part, part), part), :]
        send[part : part + 8] = about


def join_kernel(part, *refs):
    parts, out = refs[:NEAR], refs[-1]
    for k, one in enumerate(parts):
        out[part * k : part * (k + 1)] = one[:part]
        out[part * NEAR + 2 * k : part * NEAR + 2 * k + 2] = one[part : part + 2]


def pairs_kernel(pad, start, *refs):
    parts, (out, ids, size, counts) = refs[:-4], refs[-4:]
    slots = out.shape[1]
    kind = BF16 if slots <= 256 else F32
    per = LANES // pad
    total_rows = ids.shape[1]
    across = slots // LANES
    rows = total_rows // across
    for k, part in enumerate(parts):
        size[k] = jnp.broadcast_to(part[start - 7 : start - 6], (8, slots))
        for at in range(across):
            ids[k, at * rows : (at + 1) * rows] = part[start:, at * LANES : (at + 1) * LANES]
    at = iota((LANES, pad * LANES), 1)
    deal = (iota((LANES, pad * LANES), 0) == at % per * pad + at // LANES).astype(F32).astype(BF16)
    mine = iota((total_rows, pad * LANES), 1) % LANES // per == iota((total_rows, pad * LANES), 0) % pad
    slot = iota((slots, LANES), 0).astype(F32).astype(kind)
    one, zero = jnp.ones((slots, LANES), kind), jnp.zeros((slots, LANES), kind)
    diagonal = iota((slots, slots), 1) == iota((slots, slots), 0)

    def device(k, carry):
        dealt = dot(jnp.concatenate(split(ids[k]), axis=0), deal)
        dealt = jnp.where(mine, dealt[:total_rows] + dealt[total_rows:], 0.0)
        dealt = jnp.sum(dealt.reshape(total_rows // pad, pad, pad * LANES), axis=1)
        spells = dealt.astype(kind)
        for g in range(total_rows // pad):
            total = zero
            for j in range(pad):
                total += jnp.where(slot == spells[g : g + 1, j * LANES : (j + 1) * LANES], one, zero)
            counts[k, :, g * LANES : (g + 1) * LANES] = total.astype(BF16)
        valid = jnp.where(dealt >= 0.0, 1.0, 0.0)
        length = valid[:, :LANES]
        for j in range(1, pad):
            length += valid[:, j * LANES : (j + 1) * LANES]
        inverse = 1.0 / length
        inverse = jnp.concatenate([inverse[g : g + 1] for g in range(total_rows // pad)], axis=1)
        here = counts[k]
        total = dot(jnp.concatenate(split(here.astype(F32) * inverse), axis=0), here, NT)
        total = total[:slots] + total[slots:] - jnp.where(diagonal, size[k, :1], 0.0)
        hi, lo = split(total)
        out[k, :, :slots] = hi
        out[k, :, slots:] = lo
        return carry

    lax.fori_loop(0, len(parts), device, 0, unroll=len(parts) if slots <= 256 else 1)


def same_firm(own, one, part, at):
    mine, keys = ([ref[part * NEAR + 2 * k : part * NEAR + 2 * k + 1, at] for k in range(NEAR)] for ref in (own, one))
    mine = jnp.concatenate(mine, axis=1)
    down = jnp.concatenate([jnp.broadcast_to(key, (8, LANES)) for key in keys], axis=0).T
    found = [(down[:, 8 * k : 8 * k + 1] == mine).astype(F32).astype(BF16) for k in range(NEAR)]
    return jnp.concatenate(found, axis=0)


def each_tile(slots, do):
    tiles = slots // LANES
    if tiles <= 2:
        for t in range(tiles):
            do(t, slice(t * LANES, (t + 1) * LANES))
    else:
        lax.fori_loop(0, tiles, lambda t, c: (do(t, pl.ds(pl.multiple_of(t * LANES, LANES), LANES)), c)[1], 0)


def firms_kernel(part, own, one, after, out):
    each_tile(own.shape[1], lambda t, at: out.__setitem__(t, same_firm(own, one, part, at)))


def gathered(parts, part, at):
    data = [one[part * k : part * (k + 1), at] for one in parts for k in range(NEAR)]
    return jnp.concatenate(split(jnp.concatenate(data, axis=1)), axis=0)


def spread_out(means, out, part, at):
    for k in range(NEAR):
        out[part * k : part * (k + 1), at] = means[:, k * LANES : (k + 1) * LANES]


def change_kernel(far, part, *refs):
    parts, tables, pairs, (mean, sums, scale) = refs[:far], refs[far:-6], refs[-6:-3], refs[-3:]
    pairs = [(group, k) for group in pairs for k in range(group.shape[0])]
    slots = mean.shape[1]

    def tile(t, at):
        same = [table[t] for table in tables] or [same_firm(parts[0], one, part, at) for one in parts]
        same = jnp.concatenate(same, axis=0)
        count = [one[part * NEAR + 2 * k + 1 : part * NEAR + 2 * k + 2, at] for one in parts for k in range(NEAR)]
        count = jnp.concatenate(count, axis=1)
        high = count.astype(BF16).astype(F32)
        counts = jnp.where(iota((16, count.shape[1]), 0) < 8, high, count - high).astype(BF16)
        found = dot(jnp.concatenate([gathered(parts, part, at), counts], axis=0), same)
        size = found[2 * part : 2 * part + 1] + found[2 * part + 8 : 2 * part + 9]
        inverse = 1.0 / jnp.maximum(size, 1.0)
        scale[t] = jnp.broadcast_to(inverse, scale.shape[1:])
        spread_out((found[:part] + found[part : 2 * part]) * inverse, mean, part, at)

    each_tile(slots, tile)
    for k in range(NEAR):
        cut = slice(part * k, part * (k + 1))
        both = jnp.concatenate(split(mean[cut]), axis=0)
        change = dot(both, pairs[k][0][pairs[k][1]])
        change = change[:part] + change[part:]
        sums[cut] = parts[0][cut] + (change[:, :slots] + change[:, slots:])


def tables_kernel(pad, mask_ids, mean, spread, workers, *sends):
    part = mean.shape[0] // NEAR
    for k, send in enumerate(sends):
        send[...] = mean[part * k : part * (k + 1)]
    slots, width = spread.shape
    table = same_worker(pad, 256)
    for b in range(width // BLOCK):
        found = one_hot(row(mask_ids, b, BLOCK), slots)
        spread[:, b * BLOCK : (b + 1) * BLOCK] = found
        for at in range(0, BLOCK, 256):
            count = dot(found[:, at : at + 256], table)
            workers[:, b * BLOCK + at : b * BLOCK + at + 256] = count.astype(BF16)


def means_kernel(far, part, kept, *refs):
    parts, source, scale, sends, mean = refs[:far], refs[far:-7], refs[-7], refs[-5:-1], refs[-1]

    def tile(t, at):
        same = [table[t] if kept else same_firm(source[0], table, part, at) for table in source]
        same = jnp.concatenate(same, axis=0)
        found = dot(gathered(parts, part, at), same)
        spread_out((found[:part] + found[part:]) * scale[t][:1], mean, part, at)

    each_tile(mean.shape[1], tile)
    for k, send in enumerate(sends):
        send[...] = mean[part * k : part * (k + 1)]


def own_means(parts, means):
    me = lax.axis_index("rows") % NEAR
    part = parts[0].shape[0]
    for step, one in zip(NEAR_STEPS, parts):
        means[pl.ds(pl.multiple_of((me ^ step) * part, part), part), :] = one[...]
    return jnp.concatenate(split(means[...]), axis=0)


def first_kernel(pad, *refs):
    parts, (x1, mask_ids, weight), tables, (y, means) = refs[:NEAR], refs[NEAR : NEAR + 3], refs[NEAR + 3 : -2], refs[-2:]
    columns, slots = means.shape
    first = own_means(parts, means)
    table = same_worker(pad, 256)
    for b in range(y.shape[1] // BLOCK):
        at = slice(b * BLOCK, (b + 1) * BLOCK)
        found = tables[0][:, at] if tables else one_hot(row(mask_ids, b, BLOCK), slots)
        spread = dot(first, found)
        spread = spread[:columns] + spread[columns:]
        if tables:
            worker = dot(first, tables[1][:, at])
            worker = worker[:columns] + worker[columns:]
        else:
            worker = by_worker(spread, table)
        y[:, at] = x1[:, at] - spread + worker * row(weight, b, BLOCK)


def last_kernel(*refs):
    parts, (before, mask_ids), tables, (out, means, y, sems) = refs[:NEAR], refs[NEAR : NEAR + 2], refs[NEAR + 2 : -4], refs[-4:]
    outs = column_copies(y, out, sems, 2 * BLOCK)
    columns, slots = means.shape
    second = own_means(parts, means)
    for b in range(2 * len(outs)):
        at = slice(b * BLOCK, (b + 1) * BLOCK)
        found = tables[0][:, at] if tables else one_hot(row(mask_ids, b, BLOCK), slots)
        spread = dot(second, found)
        y[:, at] = before[:, at] - (spread[:columns] + spread[columns:])
        if b % 2:
            outs[b // 2].start()
    wait_all(outs)


def near_exchange(parts, n):
    steps = [[(i, i ^ step) for i in range(n)] for step in NEAR_STEPS[1:]]
    return [parts[0]] + [lax.ppermute(one, "rows", step) for one, step in zip(parts[1:], steps)]


def far_share(one, n):
    steps = [[(i, i ^ (k * NEAR)) for i in range(n)] for k in range(1, n // NEAR)]
    return [one] + [lax.ppermute(one, "rows", step) for step in steps]


def in_hbm(x):
    return pltpu.with_memory_space_constraint(x, pltpu.HBM)


def call(kernel, out_shape, in_specs, out_specs, scratch, flops, moved):
    return pl.pallas_call(
        kernel,
        out_shape=out_shape,
        in_specs=in_specs,
        out_specs=out_specs,
        scratch_shapes=scratch,
        compiler_params=pltpu.CompilerParams(vmem_limit_bytes=VMEM_BYTES),
        cost_estimate=pl.CostEstimate(flops=flops, bytes_accessed=moved, transcendentals=0),
    )


def body(probes, worker_len, spell_to_slot, slot_to_firm, *, n):
    columns, rows_dev = probes.shape
    workers = worker_len.shape[0]
    pad = rows_dev // workers
    slots = slot_to_firm.shape[0]
    tiles = slots // LANES
    part = columns // NEAR
    far = n // NEAR
    keep = tiles * NEAR * n * LANES * LANES * 2 <= 8 * 1024 * 1024
    blocks = rows_dev // BLOCK
    vmem, hbm = pl.BlockSpec(memory_space=pltpu.VMEM), pl.BlockSpec(memory_space=pltpu.HBM)
    lengths = worker_len.reshape(workers // LANES, LANES)
    ids = spell_to_slot.reshape(rows_dev // LANES, LANES)
    firms = slot_to_firm.reshape(tiles, LANES)
    array = jax.ShapeDtypeStruct
    of_rows = (rows_dev // LANES, LANES)
    work = 2 * rows_dev * slots * 2 * columns
    sems = pltpu.SemaphoreType.DMA((blocks,))
    whole = (columns, rows_dev)
    about = part + 8
    message = array((about + rows_dev // slots, slots), F32)
    of_near = array((columns, slots), F32)

    *sends, x1, mask_ids, weight = call(
        functools.partial(sums_kernel, pad, slots // n),
        [message] * NEAR + [array(whole, F32), array(of_rows, jnp.int32), array(of_rows, F32)],
        [hbm] * 4,
        [vmem] * (NEAR + 3),
        [
            pltpu.VMEM(of_rows, F32),
            pltpu.VMEM(whole, F32),
            pltpu.VMEM((columns, slots), F32),
            pltpu.VMEM(lengths.shape, jnp.int32),
            pltpu.VMEM(ids.shape, jnp.int32),
            pltpu.VMEM(firms.shape, jnp.int32),
            sems,
            pltpu.SemaphoreType.DMA((3,)),
        ],
        2 * work,
        4 * columns * rows_dev,
    )(in_hbm(probes), in_hbm(lengths), in_hbm(ids), in_hbm(firms))

    def pair_counts(parts):
        return call(
            functools.partial(pairs_kernel, pad, about),
            array((len(parts), slots, 2 * slots), BF16),
            [vmem] * len(parts),
            vmem,
            [
                pltpu.VMEM((len(parts), *of_rows), F32),
                pltpu.VMEM((len(parts), 8, slots), F32),
                pltpu.VMEM((len(parts), slots, workers), BF16),
            ],
            work * len(parts) // 4,
            4 * slots * slots,
        )(*parts)

    arrived = near_exchange(sends, n)
    pairs = [pair_counts(arrived[:1]), pair_counts(arrived[1:2])]
    joined = call(
        functools.partial(join_kernel, part),
        array((columns + 2 * NEAR, slots), F32),
        [vmem] * (NEAR + 2),
        vmem,
        [],
        0,
        message.size * 8,
    )(*arrived, *pairs)
    shared = far_share(joined, n)
    pairs.append(pair_counts(arrived[2:]))
    tables = []
    if keep:
        after = joined
        for one in [shared[0]] + shared[:0:-1]:
            after = call(
                functools.partial(firms_kernel, part),
                array((tiles, NEAR * LANES, NEAR * LANES), BF16),
                [vmem] * 3,
                vmem,
                [],
                work // 64,
                tiles * (NEAR * LANES) ** 2 * 2,
            )(joined, one, after)
            tables.append(after)
        tables = tables[:1] + tables[:0:-1]
    scale = array((tiles, 8, NEAR * LANES), F32)
    mean, sums, scales = call(
        functools.partial(change_kernel, far, part),
        [of_near, of_near, scale],
        [vmem] * (far + len(tables) + len(pairs)),
        [vmem] * 3,
        [],
        work // 4,
        slots * slots * 4,
    )(*shared, *tables, *pairs)
    again = far_share(sums, n)
    source = tables if keep else shared
    spreads = []
    sends = [mean[part * k : part * (k + 1)] for k in range(NEAR)]
    if keep:
        *spreads, a, b, c, d = call(
            functools.partial(tables_kernel, pad),
            [array((slots, rows_dev), BF16)] * 2 + [array((part, slots), F32)] * NEAR,
            [vmem] * 2,
            [vmem] * (2 + NEAR),
            [],
            work,
            4 * slots * rows_dev,
        )(mask_ids, mean)
        sends = [a, b, c, d]
    first = near_exchange(sends, n)
    sends = call(
        functools.partial(means_kernel, far, part, keep),
        [array((part, slots), F32)] * NEAR,
        [vmem] * (far + len(source) + 2),
        [vmem] * NEAR,
        [pltpu.VMEM((columns, slots), F32)],
        work // 4,
        slots * slots * 4,
    )(*again, *source, scales, spreads[1] if keep else scales)
    arrived = near_exchange(sends, n)
    before = call(
        functools.partial(first_kernel, pad),
        array(whole, F32),
        [vmem] * (NEAR + 3 + len(spreads)),
        vmem,
        [pltpu.VMEM((columns, slots), F32)],
        work,
        8 * columns * rows_dev,
    )(*first, x1, mask_ids, weight, *spreads)
    return call(
        last_kernel,
        array(whole, F32),
        [vmem] * (NEAR + 2 + len(spreads[:1])),
        hbm,
        [pltpu.VMEM((columns, slots), F32), pltpu.VMEM(whole, F32), sems],
        work,
        8 * columns * rows_dev,
    )(*arrived, before, mask_ids, *spreads[:1])


def solution(mesh):
    placed = (P(None, ("grp", "rows")), P(("grp", "rows")), P(("grp", "rows")), P(("grp", "rows")))
    return jax.shard_map(
        functools.partial(body, n=mesh.shape["rows"]),
        mesh=mesh,
        in_specs=placed,
        out_specs=P(None, ("grp", "rows")),
        check_vma=False,
    )
```

```python
import functools

import jax
import jax.numpy as jnp
from jax import lax
from jax.experimental import pallas as pl
from jax.experimental.pallas import tpu as pltpu
from jax.sharding import PartitionSpec as P

FIRMS_PER_SHARD = 1024
LANES = 128
BLOCK = 1024
VMEM_BYTES = 32 * 1024 * 1024
NEAR = 4
NEAR_STEPS = (0, 1, 2, 3)
F32, BF16 = jnp.float32, jnp.bfloat16
NT = (((1,), (1,)), ((), ()))
NN = (((1,), (0,)), ((), ()))


def dot(a, b, dims=NN):
    return lax.dot_general(a, b, dims, preferred_element_type=F32)


def iota(shape, dim):
    return lax.broadcasted_iota(jnp.int32, shape, dim)


def split(x):
    hi = x.astype(BF16)
    return hi, (x - hi.astype(F32)).astype(BF16)


def row(ref, block, size):
    per = size // LANES
    return jnp.concatenate([ref[block * per + k : block * per + k + 1, :] for k in range(per)], axis=1)


def one_hot(ids, slots):
    kind = BF16 if slots <= 256 else F32
    slot = iota((slots, LANES), 0).astype(F32).astype(kind)
    ids = ids.astype(F32).astype(kind)
    one, zero = jnp.ones((slots, LANES), kind), jnp.zeros((slots, LANES), kind)
    parts = [jnp.where(slot == ids[:, k : k + LANES], one, zero) for k in range(0, ids.shape[1], LANES)]
    return jnp.concatenate(parts, axis=1).astype(BF16)


def one_hot_down(columns, slots):
    kind = BF16 if slots <= 256 else F32
    one, zero = jnp.ones((LANES, LANES), kind), jnp.zeros((LANES, LANES), kind)
    along_slots = [(iota((LANES, LANES), 1) + at).astype(F32).astype(kind) for at in range(0, slots, LANES)]
    parts = []
    for k in range(columns.shape[1]):
        ids = jnp.broadcast_to(columns[:, k : k + 1], (LANES, LANES)).astype(kind)
        parts.append(jnp.concatenate([jnp.where(slot == ids, one, zero) for slot in along_slots], axis=1))
    return jnp.concatenate(parts, axis=0).astype(BF16)


def same_worker(pad, width):
    return (iota((width, width), 0) // pad == iota((width, width), 1) // pad).astype(F32).astype(BF16)


def by_worker(x, table):
    rows, width = x.shape
    hi, lo = split(x)
    both = jnp.concatenate([hi, lo], axis=0)
    step = table.shape[0]
    total = jnp.concatenate([dot(both[:, k : k + step], table) for k in range(0, width, step)], axis=1)
    return total[:rows] + total[rows:]


def start_all(copies):
    for copy in copies:
        copy.start()


def wait_all(copies):
    for copy in copies:
        copy.wait()


def column_copies(source, target, sems, size=BLOCK):
    width = source.shape[1]
    cuts = [pl.ds(start, size) for start in range(0, width, size)]
    return [pltpu.make_async_copy(source.at[:, cut], target.at[:, cut], sems.at[b]) for b, cut in enumerate(cuts)]


def row_lengths(lengths, pad):
    total_rows = lengths.shape[0] * pad
    here = iota((total_rows, LANES), 0)
    lane = iota((total_rows, LANES), 1)
    wide = jnp.broadcast_to(lengths.astype(F32)[:, None, :], (lengths.shape[0], pad, LANES)).reshape(total_rows, LANES)
    per = LANES // pad
    wide = jnp.where(lane // per == here % pad, wide, 0.0).astype(BF16)
    spread = (iota((LANES, LANES), 0) % per == iota((LANES, LANES), 1) // pad).astype(F32).astype(BF16)
    row_len = dot(wide, spread)
    return row_len, (lane % pad).astype(F32) < row_len


def along(ref):
    return jnp.concatenate([ref[k : k + 1, :] for k in range(ref.shape[0])], axis=1)


def sums_kernel(pad, cap, *refs):
    (probes, lengths_in, ids_in, firms_in), sends, refs = refs[:4], refs[4 : 4 + NEAR], refs[4 + NEAR :]
    x1, mask_ids, weight, valid, x, sums, lengths, ids, firms, sems, small = refs
    copies = column_copies(probes, x, sems)
    first = [
        pltpu.make_async_copy(source, target, small.at[k])
        for k, (source, target) in enumerate(((lengths_in, lengths), (ids_in, ids), (firms_in, firms)))
    ]
    start_all(first)
    start_all(copies)
    columns, slots = sums.shape
    part = columns // NEAR
    me = lax.axis_index("rows") % NEAR
    wait_all(first)
    row_len, inside = row_lengths(lengths[...], pad)
    valid[...] = jnp.where(inside, 1.0, 0.0)
    weight[...] = jnp.where(inside, 1.0 / row_len, 0.0)
    masked = jnp.where(inside, ids[...], -1)
    mask_ids[...] = masked
    turned = jnp.concatenate([masked.astype(F32)] * (LANES // masked.shape[0]), axis=0).T
    keys = (iota((1, slots), 1) // cap * FIRMS_PER_SHARD + along(firms)).astype(F32)
    across = slots // LANES
    rows = ids.shape[0] // across
    masked = jnp.concatenate([masked[k * rows : (k + 1) * rows] for k in range(across)], axis=1).astype(F32)
    for send in sends[:3]:
        send[part + 8 :] = masked

    table = same_worker(pad, 256)
    total = None
    for b in range(len(copies)):
        if b % 4 == 0:
            wait_all(copies[b : b + 4])
        ok = row(valid, b, BLOCK)
        x0 = x[:, b * BLOCK : (b + 1) * BLOCK] * ok
        rest = x0 - by_worker(x0, table) * row(weight, b, BLOCK)
        x1[:, b * BLOCK : (b + 1) * BLOCK] = rest
        counted = jnp.broadcast_to(ok, (16, BLOCK)).astype(BF16)
        data = jnp.concatenate([*split(rest), counted], axis=0)
        per = BLOCK // LANES
        block = dot(data, one_hot_down(turned[:, b * per : (b + 1) * per], slots))
        total = block if total is None else total + block
    sums[...] = total[:columns] + total[columns : 2 * columns]
    about = jnp.where(iota((8, slots), 0) == 0, keys, total[2 * columns : 2 * columns + 1])
    for step, send in zip(NEAR_STEPS, sends):
        send[:part] = sums[pl.ds(pl.multiple_of((me ^ step) * part, part), part), :]
        send[part : part + 8] = about


def join_kernel(part, *refs):
    parts, out = refs[:NEAR], refs[-1]
    for k, one in enumerate(parts):
        out[part * k : part * (k + 1)] = one[:part]
        out[part * NEAR + 2 * k : part * NEAR + 2 * k + 2] = one[part : part + 2]


def pairs_kernel(pad, start, *refs):
    parts, (out, ids, size, counts) = refs[:-4], refs[-4:]
    slots = out.shape[1]
    kind = BF16 if slots <= 256 else F32
    per = LANES // pad
    total_rows = ids.shape[1]
    across = slots // LANES
    rows = total_rows // across
    for k, part in enumerate(parts):
        size[k] = jnp.broadcast_to(part[start - 7 : start - 6], (8, slots))
        for at in range(across):
            ids[k, at * rows : (at + 1) * rows] = part[start:, at * LANES : (at + 1) * LANES]
    at = iota((LANES, pad * LANES), 1)
    deal = (iota((LANES, pad * LANES), 0) == at % per * pad + at // LANES).astype(F32).astype(BF16)
    mine = iota((total_rows, pad * LANES), 1) % LANES // per == iota((total_rows, pad * LANES), 0) % pad
    slot = iota((slots, LANES), 0).astype(F32).astype(kind)
    one, zero = jnp.ones((slots, LANES), kind), jnp.zeros((slots, LANES), kind)
    diagonal = iota((slots, slots), 1) == iota((slots, slots), 0)

    def device(k, carry):
        dealt = dot(jnp.concatenate(split(ids[k]), axis=0), deal)
        dealt = jnp.where(mine, dealt[:total_rows] + dealt[total_rows:], 0.0)
        dealt = jnp.sum(dealt.reshape(total_rows // pad, pad, pad * LANES), axis=1)
        spells = dealt.astype(kind)
        for g in range(total_rows // pad):
            total = zero
            for j in range(pad):
                total += jnp.where(slot == spells[g : g + 1, j * LANES : (j + 1) * LANES], one, zero)
            counts[k, :, g * LANES : (g + 1) * LANES] = total.astype(BF16)
        valid = jnp.where(dealt >= 0.0, 1.0, 0.0)
        length = valid[:, :LANES]
        for j in range(1, pad):
            length += valid[:, j * LANES : (j + 1) * LANES]
        inverse = 1.0 / length
        inverse = jnp.concatenate([inverse[g : g + 1] for g in range(total_rows // pad)], axis=1)
        here = counts[k]
        total = dot(jnp.concatenate(split(here.astype(F32) * inverse), axis=0), here, NT)
        total = total[:slots] + total[slots:] - jnp.where(diagonal, size[k, :1], 0.0)
        hi, lo = split(total)
        out[k, :, :slots] = hi
        out[k, :, slots:] = lo
        return carry

    lax.fori_loop(0, len(parts), device, 0, unroll=len(parts) if slots <= 256 else 1)


def same_firm(own, one, part, at):
    mine, keys = ([ref[part * NEAR + 2 * k : part * NEAR + 2 * k + 1, at] for k in range(NEAR)] for ref in (own, one))
    mine = jnp.concatenate(mine, axis=1)
    down = jnp.concatenate([jnp.broadcast_to(key, (8, LANES)) for key in keys], axis=0).T
    found = [(down[:, 8 * k : 8 * k + 1] == mine).astype(F32).astype(BF16) for k in range(NEAR)]
    return jnp.concatenate(found, axis=0)


def each_tile(slots, do):
    tiles = slots // LANES
    if tiles <= 2:
        for t in range(tiles):
            do(t, slice(t * LANES, (t + 1) * LANES))
    else:
        lax.fori_loop(0, tiles, lambda t, c: (do(t, pl.ds(pl.multiple_of(t * LANES, LANES), LANES)), c)[1], 0)


def firms_kernel(part, own, one, passed, out, *copy):
    for ref in copy:
        ref[...] = passed[...]
    each_tile(own.shape[1], lambda t, at: out.__setitem__(t, same_firm(own, one, part, at)))


def gathered(parts, part, at):
    data = [one[part * k : part * (k + 1), at] for one in parts for k in range(NEAR)]
    return jnp.concatenate(split(jnp.concatenate(data, axis=1)), axis=0)


def spread_out(means, out, part, at):
    for k in range(NEAR):
        out[part * k : part * (k + 1), at] = means[:, k * LANES : (k + 1) * LANES]


def change_kernel(far, part, ready, *refs):
    tables, pairs, refs = refs[far : far + ready], refs[far + ready : far + ready + NEAR], refs
    parts, (mean, sums, scale), made = refs[:far], refs[far + ready + NEAR :][:3], refs[far + ready + NEAR + 3 :]
    slots = mean.shape[1]

    def tile(t, at):
        if tables:
            between = [same_firm(parts[0], one, part, at) for one in parts[1:-1]]
            for ref, one in zip(made, between):
                ref[t] = one
            same = [tables[0][t], *between, tables[1][t]]
        else:
            same = [same_firm(parts[0], one, part, at) for one in parts]
        same = jnp.concatenate(same, axis=0)
        count = [one[part * NEAR + 2 * k + 1 : part * NEAR + 2 * k + 2, at] for one in parts for k in range(NEAR)]
        count = jnp.concatenate(count, axis=1)
        high = count.astype(BF16).astype(F32)
        counts = jnp.where(iota((16, count.shape[1]), 0) < 8, high, count - high).astype(BF16)
        found = dot(jnp.concatenate([gathered(parts, part, at), counts], axis=0), same)
        size = found[2 * part : 2 * part + 1] + found[2 * part + 8 : 2 * part + 9]
        inverse = 1.0 / jnp.maximum(size, 1.0)
        scale[t] = jnp.broadcast_to(inverse, scale.shape[1:])
        spread_out((found[:part] + found[part : 2 * part]) * inverse, mean, part, at)

    each_tile(slots, tile)
    for k in range(NEAR):
        cut = slice(part * k, part * (k + 1))
        both = jnp.concatenate(split(mean[cut]), axis=0)
        change = dot(both, pairs[k][0])
        change = change[:part] + change[part:]
        sums[cut] = parts[0][cut] + (change[:, :slots] + change[:, slots:])


def tables_kernel(pad, mask_ids, mean, spread, workers, *sends):
    part = mean.shape[0] // NEAR
    for k, send in enumerate(sends):
        send[...] = mean[part * k : part * (k + 1)]
    slots, width = spread.shape
    table = same_worker(pad, 256)
    for b in range(width // BLOCK):
        found = one_hot(row(mask_ids, b, BLOCK), slots)
        spread[:, b * BLOCK : (b + 1) * BLOCK] = found
        for at in range(0, BLOCK, 256):
            count = dot(found[:, at : at + 256], table)
            workers[:, b * BLOCK + at : b * BLOCK + at + 256] = count.astype(BF16)


def means_kernel(far, part, kept, *refs):
    parts, source, scale, sends, mean = refs[:far], refs[far:-7], refs[-7], refs[-5:-1], refs[-1]

    def tile(t, at):
        same = [table[t] if kept else same_firm(source[0], table, part, at) for table in source]
        same = jnp.concatenate(same, axis=0)
        found = dot(gathered(parts, part, at), same)
        spread_out((found[:part] + found[part:]) * scale[t][:1], mean, part, at)

    each_tile(mean.shape[1], tile)
    for k, send in enumerate(sends):
        send[...] = mean[part * k : part * (k + 1)]


def own_means(parts, means):
    me = lax.axis_index("rows") % NEAR
    part = parts[0].shape[0]
    for step, one in zip(NEAR_STEPS, parts):
        means[pl.ds(pl.multiple_of((me ^ step) * part, part), part), :] = one[...]
    return jnp.concatenate(split(means[...]), axis=0)


def first_kernel(pad, *refs):
    parts, (x1, mask_ids, weight), tables, (y, means) = refs[:NEAR], refs[NEAR : NEAR + 3], refs[NEAR + 3 : -2], refs[-2:]
    columns, slots = means.shape
    first = own_means(parts, means)
    table = same_worker(pad, 256)
    for b in range(y.shape[1] // BLOCK):
        at = slice(b * BLOCK, (b + 1) * BLOCK)
        found = tables[0][:, at] if tables else one_hot(row(mask_ids, b, BLOCK), slots)
        spread = dot(first, found)
        spread = spread[:columns] + spread[columns:]
        if tables:
            worker = dot(first, tables[1][:, at])
            worker = worker[:columns] + worker[columns:]
        else:
            worker = by_worker(spread, table)
        y[:, at] = x1[:, at] - spread + worker * row(weight, b, BLOCK)


def last_kernel(*refs):
    parts, (before, mask_ids), tables, (out, means, y, sems) = refs[:NEAR], refs[NEAR : NEAR + 2], refs[NEAR + 2 : -4], refs[-4:]
    outs = column_copies(y, out, sems, 2 * BLOCK)
    columns, slots = means.shape
    second = own_means(parts, means)
    for b in range(2 * len(outs)):
        at = slice(b * BLOCK, (b + 1) * BLOCK)
        found = tables[0][:, at] if tables else one_hot(row(mask_ids, b, BLOCK), slots)
        spread = dot(second, found)
        y[:, at] = before[:, at] - (spread[:columns] + spread[columns:])
        if b % 2:
            outs[b // 2].start()
    wait_all(outs)


def near_exchange(parts, n):
    steps = [[(i, i ^ step) for i in range(n)] for step in NEAR_STEPS[1:]]
    return [parts[0]] + [lax.ppermute(one, "rows", step) for one, step in zip(parts[1:], steps)]


def far_share(one, n):
    steps = [[(i, i ^ (k * NEAR)) for i in range(n)] for k in range(1, n // NEAR)]
    return [one] + [lax.ppermute(one, "rows", step) for step in steps]


def in_hbm(x):
    return pltpu.with_memory_space_constraint(x, pltpu.HBM)


def call(kernel, out_shape, in_specs, out_specs, scratch, flops, moved):
    return pl.pallas_call(
        kernel,
        out_shape=out_shape,
        in_specs=in_specs,
        out_specs=out_specs,
        scratch_shapes=scratch,
        compiler_params=pltpu.CompilerParams(vmem_limit_bytes=VMEM_BYTES),
        cost_estimate=pl.CostEstimate(flops=flops, bytes_accessed=moved, transcendentals=0),
    )


def body(probes, worker_len, spell_to_slot, slot_to_firm, *, n):
    columns, rows_dev = probes.shape
    workers = worker_len.shape[0]
    pad = rows_dev // workers
    slots = slot_to_firm.shape[0]
    tiles = slots // LANES
    part = columns // NEAR
    far = n // NEAR
    keep = tiles * NEAR * n * LANES * LANES * 2 <= 8 * 1024 * 1024
    blocks = rows_dev // BLOCK
    vmem, hbm = pl.BlockSpec(memory_space=pltpu.VMEM), pl.BlockSpec(memory_space=pltpu.HBM)
    lengths = worker_len.reshape(workers // LANES, LANES)
    ids = spell_to_slot.reshape(rows_dev // LANES, LANES)
    firms = slot_to_firm.reshape(tiles, LANES)
    array = jax.ShapeDtypeStruct
    of_rows = (rows_dev // LANES, LANES)
    work = 2 * rows_dev * slots * 2 * columns
    sems = pltpu.SemaphoreType.DMA((blocks,))
    whole = (columns, rows_dev)
    about = part + 8
    message = array((about + rows_dev // slots, slots), F32)
    of_near = array((columns, slots), F32)

    *sends, x1, mask_ids, weight = call(
        functools.partial(sums_kernel, pad, slots // n),
        [message] * 3 + [array((about, slots), F32), array(whole, F32), array(of_rows, jnp.int32), array(of_rows, F32)],
        [hbm] * 4,
        [vmem] * (NEAR + 3),
        [
            pltpu.VMEM(of_rows, F32),
            pltpu.VMEM(whole, F32),
            pltpu.VMEM((columns, slots), F32),
            pltpu.VMEM(lengths.shape, jnp.int32),
            pltpu.VMEM(ids.shape, jnp.int32),
            pltpu.VMEM(firms.shape, jnp.int32),
            sems,
            pltpu.SemaphoreType.DMA((3,)),
        ],
        2 * work,
        4 * columns * rows_dev,
    )(in_hbm(probes), in_hbm(lengths), in_hbm(ids), in_hbm(firms))

    def pair_counts(parts):
        return call(
            functools.partial(pairs_kernel, pad, about),
            array((len(parts), slots, 2 * slots), BF16),
            [vmem] * len(parts),
            vmem,
            [
                pltpu.VMEM((len(parts), *of_rows), F32),
                pltpu.VMEM((len(parts), 8, slots), F32),
                pltpu.VMEM((len(parts), slots, workers), BF16),
            ],
            work * len(parts) // 4,
            4 * slots * slots,
        )(*parts)

    arrived = near_exchange(sends, n)
    pairs = [pair_counts(arrived[:1]), pair_counts(arrived[1:2])]
    joined = call(
        functools.partial(join_kernel, part),
        array((columns + 2 * NEAR, slots), F32),
        [vmem] * (NEAR + 2),
        vmem,
        [],
        0,
        message.size * 8,
    )(*arrived, *pairs)
    shared = far_share(joined, n)
    tables, passed = [], arrived[2]
    table = array((tiles, NEAR * LANES, NEAR * LANES), BF16)

    def firm_table(one, passed, out):
        return call(
            functools.partial(firms_kernel, part),
            out,
            [vmem] * 3,
            [vmem] * len(out),
            [],
            work // 64,
            tiles * (NEAR * LANES) ** 2 * 2,
        )(joined, one, passed)

    if keep:
        first_table, passed = firm_table(joined, passed, [table, message])
        tables = [first_table, *firm_table(shared[-1], first_table, [table])]
    passed = lax.ppermute(passed, "rows", [(i, i ^ 1) for i in range(n)])
    pairs += [pair_counts(arrived[2:3]), pair_counts([passed])]
    scale = array((tiles, 8, NEAR * LANES), F32)
    made = [table] * (far - 2) * keep
    mean, sums, scales, *made = call(
        functools.partial(change_kernel, far, part, len(tables)),
        [of_near, of_near, scale, *made],
        [vmem] * (far + len(tables) + len(pairs)),
        [vmem] * (3 + len(made)),
        [],
        work // 4,
        slots * slots * 4,
    )(*shared, *tables, *pairs)
    again = far_share(sums, n)
    source = [tables[0], *made, tables[1]] if keep else shared
    spreads = []
    sends = [mean[part * k : part * (k + 1)] for k in range(NEAR)]
    if keep:
        *spreads, a, b, c, d = call(
            functools.partial(tables_kernel, pad),
            [array((slots, rows_dev), BF16)] * 2 + [array((part, slots), F32)] * NEAR,
            [vmem] * 2,
            [vmem] * (2 + NEAR),
            [],
            work,
            4 * slots * rows_dev,
        )(mask_ids, mean)
        sends = [a, b, c, d]
    first = near_exchange(sends, n)
    sends = call(
        functools.partial(means_kernel, far, part, keep),
        [array((part, slots), F32)] * NEAR,
        [vmem] * (far + len(source) + 2),
        [vmem] * NEAR,
        [pltpu.VMEM((columns, slots), F32)],
        work // 4,
        slots * slots * 4,
    )(*again, *source, scales, spreads[1] if keep else scales)
    arrived = near_exchange(sends, n)
    before = call(
        functools.partial(first_kernel, pad),
        array(whole, F32),
        [vmem] * (NEAR + 3 + len(spreads)),
        vmem,
        [pltpu.VMEM((columns, slots), F32)],
        work,
        8 * columns * rows_dev,
    )(*first, x1, mask_ids, weight, *spreads)
    return call(
        last_kernel,
        array(whole, F32),
        [vmem] * (NEAR + 2 + len(spreads[:1])),
        hbm,
        [pltpu.VMEM((columns, slots), F32), pltpu.VMEM(whole, F32), sems],
        work,
        8 * columns * rows_dev,
    )(*arrived, before, mask_ids, *spreads[:1])


def solution(mesh):
    placed = (P(None, ("grp", "rows")), P(("grp", "rows")), P(("grp", "rows")), P(("grp", "rows")))
    return jax.shard_map(
        functools.partial(body, n=mesh.shape["rows"]),
        mesh=mesh,
        in_specs=placed,
        out_specs=P(None, ("grp", "rows")),
        check_vma=False,
    )
```

```python
import functools

import jax
import jax.numpy as jnp
from jax import lax
from jax.experimental import pallas as pl
from jax.experimental.pallas import tpu as pltpu
from jax.sharding import PartitionSpec as P

FIRMS_PER_SHARD = 1024
LANES = 128
BLOCK = 1024
VMEM_BYTES = 32 * 1024 * 1024
NEAR = 4
NEAR_STEPS = (0, 1, 2, 3)
F32, BF16 = jnp.float32, jnp.bfloat16
NT = (((1,), (1,)), ((), ()))
NN = (((1,), (0,)), ((), ()))


def dot(a, b, dims=NN):
    return lax.dot_general(a, b, dims, preferred_element_type=F32)


def iota(shape, dim):
    return lax.broadcasted_iota(jnp.int32, shape, dim)


def split(x):
    hi = x.astype(BF16)
    return hi, (x - hi.astype(F32)).astype(BF16)


def row(ref, block, size):
    per = size // LANES
    return jnp.concatenate([ref[block * per + k : block * per + k + 1, :] for k in range(per)], axis=1)


def one_hot(ids, slots):
    kind = BF16 if slots <= 256 else F32
    slot = iota((slots, LANES), 0).astype(F32).astype(kind)
    ids = ids.astype(F32).astype(kind)
    one, zero = jnp.ones((slots, LANES), kind), jnp.zeros((slots, LANES), kind)
    parts = [jnp.where(slot == ids[:, k : k + LANES], one, zero) for k in range(0, ids.shape[1], LANES)]
    return jnp.concatenate(parts, axis=1).astype(BF16)


def one_hot_down(columns, slots):
    kind = BF16 if slots <= 256 else F32
    one, zero = jnp.ones((LANES, LANES), kind), jnp.zeros((LANES, LANES), kind)
    along_slots = [(iota((LANES, LANES), 1) + at).astype(F32).astype(kind) for at in range(0, slots, LANES)]
    parts = []
    for k in range(columns.shape[1]):
        ids = jnp.broadcast_to(columns[:, k : k + 1], (LANES, LANES)).astype(kind)
        parts.append(jnp.concatenate([jnp.where(slot == ids, one, zero) for slot in along_slots], axis=1))
    return jnp.concatenate(parts, axis=0).astype(BF16)


def same_worker(pad, width):
    return (iota((width, width), 0) // pad == iota((width, width), 1) // pad).astype(F32).astype(BF16)


def by_worker(x, table):
    rows, width = x.shape
    step = table.shape[1]
    both = [
        jnp.concatenate([one[:, k : k + step] for k in range(0, width, step)], axis=0) for one in split(x)
    ]
    total = dot(jnp.concatenate(both, axis=1), table)
    return jnp.concatenate([total[k : k + rows] for k in range(0, total.shape[0], rows)], axis=1)


def start_all(copies):
    for copy in copies:
        copy.start()


def wait_all(copies):
    for copy in copies:
        copy.wait()


def column_copies(source, target, sems, size=BLOCK):
    width = source.shape[1]
    cuts = [pl.ds(start, size) for start in range(0, width, size)]
    return [pltpu.make_async_copy(source.at[:, cut], target.at[:, cut], sems.at[b]) for b, cut in enumerate(cuts)]


def row_lengths(lengths, pad):
    total_rows = lengths.shape[0] * pad
    here = iota((total_rows, LANES), 0)
    lane = iota((total_rows, LANES), 1)
    wide = jnp.broadcast_to(lengths.astype(F32)[:, None, :], (lengths.shape[0], pad, LANES)).reshape(total_rows, LANES)
    per = LANES // pad
    wide = jnp.where(lane // per == here % pad, wide, 0.0).astype(BF16)
    spread = (iota((LANES, LANES), 0) % per == iota((LANES, LANES), 1) // pad).astype(F32).astype(BF16)
    row_len = dot(wide, spread)
    return row_len, (lane % pad).astype(F32) < row_len


def along(ref):
    return jnp.concatenate([ref[k : k + 1, :] for k in range(ref.shape[0])], axis=1)


def sums_kernel(pad, cap, *refs):
    (probes, lengths_in, ids_in, firms_in), sends, refs = refs[:4], refs[4 : 4 + NEAR], refs[4 + NEAR :]
    x1, mask_ids, weight, valid, x, sums, lengths, ids, firms, sems, small = refs
    copies = column_copies(probes, x, sems)
    first = [
        pltpu.make_async_copy(source, target, small.at[k])
        for k, (source, target) in enumerate(((lengths_in, lengths), (ids_in, ids), (firms_in, firms)))
    ]
    start_all(first)
    start_all(copies)
    columns, slots = sums.shape
    part = columns // NEAR
    me = lax.axis_index("rows") % NEAR
    wait_all(first)
    row_len, inside = row_lengths(lengths[...], pad)
    valid[...] = jnp.where(inside, 1.0, 0.0)
    weight[...] = jnp.where(inside, 1.0 / row_len, 0.0)
    masked = jnp.where(inside, ids[...], -1)
    mask_ids[...] = masked
    turned = jnp.concatenate([masked.astype(F32)] * (LANES // masked.shape[0]), axis=0).T
    keys = (iota((1, slots), 1) // cap * FIRMS_PER_SHARD + along(firms)).astype(F32)
    across = slots // LANES
    rows = ids.shape[0] // across
    masked = jnp.concatenate([masked[k * rows : (k + 1) * rows] for k in range(across)], axis=1).astype(F32)
    for send in sends[:3]:
        send[part + 8 :] = masked

    table = jnp.concatenate([same_worker(pad, 256)] * 2, axis=0)
    wait_all(copies)
    total = None
    for b in range(len(copies)):
        ok = row(valid, b, BLOCK)
        x0 = x[:, b * BLOCK : (b + 1) * BLOCK] * ok
        rest = x0 - by_worker(x0, table) * row(weight, b, BLOCK)
        x1[:, b * BLOCK : (b + 1) * BLOCK] = rest
        counted = jnp.broadcast_to(ok, (16, BLOCK)).astype(BF16)
        data = jnp.concatenate([*split(rest), counted], axis=0)
        per = BLOCK // LANES
        block = dot(data, one_hot_down(turned[:, b * per : (b + 1) * per], slots))
        total = block if total is None else total + block
    sums[...] = total[:columns] + total[columns : 2 * columns]
    about = jnp.where(iota((8, slots), 0) == 0, keys, total[2 * columns : 2 * columns + 1])
    for step, send in zip(NEAR_STEPS, sends):
        send[:part] = sums[pl.ds(pl.multiple_of((me ^ step) * part, part), part), :]
        send[part : part + 8] = about


def join_kernel(part, *refs):
    parts, out = refs[:NEAR], refs[-1]
    for k, one in enumerate(parts):
        out[part * k : part * (k + 1)] = one[:part]
        out[part * NEAR + 2 * k : part * NEAR + 2 * k + 2] = one[part : part + 2]


def pairs_kernel(pad, start, *refs):
    parts, (out, ids, size, counts) = refs[:-4], refs[-4:]
    slots = out.shape[1]
    kind = BF16 if slots <= 256 else F32
    per = LANES // pad
    total_rows = ids.shape[1]
    across = slots // LANES
    rows = total_rows // across
    for k, part in enumerate(parts):
        size[k] = jnp.broadcast_to(part[start - 7 : start - 6], (8, slots))
        for at in range(across):
            ids[k, at * rows : (at + 1) * rows] = part[start:, at * LANES : (at + 1) * LANES]
    at = iota((LANES, pad * LANES), 1)
    deal = (iota((LANES, pad * LANES), 0) == at % per * pad + at // LANES).astype(F32).astype(BF16)
    mine = iota((total_rows, pad * LANES), 1) % LANES // per == iota((total_rows, pad * LANES), 0) % pad
    slot = iota((slots, LANES), 0).astype(F32).astype(kind)
    one, zero = jnp.ones((slots, LANES), kind), jnp.zeros((slots, LANES), kind)
    diagonal = iota((slots, slots), 1) == iota((slots, slots), 0)

    def device(k, carry):
        dealt = dot(jnp.concatenate(split(ids[k]), axis=0), deal)
        dealt = jnp.where(mine, dealt[:total_rows] + dealt[total_rows:], 0.0)
        dealt = jnp.sum(dealt.reshape(total_rows // pad, pad, pad * LANES), axis=1)
        spells = dealt.astype(kind)
        for g in range(total_rows // pad):
            total = zero
            for j in range(pad):
                total += jnp.where(slot == spells[g : g + 1, j * LANES : (j + 1) * LANES], one, zero)
            counts[k, :, g * LANES : (g + 1) * LANES] = total.astype(BF16)
        valid = jnp.where(dealt >= 0.0, 1.0, 0.0)
        length = valid[:, :LANES]
        for j in range(1, pad):
            length += valid[:, j * LANES : (j + 1) * LANES]
        inverse = 1.0 / length
        inverse = jnp.concatenate([inverse[g : g + 1] for g in range(total_rows // pad)], axis=1)
        here = counts[k]
        total = dot(jnp.concatenate(split(here.astype(F32) * inverse), axis=0), here, NT)
        total = total[:slots] + total[slots:] - jnp.where(diagonal, size[k, :1], 0.0)
        hi, lo = split(total)
        out[k, :, :slots] = hi
        out[k, :, slots:] = lo
        return carry

    lax.fori_loop(0, len(parts), device, 0, unroll=len(parts) if slots <= 256 else 1)


def same_firm(own, one, part, at):
    mine, keys = ([ref[part * NEAR + 2 * k : part * NEAR + 2 * k + 1, at] for k in range(NEAR)] for ref in (own, one))
    mine = jnp.concatenate(mine, axis=1)
    down = jnp.concatenate([jnp.broadcast_to(key, (8, LANES)) for key in keys], axis=0).T
    found = [(down[:, 8 * k : 8 * k + 1] == mine).astype(F32).astype(BF16) for k in range(NEAR)]
    return jnp.concatenate(found, axis=0)


def each_tile(slots, do):
    tiles = slots // LANES
    if tiles <= 2:
        for t in range(tiles):
            do(t, slice(t * LANES, (t + 1) * LANES))
    else:
        lax.fori_loop(0, tiles, lambda t, c: (do(t, pl.ds(pl.multiple_of(t * LANES, LANES), LANES)), c)[1], 0)


def firms_kernel(part, own, one, passed, out, *copy):
    for ref in copy:
        ref[...] = passed[...]
    each_tile(own.shape[1], lambda t, at: out.__setitem__(t, same_firm(own, one, part, at)))


def gathered(parts, part, at):
    data = [one[part * k : part * (k + 1), at] for one in parts for k in range(NEAR)]
    return jnp.concatenate(split(jnp.concatenate(data, axis=1)), axis=0)


def spread_out(means, out, part, at):
    for k in range(NEAR):
        out[part * k : part * (k + 1), at] = means[:, k * LANES : (k + 1) * LANES]


def change_kernel(far, part, ready, *refs):
    tables, pairs, refs = refs[far : far + ready], refs[far + ready : far + ready + NEAR], refs
    parts, (mean, sums, scale), made = refs[:far], refs[far + ready + NEAR :][:3], refs[far + ready + NEAR + 3 :]
    slots = mean.shape[1]

    def tile(t, at):
        if tables:
            between = [same_firm(parts[0], one, part, at) for one in parts[1:-1]]
            for ref, one in zip(made, between):
                ref[t] = one
            same = [tables[0][t], *between, tables[1][t]]
        else:
            same = [same_firm(parts[0], one, part, at) for one in parts]
        same = jnp.concatenate(same, axis=0)
        count = [one[part * NEAR + 2 * k + 1 : part * NEAR + 2 * k + 2, at] for one in parts for k in range(NEAR)]
        count = jnp.concatenate(count, axis=1)
        high = count.astype(BF16).astype(F32)
        counts = jnp.where(iota((16, count.shape[1]), 0) < 8, high, count - high).astype(BF16)
        found = dot(jnp.concatenate([gathered(parts, part, at), counts], axis=0), same)
        size = found[2 * part : 2 * part + 1] + found[2 * part + 8 : 2 * part + 9]
        inverse = 1.0 / jnp.maximum(size, 1.0)
        scale[t] = jnp.broadcast_to(inverse, scale.shape[1:])
        spread_out((found[:part] + found[part : 2 * part]) * inverse, mean, part, at)

    each_tile(slots, tile)
    for k in range(NEAR):
        cut = slice(part * k, part * (k + 1))
        both = jnp.concatenate(split(mean[cut]), axis=0)
        change = dot(both, pairs[k][0])
        change = change[:part] + change[part:]
        sums[cut] = parts[0][cut] + (change[:, :slots] + change[:, slots:])


def tables_kernel(pad, mask_ids, mean, spread, workers, *sends):
    part = mean.shape[0] // NEAR
    for k, send in enumerate(sends):
        send[...] = mean[part * k : part * (k + 1)]
    slots, width = spread.shape
    table = jnp.concatenate([same_worker(pad, 256)] * 2, axis=0)
    for b in range(width // BLOCK):
        found = one_hot(row(mask_ids, b, BLOCK), slots)
        spread[:, b * BLOCK : (b + 1) * BLOCK] = found
        for at in range(0, BLOCK, 256):
            count = dot(found[:, at : at + 256], table[:256])
            workers[:, b * BLOCK + at : b * BLOCK + at + 256] = count.astype(BF16)


def means_kernel(far, part, kept, *refs):
    parts, source, scale, sends, mean = refs[:far], refs[far:-7], refs[-7], refs[-5:-1], refs[-1]

    def tile(t, at):
        same = [table[t] if kept else same_firm(source[0], table, part, at) for table in source]
        same = jnp.concatenate(same, axis=0)
        found = dot(gathered(parts, part, at), same)
        spread_out((found[:part] + found[part:]) * scale[t][:1], mean, part, at)

    each_tile(mean.shape[1], tile)
    for k, send in enumerate(sends):
        send[...] = mean[part * k : part * (k + 1)]


def own_means(parts, means):
    me = lax.axis_index("rows") % NEAR
    part = parts[0].shape[0]
    for step, one in zip(NEAR_STEPS, parts):
        means[pl.ds(pl.multiple_of((me ^ step) * part, part), part), :] = one[...]
    return jnp.concatenate(split(means[...]), axis=0)


def first_kernel(pad, *refs):
    parts, (x1, mask_ids, weight), tables, (y, means) = refs[:NEAR], refs[NEAR : NEAR + 3], refs[NEAR + 3 : -2], refs[-2:]
    columns, slots = means.shape
    first = own_means(parts, means)
    table = jnp.concatenate([same_worker(pad, 256)] * 2, axis=0)
    for b in range(y.shape[1] // BLOCK):
        at = slice(b * BLOCK, (b + 1) * BLOCK)
        found = tables[0][:, at] if tables else one_hot(row(mask_ids, b, BLOCK), slots)
        spread = dot(first, found)
        spread = spread[:columns] + spread[columns:]
        if tables:
            worker = dot(first, tables[1][:, at])
            worker = worker[:columns] + worker[columns:]
        else:
            worker = by_worker(spread, table)
        y[:, at] = x1[:, at] - spread + worker * row(weight, b, BLOCK)


def last_kernel(*refs):
    parts, (before, mask_ids), tables, (out, means, y, sems) = refs[:NEAR], refs[NEAR : NEAR + 2], refs[NEAR + 2 : -4], refs[-4:]
    outs = column_copies(y, out, sems, 2 * BLOCK)
    columns, slots = means.shape
    second = own_means(parts, means)
    for b in range(2 * len(outs)):
        at = slice(b * BLOCK, (b + 1) * BLOCK)
        found = tables[0][:, at] if tables else one_hot(row(mask_ids, b, BLOCK), slots)
        spread = dot(second, found)
        y[:, at] = before[:, at] - (spread[:columns] + spread[columns:])
        if b % 2:
            outs[b // 2].start()
    wait_all(outs)


def near_exchange(parts, n):
    steps = [[(i, i ^ step) for i in range(n)] for step in NEAR_STEPS[1:]]
    return [parts[0]] + [lax.ppermute(one, "rows", step) for one, step in zip(parts[1:], steps)]


def far_share(one, n):
    steps = [[(i, i ^ (k * NEAR)) for i in range(n)] for k in range(1, n // NEAR)]
    return [one] + [lax.ppermute(one, "rows", step) for step in steps]


def in_hbm(x):
    return pltpu.with_memory_space_constraint(x, pltpu.HBM)


def call(kernel, out_shape, in_specs, out_specs, scratch, flops, moved):
    return pl.pallas_call(
        kernel,
        out_shape=out_shape,
        in_specs=in_specs,
        out_specs=out_specs,
        scratch_shapes=scratch,
        compiler_params=pltpu.CompilerParams(vmem_limit_bytes=VMEM_BYTES),
        cost_estimate=pl.CostEstimate(flops=flops, bytes_accessed=moved, transcendentals=0),
    )


def body(probes, worker_len, spell_to_slot, slot_to_firm, *, n):
    columns, rows_dev = probes.shape
    workers = worker_len.shape[0]
    pad = rows_dev // workers
    slots = slot_to_firm.shape[0]
    tiles = slots // LANES
    part = columns // NEAR
    far = n // NEAR
    keep = tiles * NEAR * n * LANES * LANES * 2 <= 8 * 1024 * 1024
    blocks = rows_dev // BLOCK
    vmem, hbm = pl.BlockSpec(memory_space=pltpu.VMEM), pl.BlockSpec(memory_space=pltpu.HBM)
    lengths = worker_len.reshape(workers // LANES, LANES)
    ids = spell_to_slot.reshape(rows_dev // LANES, LANES)
    firms = slot_to_firm.reshape(tiles, LANES)
    array = jax.ShapeDtypeStruct
    of_rows = (rows_dev // LANES, LANES)
    work = 2 * rows_dev * slots * 2 * columns
    sems = pltpu.SemaphoreType.DMA((blocks,))
    whole = (columns, rows_dev)
    about = part + 8
    message = array((about + rows_dev // slots, slots), F32)
    of_near = array((columns, slots), F32)

    *sends, x1, mask_ids, weight = call(
        functools.partial(sums_kernel, pad, slots // n),
        [message] * 3 + [array((about, slots), F32), array(whole, F32), array(of_rows, jnp.int32), array(of_rows, F32)],
        [hbm] * 4,
        [vmem] * (NEAR + 3),
        [
            pltpu.VMEM(of_rows, F32),
            pltpu.VMEM(whole, F32),
            pltpu.VMEM((columns, slots), F32),
            pltpu.VMEM(lengths.shape, jnp.int32),
            pltpu.VMEM(ids.shape, jnp.int32),
            pltpu.VMEM(firms.shape, jnp.int32),
            sems,
            pltpu.SemaphoreType.DMA((3,)),
        ],
        2 * work,
        4 * columns * rows_dev,
    )(in_hbm(probes), in_hbm(lengths), in_hbm(ids), in_hbm(firms))

    def pair_counts(parts):
        return call(
            functools.partial(pairs_kernel, pad, about),
            array((len(parts), slots, 2 * slots), BF16),
            [vmem] * len(parts),
            vmem,
            [
                pltpu.VMEM((len(parts), *of_rows), F32),
                pltpu.VMEM((len(parts), 8, slots), F32),
                pltpu.VMEM((len(parts), slots, workers), BF16),
            ],
            work * len(parts) // 4,
            4 * slots * slots,
        )(*parts)

    arrived = near_exchange(sends, n)
    pairs = [pair_counts(arrived[:1]), pair_counts(arrived[1:2])]
    joined = call(
        functools.partial(join_kernel, part),
        array((columns + 2 * NEAR, slots), F32),
        [vmem] * (NEAR + 2),
        vmem,
        [],
        0,
        message.size * 8,
    )(*arrived, *pairs)
    shared = far_share(joined, n)
    tables, passed = [], arrived[2]
    table = array((tiles, NEAR * LANES, NEAR * LANES), BF16)

    def firm_table(one, passed, out):
        return call(
            functools.partial(firms_kernel, part),
            out,
            [vmem] * 3,
            [vmem] * len(out),
            [],
            work // 64,
            tiles * (NEAR * LANES) ** 2 * 2,
        )(joined, one, passed)

    if keep:
        first_table, passed = firm_table(joined, passed, [table, message])
        tables = [first_table, *firm_table(shared[-1], first_table, [table])]
    passed = lax.ppermute(passed, "rows", [(i, i ^ 1) for i in range(n)])
    pairs += [pair_counts(arrived[2:3]), pair_counts([passed])]
    scale = array((tiles, 8, NEAR * LANES), F32)
    made = [table] * (far - 2) * keep
    mean, sums, scales, *made = call(
        functools.partial(change_kernel, far, part, len(tables)),
        [of_near, of_near, scale, *made],
        [vmem] * (far + len(tables) + len(pairs)),
        [vmem] * (3 + len(made)),
        [],
        work // 4,
        slots * slots * 4,
    )(*shared, *tables, *pairs)
    again = far_share(sums, n)
    source = [tables[0], *made, tables[1]] if keep else shared
    spreads = []
    sends = [mean[part * k : part * (k + 1)] for k in range(NEAR)]
    if keep:
        *spreads, a, b, c, d = call(
            functools.partial(tables_kernel, pad),
            [array((slots, rows_dev), BF16)] * 2 + [array((part, slots), F32)] * NEAR,
            [vmem] * 2,
            [vmem] * (2 + NEAR),
            [],
            work,
            4 * slots * rows_dev,
        )(mask_ids, mean)
        sends = [a, b, c, d]
    first = near_exchange(sends, n)
    sends = call(
        functools.partial(means_kernel, far, part, keep),
        [array((part, slots), F32)] * NEAR,
        [vmem] * (far + len(source) + 2),
        [vmem] * NEAR,
        [pltpu.VMEM((columns, slots), F32)],
        work // 4,
        slots * slots * 4,
    )(*again, *source, scales, spreads[1] if keep else scales)
    arrived = near_exchange(sends, n)
    before = call(
        functools.partial(first_kernel, pad),
        array(whole, F32),
        [vmem] * (NEAR + 3 + len(spreads)),
        vmem,
        [pltpu.VMEM((columns, slots), F32)],
        work,
        8 * columns * rows_dev,
    )(*first, x1, mask_ids, weight, *spreads)
    return call(
        last_kernel,
        array(whole, F32),
        [vmem] * (NEAR + 2 + len(spreads[:1])),
        hbm,
        [pltpu.VMEM((columns, slots), F32), pltpu.VMEM(whole, F32), sems],
        work,
        8 * columns * rows_dev,
    )(*arrived, before, mask_ids, *spreads[:1])


def solution(mesh):
    placed = (P(None, ("grp", "rows")), P(("grp", "rows")), P(("grp", "rows")), P(("grp", "rows")))
    return jax.shard_map(
        functools.partial(body, n=mesh.shape["rows"]),
        mesh=mesh,
        in_specs=placed,
        out_specs=P(None, ("grp", "rows")),
        check_vma=False,
    )
```

```python
import functools

import jax
import jax.numpy as jnp
from jax import lax
from jax.experimental import pallas as pl
from jax.experimental.pallas import tpu as pltpu
from jax.sharding import PartitionSpec as P

FIRMS_PER_SHARD = 1024
LANES = 128
BLOCK = 1024
VMEM_BYTES = 32 * 1024 * 1024
NEAR = 4
NEAR_STEPS = (0, 1, 2, 3)
F32, BF16 = jnp.float32, jnp.bfloat16
NT = (((1,), (1,)), ((), ()))
NN = (((1,), (0,)), ((), ()))


def dot(a, b, dims=NN):
    return lax.dot_general(a, b, dims, preferred_element_type=F32)


def iota(shape, dim):
    return lax.broadcasted_iota(jnp.int32, shape, dim)


def split(x):
    hi = x.astype(BF16)
    return hi, (x - hi.astype(F32)).astype(BF16)


def row(ref, block, size):
    per = size // LANES
    return jnp.concatenate([ref[block * per + k : block * per + k + 1, :] for k in range(per)], axis=1)


def one_hot(ids, slots):
    kind = BF16 if slots <= 256 else F32
    slot = iota((slots, LANES), 0).astype(F32).astype(kind)
    ids = ids.astype(F32).astype(kind)
    one, zero = jnp.ones((slots, LANES), kind), jnp.zeros((slots, LANES), kind)
    parts = [jnp.where(slot == ids[:, k : k + LANES], one, zero) for k in range(0, ids.shape[1], LANES)]
    return jnp.concatenate(parts, axis=1).astype(BF16)


def one_hot_down(columns, slots):
    kind = BF16 if slots <= 256 else F32
    one, zero = jnp.ones((LANES, LANES), kind), jnp.zeros((LANES, LANES), kind)
    along_slots = [(iota((LANES, LANES), 1) + at).astype(F32).astype(kind) for at in range(0, slots, LANES)]
    parts, columns = [], columns.astype(kind)
    for k in range(columns.shape[1]):
        ids = jnp.broadcast_to(columns[:, k : k + 1], (LANES, LANES))
        parts.append(jnp.concatenate([jnp.where(slot == ids, one, zero) for slot in along_slots], axis=1))
    return jnp.concatenate(parts, axis=0).astype(BF16)


def same_worker(pad, width):
    return (iota((width, width), 0) // pad == iota((width, width), 1) // pad).astype(F32).astype(BF16)


def by_worker(x, table):
    rows, width = x.shape
    step = table.shape[1]
    both = [
        jnp.concatenate([one[:, k : k + step] for k in range(0, width, step)], axis=0) for one in split(x)
    ]
    total = dot(jnp.concatenate(both, axis=1), table)
    return jnp.concatenate([total[k : k + rows] for k in range(0, total.shape[0], rows)], axis=1)


def start_all(copies):
    for copy in copies:
        copy.start()


def wait_all(copies):
    for copy in copies:
        copy.wait()


def column_copies(source, target, sems, size=BLOCK):
    width = source.shape[1]
    cuts = [pl.ds(start, size) for start in range(0, width, size)]
    return [pltpu.make_async_copy(source.at[:, cut], target.at[:, cut], sems.at[b]) for b, cut in enumerate(cuts)]


def row_lengths(lengths, pad):
    total_rows = lengths.shape[0] * pad
    here = iota((total_rows, LANES), 0)
    lane = iota((total_rows, LANES), 1)
    wide = jnp.broadcast_to(lengths.astype(F32)[:, None, :], (lengths.shape[0], pad, LANES)).reshape(total_rows, LANES)
    per = LANES // pad
    wide = jnp.where(lane // per == here % pad, wide, 0.0).astype(BF16)
    spread = (iota((LANES, LANES), 0) % per == iota((LANES, LANES), 1) // pad).astype(F32).astype(BF16)
    row_len = dot(wide, spread)
    return row_len, (lane % pad).astype(F32) < row_len


def along(ref):
    return jnp.concatenate([ref[k : k + 1, :] for k in range(ref.shape[0])], axis=1)


def sums_kernel(pad, cap, *refs):
    (probes, lengths_in, ids_in, firms_in), sends, refs = refs[:4], refs[4 : 4 + NEAR], refs[4 + NEAR :]
    x1, mask_ids, weight, valid, x, sums, lengths, ids, firms, sems, small = refs
    copies = column_copies(probes, x, sems)
    first = [
        pltpu.make_async_copy(source, target, small.at[k])
        for k, (source, target) in enumerate(((lengths_in, lengths), (ids_in, ids), (firms_in, firms)))
    ]
    start_all(first)
    start_all(copies)
    columns, slots = sums.shape
    part = columns // NEAR
    me = lax.axis_index("rows") % NEAR
    wait_all(first)
    row_len, inside = row_lengths(lengths[...], pad)
    valid[...] = jnp.where(inside, 1.0, 0.0)
    weight[...] = jnp.where(inside, 1.0 / row_len, 0.0)
    masked = jnp.where(inside, ids[...], -1)
    mask_ids[...] = masked
    turned = jnp.concatenate([masked.astype(F32)] * (LANES // masked.shape[0]), axis=0).T
    keys = (iota((1, slots), 1) // cap * FIRMS_PER_SHARD + along(firms)).astype(F32)
    across = slots // LANES
    rows = ids.shape[0] // across
    masked = jnp.concatenate([masked[k * rows : (k + 1) * rows] for k in range(across)], axis=1).astype(F32)
    for send in sends[:3]:
        send[part + 8 :] = masked

    table = jnp.concatenate([same_worker(pad, 256)] * 2, axis=0)
    wait_all(copies)
    total = None
    for b in range(len(copies)):
        ok = row(valid, b, BLOCK)
        x0 = x[:, b * BLOCK : (b + 1) * BLOCK] * ok
        rest = x0 - by_worker(x0, table) * row(weight, b, BLOCK)
        x1[:, b * BLOCK : (b + 1) * BLOCK] = rest
        counted = jnp.broadcast_to(ok, (16, BLOCK)).astype(BF16)
        data = jnp.concatenate([*split(rest), counted], axis=0)
        per = BLOCK // LANES
        block = dot(data, one_hot_down(turned[:, b * per : (b + 1) * per], slots))
        total = block if total is None else total + block
    sums[...] = total[:columns] + total[columns : 2 * columns]
    about = jnp.where(iota((8, slots), 0) == 0, keys, total[2 * columns : 2 * columns + 1])
    for step, send in zip(NEAR_STEPS, sends):
        send[:part] = sums[pl.ds(pl.multiple_of((me ^ step) * part, part), part), :]
        send[part : part + 8] = about


def join_kernel(part, *refs):
    parts, out = refs[:NEAR], refs[-1]
    for k, one in enumerate(parts):
        out[part * k : part * (k + 1)] = one[:part]
        out[part * NEAR + 2 * k : part * NEAR + 2 * k + 2] = one[part : part + 2]


def pairs_kernel(pad, start, *refs):
    parts, (out, ids, size, counts) = refs[:-4], refs[-4:]
    slots = out.shape[1]
    kind = BF16 if slots <= 256 else F32
    per = LANES // pad
    total_rows = ids.shape[1]
    across = slots // LANES
    rows = total_rows // across
    for k, part in enumerate(parts):
        size[k] = jnp.broadcast_to(part[start - 7 : start - 6], (8, slots))
        for at in range(across):
            ids[k, at * rows : (at + 1) * rows] = part[start:, at * LANES : (at + 1) * LANES]
    at = iota((LANES, pad * LANES), 1)
    deal = (iota((LANES, pad * LANES), 0) == at % per * pad + at // LANES).astype(F32).astype(BF16)
    mine = iota((total_rows, pad * LANES), 1) % LANES // per == iota((total_rows, pad * LANES), 0) % pad
    slot = iota((slots, LANES), 0).astype(F32).astype(kind)
    one, zero = jnp.ones((slots, LANES), kind), jnp.zeros((slots, LANES), kind)
    diagonal = iota((slots, slots), 1) == iota((slots, slots), 0)

    def device(k, carry):
        dealt = dot(jnp.concatenate(split(ids[k]), axis=0), deal)
        dealt = jnp.where(mine, dealt[:total_rows] + dealt[total_rows:], 0.0)
        dealt = jnp.sum(dealt.reshape(total_rows // pad, pad, pad * LANES), axis=1)
        spells = dealt.astype(kind)
        for g in range(total_rows // pad):
            total = zero
            for j in range(pad):
                total += jnp.where(slot == spells[g : g + 1, j * LANES : (j + 1) * LANES], one, zero)
            counts[k, :, g * LANES : (g + 1) * LANES] = total.astype(BF16)
        valid = jnp.where(dealt >= 0.0, 1.0, 0.0)
        length = valid[:, :LANES]
        for j in range(1, pad):
            length += valid[:, j * LANES : (j + 1) * LANES]
        inverse = 1.0 / length
        inverse = jnp.concatenate([inverse[g : g + 1] for g in range(total_rows // pad)], axis=1)
        here = counts[k]
        total = dot(jnp.concatenate(split(here.astype(F32) * inverse), axis=0), here, NT)
        total = total[:slots] + total[slots:] - jnp.where(diagonal, size[k, :1], 0.0)
        hi, lo = split(total)
        out[k, :, :slots] = hi
        out[k, :, slots:] = lo
        return carry

    lax.fori_loop(0, len(parts), device, 0, unroll=len(parts) if slots <= 256 else 1)


def same_firm(own, one, part, at):
    mine, keys = ([ref[part * NEAR + 2 * k : part * NEAR + 2 * k + 1, at] for k in range(NEAR)] for ref in (own, one))
    mine = jnp.concatenate(mine, axis=1)
    down = jnp.concatenate([jnp.broadcast_to(key, (8, LANES)) for key in keys], axis=0).T
    found = [(down[:, 8 * k : 8 * k + 1] == mine).astype(F32).astype(BF16) for k in range(NEAR)]
    return jnp.concatenate(found, axis=0)


def each_tile(slots, do):
    tiles = slots // LANES
    if tiles <= 2:
        for t in range(tiles):
            do(t, slice(t * LANES, (t + 1) * LANES))
    else:
        lax.fori_loop(0, tiles, lambda t, c: (do(t, pl.ds(pl.multiple_of(t * LANES, LANES), LANES)), c)[1], 0)


def firms_kernel(part, own, one, passed, out, *copy):
    for ref in copy:
        ref[...] = passed[...]
    each_tile(own.shape[1], lambda t, at: out.__setitem__(t, same_firm(own, one, part, at)))


def gathered(parts, part, at):
    data = [one[part * k : part * (k + 1), at] for one in parts for k in range(NEAR)]
    return jnp.concatenate(split(jnp.concatenate(data, axis=1)), axis=0)


def spread_out(means, out, part, at):
    for k in range(NEAR):
        out[part * k : part * (k + 1), at] = means[:, k * LANES : (k + 1) * LANES]


def change_kernel(far, part, ready, *refs):
    tables, pairs, refs = refs[far : far + ready], refs[far + ready : far + ready + NEAR], refs
    parts, (mean, sums, scale), made = refs[:far], refs[far + ready + NEAR :][:3], refs[far + ready + NEAR + 3 :]
    slots = mean.shape[1]

    def tile(t, at):
        if tables:
            between = [same_firm(parts[0], one, part, at) for one in parts[1:-1]]
            for ref, one in zip(made, between):
                ref[t] = one
            same = [tables[0][t], *between, tables[1][t]]
        else:
            same = [same_firm(parts[0], one, part, at) for one in parts]
        same = jnp.concatenate(same, axis=0)
        count = [one[part * NEAR + 2 * k + 1 : part * NEAR + 2 * k + 2, at] for one in parts for k in range(NEAR)]
        count = jnp.concatenate(count, axis=1)
        high = count.astype(BF16).astype(F32)
        counts = jnp.where(iota((16, count.shape[1]), 0) < 8, high, count - high).astype(BF16)
        found = dot(jnp.concatenate([gathered(parts, part, at), counts], axis=0), same)
        size = found[2 * part : 2 * part + 1] + found[2 * part + 8 : 2 * part + 9]
        inverse = 1.0 / jnp.maximum(size, 1.0)
        scale[t] = jnp.broadcast_to(inverse, scale.shape[1:])
        spread_out((found[:part] + found[part : 2 * part]) * inverse, mean, part, at)

    each_tile(slots, tile)
    for k in range(NEAR):
        cut = slice(part * k, part * (k + 1))
        both = jnp.concatenate(split(mean[cut]), axis=0)
        change = dot(both, pairs[k][0])
        change = change[:part] + change[part:]
        sums[cut] = parts[0][cut] + (change[:, :slots] + change[:, slots:])


def tables_kernel(pad, mask_ids, mean, spread, workers, *sends):
    part = mean.shape[0] // NEAR
    for k, send in enumerate(sends):
        send[...] = mean[part * k : part * (k + 1)]
    slots, width = spread.shape
    table = jnp.concatenate([same_worker(pad, 256)] * 2, axis=0)
    for b in range(width // BLOCK):
        found = one_hot(row(mask_ids, b, BLOCK), slots)
        spread[:, b * BLOCK : (b + 1) * BLOCK] = found
        for at in range(0, BLOCK, 256):
            count = dot(found[:, at : at + 256], table[:256])
            workers[:, b * BLOCK + at : b * BLOCK + at + 256] = count.astype(BF16)


def means_kernel(far, part, kept, *refs):
    parts, source, scale, sends, mean = refs[:far], refs[far:-7], refs[-7], refs[-5:-1], refs[-1]

    def tile(t, at):
        same = [table[t] if kept else same_firm(source[0], table, part, at) for table in source]
        same = jnp.concatenate(same, axis=0)
        found = dot(gathered(parts, part, at), same)
        spread_out((found[:part] + found[part:]) * scale[t][:1], mean, part, at)

    each_tile(mean.shape[1], tile)
    for k, send in enumerate(sends):
        send[...] = mean[part * k : part * (k + 1)]


def own_means(parts, means):
    me = lax.axis_index("rows") % NEAR
    part = parts[0].shape[0]
    for step, one in zip(NEAR_STEPS, parts):
        means[pl.ds(pl.multiple_of((me ^ step) * part, part), part), :] = one[...]
    return jnp.concatenate(split(means[...]), axis=0)


def first_kernel(pad, *refs):
    parts, (x1, mask_ids, weight), tables, (y, means) = refs[:NEAR], refs[NEAR : NEAR + 3], refs[NEAR + 3 : -2], refs[-2:]
    columns, slots = means.shape
    first = own_means(parts, means)
    table = jnp.concatenate([same_worker(pad, 256)] * 2, axis=0)
    for b in range(y.shape[1] // BLOCK):
        at = slice(b * BLOCK, (b + 1) * BLOCK)
        found = tables[0][:, at] if tables else one_hot(row(mask_ids, b, BLOCK), slots)
        spread = dot(first, found)
        spread = spread[:columns] + spread[columns:]
        if tables:
            worker = dot(first, tables[1][:, at])
            worker = worker[:columns] + worker[columns:]
        else:
            worker = by_worker(spread, table)
        y[:, at] = x1[:, at] - spread + worker * row(weight, b, BLOCK)


def last_kernel(*refs):
    parts, (before, mask_ids), tables, (out, means, y, sems) = refs[:NEAR], refs[NEAR : NEAR + 2], refs[NEAR + 2 : -4], refs[-4:]
    outs = column_copies(y, out, sems)
    columns, slots = means.shape
    second = own_means(parts, means)
    for b in range(len(outs)):
        at = slice(b * BLOCK, (b + 1) * BLOCK)
        found = tables[0][:, at] if tables else one_hot(row(mask_ids, b, BLOCK), slots)
        spread = dot(second, found)
        y[:, at] = before[:, at] - (spread[:columns] + spread[columns:])
        outs[b].start()
    wait_all(outs)


def near_exchange(parts, n):
    steps = [[(i, i ^ step) for i in range(n)] for step in NEAR_STEPS[1:]]
    return [parts[0]] + [lax.ppermute(one, "rows", step) for one, step in zip(parts[1:], steps)]


def far_share(one, n):
    steps = [[(i, i ^ (k * NEAR)) for i in range(n)] for k in range(1, n // NEAR)]
    return [one] + [lax.ppermute(one, "rows", step) for step in steps]


def in_hbm(x):
    return pltpu.with_memory_space_constraint(x, pltpu.HBM)


def call(kernel, out_shape, in_specs, out_specs, scratch, flops, moved):
    return pl.pallas_call(
        kernel,
        out_shape=out_shape,
        in_specs=in_specs,
        out_specs=out_specs,
        scratch_shapes=scratch,
        compiler_params=pltpu.CompilerParams(vmem_limit_bytes=VMEM_BYTES),
        cost_estimate=pl.CostEstimate(flops=flops, bytes_accessed=moved, transcendentals=0),
    )


def body(probes, worker_len, spell_to_slot, slot_to_firm, *, n):
    columns, rows_dev = probes.shape
    workers = worker_len.shape[0]
    pad = rows_dev // workers
    slots = slot_to_firm.shape[0]
    tiles = slots // LANES
    part = columns // NEAR
    far = n // NEAR
    keep = tiles * NEAR * n * LANES * LANES * 2 <= 8 * 1024 * 1024
    blocks = rows_dev // BLOCK
    vmem, hbm = pl.BlockSpec(memory_space=pltpu.VMEM), pl.BlockSpec(memory_space=pltpu.HBM)
    lengths = worker_len.reshape(workers // LANES, LANES)
    ids = spell_to_slot.reshape(rows_dev // LANES, LANES)
    firms = slot_to_firm.reshape(tiles, LANES)
    array = jax.ShapeDtypeStruct
    of_rows = (rows_dev // LANES, LANES)
    work = 2 * rows_dev * slots * 2 * columns
    sems = pltpu.SemaphoreType.DMA((blocks,))
    whole = (columns, rows_dev)
    about = part + 8
    message = array((about + rows_dev // slots, slots), F32)
    of_near = array((columns, slots), F32)

    *sends, x1, mask_ids, weight = call(
        functools.partial(sums_kernel, pad, slots // n),
        [message] * 3 + [array((about, slots), F32), array(whole, F32), array(of_rows, jnp.int32), array(of_rows, F32)],
        [hbm] * 4,
        [vmem] * (NEAR + 3),
        [
            pltpu.VMEM(of_rows, F32),
            pltpu.VMEM(whole, F32),
            pltpu.VMEM((columns, slots), F32),
            pltpu.VMEM(lengths.shape, jnp.int32),
            pltpu.VMEM(ids.shape, jnp.int32),
            pltpu.VMEM(firms.shape, jnp.int32),
            sems,
            pltpu.SemaphoreType.DMA((3,)),
        ],
        2 * work,
        4 * columns * rows_dev,
    )(in_hbm(probes), in_hbm(lengths), in_hbm(ids), in_hbm(firms))

    def pair_counts(parts):
        return call(
            functools.partial(pairs_kernel, pad, about),
            array((len(parts), slots, 2 * slots), BF16),
            [vmem] * len(parts),
            vmem,
            [
                pltpu.VMEM((len(parts), *of_rows), F32),
                pltpu.VMEM((len(parts), 8, slots), F32),
                pltpu.VMEM((len(parts), slots, workers), BF16),
            ],
            work * len(parts) // 4,
            4 * slots * slots,
        )(*parts)

    arrived = near_exchange(sends, n)
    pairs = [pair_counts(arrived[:1]), pair_counts(arrived[1:2])]
    joined = call(
        functools.partial(join_kernel, part),
        array((columns + 2 * NEAR, slots), F32),
        [vmem] * (NEAR + 2),
        vmem,
        [],
        0,
        message.size * 8,
    )(*arrived, *pairs)
    shared = far_share(joined, n)
    tables, passed = [], arrived[2]
    table = array((tiles, NEAR * LANES, NEAR * LANES), BF16)

    def firm_table(one, passed, out):
        return call(
            functools.partial(firms_kernel, part),
            out,
            [vmem] * 3,
            [vmem] * len(out),
            [],
            work // 64,
            tiles * (NEAR * LANES) ** 2 * 2,
        )(joined, one, passed)

    if keep:
        first_table, passed = firm_table(joined, passed, [table, message])
        tables = [first_table, *firm_table(shared[-1], first_table, [table])]
    passed = lax.ppermute(passed, "rows", [(i, i ^ 1) for i in range(n)])
    pairs += [pair_counts(arrived[2:3]), pair_counts([passed])]
    scale = array((tiles, 8, NEAR * LANES), F32)
    made = [table] * (far - 2) * keep
    mean, sums, scales, *made = call(
        functools.partial(change_kernel, far, part, len(tables)),
        [of_near, of_near, scale, *made],
        [vmem] * (far + len(tables) + len(pairs)),
        [vmem] * (3 + len(made)),
        [],
        work // 4,
        slots * slots * 4,
    )(*shared, *tables, *pairs)
    again = far_share(sums, n)
    source = [tables[0], *made, tables[1]] if keep else shared
    spreads = []
    sends = [mean[part * k : part * (k + 1)] for k in range(NEAR)]
    if keep:
        *spreads, a, b, c, d = call(
            functools.partial(tables_kernel, pad),
            [array((slots, rows_dev), BF16)] * 2 + [array((part, slots), F32)] * NEAR,
            [vmem] * 2,
            [vmem] * (2 + NEAR),
            [],
            work,
            4 * slots * rows_dev,
        )(mask_ids, mean)
        sends = [a, b, c, d]
    first = near_exchange(sends, n)
    sends = call(
        functools.partial(means_kernel, far, part, keep),
        [array((part, slots), F32)] * NEAR,
        [vmem] * (far + len(source) + 2),
        [vmem] * NEAR,
        [pltpu.VMEM((columns, slots), F32)],
        work // 4,
        slots * slots * 4,
    )(*again, *source, scales, spreads[1] if keep else scales)
    arrived = near_exchange(sends, n)
    before = call(
        functools.partial(first_kernel, pad),
        array(whole, F32),
        [vmem] * (NEAR + 3 + len(spreads)),
        vmem,
        [pltpu.VMEM((columns, slots), F32)],
        work,
        8 * columns * rows_dev,
    )(*first, x1, mask_ids, weight, *spreads)
    return call(
        last_kernel,
        array(whole, F32),
        [vmem] * (NEAR + 2 + len(spreads[:1])),
        hbm,
        [pltpu.VMEM((columns, slots), F32), pltpu.VMEM(whole, F32), sems],
        work,
        8 * columns * rows_dev,
    )(*arrived, before, mask_ids, *spreads[:1])


def solution(mesh):
    placed = (P(None, ("grp", "rows")), P(("grp", "rows")), P(("grp", "rows")), P(("grp", "rows")))
    return jax.shard_map(
        functools.partial(body, n=mesh.shape["rows"]),
        mesh=mesh,
        in_specs=placed,
        out_specs=P(None, ("grp", "rows")),
        check_vma=False,
    )
```

```python
import functools

import jax
import jax.numpy as jnp
from jax import lax
from jax.experimental import pallas as pl
from jax.experimental.pallas import tpu as pltpu
from jax.sharding import PartitionSpec as P

FIRMS_PER_SHARD = 1024
LANES = 128
BLOCK = 1024
PIECE = 512
VMEM_BYTES = 32 * 1024 * 1024
NEAR = 4
NEAR_STEPS = (0, 1, 2, 3)
F32, BF16 = jnp.float32, jnp.bfloat16
NT = (((1,), (1,)), ((), ()))
NN = (((1,), (0,)), ((), ()))


def dot(a, b, dims=NN):
    return lax.dot_general(a, b, dims, preferred_element_type=F32)


def iota(shape, dim):
    return lax.broadcasted_iota(jnp.int32, shape, dim)


def split(x):
    hi = x.astype(BF16)
    return hi, (x - hi.astype(F32)).astype(BF16)


def row(ref, block, size):
    per = size // LANES
    return jnp.concatenate([ref[block * per + k : block * per + k + 1, :] for k in range(per)], axis=1)


def one_hot(ids, slots):
    kind = BF16 if slots <= 256 else F32
    slot = iota((slots, LANES), 0).astype(F32).astype(kind)
    ids = ids.astype(F32).astype(kind)
    one, zero = jnp.ones((slots, LANES), kind), jnp.zeros((slots, LANES), kind)
    parts = [jnp.where(slot == ids[:, k : k + LANES], one, zero) for k in range(0, ids.shape[1], LANES)]
    return jnp.concatenate(parts, axis=1).astype(BF16)


def one_hot_down(columns, slots):
    kind = BF16 if slots <= 256 else F32
    one, zero = jnp.ones((LANES, LANES), kind), jnp.zeros((LANES, LANES), kind)
    along_slots = [(iota((LANES, LANES), 1) + at).astype(F32).astype(kind) for at in range(0, slots, LANES)]
    parts, columns = [], columns.astype(kind)
    for k in range(columns.shape[1]):
        ids = jnp.broadcast_to(columns[:, k : k + 1], (LANES, LANES))
        parts.append(jnp.concatenate([jnp.where(slot == ids, one, zero) for slot in along_slots], axis=1))
    return jnp.concatenate(parts, axis=0).astype(BF16)


def same_worker(pad, width):
    return (iota((width, width), 0) // pad == iota((width, width), 1) // pad).astype(F32).astype(BF16)


def by_worker(x, table):
    rows, width = x.shape
    step = table.shape[1]
    both = [
        jnp.concatenate([one[:, k : k + step] for k in range(0, width, step)], axis=0) for one in split(x)
    ]
    total = dot(jnp.concatenate(both, axis=1), table)
    return jnp.concatenate([total[k : k + rows] for k in range(0, total.shape[0], rows)], axis=1)


def start_all(copies):
    for copy in copies:
        copy.start()


def wait_all(copies):
    for copy in copies:
        copy.wait()


def column_copies(source, target, sems, size=BLOCK):
    width = source.shape[1]
    cuts = [pl.ds(start, size) for start in range(0, width, size)]
    return [pltpu.make_async_copy(source.at[:, cut], target.at[:, cut], sems.at[b]) for b, cut in enumerate(cuts)]


def row_lengths(lengths, pad):
    total_rows = lengths.shape[0] * pad
    here = iota((total_rows, LANES), 0)
    lane = iota((total_rows, LANES), 1)
    wide = jnp.broadcast_to(lengths.astype(F32)[:, None, :], (lengths.shape[0], pad, LANES)).reshape(total_rows, LANES)
    per = LANES // pad
    wide = jnp.where(lane // per == here % pad, wide, 0.0).astype(BF16)
    spread = (iota((LANES, LANES), 0) % per == iota((LANES, LANES), 1) // pad).astype(F32).astype(BF16)
    row_len = dot(wide, spread)
    return row_len, (lane % pad).astype(F32) < row_len


def along(ref):
    return jnp.concatenate([ref[k : k + 1, :] for k in range(ref.shape[0])], axis=1)


def sums_kernel(pad, cap, *refs):
    (probes, lengths_in, ids_in, firms_in), sends, refs = refs[:4], refs[4 : 4 + NEAR], refs[4 + NEAR :]
    x1, mask_ids, weight, valid, x, sums, lengths, ids, firms, sems, small = refs
    copies = column_copies(probes, x, sems)
    first = [
        pltpu.make_async_copy(source, target, small.at[k])
        for k, (source, target) in enumerate(((lengths_in, lengths), (ids_in, ids), (firms_in, firms)))
    ]
    start_all(first)
    start_all(copies)
    columns, slots = sums.shape
    part = columns // NEAR
    me = lax.axis_index("rows") % NEAR
    wait_all(first)
    row_len, inside = row_lengths(lengths[...], pad)
    valid[...] = jnp.where(inside, 1.0, 0.0)
    weight[...] = jnp.where(inside, 1.0 / row_len, 0.0)
    masked = jnp.where(inside, ids[...], -1)
    mask_ids[...] = masked
    turned = jnp.concatenate([masked.astype(F32)] * (LANES // masked.shape[0]), axis=0).T
    keys = (iota((1, slots), 1) // cap * FIRMS_PER_SHARD + along(firms)).astype(F32)
    across = slots // LANES
    rows = ids.shape[0] // across
    masked = jnp.concatenate([masked[k * rows : (k + 1) * rows] for k in range(across)], axis=1).astype(F32)
    for send in sends[:3]:
        send[part + 8 :] = masked

    table = jnp.concatenate([same_worker(pad, 256)] * 2, axis=0)
    wait_all(copies)
    total = None
    for b in range(x.shape[1] // PIECE):
        ok = row(valid, b, PIECE)
        x0 = x[:, b * PIECE : (b + 1) * PIECE] * ok
        rest = x0 - by_worker(x0, table) * row(weight, b, PIECE)
        x1[:, b * PIECE : (b + 1) * PIECE] = rest
        counted = jnp.broadcast_to(ok, (16, PIECE)).astype(BF16)
        data = jnp.concatenate([*split(rest), counted], axis=0)
        per = PIECE // LANES
        block = dot(data, one_hot_down(turned[:, b * per : (b + 1) * per], slots))
        total = block if total is None else total + block
    sums[...] = total[:columns] + total[columns : 2 * columns]
    about = jnp.where(iota((8, slots), 0) == 0, keys, total[2 * columns : 2 * columns + 1])
    for step, send in zip(NEAR_STEPS, sends):
        send[:part] = sums[pl.ds(pl.multiple_of((me ^ step) * part, part), part), :]
        send[part : part + 8] = about


def join_kernel(part, *refs):
    parts, out = refs[:NEAR], refs[-1]
    for k, one in enumerate(parts):
        out[part * k : part * (k + 1)] = one[:part]
        out[part * NEAR + 2 * k : part * NEAR + 2 * k + 2] = one[part : part + 2]


def pairs_kernel(pad, start, *refs):
    parts, (out, ids, size, counts) = refs[:-4], refs[-4:]
    slots = out.shape[1]
    kind = BF16 if slots <= 256 else F32
    per = LANES // pad
    total_rows = ids.shape[1]
    across = slots // LANES
    rows = total_rows // across
    for k, part in enumerate(parts):
        size[k] = jnp.broadcast_to(part[start - 7 : start - 6], (8, slots))
        for at in range(across):
            ids[k, at * rows : (at + 1) * rows] = part[start:, at * LANES : (at + 1) * LANES]
    at = iota((LANES, pad * LANES), 1)
    deal = (iota((LANES, pad * LANES), 0) == at % per * pad + at // LANES).astype(F32).astype(BF16)
    mine = iota((total_rows, pad * LANES), 1) % LANES // per == iota((total_rows, pad * LANES), 0) % pad
    slot = iota((slots, LANES), 0).astype(F32).astype(kind)
    one, zero = jnp.ones((slots, LANES), kind), jnp.zeros((slots, LANES), kind)
    diagonal = iota((slots, slots), 1) == iota((slots, slots), 0)

    def device(k, carry):
        dealt = dot(jnp.concatenate(split(ids[k]), axis=0), deal)
        dealt = jnp.where(mine, dealt[:total_rows] + dealt[total_rows:], 0.0)
        dealt = jnp.sum(dealt.reshape(total_rows // pad, pad, pad * LANES), axis=1)
        spells = dealt.astype(kind)
        for g in range(total_rows // pad):
            total = zero
            for j in range(pad):
                total += jnp.where(slot == spells[g : g + 1, j * LANES : (j + 1) * LANES], one, zero)
            counts[k, :, g * LANES : (g + 1) * LANES] = total.astype(BF16)
        valid = jnp.where(dealt >= 0.0, 1.0, 0.0)
        length = valid[:, :LANES]
        for j in range(1, pad):
            length += valid[:, j * LANES : (j + 1) * LANES]
        inverse = 1.0 / length
        inverse = jnp.concatenate([inverse[g : g + 1] for g in range(total_rows // pad)], axis=1)
        here = counts[k]
        total = dot(jnp.concatenate(split(here.astype(F32) * inverse), axis=0), here, NT)
        total = total[:slots] + total[slots:] - jnp.where(diagonal, size[k, :1], 0.0)
        hi, lo = split(total)
        out[k, :, :slots] = hi
        out[k, :, slots:] = lo
        return carry

    lax.fori_loop(0, len(parts), device, 0, unroll=len(parts) if slots <= 256 else 1)


def same_firm(own, one, part, at):
    mine, keys = ([ref[part * NEAR + 2 * k : part * NEAR + 2 * k + 1, at] for k in range(NEAR)] for ref in (own, one))
    mine = jnp.concatenate(mine, axis=1)
    down = jnp.concatenate([jnp.broadcast_to(key, (8, LANES)) for key in keys], axis=0).T
    found = [(down[:, 8 * k : 8 * k + 1] == mine).astype(F32).astype(BF16) for k in range(NEAR)]
    return jnp.concatenate(found, axis=0)


def each_tile(slots, do):
    tiles = slots // LANES
    if tiles <= 2:
        for t in range(tiles):
            do(t, slice(t * LANES, (t + 1) * LANES))
    else:
        lax.fori_loop(0, tiles, lambda t, c: (do(t, pl.ds(pl.multiple_of(t * LANES, LANES), LANES)), c)[1], 0)


def firms_kernel(part, own, one, passed, out, *copy):
    for ref in copy:
        ref[...] = passed[...]
    each_tile(own.shape[1], lambda t, at: out.__setitem__(t, same_firm(own, one, part, at)))


def gathered(parts, part, at):
    data = [one[part * k : part * (k + 1), at] for one in parts for k in range(NEAR)]
    return jnp.concatenate(split(jnp.concatenate(data, axis=1)), axis=0)


def spread_out(means, out, part, at):
    for k in range(NEAR):
        out[part * k : part * (k + 1), at] = means[:, k * LANES : (k + 1) * LANES]


def change_kernel(far, part, ready, *refs):
    tables, pairs, refs = refs[far : far + ready], refs[far + ready : far + ready + NEAR], refs
    parts, (mean, sums, scale), made = refs[:far], refs[far + ready + NEAR :][:3], refs[far + ready + NEAR + 3 :]
    slots = mean.shape[1]

    def tile(t, at):
        if tables:
            between = [same_firm(parts[0], one, part, at) for one in parts[1:-1]]
            for ref, one in zip(made, between):
                ref[t] = one
            same = [tables[0][t], *between, tables[1][t]]
        else:
            same = [same_firm(parts[0], one, part, at) for one in parts]
        same = jnp.concatenate(same, axis=0)
        count = [one[part * NEAR + 2 * k + 1 : part * NEAR + 2 * k + 2, at] for one in parts for k in range(NEAR)]
        count = jnp.concatenate(count, axis=1)
        high = count.astype(BF16).astype(F32)
        counts = jnp.where(iota((16, count.shape[1]), 0) < 8, high, count - high).astype(BF16)
        found = dot(jnp.concatenate([gathered(parts, part, at), counts], axis=0), same)
        size = found[2 * part : 2 * part + 1] + found[2 * part + 8 : 2 * part + 9]
        inverse = 1.0 / jnp.maximum(size, 1.0)
        scale[t] = jnp.broadcast_to(inverse, scale.shape[1:])
        spread_out((found[:part] + found[part : 2 * part]) * inverse, mean, part, at)

    each_tile(slots, tile)
    for k in range(NEAR):
        cut = slice(part * k, part * (k + 1))
        both = jnp.concatenate(split(mean[cut]), axis=0)
        change = dot(both, pairs[k][0])
        change = change[:part] + change[part:]
        sums[cut] = parts[0][cut] + (change[:, :slots] + change[:, slots:])


def tables_kernel(pad, mask_ids, mean, spread, workers, *sends):
    part = mean.shape[0] // NEAR
    for k, send in enumerate(sends):
        send[...] = mean[part * k : part * (k + 1)]
    slots, width = spread.shape
    table = jnp.concatenate([same_worker(pad, 256)] * 2, axis=0)
    for b in range(width // BLOCK):
        found = one_hot(row(mask_ids, b, BLOCK), slots)
        spread[:, b * BLOCK : (b + 1) * BLOCK] = found
        for at in range(0, BLOCK, 256):
            count = dot(found[:, at : at + 256], table[:256])
            workers[:, b * BLOCK + at : b * BLOCK + at + 256] = count.astype(BF16)


def means_kernel(far, part, kept, *refs):
    parts, source, scale, sends, mean = refs[:far], refs[far:-7], refs[-7], refs[-5:-1], refs[-1]

    def tile(t, at):
        same = [table[t] if kept else same_firm(source[0], table, part, at) for table in source]
        same = jnp.concatenate(same, axis=0)
        found = dot(gathered(parts, part, at), same)
        spread_out((found[:part] + found[part:]) * scale[t][:1], mean, part, at)

    each_tile(mean.shape[1], tile)
    for k, send in enumerate(sends):
        send[...] = mean[part * k : part * (k + 1)]


def own_means(parts, means):
    me = lax.axis_index("rows") % NEAR
    part = parts[0].shape[0]
    for step, one in zip(NEAR_STEPS, parts):
        means[pl.ds(pl.multiple_of((me ^ step) * part, part), part), :] = one[...]
    return jnp.concatenate(split(means[...]), axis=0)


def first_kernel(pad, *refs):
    parts, (x1, mask_ids, weight), tables, (y, means) = refs[:NEAR], refs[NEAR : NEAR + 3], refs[NEAR + 3 : -2], refs[-2:]
    columns, slots = means.shape
    first = own_means(parts, means)
    table = jnp.concatenate([same_worker(pad, 256)] * 2, axis=0)
    for b in range(y.shape[1] // BLOCK):
        at = slice(b * BLOCK, (b + 1) * BLOCK)
        found = tables[0][:, at] if tables else one_hot(row(mask_ids, b, BLOCK), slots)
        spread = dot(first, found)
        spread = spread[:columns] + spread[columns:]
        if tables:
            worker = dot(first, tables[1][:, at])
            worker = worker[:columns] + worker[columns:]
        else:
            worker = by_worker(spread, table)
        y[:, at] = x1[:, at] - spread + worker * row(weight, b, BLOCK)


def last_kernel(*refs):
    parts, (before, mask_ids), tables, (out, means, y, sems) = refs[:NEAR], refs[NEAR : NEAR + 2], refs[NEAR + 2 : -4], refs[-4:]
    outs = column_copies(y, out, sems)
    columns, slots = means.shape
    second = own_means(parts, means)
    for b in range(y.shape[1] // PIECE):
        at = slice(b * PIECE, (b + 1) * PIECE)
        found = tables[0][:, at] if tables else one_hot(row(mask_ids, b, PIECE), slots)
        spread = dot(second, found)
        y[:, at] = before[:, at] - (spread[:columns] + spread[columns:])
        if (b + 1) * PIECE % BLOCK == 0:
            outs[b * PIECE // BLOCK].start()
    wait_all(outs)


def near_exchange(parts, n):
    steps = [[(i, i ^ step) for i in range(n)] for step in NEAR_STEPS[1:]]
    return [parts[0]] + [lax.ppermute(one, "rows", step) for one, step in zip(parts[1:], steps)]


def far_share(one, n):
    steps = [[(i, i ^ (k * NEAR)) for i in range(n)] for k in range(1, n // NEAR)]
    return [one] + [lax.ppermute(one, "rows", step) for step in steps]


def in_hbm(x):
    return pltpu.with_memory_space_constraint(x, pltpu.HBM)


def call(kernel, out_shape, in_specs, out_specs, scratch, flops, moved):
    return pl.pallas_call(
        kernel,
        out_shape=out_shape,
        in_specs=in_specs,
        out_specs=out_specs,
        scratch_shapes=scratch,
        compiler_params=pltpu.CompilerParams(vmem_limit_bytes=VMEM_BYTES),
        cost_estimate=pl.CostEstimate(flops=flops, bytes_accessed=moved, transcendentals=0),
    )


def body(probes, worker_len, spell_to_slot, slot_to_firm, *, n):
    columns, rows_dev = probes.shape
    workers = worker_len.shape[0]
    pad = rows_dev // workers
    slots = slot_to_firm.shape[0]
    tiles = slots // LANES
    part = columns // NEAR
    far = n // NEAR
    keep = tiles * NEAR * n * LANES * LANES * 2 <= 8 * 1024 * 1024
    blocks = rows_dev // BLOCK
    vmem, hbm = pl.BlockSpec(memory_space=pltpu.VMEM), pl.BlockSpec(memory_space=pltpu.HBM)
    lengths = worker_len.reshape(workers // LANES, LANES)
    ids = spell_to_slot.reshape(rows_dev // LANES, LANES)
    firms = slot_to_firm.reshape(tiles, LANES)
    array = jax.ShapeDtypeStruct
    of_rows = (rows_dev // LANES, LANES)
    work = 2 * rows_dev * slots * 2 * columns
    sems = pltpu.SemaphoreType.DMA((blocks,))
    whole = (columns, rows_dev)
    about = part + 8
    message = array((about + rows_dev // slots, slots), F32)
    of_near = array((columns, slots), F32)

    *sends, x1, mask_ids, weight = call(
        functools.partial(sums_kernel, pad, slots // n),
        [message] * 3 + [array((about, slots), F32), array(whole, F32), array(of_rows, jnp.int32), array(of_rows, F32)],
        [hbm] * 4,
        [vmem] * (NEAR + 3),
        [
            pltpu.VMEM(of_rows, F32),
            pltpu.VMEM(whole, F32),
            pltpu.VMEM((columns, slots), F32),
            pltpu.VMEM(lengths.shape, jnp.int32),
            pltpu.VMEM(ids.shape, jnp.int32),
            pltpu.VMEM(firms.shape, jnp.int32),
            sems,
            pltpu.SemaphoreType.DMA((3,)),
        ],
        2 * work,
        4 * columns * rows_dev,
    )(in_hbm(probes), in_hbm(lengths), in_hbm(ids), in_hbm(firms))

    def pair_counts(parts):
        return call(
            functools.partial(pairs_kernel, pad, about),
            array((len(parts), slots, 2 * slots), BF16),
            [vmem] * len(parts),
            vmem,
            [
                pltpu.VMEM((len(parts), *of_rows), F32),
                pltpu.VMEM((len(parts), 8, slots), F32),
                pltpu.VMEM((len(parts), slots, workers), BF16),
            ],
            work * len(parts) // 4,
            4 * slots * slots,
        )(*parts)

    arrived = near_exchange(sends, n)
    pairs = [pair_counts(arrived[:1]), pair_counts(arrived[1:2])]
    joined = call(
        functools.partial(join_kernel, part),
        array((columns + 2 * NEAR, slots), F32),
        [vmem] * (NEAR + 2),
        vmem,
        [],
        0,
        message.size * 8,
    )(*arrived, *pairs)
    shared = far_share(joined, n)
    tables, passed = [], arrived[2]
    table = array((tiles, NEAR * LANES, NEAR * LANES), BF16)

    def firm_table(one, passed, out):
        return call(
            functools.partial(firms_kernel, part),
            out,
            [vmem] * 3,
            [vmem] * len(out),
            [],
            work // 64,
            tiles * (NEAR * LANES) ** 2 * 2,
        )(joined, one, passed)

    if keep:
        first_table, passed = firm_table(joined, passed, [table, message])
        tables = [first_table, *firm_table(shared[-1], first_table, [table])]
    passed = lax.ppermute(passed, "rows", [(i, i ^ 1) for i in range(n)])
    pairs += [pair_counts(arrived[2:3]), pair_counts([passed])]
    scale = array((tiles, 8, NEAR * LANES), F32)
    made = [table] * (far - 2) * keep
    mean, sums, scales, *made = call(
        functools.partial(change_kernel, far, part, len(tables)),
        [of_near, of_near, scale, *made],
        [vmem] * (far + len(tables) + len(pairs)),
        [vmem] * (3 + len(made)),
        [],
        work // 4,
        slots * slots * 4,
    )(*shared, *tables, *pairs)
    again = far_share(sums, n)
    source = [tables[0], *made, tables[1]] if keep else shared
    spreads = []
    sends = [mean[part * k : part * (k + 1)] for k in range(NEAR)]
    if keep:
        *spreads, a, b, c, d = call(
            functools.partial(tables_kernel, pad),
            [array((slots, rows_dev), BF16)] * 2 + [array((part, slots), F32)] * NEAR,
            [vmem] * 2,
            [vmem] * (2 + NEAR),
            [],
            work,
            4 * slots * rows_dev,
        )(mask_ids, mean)
        sends = [a, b, c, d]
    first = near_exchange(sends, n)
    sends = call(
        functools.partial(means_kernel, far, part, keep),
        [array((part, slots), F32)] * NEAR,
        [vmem] * (far + len(source) + 2),
        [vmem] * NEAR,
        [pltpu.VMEM((columns, slots), F32)],
        work // 4,
        slots * slots * 4,
    )(*again, *source, scales, spreads[1] if keep else scales)
    arrived = near_exchange(sends, n)
    before = call(
        functools.partial(first_kernel, pad),
        array(whole, F32),
        [vmem] * (NEAR + 3 + len(spreads)),
        vmem,
        [pltpu.VMEM((columns, slots), F32)],
        work,
        8 * columns * rows_dev,
    )(*first, x1, mask_ids, weight, *spreads)
    return call(
        last_kernel,
        array(whole, F32),
        [vmem] * (NEAR + 2 + len(spreads[:1])),
        hbm,
        [pltpu.VMEM((columns, slots), F32), pltpu.VMEM(whole, F32), sems],
        work,
        8 * columns * rows_dev,
    )(*arrived, before, mask_ids, *spreads[:1])


def solution(mesh):
    placed = (P(None, ("grp", "rows")), P(("grp", "rows")), P(("grp", "rows")), P(("grp", "rows")))
    return jax.shard_map(
        functools.partial(body, n=mesh.shape["rows"]),
        mesh=mesh,
        in_specs=placed,
        out_specs=P(None, ("grp", "rows")),
        check_vma=False,
    )
```

```python
import functools

import jax
import jax.numpy as jnp
from jax import lax
from jax.experimental import pallas as pl
from jax.experimental.pallas import tpu as pltpu
from jax.sharding import PartitionSpec as P

FIRMS_PER_SHARD = 1024
LANES = 128
BLOCK = 1024
VMEM_BYTES = 32 * 1024 * 1024
NEAR = 4
NEAR_STEPS = (0, 1, 2, 3)
F32, BF16 = jnp.float32, jnp.bfloat16
NT = (((1,), (1,)), ((), ()))
NN = (((1,), (0,)), ((), ()))


def dot(a, b, dims=NN):
    return lax.dot_general(a, b, dims, preferred_element_type=F32)


def iota(shape, dim):
    return lax.broadcasted_iota(jnp.int32, shape, dim)


def split(x):
    hi = x.astype(BF16)
    return hi, (x - hi.astype(F32)).astype(BF16)


def row(ref, block, size):
    per = size // LANES
    return jnp.concatenate([ref[block * per + k : block * per + k + 1, :] for k in range(per)], axis=1)


def one_hot(ids, slots):
    kind = BF16 if slots <= 256 else F32
    slot = iota((slots, LANES), 0).astype(F32).astype(kind)
    ids = ids.astype(F32).astype(kind)
    one, zero = jnp.ones((slots, LANES), kind), jnp.zeros((slots, LANES), kind)
    parts = [jnp.where(slot == ids[:, k : k + LANES], one, zero) for k in range(0, ids.shape[1], LANES)]
    return jnp.concatenate(parts, axis=1).astype(BF16)


def one_hot_down(columns, slots):
    kind = BF16 if slots <= 256 else F32
    one, zero = jnp.ones((LANES, LANES), kind), jnp.zeros((LANES, LANES), kind)
    along_slots = [(iota((LANES, LANES), 1) + at).astype(F32).astype(kind) for at in range(0, slots, LANES)]
    parts, columns = [], columns.astype(kind)
    for k in range(columns.shape[1]):
        ids = jnp.broadcast_to(columns[:, k : k + 1], (LANES, LANES))
        parts.append(jnp.concatenate([jnp.where(slot == ids, one, zero) for slot in along_slots], axis=1))
    return jnp.concatenate(parts, axis=0).astype(BF16)


def same_worker(pad, width):
    return (iota((width, width), 0) // pad == iota((width, width), 1) // pad).astype(F32).astype(BF16)


def by_worker(x, table):
    rows, width = x.shape
    step = table.shape[1]
    both = [
        jnp.concatenate([one[:, k : k + step] for k in range(0, width, step)], axis=0) for one in split(x)
    ]
    total = dot(jnp.concatenate(both, axis=1), table)
    return jnp.concatenate([total[k : k + rows] for k in range(0, total.shape[0], rows)], axis=1)


def start_all(copies):
    for copy in copies:
        copy.start()


def wait_all(copies):
    for copy in copies:
        copy.wait()


def column_copies(source, target, sems, size=BLOCK):
    width = source.shape[1]
    cuts = [pl.ds(start, size) for start in range(0, width, size)]
    return [pltpu.make_async_copy(source.at[:, cut], target.at[:, cut], sems.at[b]) for b, cut in enumerate(cuts)]


def row_lengths(lengths, pad):
    total_rows = lengths.shape[0] * pad
    here = iota((total_rows, LANES), 0)
    lane = iota((total_rows, LANES), 1)
    wide = jnp.broadcast_to(lengths.astype(F32)[:, None, :], (lengths.shape[0], pad, LANES)).reshape(total_rows, LANES)
    per = LANES // pad
    wide = jnp.where(lane // per == here % pad, wide, 0.0).astype(BF16)
    spread = (iota((LANES, LANES), 0) % per == iota((LANES, LANES), 1) // pad).astype(F32).astype(BF16)
    row_len = dot(wide, spread)
    return row_len, (lane % pad).astype(F32) < row_len


def along(ref):
    return jnp.concatenate([ref[k : k + 1, :] for k in range(ref.shape[0])], axis=1)


def sums_kernel(pad, cap, *refs):
    (probes, lengths_in, ids_in, firms_in), sends, refs = refs[:4], refs[4 : 4 + NEAR], refs[4 + NEAR :]
    x1, mask_ids, weight, valid, x, sums, lengths, ids, firms, sems, small = refs
    copies = column_copies(probes, x, sems)
    first = [
        pltpu.make_async_copy(source, target, small.at[k])
        for k, (source, target) in enumerate(((lengths_in, lengths), (ids_in, ids), (firms_in, firms)))
    ]
    start_all(first)
    start_all(copies)
    columns, slots = sums.shape
    part = columns // NEAR
    me = lax.axis_index("rows") % NEAR
    wait_all(first)
    row_len, inside = row_lengths(lengths[...], pad)
    valid[...] = jnp.where(inside, 1.0, 0.0)
    weight[...] = jnp.where(inside, 1.0 / row_len, 0.0)
    masked = jnp.where(inside, ids[...], -1)
    mask_ids[...] = masked
    turned = jnp.concatenate([masked.astype(F32)] * (LANES // masked.shape[0]), axis=0).T
    keys = (iota((1, slots), 1) // cap * FIRMS_PER_SHARD + along(firms)).astype(F32)
    across = slots // LANES
    rows = ids.shape[0] // across
    masked = jnp.concatenate([masked[k * rows : (k + 1) * rows] for k in range(across)], axis=1).astype(F32)
    for send in sends[:3]:
        send[part + 8 :] = masked

    table = jnp.concatenate([same_worker(pad, 256)] * 2, axis=0)
    wait_all(copies)
    total = None
    for b in range(len(copies)):
        ok = row(valid, b, BLOCK)
        x0 = x[:, b * BLOCK : (b + 1) * BLOCK] * ok
        rest = x0 - by_worker(x0, table) * row(weight, b, BLOCK)
        x1[:, b * BLOCK : (b + 1) * BLOCK] = rest
        counted = jnp.broadcast_to(ok, (16, BLOCK)).astype(BF16)
        data = jnp.concatenate([*split(rest), counted], axis=0)
        per = BLOCK // LANES
        block = dot(data, one_hot_down(turned[:, b * per : (b + 1) * per], slots))
        total = block if total is None else total + block
    sums[...] = total[:columns] + total[columns : 2 * columns]
    about = jnp.where(iota((8, slots), 0) == 0, keys, total[2 * columns : 2 * columns + 1])
    for step, send in zip(NEAR_STEPS, sends):
        send[:part] = sums[pl.ds(pl.multiple_of((me ^ step) * part, part), part), :]
        send[part : part + 8] = about


def join_kernel(part, *refs):
    parts, out = refs[:NEAR], refs[-1]
    for k, one in enumerate(parts):
        out[part * k : part * (k + 1)] = one[:part]
        out[part * NEAR + 2 * k : part * NEAR + 2 * k + 2] = one[part : part + 2]


def pairs_kernel(pad, start, *refs):
    parts, (out, ids, size, counts) = refs[:-4], refs[-4:]
    slots = out.shape[1]
    kind = BF16 if slots <= 256 else F32
    per = LANES // pad
    total_rows = ids.shape[1]
    across = slots // LANES
    rows = total_rows // across
    for k, part in enumerate(parts):
        size[k] = jnp.broadcast_to(part[start - 7 : start - 6], (8, slots))
        for at in range(across):
            ids[k, at * rows : (at + 1) * rows] = part[start:, at * LANES : (at + 1) * LANES]
    at = iota((LANES, pad * LANES), 1)
    deal = (iota((LANES, pad * LANES), 0) == at % per * pad + at // LANES).astype(F32).astype(BF16)
    mine = iota((total_rows, pad * LANES), 1) % LANES // per == iota((total_rows, pad * LANES), 0) % pad
    slot = iota((slots, LANES), 0).astype(F32).astype(kind)
    one, zero = jnp.ones((slots, LANES), kind), jnp.zeros((slots, LANES), kind)
    diagonal = iota((slots, slots), 1) == iota((slots, slots), 0)

    def device(k, carry):
        dealt = dot(jnp.concatenate(split(ids[k]), axis=0), deal)
        dealt = jnp.where(mine, dealt[:total_rows] + dealt[total_rows:], 0.0)
        dealt = jnp.sum(dealt.reshape(total_rows // pad, pad, pad * LANES), axis=1)
        spells = dealt.astype(kind)
        for g in range(total_rows // pad):
            total = zero
            for j in range(pad):
                total += jnp.where(slot == spells[g : g + 1, j * LANES : (j + 1) * LANES], one, zero)
            counts[k, :, g * LANES : (g + 1) * LANES] = total.astype(BF16)
        valid = jnp.where(dealt >= 0.0, 1.0, 0.0)
        length = valid[:, :LANES]
        for j in range(1, pad):
            length += valid[:, j * LANES : (j + 1) * LANES]
        inverse = 1.0 / length
        inverse = jnp.concatenate([inverse[g : g + 1] for g in range(total_rows // pad)], axis=1)
        here = counts[k]
        total = dot(jnp.concatenate(split(here.astype(F32) * inverse), axis=0), here, NT)
        total = total[:slots] + total[slots:] - jnp.where(diagonal, size[k, :1], 0.0)
        hi, lo = split(total)
        out[k, :, :slots] = hi
        out[k, :, slots:] = lo
        return carry

    lax.fori_loop(0, len(parts), device, 0, unroll=len(parts) if slots <= 256 else 1)


def same_firm(own, one, part, at):
    mine, keys = ([ref[part * NEAR + 2 * k : part * NEAR + 2 * k + 1, at] for k in range(NEAR)] for ref in (own, one))
    mine = jnp.concatenate(mine, axis=1)
    down = jnp.concatenate([jnp.broadcast_to(key, (8, LANES)) for key in keys], axis=0).T
    found = [(down[:, 8 * k : 8 * k + 1] == mine).astype(F32).astype(BF16) for k in range(NEAR)]
    return jnp.concatenate(found, axis=0)


def each_tile(slots, do):
    tiles = slots // LANES
    if tiles <= 2:
        for t in range(tiles):
            do(t, slice(t * LANES, (t + 1) * LANES))
    else:
        lax.fori_loop(0, tiles, lambda t, c: (do(t, pl.ds(pl.multiple_of(t * LANES, LANES), LANES)), c)[1], 0)


def firms_kernel(part, own, one, passed, out, *copy):
    for ref in copy:
        ref[...] = passed[...]
    each_tile(own.shape[1], lambda t, at: out.__setitem__(t, same_firm(own, one, part, at)))


def gathered(parts, part, at):
    data = [one[part * k : part * (k + 1), at] for one in parts for k in range(NEAR)]
    return jnp.concatenate(split(jnp.concatenate(data, axis=1)), axis=0)


def spread_out(means, out, part, at):
    for k in range(NEAR):
        out[part * k : part * (k + 1), at] = means[:, k * LANES : (k + 1) * LANES]


def change_kernel(far, part, ready, *refs):
    tables, pairs, refs = refs[far : far + ready], refs[far + ready : far + ready + NEAR], refs
    parts, (mean, sums, scale), made = refs[:far], refs[far + ready + NEAR :][:3], refs[far + ready + NEAR + 3 :]
    slots = mean.shape[1]

    def tile(t, at):
        if tables:
            between = [same_firm(parts[0], one, part, at) for one in parts[1:-1]]
            for ref, one in zip(made, between):
                ref[t] = one
            same = [tables[0][t], *between, tables[1][t]]
        else:
            same = [same_firm(parts[0], one, part, at) for one in parts]
        same = jnp.concatenate(same, axis=0)
        count = [one[part * NEAR + 2 * k + 1 : part * NEAR + 2 * k + 2, at] for one in parts for k in range(NEAR)]
        count = jnp.concatenate(count, axis=1)
        high = count.astype(BF16).astype(F32)
        counts = jnp.where(iota((16, count.shape[1]), 0) < 8, high, count - high).astype(BF16)
        found = dot(jnp.concatenate([gathered(parts, part, at), counts], axis=0), same)
        size = found[2 * part : 2 * part + 1] + found[2 * part + 8 : 2 * part + 9]
        inverse = 1.0 / jnp.maximum(size, 1.0)
        scale[t] = jnp.broadcast_to(inverse, scale.shape[1:])
        spread_out((found[:part] + found[part : 2 * part]) * inverse, mean, part, at)

    each_tile(slots, tile)
    for k in range(NEAR):
        cut = slice(part * k, part * (k + 1))
        both = jnp.concatenate(split(mean[cut]), axis=0)
        change = dot(both, pairs[k][0])
        change = change[:part] + change[part:]
        sums[cut] = parts[0][cut] + (change[:, :slots] + change[:, slots:])


def tables_kernel(pad, mask_ids, mean, spread, workers, *sends):
    part = mean.shape[0] // NEAR
    for k, send in enumerate(sends):
        send[...] = mean[part * k : part * (k + 1)]
    slots, width = spread.shape
    table = jnp.concatenate([same_worker(pad, 256)] * 2, axis=0)
    for b in range(width // BLOCK):
        found = one_hot(row(mask_ids, b, BLOCK), slots)
        spread[:, b * BLOCK : (b + 1) * BLOCK] = found
        for at in range(0, BLOCK, 256):
            count = dot(found[:, at : at + 256], table[:256])
            workers[:, b * BLOCK + at : b * BLOCK + at + 256] = count.astype(BF16)


def means_kernel(far, part, kept, *refs):
    parts, source, scale, sends, mean = refs[:far], refs[far:-7], refs[-7], refs[-5:-1], refs[-1]

    def tile(t, at):
        same = [table[t] if kept else same_firm(source[0], table, part, at) for table in source]
        same = jnp.concatenate(same, axis=0)
        found = dot(gathered(parts, part, at), same)
        spread_out((found[:part] + found[part:]) * scale[t][:1], mean, part, at)

    each_tile(mean.shape[1], tile)
    for k, send in enumerate(sends):
        send[...] = mean[part * k : part * (k + 1)]


def own_means(parts, means):
    me = lax.axis_index("rows") % NEAR
    part = parts[0].shape[0]
    for step, one in zip(NEAR_STEPS, parts):
        means[pl.ds(pl.multiple_of((me ^ step) * part, part), part), :] = one[...]
    return jnp.concatenate(split(means[...]), axis=0)


def first_kernel(pad, *refs):
    parts, (x1, mask_ids, weight), tables, (y, means) = refs[:NEAR], refs[NEAR : NEAR + 3], refs[NEAR + 3 : -2], refs[-2:]
    columns, slots = means.shape
    first = own_means(parts, means)
    table = jnp.concatenate([same_worker(pad, 256)] * 2, axis=0)
    for b in range(y.shape[1] // BLOCK):
        at = slice(b * BLOCK, (b + 1) * BLOCK)
        found = tables[0][:, at] if tables else one_hot(row(mask_ids, b, BLOCK), slots)
        spread = dot(first, found)
        spread = spread[:columns] + spread[columns:]
        if tables:
            worker = dot(first, tables[1][:, at])
            worker = worker[:columns] + worker[columns:]
        else:
            worker = by_worker(spread, table)
        y[:, at] = x1[:, at] - spread + worker * row(weight, b, BLOCK)


def last_kernel(*refs):
    parts, (before, mask_ids), tables, (out, means, y, sems) = refs[:NEAR], refs[NEAR : NEAR + 2], refs[NEAR + 2 : -4], refs[-4:]
    outs = column_copies(y, out, sems)
    columns, slots = means.shape
    second = own_means(parts, means)
    for b in range(len(outs)):
        at = slice(b * BLOCK, (b + 1) * BLOCK)
        found = tables[0][:, at] if tables else one_hot(row(mask_ids, b, BLOCK), slots)
        spread = dot(second, found)
        y[:, at] = before[:, at] - (spread[:columns] + spread[columns:])
        outs[b].start()
    wait_all(outs)


def near_exchange(parts, n):
    steps = [[(i, i ^ step) for i in range(n)] for step in NEAR_STEPS[1:]]
    return [parts[0]] + [lax.ppermute(one, "rows", step) for one, step in zip(parts[1:], steps)]


def far_share(one, n):
    order = sorted(range(1, n // NEAR), key=lambda k: k == 2)
    steps = [[(i, i ^ (k * NEAR)) for i in range(n)] for k in order]
    return [one] + [lax.ppermute(one, "rows", step) for step in steps]


def in_hbm(x):
    return pltpu.with_memory_space_constraint(x, pltpu.HBM)


def call(kernel, out_shape, in_specs, out_specs, scratch, flops, moved):
    return pl.pallas_call(
        kernel,
        out_shape=out_shape,
        in_specs=in_specs,
        out_specs=out_specs,
        scratch_shapes=scratch,
        compiler_params=pltpu.CompilerParams(vmem_limit_bytes=VMEM_BYTES),
        cost_estimate=pl.CostEstimate(flops=flops, bytes_accessed=moved, transcendentals=0),
    )


def body(probes, worker_len, spell_to_slot, slot_to_firm, *, n):
    columns, rows_dev = probes.shape
    workers = worker_len.shape[0]
    pad = rows_dev // workers
    slots = slot_to_firm.shape[0]
    tiles = slots // LANES
    part = columns // NEAR
    far = n // NEAR
    keep = tiles * NEAR * n * LANES * LANES * 2 <= 8 * 1024 * 1024
    blocks = rows_dev // BLOCK
    vmem, hbm = pl.BlockSpec(memory_space=pltpu.VMEM), pl.BlockSpec(memory_space=pltpu.HBM)
    lengths = worker_len.reshape(workers // LANES, LANES)
    ids = spell_to_slot.reshape(rows_dev // LANES, LANES)
    firms = slot_to_firm.reshape(tiles, LANES)
    array = jax.ShapeDtypeStruct
    of_rows = (rows_dev // LANES, LANES)
    work = 2 * rows_dev * slots * 2 * columns
    sems = pltpu.SemaphoreType.DMA((blocks,))
    whole = (columns, rows_dev)
    about = part + 8
    message = array((about + rows_dev // slots, slots), F32)
    of_near = array((columns, slots), F32)

    *sends, x1, mask_ids, weight = call(
        functools.partial(sums_kernel, pad, slots // n),
        [message] * 3 + [array((about, slots), F32), array(whole, F32), array(of_rows, jnp.int32), array(of_rows, F32)],
        [hbm] * 4,
        [vmem] * (NEAR + 3),
        [
            pltpu.VMEM(of_rows, F32),
            pltpu.VMEM(whole, F32),
            pltpu.VMEM((columns, slots), F32),
            pltpu.VMEM(lengths.shape, jnp.int32),
            pltpu.VMEM(ids.shape, jnp.int32),
            pltpu.VMEM(firms.shape, jnp.int32),
            sems,
            pltpu.SemaphoreType.DMA((3,)),
        ],
        2 * work,
        4 * columns * rows_dev,
    )(in_hbm(probes), in_hbm(lengths), in_hbm(ids), in_hbm(firms))

    def pair_counts(parts):
        return call(
            functools.partial(pairs_kernel, pad, about),
            array((len(parts), slots, 2 * slots), BF16),
            [vmem] * len(parts),
            vmem,
            [
                pltpu.VMEM((len(parts), *of_rows), F32),
                pltpu.VMEM((len(parts), 8, slots), F32),
                pltpu.VMEM((len(parts), slots, workers), BF16),
            ],
            work * len(parts) // 4,
            4 * slots * slots,
        )(*parts)

    arrived = near_exchange(sends, n)
    pairs = [pair_counts(arrived[:1]), pair_counts(arrived[1:2])]
    joined = call(
        functools.partial(join_kernel, part),
        array((columns + 2 * NEAR, slots), F32),
        [vmem] * (NEAR + 2),
        vmem,
        [],
        0,
        message.size * 8,
    )(*arrived, *pairs)
    shared = far_share(joined, n)
    tables, passed = [], arrived[2]
    table = array((tiles, NEAR * LANES, NEAR * LANES), BF16)

    def firm_table(one, passed, out):
        return call(
            functools.partial(firms_kernel, part),
            out,
            [vmem] * 3,
            [vmem] * len(out),
            [],
            work // 64,
            tiles * (NEAR * LANES) ** 2 * 2,
        )(joined, one, passed)

    if keep:
        first_table, passed = firm_table(joined, passed, [table, message])
        tables = [first_table, *firm_table(shared[-1], first_table, [table])]
    passed = lax.ppermute(passed, "rows", [(i, i ^ 1) for i in range(n)])
    pairs += [pair_counts(arrived[2:3]), pair_counts([passed])]
    scale = array((tiles, 8, NEAR * LANES), F32)
    made = [table] * (far - 2) * keep
    mean, sums, scales, *made = call(
        functools.partial(change_kernel, far, part, len(tables)),
        [of_near, of_near, scale, *made],
        [vmem] * (far + len(tables) + len(pairs)),
        [vmem] * (3 + len(made)),
        [],
        work // 4,
        slots * slots * 4,
    )(*shared, *tables, *pairs)
    again = far_share(sums, n)
    source = [tables[0], *made, tables[1]] if keep else shared
    spreads = []
    sends = [mean[part * k : part * (k + 1)] for k in range(NEAR)]
    if keep:
        *spreads, a, b, c, d = call(
            functools.partial(tables_kernel, pad),
            [array((slots, rows_dev), BF16)] * 2 + [array((part, slots), F32)] * NEAR,
            [vmem] * 2,
            [vmem] * (2 + NEAR),
            [],
            work,
            4 * slots * rows_dev,
        )(mask_ids, mean)
        sends = [a, b, c, d]
    first = near_exchange(sends, n)
    sends = call(
        functools.partial(means_kernel, far, part, keep),
        [array((part, slots), F32)] * NEAR,
        [vmem] * (far + len(source) + 2),
        [vmem] * NEAR,
        [pltpu.VMEM((columns, slots), F32)],
        work // 4,
        slots * slots * 4,
    )(*again, *source, scales, spreads[1] if keep else scales)
    arrived = near_exchange(sends, n)
    before = call(
        functools.partial(first_kernel, pad),
        array(whole, F32),
        [vmem] * (NEAR + 3 + len(spreads)),
        vmem,
        [pltpu.VMEM((columns, slots), F32)],
        work,
        8 * columns * rows_dev,
    )(*first, x1, mask_ids, weight, *spreads)
    return call(
        last_kernel,
        array(whole, F32),
        [vmem] * (NEAR + 2 + len(spreads[:1])),
        hbm,
        [pltpu.VMEM((columns, slots), F32), pltpu.VMEM(whole, F32), sems],
        work,
        8 * columns * rows_dev,
    )(*arrived, before, mask_ids, *spreads[:1])


def solution(mesh):
    placed = (P(None, ("grp", "rows")), P(("grp", "rows")), P(("grp", "rows")), P(("grp", "rows")))
    return jax.shard_map(
        functools.partial(body, n=mesh.shape["rows"]),
        mesh=mesh,
        in_specs=placed,
        out_specs=P(None, ("grp", "rows")),
        check_vma=False,
    )
```

```python
import functools

import jax
import jax.numpy as jnp
from jax import lax
from jax.experimental import pallas as pl
from jax.experimental.pallas import tpu as pltpu
from jax.sharding import PartitionSpec as P

FIRMS_PER_SHARD = 1024
LANES = 128
BLOCK = 1024
VMEM_BYTES = 32 * 1024 * 1024
NEAR = 4
F32, BF16 = jnp.float32, jnp.bfloat16
NT = (((1,), (1,)), ((), ()))
NN = (((1,), (0,)), ((), ()))


def dot(a, b, dims=NN):
    return lax.dot_general(a, b, dims, preferred_element_type=F32)


def iota(shape, dim):
    return lax.broadcasted_iota(jnp.int32, shape, dim)


def split(x):
    hi = x.astype(BF16)
    return hi, (x - hi.astype(F32)).astype(BF16)


def row(ref, block, size):
    per = size // LANES
    return jnp.concatenate([ref[block * per + k : block * per + k + 1, :] for k in range(per)], axis=1)


def one_hot(ids, slots):
    kind = BF16 if slots <= 256 else F32
    slot = iota((slots, LANES), 0).astype(F32).astype(kind)
    ids = ids.astype(F32).astype(kind)
    one, zero = jnp.ones((slots, LANES), kind), jnp.zeros((slots, LANES), kind)
    parts = [jnp.where(slot == ids[:, k : k + LANES], one, zero) for k in range(0, ids.shape[1], LANES)]
    return jnp.concatenate(parts, axis=1).astype(BF16)


def one_hot_down(columns, slots):
    kind = BF16 if slots <= 256 else F32
    one, zero = jnp.ones((LANES, LANES), kind), jnp.zeros((LANES, LANES), kind)
    along_slots = [(iota((LANES, LANES), 1) + at).astype(F32).astype(kind) for at in range(0, slots, LANES)]
    parts, columns = [], columns.astype(kind)
    for k in range(columns.shape[1]):
        ids = jnp.broadcast_to(columns[:, k : k + 1], (LANES, LANES))
        parts.append(jnp.concatenate([jnp.where(slot == ids, one, zero) for slot in along_slots], axis=1))
    return jnp.concatenate(parts, axis=0).astype(BF16)


def same_worker(pad, width):
    return (iota((width, width), 0) // pad == iota((width, width), 1) // pad).astype(F32).astype(BF16)


def by_worker(x, table):
    rows, width = x.shape
    step = table.shape[1]
    both = [
        jnp.concatenate([one[:, k : k + step] for k in range(0, width, step)], axis=0) for one in split(x)
    ]
    total = dot(jnp.concatenate(both, axis=1), table)
    return jnp.concatenate([total[k : k + rows] for k in range(0, total.shape[0], rows)], axis=1)


def start_all(copies):
    for copy in copies:
        copy.start()


def wait_all(copies):
    for copy in copies:
        copy.wait()


def column_copies(source, target, sems, size=BLOCK):
    width = source.shape[1]
    cuts = [pl.ds(start, size) for start in range(0, width, size)]
    return [pltpu.make_async_copy(source.at[:, cut], target.at[:, cut], sems.at[b]) for b, cut in enumerate(cuts)]


def row_lengths(lengths, pad):
    total_rows = lengths.shape[0] * pad
    here = iota((total_rows, LANES), 0)
    lane = iota((total_rows, LANES), 1)
    wide = jnp.broadcast_to(lengths.astype(F32)[:, None, :], (lengths.shape[0], pad, LANES)).reshape(total_rows, LANES)
    per = LANES // pad
    wide = jnp.where(lane // per == here % pad, wide, 0.0).astype(BF16)
    spread = (iota((LANES, LANES), 0) % per == iota((LANES, LANES), 1) // pad).astype(F32).astype(BF16)
    row_len = dot(wide, spread)
    return row_len, (lane % pad).astype(F32) < row_len


def near_index(n):
    me = lax.axis_index("rows")
    return me % 2 + 2 * (me // (n // 2))


def along(ref):
    return jnp.concatenate([ref[k : k + 1, :] for k in range(ref.shape[0])], axis=1)


def sums_kernel(pad, n, *refs):
    (probes, lengths_in, ids_in, firms_in), sends, refs = refs[:4], refs[4 : 4 + NEAR], refs[4 + NEAR :]
    x1, mask_ids, weight, valid, x, sums, lengths, ids, firms, sems, small = refs
    copies = column_copies(probes, x, sems)
    first = [
        pltpu.make_async_copy(source, target, small.at[k])
        for k, (source, target) in enumerate(((lengths_in, lengths), (ids_in, ids), (firms_in, firms)))
    ]
    start_all(first)
    start_all(copies)
    columns, slots = sums.shape
    part = columns // NEAR
    me = near_index(n)
    wait_all(first)
    row_len, inside = row_lengths(lengths[...], pad)
    valid[...] = jnp.where(inside, 1.0, 0.0)
    weight[...] = jnp.where(inside, 1.0 / row_len, 0.0)
    masked = jnp.where(inside, ids[...], -1)
    mask_ids[...] = masked
    turned = jnp.concatenate([masked.astype(F32)] * (LANES // masked.shape[0]), axis=0).T
    keys = (iota((1, slots), 1) // (slots // n) * FIRMS_PER_SHARD + along(firms)).astype(F32)
    across = slots // LANES
    rows = ids.shape[0] // across
    masked = jnp.concatenate([masked[k * rows : (k + 1) * rows] for k in range(across)], axis=1).astype(F32)
    for send in sends[:3]:
        send[part + 8 :] = masked

    table = jnp.concatenate([same_worker(pad, 256)] * 2, axis=0)
    wait_all(copies)
    total = None
    for b in range(len(copies)):
        ok = row(valid, b, BLOCK)
        x0 = x[:, b * BLOCK : (b + 1) * BLOCK] * ok
        rest = x0 - by_worker(x0, table) * row(weight, b, BLOCK)
        x1[:, b * BLOCK : (b + 1) * BLOCK] = rest
        counted = jnp.broadcast_to(ok, (16, BLOCK)).astype(BF16)
        data = jnp.concatenate([*split(rest), counted], axis=0)
        per = BLOCK // LANES
        block = dot(data, one_hot_down(turned[:, b * per : (b + 1) * per], slots))
        total = block if total is None else total + block
    sums[...] = total[:columns] + total[columns : 2 * columns]
    about = jnp.where(iota((8, slots), 0) == 0, keys, total[2 * columns : 2 * columns + 1])
    for step, send in enumerate(sends):
        send[:part] = sums[pl.ds(pl.multiple_of((me ^ step) * part, part), part), :]
        send[part : part + 8] = about


def join_kernel(part, *refs):
    parts, out = refs[:NEAR], refs[-1]
    for k, one in enumerate(parts):
        out[part * k : part * (k + 1)] = one[:part]
        out[part * NEAR + 2 * k : part * NEAR + 2 * k + 2] = one[part : part + 2]


def pairs_kernel(pad, start, *refs):
    parts, (out, ids, size, counts) = refs[:-4], refs[-4:]
    slots = out.shape[1]
    kind = BF16 if slots <= 256 else F32
    per = LANES // pad
    total_rows = ids.shape[1]
    across = slots // LANES
    rows = total_rows // across
    for k, part in enumerate(parts):
        size[k] = jnp.broadcast_to(part[start - 7 : start - 6], (8, slots))
        for at in range(across):
            ids[k, at * rows : (at + 1) * rows] = part[start:, at * LANES : (at + 1) * LANES]
    at = iota((LANES, pad * LANES), 1)
    deal = (iota((LANES, pad * LANES), 0) == at % per * pad + at // LANES).astype(F32).astype(BF16)
    mine = iota((total_rows, pad * LANES), 1) % LANES // per == iota((total_rows, pad * LANES), 0) % pad
    slot = iota((slots, LANES), 0).astype(F32).astype(kind)
    one, zero = jnp.ones((slots, LANES), kind), jnp.zeros((slots, LANES), kind)
    diagonal = iota((slots, slots), 1) == iota((slots, slots), 0)

    def device(k, carry):
        dealt = dot(jnp.concatenate(split(ids[k]), axis=0), deal)
        dealt = jnp.where(mine, dealt[:total_rows] + dealt[total_rows:], 0.0)
        dealt = jnp.sum(dealt.reshape(total_rows // pad, pad, pad * LANES), axis=1)
        spells = dealt.astype(kind)
        for g in range(total_rows // pad):
            total = zero
            for j in range(pad):
                total += jnp.where(slot == spells[g : g + 1, j * LANES : (j + 1) * LANES], one, zero)
            counts[k, :, g * LANES : (g + 1) * LANES] = total.astype(BF16)
        valid = jnp.where(dealt >= 0.0, 1.0, 0.0)
        length = valid[:, :LANES]
        for j in range(1, pad):
            length += valid[:, j * LANES : (j + 1) * LANES]
        inverse = 1.0 / length
        inverse = jnp.concatenate([inverse[g : g + 1] for g in range(total_rows // pad)], axis=1)
        here = counts[k]
        total = dot(jnp.concatenate(split(here.astype(F32) * inverse), axis=0), here, NT)
        total = total[:slots] + total[slots:] - jnp.where(diagonal, size[k, :1], 0.0)
        hi, lo = split(total)
        out[k, :, :slots] = hi
        out[k, :, slots:] = lo
        return carry

    lax.fori_loop(0, len(parts), device, 0, unroll=len(parts) if slots <= 256 else 1)


def same_firm(own, one, part, at):
    mine, keys = ([ref[part * NEAR + 2 * k : part * NEAR + 2 * k + 1, at] for k in range(NEAR)] for ref in (own, one))
    mine = jnp.concatenate(mine, axis=1)
    down = jnp.concatenate([jnp.broadcast_to(key, (8, LANES)) for key in keys], axis=0).T
    found = [(down[:, 8 * k : 8 * k + 1] == mine).astype(F32).astype(BF16) for k in range(NEAR)]
    return jnp.concatenate(found, axis=0)


def each_tile(slots, do):
    tiles = slots // LANES
    if tiles <= 2:
        for t in range(tiles):
            do(t, slice(t * LANES, (t + 1) * LANES))
    else:
        lax.fori_loop(0, tiles, lambda t, c: (do(t, pl.ds(pl.multiple_of(t * LANES, LANES), LANES)), c)[1], 0)


def firms_kernel(part, own, one, passed, out, *copy):
    for ref in copy:
        ref[...] = passed[...]
    each_tile(own.shape[1], lambda t, at: out.__setitem__(t, same_firm(own, one, part, at)))


def gathered(parts, part, at):
    data = [one[part * k : part * (k + 1), at] for one in parts for k in range(NEAR)]
    return jnp.concatenate(split(jnp.concatenate(data, axis=1)), axis=0)


def spread_out(means, out, part, at):
    for k in range(NEAR):
        out[part * k : part * (k + 1), at] = means[:, k * LANES : (k + 1) * LANES]


def change_kernel(far, part, ready, *refs):
    tables, pairs, refs = refs[far : far + ready], refs[far + ready : far + ready + NEAR], refs
    parts, (mean, sums, scale), made = refs[:far], refs[far + ready + NEAR :][:3], refs[far + ready + NEAR + 3 :]
    slots = mean.shape[1]

    def tile(t, at):
        if tables:
            between = [same_firm(parts[0], one, part, at) for one in parts[1:-1]]
            for ref, one in zip(made, between):
                ref[t] = one
            same = [tables[0][t], *between, tables[1][t]]
        else:
            same = [same_firm(parts[0], one, part, at) for one in parts]
        same = jnp.concatenate(same, axis=0)
        count = [one[part * NEAR + 2 * k + 1 : part * NEAR + 2 * k + 2, at] for one in parts for k in range(NEAR)]
        count = jnp.concatenate(count, axis=1)
        high = count.astype(BF16).astype(F32)
        counts = jnp.where(iota((16, count.shape[1]), 0) < 8, high, count - high).astype(BF16)
        found = dot(jnp.concatenate([gathered(parts, part, at), counts], axis=0), same)
        size = found[2 * part : 2 * part + 1] + found[2 * part + 8 : 2 * part + 9]
        inverse = 1.0 / jnp.maximum(size, 1.0)
        scale[t] = jnp.broadcast_to(inverse, scale.shape[1:])
        spread_out((found[:part] + found[part : 2 * part]) * inverse, mean, part, at)

    each_tile(slots, tile)
    for k in range(NEAR):
        cut = slice(part * k, part * (k + 1))
        both = jnp.concatenate(split(mean[cut]), axis=0)
        change = dot(both, pairs[k][0])
        change = change[:part] + change[part:]
        sums[cut] = parts[0][cut] + (change[:, :slots] + change[:, slots:])


def tables_kernel(pad, mask_ids, mean, spread, workers, *sends):
    part = mean.shape[0] // NEAR
    for k, send in enumerate(sends):
        send[...] = mean[part * k : part * (k + 1)]
    slots, width = spread.shape
    table = jnp.concatenate([same_worker(pad, 256)] * 2, axis=0)
    for b in range(width // BLOCK):
        found = one_hot(row(mask_ids, b, BLOCK), slots)
        spread[:, b * BLOCK : (b + 1) * BLOCK] = found
        for at in range(0, BLOCK, 256):
            count = dot(found[:, at : at + 256], table[:256])
            workers[:, b * BLOCK + at : b * BLOCK + at + 256] = count.astype(BF16)


def means_kernel(far, part, kept, *refs):
    parts, source, scale, sends, mean = refs[:far], refs[far:-7], refs[-7], refs[-5:-1], refs[-1]

    def tile(t, at):
        same = [table[t] if kept else same_firm(source[0], table, part, at) for table in source]
        same = jnp.concatenate(same, axis=0)
        found = dot(gathered(parts, part, at), same)
        spread_out((found[:part] + found[part:]) * scale[t][:1], mean, part, at)

    each_tile(mean.shape[1], tile)
    for k, send in enumerate(sends):
        send[...] = mean[part * k : part * (k + 1)]


def own_means(n, parts, means):
    me = near_index(n)
    part = parts[0].shape[0]
    for step, one in enumerate(parts):
        means[pl.ds(pl.multiple_of((me ^ step) * part, part), part), :] = one[...]
    return jnp.concatenate(split(means[...]), axis=0)


def first_kernel(pad, n, *refs):
    parts, (x1, mask_ids, weight), tables, (y, means) = refs[:NEAR], refs[NEAR : NEAR + 3], refs[NEAR + 3 : -2], refs[-2:]
    columns, slots = means.shape
    first = own_means(n, parts, means)
    table = jnp.concatenate([same_worker(pad, 256)] * 2, axis=0)
    for b in range(y.shape[1] // BLOCK):
        at = slice(b * BLOCK, (b + 1) * BLOCK)
        found = tables[0][:, at] if tables else one_hot(row(mask_ids, b, BLOCK), slots)
        spread = dot(first, found)
        spread = spread[:columns] + spread[columns:]
        if tables:
            worker = dot(first, tables[1][:, at])
            worker = worker[:columns] + worker[columns:]
        else:
            worker = by_worker(spread, table)
        y[:, at] = x1[:, at] - spread + worker * row(weight, b, BLOCK)


def last_kernel(n, *refs):
    parts, (before, mask_ids), tables, (out, means, y, sems) = refs[:NEAR], refs[NEAR : NEAR + 2], refs[NEAR + 2 : -4], refs[-4:]
    outs = column_copies(y, out, sems)
    columns, slots = means.shape
    second = own_means(n, parts, means)
    for b in range(len(outs)):
        at = slice(b * BLOCK, (b + 1) * BLOCK)
        found = tables[0][:, at] if tables else one_hot(row(mask_ids, b, BLOCK), slots)
        spread = dot(second, found)
        y[:, at] = before[:, at] - (spread[:columns] + spread[columns:])
        outs[b].start()
    wait_all(outs)


def near_exchange(parts, n):
    steps = [[(i, i ^ step) for i in range(n)] for step in (1, n // 2, n // 2 + 1)]
    return [parts[0]] + [lax.ppermute(one, "rows", step) for one, step in zip(parts[1:], steps)]


def far_share(one, n):
    steps = [[(i, i ^ (2 * k)) for i in range(n)] for k in range(1, n // NEAR)]
    return [one] + [lax.ppermute(one, "rows", step) for step in steps]


def in_hbm(x):
    return pltpu.with_memory_space_constraint(x, pltpu.HBM)


def call(kernel, out_shape, in_specs, out_specs, scratch, flops, moved):
    return pl.pallas_call(
        kernel,
        out_shape=out_shape,
        in_specs=in_specs,
        out_specs=out_specs,
        scratch_shapes=scratch,
        compiler_params=pltpu.CompilerParams(vmem_limit_bytes=VMEM_BYTES),
        cost_estimate=pl.CostEstimate(flops=flops, bytes_accessed=moved, transcendentals=0),
    )


def body(probes, worker_len, spell_to_slot, slot_to_firm, *, n):
    columns, rows_dev = probes.shape
    workers = worker_len.shape[0]
    pad = rows_dev // workers
    slots = slot_to_firm.shape[0]
    tiles = slots // LANES
    part = columns // NEAR
    far = n // NEAR
    keep = tiles * NEAR * n * LANES * LANES * 2 <= 8 * 1024 * 1024
    blocks = rows_dev // BLOCK
    vmem, hbm = pl.BlockSpec(memory_space=pltpu.VMEM), pl.BlockSpec(memory_space=pltpu.HBM)
    lengths = worker_len.reshape(workers // LANES, LANES)
    ids = spell_to_slot.reshape(rows_dev // LANES, LANES)
    firms = slot_to_firm.reshape(tiles, LANES)
    array = jax.ShapeDtypeStruct
    of_rows = (rows_dev // LANES, LANES)
    work = 2 * rows_dev * slots * 2 * columns
    sems = pltpu.SemaphoreType.DMA((blocks,))
    whole = (columns, rows_dev)
    about = part + 8
    message = array((about + rows_dev // slots, slots), F32)
    of_near = array((columns, slots), F32)

    *sends, x1, mask_ids, weight = call(
        functools.partial(sums_kernel, pad, n),
        [message] * 3 + [array((about, slots), F32), array(whole, F32), array(of_rows, jnp.int32), array(of_rows, F32)],
        [hbm] * 4,
        [vmem] * (NEAR + 3),
        [
            pltpu.VMEM(of_rows, F32),
            pltpu.VMEM(whole, F32),
            pltpu.VMEM((columns, slots), F32),
            pltpu.VMEM(lengths.shape, jnp.int32),
            pltpu.VMEM(ids.shape, jnp.int32),
            pltpu.VMEM(firms.shape, jnp.int32),
            sems,
            pltpu.SemaphoreType.DMA((3,)),
        ],
        2 * work,
        4 * columns * rows_dev,
    )(in_hbm(probes), in_hbm(lengths), in_hbm(ids), in_hbm(firms))

    def pair_counts(parts):
        return call(
            functools.partial(pairs_kernel, pad, about),
            array((len(parts), slots, 2 * slots), BF16),
            [vmem] * len(parts),
            vmem,
            [
                pltpu.VMEM((len(parts), *of_rows), F32),
                pltpu.VMEM((len(parts), 8, slots), F32),
                pltpu.VMEM((len(parts), slots, workers), BF16),
            ],
            work * len(parts) // 4,
            4 * slots * slots,
        )(*parts)

    arrived = near_exchange(sends, n)
    pairs = [pair_counts(arrived[:1]), pair_counts(arrived[1:2])]
    joined = call(
        functools.partial(join_kernel, part),
        array((columns + 2 * NEAR, slots), F32),
        [vmem] * (NEAR + 2),
        vmem,
        [],
        0,
        message.size * 8,
    )(*arrived, *pairs)
    shared = far_share(joined, n)
    tables, passed = [], arrived[2]
    table = array((tiles, NEAR * LANES, NEAR * LANES), BF16)

    def firm_table(one, passed, out):
        return call(
            functools.partial(firms_kernel, part),
            out,
            [vmem] * 3,
            [vmem] * len(out),
            [],
            work // 64,
            tiles * (NEAR * LANES) ** 2 * 2,
        )(joined, one, passed)

    if keep:
        first_table, passed = firm_table(joined, passed, [table, message])
        tables = [first_table, *firm_table(shared[-1], first_table, [table])]
    passed = lax.ppermute(passed, "rows", [(i, i ^ 1) for i in range(n)])
    pairs += [pair_counts(arrived[2:3]), pair_counts([passed])]
    scale = array((tiles, 8, NEAR * LANES), F32)
    made = [table] * (far - 2) * keep
    mean, sums, scales, *made = call(
        functools.partial(change_kernel, far, part, len(tables)),
        [of_near, of_near, scale, *made],
        [vmem] * (far + len(tables) + len(pairs)),
        [vmem] * (3 + len(made)),
        [],
        work // 4,
        slots * slots * 4,
    )(*shared, *tables, *pairs)
    again = far_share(sums, n)
    source = [tables[0], *made, tables[1]] if keep else shared
    spreads = []
    sends = [mean[part * k : part * (k + 1)] for k in range(NEAR)]
    if keep:
        *spreads, a, b, c, d = call(
            functools.partial(tables_kernel, pad),
            [array((slots, rows_dev), BF16)] * 2 + [array((part, slots), F32)] * NEAR,
            [vmem] * 2,
            [vmem] * (2 + NEAR),
            [],
            work,
            4 * slots * rows_dev,
        )(mask_ids, mean)
        sends = [a, b, c, d]
    first = near_exchange(sends, n)
    sends = call(
        functools.partial(means_kernel, far, part, keep),
        [array((part, slots), F32)] * NEAR,
        [vmem] * (far + len(source) + 2),
        [vmem] * NEAR,
        [pltpu.VMEM((columns, slots), F32)],
        work // 4,
        slots * slots * 4,
    )(*again, *source, scales, spreads[1] if keep else scales)
    arrived = near_exchange(sends, n)
    before = call(
        functools.partial(first_kernel, pad, n),
        array(whole, F32),
        [vmem] * (NEAR + 3 + len(spreads)),
        vmem,
        [pltpu.VMEM((columns, slots), F32)],
        work,
        8 * columns * rows_dev,
    )(*first, x1, mask_ids, weight, *spreads)
    return call(
        functools.partial(last_kernel, n),
        array(whole, F32),
        [vmem] * (NEAR + 2 + len(spreads[:1])),
        hbm,
        [pltpu.VMEM((columns, slots), F32), pltpu.VMEM(whole, F32), sems],
        work,
        8 * columns * rows_dev,
    )(*arrived, before, mask_ids, *spreads[:1])


def solution(mesh):
    placed = (P(None, ("grp", "rows")), P(("grp", "rows")), P(("grp", "rows")), P(("grp", "rows")))
    return jax.shard_map(
        functools.partial(body, n=mesh.shape["rows"]),
        mesh=mesh,
        in_specs=placed,
        out_specs=P(None, ("grp", "rows")),
        check_vma=False,
    )
```

```python
import functools

import jax
import jax.numpy as jnp
from jax import lax
from jax.experimental import pallas as pl
from jax.experimental.pallas import tpu as pltpu
from jax.sharding import PartitionSpec as P

FIRMS_PER_SHARD = 1024
LANES = 128
BLOCK = 1024
VMEM_BYTES = 32 * 1024 * 1024
NEAR = 4
NEAR_STEPS = (0, 1, 2, 3)
F32, BF16 = jnp.float32, jnp.bfloat16
NT = (((1,), (1,)), ((), ()))
NN = (((1,), (0,)), ((), ()))


def dot(a, b, dims=NN):
    return lax.dot_general(a, b, dims, preferred_element_type=F32)


def iota(shape, dim):
    return lax.broadcasted_iota(jnp.int32, shape, dim)


def split(x):
    hi = x.astype(BF16)
    return hi, (x - hi.astype(F32)).astype(BF16)


def row(ref, block, size):
    per = size // LANES
    return jnp.concatenate([ref[block * per + k : block * per + k + 1, :] for k in range(per)], axis=1)


def one_hot(ids, slots):
    kind = BF16 if slots <= 256 else F32
    slot = iota((slots, LANES), 0).astype(F32).astype(kind)
    ids = ids.astype(F32).astype(kind)
    one, zero = jnp.ones((slots, LANES), kind), jnp.zeros((slots, LANES), kind)
    parts = [jnp.where(slot == ids[:, k : k + LANES], one, zero) for k in range(0, ids.shape[1], LANES)]
    return jnp.concatenate(parts, axis=1).astype(BF16)


def one_hot_down(columns, slots):
    kind = BF16 if slots <= 256 else F32
    one, zero = jnp.ones((LANES, LANES), kind), jnp.zeros((LANES, LANES), kind)
    along_slots = [(iota((LANES, LANES), 1) + at).astype(F32).astype(kind) for at in range(0, slots, LANES)]
    parts, columns = [], columns.astype(kind)
    for k in range(columns.shape[1]):
        ids = jnp.broadcast_to(columns[:, k : k + 1], (LANES, LANES))
        parts.append(jnp.concatenate([jnp.where(slot == ids, one, zero) for slot in along_slots], axis=1))
    return jnp.concatenate(parts, axis=0).astype(BF16)


def same_worker(pad, width):
    return (iota((width, width), 0) // pad == iota((width, width), 1) // pad).astype(F32).astype(BF16)


def by_worker(x, table):
    rows, width = x.shape
    step = table.shape[1]
    both = [
        jnp.concatenate([one[:, k : k + step] for k in range(0, width, step)], axis=0) for one in split(x)
    ]
    total = dot(jnp.concatenate(both, axis=1), table)
    return jnp.concatenate([total[k : k + rows] for k in range(0, total.shape[0], rows)], axis=1)


def start_all(copies):
    for copy in copies:
        copy.start()


def wait_all(copies):
    for copy in copies:
        copy.wait()


def column_copies(source, target, sems, size=BLOCK):
    width = source.shape[1]
    cuts = [pl.ds(start, size) for start in range(0, width, size)]
    return [pltpu.make_async_copy(source.at[:, cut], target.at[:, cut], sems.at[b]) for b, cut in enumerate(cuts)]


def row_lengths(lengths, pad):
    total_rows = lengths.shape[0] * pad
    here = iota((total_rows, LANES), 0)
    lane = iota((total_rows, LANES), 1)
    wide = jnp.broadcast_to(lengths.astype(F32)[:, None, :], (lengths.shape[0], pad, LANES)).reshape(total_rows, LANES)
    per = LANES // pad
    wide = jnp.where(lane // per == here % pad, wide, 0.0).astype(BF16)
    spread = (iota((LANES, LANES), 0) % per == iota((LANES, LANES), 1) // pad).astype(F32).astype(BF16)
    row_len = dot(wide, spread)
    return row_len, (lane % pad).astype(F32) < row_len


def along(ref):
    return jnp.concatenate([ref[k : k + 1, :] for k in range(ref.shape[0])], axis=1)


def sums_kernel(pad, cap, *refs):
    (probes, lengths_in, ids_in, firms_in), sends, refs = refs[:4], refs[4 : 4 + NEAR], refs[4 + NEAR :]
    x1, mask_ids, weight, valid, x, sums, lengths, ids, firms, bands_sem, small = refs
    bands = [pl.ds(at, 8) for at in range(0, x.shape[0], 8)]
    copies = [pltpu.make_async_copy(probes.at[at], x.at[at], bands_sem.at[b]) for b, at in enumerate(bands)]
    first = [
        pltpu.make_async_copy(source, target, small.at[k])
        for k, (source, target) in enumerate(((lengths_in, lengths), (ids_in, ids), (firms_in, firms)))
    ]
    start_all(first)
    start_all(copies)
    columns, slots = sums.shape
    part = columns // NEAR
    me = lax.axis_index("rows") % NEAR
    wait_all(first)
    row_len, inside = row_lengths(lengths[...], pad)
    valid[...] = jnp.where(inside, 1.0, 0.0)
    weight[...] = jnp.where(inside, 1.0 / row_len, 0.0)
    masked = jnp.where(inside, ids[...], -1)
    mask_ids[...] = masked
    turned = jnp.concatenate([masked.astype(F32)] * (LANES // masked.shape[0]), axis=0).T
    keys = (iota((1, slots), 1) // cap * FIRMS_PER_SHARD + along(firms)).astype(F32)
    across = slots // LANES
    rows = ids.shape[0] // across
    masked = jnp.concatenate([masked[k * rows : (k + 1) * rows] for k in range(across)], axis=1).astype(F32)
    for send in sends[:3]:
        send[part + 8 :] = masked

    table = jnp.concatenate([same_worker(pad, 256)] * 2, axis=0)
    wait_all(copies)
    total = None
    for b in range(x.shape[1] // BLOCK):
        ok = row(valid, b, BLOCK)
        x0 = x[:, b * BLOCK : (b + 1) * BLOCK] * ok
        rest = x0 - by_worker(x0, table) * row(weight, b, BLOCK)
        x1[:, b * BLOCK : (b + 1) * BLOCK] = rest
        counted = jnp.broadcast_to(ok, (16, BLOCK)).astype(BF16)
        data = jnp.concatenate([*split(rest), counted], axis=0)
        per = BLOCK // LANES
        block = dot(data, one_hot_down(turned[:, b * per : (b + 1) * per], slots))
        total = block if total is None else total + block
    sums[...] = total[:columns] + total[columns : 2 * columns]
    about = jnp.where(iota((8, slots), 0) == 0, keys, total[2 * columns : 2 * columns + 1])
    for step, send in zip(NEAR_STEPS, sends):
        send[:part] = sums[pl.ds(pl.multiple_of((me ^ step) * part, part), part), :]
        send[part : part + 8] = about


def join_kernel(part, *refs):
    parts, out = refs[:NEAR], refs[-1]
    for k, one in enumerate(parts):
        out[part * k : part * (k + 1)] = one[:part]
        out[part * NEAR + 2 * k : part * NEAR + 2 * k + 2] = one[part : part + 2]


def pairs_kernel(pad, start, *refs):
    parts, (out, ids, size, counts) = refs[:-4], refs[-4:]
    slots = out.shape[1]
    kind = BF16 if slots <= 256 else F32
    per = LANES // pad
    total_rows = ids.shape[1]
    across = slots // LANES
    rows = total_rows // across
    for k, part in enumerate(parts):
        size[k] = jnp.broadcast_to(part[start - 7 : start - 6], (8, slots))
        for at in range(across):
            ids[k, at * rows : (at + 1) * rows] = part[start:, at * LANES : (at + 1) * LANES]
    at = iota((LANES, pad * LANES), 1)
    deal = (iota((LANES, pad * LANES), 0) == at % per * pad + at // LANES).astype(F32).astype(BF16)
    mine = iota((total_rows, pad * LANES), 1) % LANES // per == iota((total_rows, pad * LANES), 0) % pad
    slot = iota((slots, LANES), 0).astype(F32).astype(kind)
    one, zero = jnp.ones((slots, LANES), kind), jnp.zeros((slots, LANES), kind)
    diagonal = iota((slots, slots), 1) == iota((slots, slots), 0)

    def device(k, carry):
        dealt = dot(jnp.concatenate(split(ids[k]), axis=0), deal)
        dealt = jnp.where(mine, dealt[:total_rows] + dealt[total_rows:], 0.0)
        dealt = jnp.sum(dealt.reshape(total_rows // pad, pad, pad * LANES), axis=1)
        spells = dealt.astype(kind)
        for g in range(total_rows // pad):
            total = zero
            for j in range(pad):
                total += jnp.where(slot == spells[g : g + 1, j * LANES : (j + 1) * LANES], one, zero)
            counts[k, :, g * LANES : (g + 1) * LANES] = total.astype(BF16)
        valid = jnp.where(dealt >= 0.0, 1.0, 0.0)
        length = valid[:, :LANES]
        for j in range(1, pad):
            length += valid[:, j * LANES : (j + 1) * LANES]
        inverse = 1.0 / length
        inverse = jnp.concatenate([inverse[g : g + 1] for g in range(total_rows // pad)], axis=1)
        here = counts[k]
        total = dot(jnp.concatenate(split(here.astype(F32) * inverse), axis=0), here, NT)
        total = total[:slots] + total[slots:] - jnp.where(diagonal, size[k, :1], 0.0)
        hi, lo = split(total)
        out[k, :, :slots] = hi
        out[k, :, slots:] = lo
        return carry

    lax.fori_loop(0, len(parts), device, 0, unroll=len(parts) if slots <= 256 else 1)


def same_firm(own, one, part, at):
    mine, keys = ([ref[part * NEAR + 2 * k : part * NEAR + 2 * k + 1, at] for k in range(NEAR)] for ref in (own, one))
    mine = jnp.concatenate(mine, axis=1)
    down = jnp.concatenate([jnp.broadcast_to(key, (8, LANES)) for key in keys], axis=0).T
    found = [(down[:, 8 * k : 8 * k + 1] == mine).astype(F32).astype(BF16) for k in range(NEAR)]
    return jnp.concatenate(found, axis=0)


def each_tile(slots, do):
    tiles = slots // LANES
    if tiles <= 2:
        for t in range(tiles):
            do(t, slice(t * LANES, (t + 1) * LANES))
    else:
        lax.fori_loop(0, tiles, lambda t, c: (do(t, pl.ds(pl.multiple_of(t * LANES, LANES), LANES)), c)[1], 0)


def firms_kernel(part, own, one, passed, out, *copy):
    for ref in copy:
        ref[...] = passed[...]
    each_tile(own.shape[1], lambda t, at: out.__setitem__(t, same_firm(own, one, part, at)))


def gathered(parts, part, at):
    data = [one[part * k : part * (k + 1), at] for one in parts for k in range(NEAR)]
    return jnp.concatenate(split(jnp.concatenate(data, axis=1)), axis=0)


def spread_out(means, out, part, at):
    for k in range(NEAR):
        out[part * k : part * (k + 1), at] = means[:, k * LANES : (k + 1) * LANES]


def change_kernel(far, part, ready, *refs):
    tables, pairs, refs = refs[far : far + ready], refs[far + ready : far + ready + NEAR], refs
    parts, (mean, sums, scale), made = refs[:far], refs[far + ready + NEAR :][:3], refs[far + ready + NEAR + 3 :]
    slots = mean.shape[1]

    def tile(t, at):
        if tables:
            between = [same_firm(parts[0], one, part, at) for one in parts[1:-1]]
            for ref, one in zip(made, between):
                ref[t] = one
            same = [tables[0][t], *between, tables[1][t]]
        else:
            same = [same_firm(parts[0], one, part, at) for one in parts]
        same = jnp.concatenate(same, axis=0)
        count = [one[part * NEAR + 2 * k + 1 : part * NEAR + 2 * k + 2, at] for one in parts for k in range(NEAR)]
        count = jnp.concatenate(count, axis=1)
        high = count.astype(BF16).astype(F32)
        counts = jnp.where(iota((16, count.shape[1]), 0) < 8, high, count - high).astype(BF16)
        found = dot(jnp.concatenate([gathered(parts, part, at), counts], axis=0), same)
        size = found[2 * part : 2 * part + 1] + found[2 * part + 8 : 2 * part + 9]
        inverse = 1.0 / jnp.maximum(size, 1.0)
        scale[t] = jnp.broadcast_to(inverse, scale.shape[1:])
        spread_out((found[:part] + found[part : 2 * part]) * inverse, mean, part, at)

    each_tile(slots, tile)
    for k in range(NEAR):
        cut = slice(part * k, part * (k + 1))
        both = jnp.concatenate(split(mean[cut]), axis=0)
        change = dot(both, pairs[k][0])
        change = change[:part] + change[part:]
        sums[cut] = parts[0][cut] + (change[:, :slots] + change[:, slots:])


def tables_kernel(pad, mask_ids, mean, spread, workers, *sends):
    part = mean.shape[0] // NEAR
    for k, send in enumerate(sends):
        send[...] = mean[part * k : part * (k + 1)]
    slots, width = spread.shape
    table = jnp.concatenate([same_worker(pad, 256)] * 2, axis=0)
    for b in range(width // BLOCK):
        found = one_hot(row(mask_ids, b, BLOCK), slots)
        spread[:, b * BLOCK : (b + 1) * BLOCK] = found
        for at in range(0, BLOCK, 256):
            count = dot(found[:, at : at + 256], table[:256])
            workers[:, b * BLOCK + at : b * BLOCK + at + 256] = count.astype(BF16)


def means_kernel(far, part, kept, *refs):
    parts, source, scale, sends, mean = refs[:far], refs[far:-7], refs[-7], refs[-5:-1], refs[-1]

    def tile(t, at):
        same = [table[t] if kept else same_firm(source[0], table, part, at) for table in source]
        same = jnp.concatenate(same, axis=0)
        found = dot(gathered(parts, part, at), same)
        spread_out((found[:part] + found[part:]) * scale[t][:1], mean, part, at)

    each_tile(mean.shape[1], tile)
    for k, send in enumerate(sends):
        send[...] = mean[part * k : part * (k + 1)]


def own_means(parts, means):
    me = lax.axis_index("rows") % NEAR
    part = parts[0].shape[0]
    for step, one in zip(NEAR_STEPS, parts):
        means[pl.ds(pl.multiple_of((me ^ step) * part, part), part), :] = one[...]
    return jnp.concatenate(split(means[...]), axis=0)


def first_kernel(pad, *refs):
    parts, (x1, mask_ids, weight), tables, (y, means) = refs[:NEAR], refs[NEAR : NEAR + 3], refs[NEAR + 3 : -2], refs[-2:]
    columns, slots = means.shape
    first = own_means(parts, means)
    table = jnp.concatenate([same_worker(pad, 256)] * 2, axis=0)
    for b in range(y.shape[1] // BLOCK):
        at = slice(b * BLOCK, (b + 1) * BLOCK)
        found = tables[0][:, at] if tables else one_hot(row(mask_ids, b, BLOCK), slots)
        spread = dot(first, found)
        spread = spread[:columns] + spread[columns:]
        if tables:
            worker = dot(first, tables[1][:, at])
            worker = worker[:columns] + worker[columns:]
        else:
            worker = by_worker(spread, table)
        y[:, at] = x1[:, at] - spread + worker * row(weight, b, BLOCK)


def last_kernel(*refs):
    parts, (before, mask_ids), tables, (out, means, y, sems) = refs[:NEAR], refs[NEAR : NEAR + 2], refs[NEAR + 2 : -4], refs[-4:]
    outs = column_copies(y, out, sems)
    columns, slots = means.shape
    second = own_means(parts, means)
    for b in range(len(outs)):
        at = slice(b * BLOCK, (b + 1) * BLOCK)
        found = tables[0][:, at] if tables else one_hot(row(mask_ids, b, BLOCK), slots)
        spread = dot(second, found)
        y[:, at] = before[:, at] - (spread[:columns] + spread[columns:])
        outs[b].start()
    wait_all(outs)


def near_exchange(parts, n):
    steps = [[(i, i ^ step) for i in range(n)] for step in NEAR_STEPS[1:]]
    return [parts[0]] + [lax.ppermute(one, "rows", step) for one, step in zip(parts[1:], steps)]


def far_share(one, n):
    steps = [[(i, i ^ (k * NEAR)) for i in range(n)] for k in range(1, n // NEAR)]
    return [one] + [lax.ppermute(one, "rows", step) for step in steps]


def in_hbm(x):
    return pltpu.with_memory_space_constraint(x, pltpu.HBM)


def call(kernel, out_shape, in_specs, out_specs, scratch, flops, moved):
    return pl.pallas_call(
        kernel,
        out_shape=out_shape,
        in_specs=in_specs,
        out_specs=out_specs,
        scratch_shapes=scratch,
        compiler_params=pltpu.CompilerParams(vmem_limit_bytes=VMEM_BYTES),
        cost_estimate=pl.CostEstimate(flops=flops, bytes_accessed=moved, transcendentals=0),
    )


def body(probes, worker_len, spell_to_slot, slot_to_firm, *, n):
    columns, rows_dev = probes.shape
    workers = worker_len.shape[0]
    pad = rows_dev // workers
    slots = slot_to_firm.shape[0]
    tiles = slots // LANES
    part = columns // NEAR
    far = n // NEAR
    keep = tiles * NEAR * n * LANES * LANES * 2 <= 8 * 1024 * 1024
    blocks = rows_dev // BLOCK
    vmem, hbm = pl.BlockSpec(memory_space=pltpu.VMEM), pl.BlockSpec(memory_space=pltpu.HBM)
    lengths = worker_len.reshape(workers // LANES, LANES)
    ids = spell_to_slot.reshape(rows_dev // LANES, LANES)
    firms = slot_to_firm.reshape(tiles, LANES)
    array = jax.ShapeDtypeStruct
    of_rows = (rows_dev // LANES, LANES)
    work = 2 * rows_dev * slots * 2 * columns
    sems = pltpu.SemaphoreType.DMA((blocks,))
    whole = (columns, rows_dev)
    about = part + 8
    message = array((about + rows_dev // slots, slots), F32)
    of_near = array((columns, slots), F32)

    *sends, x1, mask_ids, weight = call(
        functools.partial(sums_kernel, pad, slots // n),
        [message] * 3 + [array((about, slots), F32), array(whole, F32), array(of_rows, jnp.int32), array(of_rows, F32)],
        [hbm] * 4,
        [vmem] * (NEAR + 3),
        [
            pltpu.VMEM(of_rows, F32),
            pltpu.VMEM(whole, F32),
            pltpu.VMEM((columns, slots), F32),
            pltpu.VMEM(lengths.shape, jnp.int32),
            pltpu.VMEM(ids.shape, jnp.int32),
            pltpu.VMEM(firms.shape, jnp.int32),
            pltpu.SemaphoreType.DMA((columns // 8,)),
            pltpu.SemaphoreType.DMA((3,)),
        ],
        2 * work,
        4 * columns * rows_dev,
    )(in_hbm(probes), in_hbm(lengths), in_hbm(ids), in_hbm(firms))

    def pair_counts(parts):
        return call(
            functools.partial(pairs_kernel, pad, about),
            array((len(parts), slots, 2 * slots), BF16),
            [vmem] * len(parts),
            vmem,
            [
                pltpu.VMEM((len(parts), *of_rows), F32),
                pltpu.VMEM((len(parts), 8, slots), F32),
                pltpu.VMEM((len(parts), slots, workers), BF16),
            ],
            work * len(parts) // 4,
            4 * slots * slots,
        )(*parts)

    arrived = near_exchange(sends, n)
    pairs = [pair_counts(arrived[:1]), pair_counts(arrived[1:2])]
    joined = call(
        functools.partial(join_kernel, part),
        array((columns + 2 * NEAR, slots), F32),
        [vmem] * (NEAR + 2),
        vmem,
        [],
        0,
        message.size * 8,
    )(*arrived, *pairs)
    shared = far_share(joined, n)
    tables, passed = [], arrived[2]
    table = array((tiles, NEAR * LANES, NEAR * LANES), BF16)

    def firm_table(one, passed, out):
        return call(
            functools.partial(firms_kernel, part),
            out,
            [vmem] * 3,
            [vmem] * len(out),
            [],
            work // 64,
            tiles * (NEAR * LANES) ** 2 * 2,
        )(joined, one, passed)

    if keep:
        first_table, passed = firm_table(joined, passed, [table, message])
        tables = [first_table, *firm_table(shared[-1], first_table, [table])]
    passed = lax.ppermute(passed, "rows", [(i, i ^ 1) for i in range(n)])
    pairs += [pair_counts(arrived[2:3]), pair_counts([passed])]
    scale = array((tiles, 8, NEAR * LANES), F32)
    made = [table] * (far - 2) * keep
    mean, sums, scales, *made = call(
        functools.partial(change_kernel, far, part, len(tables)),
        [of_near, of_near, scale, *made],
        [vmem] * (far + len(tables) + len(pairs)),
        [vmem] * (3 + len(made)),
        [],
        work // 4,
        slots * slots * 4,
    )(*shared, *tables, *pairs)
    again = far_share(sums, n)
    source = [tables[0], *made, tables[1]] if keep else shared
    spreads = []
    sends = [mean[part * k : part * (k + 1)] for k in range(NEAR)]
    if keep:
        *spreads, a, b, c, d = call(
            functools.partial(tables_kernel, pad),
            [array((slots, rows_dev), BF16)] * 2 + [array((part, slots), F32)] * NEAR,
            [vmem] * 2,
            [vmem] * (2 + NEAR),
            [],
            work,
            4 * slots * rows_dev,
        )(mask_ids, mean)
        sends = [a, b, c, d]
    first = near_exchange(sends, n)
    sends = call(
        functools.partial(means_kernel, far, part, keep),
        [array((part, slots), F32)] * NEAR,
        [vmem] * (far + len(source) + 2),
        [vmem] * NEAR,
        [pltpu.VMEM((columns, slots), F32)],
        work // 4,
        slots * slots * 4,
    )(*again, *source, scales, spreads[1] if keep else scales)
    arrived = near_exchange(sends, n)
    before = call(
        functools.partial(first_kernel, pad),
        array(whole, F32),
        [vmem] * (NEAR + 3 + len(spreads)),
        vmem,
        [pltpu.VMEM((columns, slots), F32)],
        work,
        8 * columns * rows_dev,
    )(*first, x1, mask_ids, weight, *spreads)
    return call(
        last_kernel,
        array(whole, F32),
        [vmem] * (NEAR + 2 + len(spreads[:1])),
        hbm,
        [pltpu.VMEM((columns, slots), F32), pltpu.VMEM(whole, F32), sems],
        work,
        8 * columns * rows_dev,
    )(*arrived, before, mask_ids, *spreads[:1])


def solution(mesh):
    placed = (P(None, ("grp", "rows")), P(("grp", "rows")), P(("grp", "rows")), P(("grp", "rows")))
    return jax.shard_map(
        functools.partial(body, n=mesh.shape["rows"]),
        mesh=mesh,
        in_specs=placed,
        out_specs=P(None, ("grp", "rows")),
        check_vma=False,
    )
```

```python
import functools

import jax
import jax.numpy as jnp
from jax import lax
from jax.experimental import pallas as pl
from jax.experimental.pallas import tpu as pltpu
from jax.sharding import PartitionSpec as P

FIRMS_PER_SHARD = 1024
LANES = 128
BLOCK = 1024
VMEM_BYTES = 32 * 1024 * 1024
NEAR = 4
NEAR_STEPS = (0, 1, 2, 3)
F32, BF16 = jnp.float32, jnp.bfloat16
NT = (((1,), (1,)), ((), ()))
NN = (((1,), (0,)), ((), ()))


def dot(a, b, dims=NN):
    return lax.dot_general(a, b, dims, preferred_element_type=F32)


def iota(shape, dim):
    return lax.broadcasted_iota(jnp.int32, shape, dim)


def split(x):
    hi = x.astype(BF16)
    return hi, (x - hi.astype(F32)).astype(BF16)


def row(ref, block, size):
    per = size // LANES
    return jnp.concatenate([ref[block * per + k : block * per + k + 1, :] for k in range(per)], axis=1)


def one_hot(ids, slots):
    kind = BF16 if slots <= 256 else F32
    slot = iota((slots, LANES), 0).astype(F32).astype(kind)
    ids = ids.astype(F32).astype(kind)
    one, zero = jnp.ones((slots, LANES), kind), jnp.zeros((slots, LANES), kind)
    parts = [jnp.where(slot == ids[:, k : k + LANES], one, zero) for k in range(0, ids.shape[1], LANES)]
    return jnp.concatenate(parts, axis=1).astype(BF16)


def one_hot_down(columns, slots):
    kind = BF16 if slots <= 256 else F32
    one, zero = jnp.ones((LANES, LANES), kind), jnp.zeros((LANES, LANES), kind)
    along_slots = [(iota((LANES, LANES), 1) + at).astype(F32).astype(kind) for at in range(0, slots, LANES)]
    parts, columns = [], columns.astype(kind)
    for k in range(columns.shape[1]):
        ids = jnp.broadcast_to(columns[:, k : k + 1], (LANES, LANES))
        parts.append(jnp.concatenate([jnp.where(slot == ids, one, zero) for slot in along_slots], axis=1))
    return jnp.concatenate(parts, axis=0).astype(BF16)


def same_worker(pad, width):
    return (iota((width, width), 0) // pad == iota((width, width), 1) // pad).astype(F32).astype(BF16)


def by_worker(x, table):
    rows, width = x.shape
    step = table.shape[1]
    both = [
        jnp.concatenate([one[:, k : k + step] for k in range(0, width, step)], axis=0) for one in split(x)
    ]
    total = dot(jnp.concatenate(both, axis=1), table)
    return jnp.concatenate([total[k : k + rows] for k in range(0, total.shape[0], rows)], axis=1)


def start_all(copies):
    for copy in copies:
        copy.start()


def wait_all(copies):
    for copy in copies:
        copy.wait()


def column_copies(source, target, sems, size=BLOCK):
    width = source.shape[1]
    cuts = [pl.ds(start, size) for start in range(0, width, size)]
    return [pltpu.make_async_copy(source.at[:, cut], target.at[:, cut], sems.at[b]) for b, cut in enumerate(cuts)]


def row_lengths(lengths, pad):
    total_rows = lengths.shape[0] * pad
    here = iota((total_rows, LANES), 0)
    lane = iota((total_rows, LANES), 1)
    wide = jnp.broadcast_to(lengths.astype(F32)[:, None, :], (lengths.shape[0], pad, LANES)).reshape(total_rows, LANES)
    per = LANES // pad
    wide = jnp.where(lane // per == here % pad, wide, 0.0).astype(BF16)
    spread = (iota((LANES, LANES), 0) % per == iota((LANES, LANES), 1) // pad).astype(F32).astype(BF16)
    row_len = dot(wide, spread)
    return row_len, (lane % pad).astype(F32) < row_len


def along(ref):
    return jnp.concatenate([ref[k : k + 1, :] for k in range(ref.shape[0])], axis=1)


def sums_kernel(pad, cap, *refs):
    (probes, lengths_in, ids_in, firms_in), sends, slots_out = refs[:4], refs[4 : 4 + NEAR], refs[4 + NEAR]
    refs = refs[5 + NEAR :]
    x1, mask_ids, weight, valid, x, sums, lengths, ids, firms, bands_sem, small = refs
    bands = [pl.ds(at, 8) for at in range(0, x.shape[0], 8)]
    copies = [pltpu.make_async_copy(probes.at[at], x.at[at], bands_sem.at[b]) for b, at in enumerate(bands)]
    first = [
        pltpu.make_async_copy(source, target, small.at[k])
        for k, (source, target) in enumerate(((lengths_in, lengths), (ids_in, ids), (firms_in, firms)))
    ]
    start_all(first)
    start_all(copies)
    columns, slots = sums.shape
    part = columns // NEAR
    me = lax.axis_index("rows") % NEAR
    wait_all(first)
    row_len, inside = row_lengths(lengths[...], pad)
    valid[...] = jnp.where(inside, 1.0, 0.0)
    weight[...] = jnp.where(inside, 1.0 / row_len, 0.0)
    masked = jnp.where(inside, ids[...], -1)
    mask_ids[...] = masked
    turned = jnp.concatenate([masked.astype(F32)] * (LANES // masked.shape[0]), axis=0).T
    keys = (iota((1, slots), 1) // cap * FIRMS_PER_SHARD + along(firms)).astype(F32)
    across = slots // LANES
    rows = ids.shape[0] // across
    masked = jnp.concatenate([masked[k * rows : (k + 1) * rows] for k in range(across)], axis=1).astype(F32)
    sends[1][part + 8 :] = masked
    slots_out[8:] = masked

    table = jnp.concatenate([same_worker(pad, 256)] * 2, axis=0)
    wait_all(copies)
    total = None
    for b in range(x.shape[1] // BLOCK):
        ok = row(valid, b, BLOCK)
        x0 = x[:, b * BLOCK : (b + 1) * BLOCK] * ok
        rest = x0 - by_worker(x0, table) * row(weight, b, BLOCK)
        x1[:, b * BLOCK : (b + 1) * BLOCK] = rest
        counted = jnp.broadcast_to(ok, (16, BLOCK)).astype(BF16)
        data = jnp.concatenate([*split(rest), counted], axis=0)
        per = BLOCK // LANES
        block = dot(data, one_hot_down(turned[:, b * per : (b + 1) * per], slots))
        total = block if total is None else total + block
    sums[...] = total[:columns] + total[columns : 2 * columns]
    about = jnp.where(iota((8, slots), 0) == 0, keys, total[2 * columns : 2 * columns + 1])
    for step, send in zip(NEAR_STEPS, sends):
        send[:part] = sums[pl.ds(pl.multiple_of((me ^ step) * part, part), part), :]
        send[part : part + 8] = about
    slots_out[:8] = about


def join_kernel(part, *refs):
    parts, out = refs[:NEAR], refs[-1]
    for k, one in enumerate(parts):
        out[part * k : part * (k + 1)] = one[:part]
        out[part * NEAR + 2 * k : part * NEAR + 2 * k + 2] = one[part : part + 2]


def pairs_kernel(pad, start, several, *refs):
    parts, (out, *copy, ids, size, counts) = refs[:several], refs[several:]
    for ref in copy:
        ref[...] = parts[0][...]
    slots = out.shape[1]
    kind = BF16 if slots <= 256 else F32
    per = LANES // pad
    total_rows = ids.shape[1]
    across = slots // LANES
    rows = total_rows // across
    for k, part in enumerate(parts):
        size[k] = jnp.broadcast_to(part[start - 7 : start - 6], (8, slots))
        for at in range(across):
            ids[k, at * rows : (at + 1) * rows] = part[start:, at * LANES : (at + 1) * LANES]
    at = iota((LANES, pad * LANES), 1)
    deal = (iota((LANES, pad * LANES), 0) == at % per * pad + at // LANES).astype(F32).astype(BF16)
    mine = iota((total_rows, pad * LANES), 1) % LANES // per == iota((total_rows, pad * LANES), 0) % pad
    slot = iota((slots, LANES), 0).astype(F32).astype(kind)
    one, zero = jnp.ones((slots, LANES), kind), jnp.zeros((slots, LANES), kind)
    diagonal = iota((slots, slots), 1) == iota((slots, slots), 0)

    def device(k, carry):
        dealt = dot(jnp.concatenate(split(ids[k]), axis=0), deal)
        dealt = jnp.where(mine, dealt[:total_rows] + dealt[total_rows:], 0.0)
        dealt = jnp.sum(dealt.reshape(total_rows // pad, pad, pad * LANES), axis=1)
        spells = dealt.astype(kind)
        for g in range(total_rows // pad):
            total = zero
            for j in range(pad):
                total += jnp.where(slot == spells[g : g + 1, j * LANES : (j + 1) * LANES], one, zero)
            counts[k, :, g * LANES : (g + 1) * LANES] = total.astype(BF16)
        valid = jnp.where(dealt >= 0.0, 1.0, 0.0)
        length = valid[:, :LANES]
        for j in range(1, pad):
            length += valid[:, j * LANES : (j + 1) * LANES]
        inverse = 1.0 / length
        inverse = jnp.concatenate([inverse[g : g + 1] for g in range(total_rows // pad)], axis=1)
        here = counts[k]
        total = dot(jnp.concatenate(split(here.astype(F32) * inverse), axis=0), here, NT)
        total = total[:slots] + total[slots:] - jnp.where(diagonal, size[k, :1], 0.0)
        hi, lo = split(total)
        out[k, :, :slots] = hi
        out[k, :, slots:] = lo
        return carry

    lax.fori_loop(0, len(parts), device, 0, unroll=len(parts) if slots <= 256 else 1)


def same_firm(own, one, part, at):
    mine, keys = ([ref[part * NEAR + 2 * k : part * NEAR + 2 * k + 1, at] for k in range(NEAR)] for ref in (own, one))
    mine = jnp.concatenate(mine, axis=1)
    down = jnp.concatenate([jnp.broadcast_to(key, (8, LANES)) for key in keys], axis=0).T
    found = [(down[:, 8 * k : 8 * k + 1] == mine).astype(F32).astype(BF16) for k in range(NEAR)]
    return jnp.concatenate(found, axis=0)


def each_tile(slots, do):
    tiles = slots // LANES
    if tiles <= 2:
        for t in range(tiles):
            do(t, slice(t * LANES, (t + 1) * LANES))
    else:
        lax.fori_loop(0, tiles, lambda t, c: (do(t, pl.ds(pl.multiple_of(t * LANES, LANES), LANES)), c)[1], 0)


def firms_kernel(part, own, one, passed, out, *copy):
    for ref in copy:
        ref[...] = passed[...]
    each_tile(own.shape[1], lambda t, at: out.__setitem__(t, same_firm(own, one, part, at)))


def gathered(parts, part, at):
    data = [one[part * k : part * (k + 1), at] for one in parts for k in range(NEAR)]
    return jnp.concatenate(split(jnp.concatenate(data, axis=1)), axis=0)


def spread_out(means, out, part, at):
    for k in range(NEAR):
        out[part * k : part * (k + 1), at] = means[:, k * LANES : (k + 1) * LANES]


def change_kernel(far, part, ready, *refs):
    tables, pairs, refs = refs[far : far + ready], refs[far + ready : far + ready + NEAR], refs
    parts, (mean, sums, scale), made = refs[:far], refs[far + ready + NEAR :][:3], refs[far + ready + NEAR + 3 :]
    slots = mean.shape[1]

    def tile(t, at):
        if tables:
            between = [same_firm(parts[0], one, part, at) for one in parts[1:-1]]
            for ref, one in zip(made, between):
                ref[t] = one
            same = [tables[0][t], *between, tables[1][t]]
        else:
            same = [same_firm(parts[0], one, part, at) for one in parts]
        same = jnp.concatenate(same, axis=0)
        count = [one[part * NEAR + 2 * k + 1 : part * NEAR + 2 * k + 2, at] for one in parts for k in range(NEAR)]
        count = jnp.concatenate(count, axis=1)
        high = count.astype(BF16).astype(F32)
        counts = jnp.where(iota((16, count.shape[1]), 0) < 8, high, count - high).astype(BF16)
        found = dot(jnp.concatenate([gathered(parts, part, at), counts], axis=0), same)
        size = found[2 * part : 2 * part + 1] + found[2 * part + 8 : 2 * part + 9]
        inverse = 1.0 / jnp.maximum(size, 1.0)
        scale[t] = jnp.broadcast_to(inverse, scale.shape[1:])
        spread_out((found[:part] + found[part : 2 * part]) * inverse, mean, part, at)

    each_tile(slots, tile)
    for k in range(NEAR):
        cut = slice(part * k, part * (k + 1))
        both = jnp.concatenate(split(mean[cut]), axis=0)
        change = dot(both, pairs[k][0])
        change = change[:part] + change[part:]
        sums[cut] = parts[0][cut] + (change[:, :slots] + change[:, slots:])


def tables_kernel(pad, mask_ids, mean, spread, workers, *sends):
    part = mean.shape[0] // NEAR
    for k, send in enumerate(sends):
        send[...] = mean[part * k : part * (k + 1)]
    slots, width = spread.shape
    table = jnp.concatenate([same_worker(pad, 256)] * 2, axis=0)
    for b in range(width // BLOCK):
        found = one_hot(row(mask_ids, b, BLOCK), slots)
        spread[:, b * BLOCK : (b + 1) * BLOCK] = found
        for at in range(0, BLOCK, 256):
            count = dot(found[:, at : at + 256], table[:256])
            workers[:, b * BLOCK + at : b * BLOCK + at + 256] = count.astype(BF16)


def means_kernel(far, part, kept, *refs):
    parts, source, scale, sends, mean = refs[:far], refs[far:-7], refs[-7], refs[-5:-1], refs[-1]

    def tile(t, at):
        same = [table[t] if kept else same_firm(source[0], table, part, at) for table in source]
        same = jnp.concatenate(same, axis=0)
        found = dot(gathered(parts, part, at), same)
        spread_out((found[:part] + found[part:]) * scale[t][:1], mean, part, at)

    each_tile(mean.shape[1], tile)
    for k, send in enumerate(sends):
        send[...] = mean[part * k : part * (k + 1)]


def own_means(parts, means):
    me = lax.axis_index("rows") % NEAR
    part = parts[0].shape[0]
    for step, one in zip(NEAR_STEPS, parts):
        means[pl.ds(pl.multiple_of((me ^ step) * part, part), part), :] = one[...]
    return jnp.concatenate(split(means[...]), axis=0)


def first_kernel(pad, *refs):
    parts, (x1, mask_ids, weight), tables, (y, means) = refs[:NEAR], refs[NEAR : NEAR + 3], refs[NEAR + 3 : -2], refs[-2:]
    columns, slots = means.shape
    first = own_means(parts, means)
    table = jnp.concatenate([same_worker(pad, 256)] * 2, axis=0)
    for b in range(y.shape[1] // BLOCK):
        at = slice(b * BLOCK, (b + 1) * BLOCK)
        found = tables[0][:, at] if tables else one_hot(row(mask_ids, b, BLOCK), slots)
        spread = dot(first, found)
        spread = spread[:columns] + spread[columns:]
        if tables:
            worker = dot(first, tables[1][:, at])
            worker = worker[:columns] + worker[columns:]
        else:
            worker = by_worker(spread, table)
        y[:, at] = x1[:, at] - spread + worker * row(weight, b, BLOCK)


def last_kernel(*refs):
    parts, (before, mask_ids), tables, (out, means, y, sems) = refs[:NEAR], refs[NEAR : NEAR + 2], refs[NEAR + 2 : -4], refs[-4:]
    outs = column_copies(y, out, sems)
    columns, slots = means.shape
    second = own_means(parts, means)
    for b in range(len(outs)):
        at = slice(b * BLOCK, (b + 1) * BLOCK)
        found = tables[0][:, at] if tables else one_hot(row(mask_ids, b, BLOCK), slots)
        spread = dot(second, found)
        y[:, at] = before[:, at] - (spread[:columns] + spread[columns:])
        outs[b].start()
    wait_all(outs)


def near_exchange(parts, n):
    steps = [[(i, i ^ step) for i in range(n)] for step in NEAR_STEPS[1:]]
    return [parts[0]] + [lax.ppermute(one, "rows", step) for one, step in zip(parts[1:], steps)]


def far_share(one, n):
    steps = [[(i, i ^ (k * NEAR)) for i in range(n)] for k in range(1, n // NEAR)]
    return [one] + [lax.ppermute(one, "rows", step) for step in steps]


def in_hbm(x):
    return pltpu.with_memory_space_constraint(x, pltpu.HBM)


def call(kernel, out_shape, in_specs, out_specs, scratch, flops, moved):
    return pl.pallas_call(
        kernel,
        out_shape=out_shape,
        in_specs=in_specs,
        out_specs=out_specs,
        scratch_shapes=scratch,
        compiler_params=pltpu.CompilerParams(vmem_limit_bytes=VMEM_BYTES),
        cost_estimate=pl.CostEstimate(flops=flops, bytes_accessed=moved, transcendentals=0),
    )


def body(probes, worker_len, spell_to_slot, slot_to_firm, *, n):
    columns, rows_dev = probes.shape
    workers = worker_len.shape[0]
    pad = rows_dev // workers
    slots = slot_to_firm.shape[0]
    tiles = slots // LANES
    part = columns // NEAR
    far = n // NEAR
    keep = tiles * NEAR * n * LANES * LANES * 2 <= 8 * 1024 * 1024
    blocks = rows_dev // BLOCK
    vmem, hbm = pl.BlockSpec(memory_space=pltpu.VMEM), pl.BlockSpec(memory_space=pltpu.HBM)
    lengths = worker_len.reshape(workers // LANES, LANES)
    ids = spell_to_slot.reshape(rows_dev // LANES, LANES)
    firms = slot_to_firm.reshape(tiles, LANES)
    array = jax.ShapeDtypeStruct
    of_rows = (rows_dev // LANES, LANES)
    work = 2 * rows_dev * slots * 2 * columns
    sems = pltpu.SemaphoreType.DMA((blocks,))
    whole = (columns, rows_dev)
    about = part + 8
    message = array((about + rows_dev // slots, slots), F32)
    short = array((about, slots), F32)
    slots_message = array((message.shape[0] - part, slots), F32)
    of_near = array((columns, slots), F32)

    *sends, own_slots, x1, mask_ids, weight = call(
        functools.partial(sums_kernel, pad, slots // n),
        [short, message, short, short, slots_message, array(whole, F32), array(of_rows, jnp.int32), array(of_rows, F32)],
        [hbm] * 4,
        [vmem] * (NEAR + 4),
        [
            pltpu.VMEM(of_rows, F32),
            pltpu.VMEM(whole, F32),
            pltpu.VMEM((columns, slots), F32),
            pltpu.VMEM(lengths.shape, jnp.int32),
            pltpu.VMEM(ids.shape, jnp.int32),
            pltpu.VMEM(firms.shape, jnp.int32),
            pltpu.SemaphoreType.DMA((columns // 8,)),
            pltpu.SemaphoreType.DMA((3,)),
        ],
        2 * work,
        4 * columns * rows_dev,
    )(in_hbm(probes), in_hbm(lengths), in_hbm(ids), in_hbm(firms))

    def pair_counts(one, start, copy=()):
        return call(
            functools.partial(pairs_kernel, pad, start, 1),
            [array((1, slots, 2 * slots), BF16), *copy],
            [vmem],
            [vmem] * (1 + len(copy)),
            [
                pltpu.VMEM((1, *of_rows), F32),
                pltpu.VMEM((1, 8, slots), F32),
                pltpu.VMEM((1, slots, workers), BF16),
            ],
            work // 4,
            4 * slots * slots,
        )(one)

    def near_step(one, step):
        return lax.ppermute(one, "rows", [(i, i ^ step) for i in range(n)])

    arrived = near_exchange(sends, n)
    own_pairs, own_slots = pair_counts(own_slots, 8, [slots_message])
    passed = near_step(own_slots, 2)
    pairs = [own_pairs]
    joined = call(
        functools.partial(join_kernel, part),
        array((columns + 2 * NEAR, slots), F32),
        [vmem] * (NEAR + 1),
        vmem,
        [],
        0,
        message.size * 8,
    )(*arrived, *pairs)
    shared = far_share(joined, n)
    tables, beside = [], passed
    table = array((tiles, NEAR * LANES, NEAR * LANES), BF16)

    def firm_table(one, passed, out):
        return call(
            functools.partial(firms_kernel, part),
            out,
            [vmem] * 3,
            [vmem] * len(out),
            [],
            work // 64,
            tiles * (NEAR * LANES) ** 2 * 2,
        )(joined, one, passed)

    if keep:
        first_table, beside = firm_table(joined, passed, [table, slots_message])
        tables = [first_table, *firm_table(shared[-1], first_table, [table])]
    pairs += pair_counts(arrived[1], about) + pair_counts(passed, 8) + pair_counts(near_step(beside, 1), 8)
    scale = array((tiles, 8, NEAR * LANES), F32)
    made = [table] * (far - 2) * keep
    mean, sums, scales, *made = call(
        functools.partial(change_kernel, far, part, len(tables)),
        [of_near, of_near, scale, *made],
        [vmem] * (far + len(tables) + len(pairs)),
        [vmem] * (3 + len(made)),
        [],
        work // 4,
        slots * slots * 4,
    )(*shared, *tables, *pairs)
    again = far_share(sums, n)
    source = [tables[0], *made, tables[1]] if keep else shared
    spreads = []
    sends = [mean[part * k : part * (k + 1)] for k in range(NEAR)]
    if keep:
        *spreads, a, b, c, d = call(
            functools.partial(tables_kernel, pad),
            [array((slots, rows_dev), BF16)] * 2 + [array((part, slots), F32)] * NEAR,
            [vmem] * 2,
            [vmem] * (2 + NEAR),
            [],
            work,
            4 * slots * rows_dev,
        )(mask_ids, mean)
        sends = [a, b, c, d]
    first = near_exchange(sends, n)
    sends = call(
        functools.partial(means_kernel, far, part, keep),
        [array((part, slots), F32)] * NEAR,
        [vmem] * (far + len(source) + 2),
        [vmem] * NEAR,
        [pltpu.VMEM((columns, slots), F32)],
        work // 4,
        slots * slots * 4,
    )(*again, *source, scales, spreads[1] if keep else scales)
    arrived = near_exchange(sends, n)
    before = call(
        functools.partial(first_kernel, pad),
        array(whole, F32),
        [vmem] * (NEAR + 3 + len(spreads)),
        vmem,
        [pltpu.VMEM((columns, slots), F32)],
        work,
        8 * columns * rows_dev,
    )(*first, x1, mask_ids, weight, *spreads)
    return call(
        last_kernel,
        array(whole, F32),
        [vmem] * (NEAR + 2 + len(spreads[:1])),
        hbm,
        [pltpu.VMEM((columns, slots), F32), pltpu.VMEM(whole, F32), sems],
        work,
        8 * columns * rows_dev,
    )(*arrived, before, mask_ids, *spreads[:1])


def solution(mesh):
    placed = (P(None, ("grp", "rows")), P(("grp", "rows")), P(("grp", "rows")), P(("grp", "rows")))
    return jax.shard_map(
        functools.partial(body, n=mesh.shape["rows"]),
        mesh=mesh,
        in_specs=placed,
        out_specs=P(None, ("grp", "rows")),
        check_vma=False,
    )
```

```python
import functools

import jax
import jax.numpy as jnp
from jax import lax
from jax.experimental import pallas as pl
from jax.experimental.pallas import tpu as pltpu
from jax.sharding import PartitionSpec as P

FIRMS_PER_SHARD = 1024
LANES = 128
BLOCK = 1024
VMEM_BYTES = 32 * 1024 * 1024
NEAR = 4
NEAR_STEPS = (0, 1, 2, 3)
F32, BF16 = jnp.float32, jnp.bfloat16
NT = (((1,), (1,)), ((), ()))
NN = (((1,), (0,)), ((), ()))


def dot(a, b, dims=NN):
    return lax.dot_general(a, b, dims, preferred_element_type=F32)


def iota(shape, dim):
    return lax.broadcasted_iota(jnp.int32, shape, dim)


def split(x):
    hi = x.astype(BF16)
    return hi, (x - hi.astype(F32)).astype(BF16)


def row(ref, block, size):
    per = size // LANES
    return jnp.concatenate([ref[block * per + k : block * per + k + 1, :] for k in range(per)], axis=1)


def one_hot(ids, slots):
    kind = BF16 if slots <= 256 else F32
    slot = iota((slots, LANES), 0).astype(F32).astype(kind)
    ids = ids.astype(F32).astype(kind)
    one, zero = jnp.ones((slots, LANES), kind), jnp.zeros((slots, LANES), kind)
    parts = [jnp.where(slot == ids[:, k : k + LANES], one, zero) for k in range(0, ids.shape[1], LANES)]
    return jnp.concatenate(parts, axis=1).astype(BF16)


def one_hot_down(columns, slots):
    kind = BF16 if slots <= 256 else F32
    one, zero = jnp.ones((LANES, LANES), kind), jnp.zeros((LANES, LANES), kind)
    along_slots = [(iota((LANES, LANES), 1) + at).astype(F32).astype(kind) for at in range(0, slots, LANES)]
    parts, columns = [], columns.astype(kind)
    for k in range(columns.shape[1]):
        ids = jnp.broadcast_to(columns[:, k : k + 1], (LANES, LANES))
        parts.append(jnp.concatenate([jnp.where(slot == ids, one, zero) for slot in along_slots], axis=1))
    return jnp.concatenate(parts, axis=0).astype(BF16)


def same_worker(pad, width):
    return (iota((width, width), 0) // pad == iota((width, width), 1) // pad).astype(F32).astype(BF16)


def by_worker(x, table):
    rows, width = x.shape
    step = table.shape[1]
    both = [
        jnp.concatenate([one[:, k : k + step] for k in range(0, width, step)], axis=0) for one in split(x)
    ]
    total = dot(jnp.concatenate(both, axis=1), table)
    return jnp.concatenate([total[k : k + rows] for k in range(0, total.shape[0], rows)], axis=1)


def start_all(copies):
    for copy in copies:
        copy.start()


def wait_all(copies):
    for copy in copies:
        copy.wait()


def column_copies(source, target, sems, size=BLOCK):
    width = source.shape[1]
    cuts = [pl.ds(start, size) for start in range(0, width, size)]
    return [pltpu.make_async_copy(source.at[:, cut], target.at[:, cut], sems.at[b]) for b, cut in enumerate(cuts)]


def row_lengths(lengths, pad):
    total_rows = lengths.shape[0] * pad
    here = iota((total_rows, LANES), 0)
    lane = iota((total_rows, LANES), 1)
    wide = jnp.broadcast_to(lengths.astype(F32)[:, None, :], (lengths.shape[0], pad, LANES)).reshape(total_rows, LANES)
    per = LANES // pad
    wide = jnp.where(lane // per == here % pad, wide, 0.0).astype(BF16)
    spread = (iota((LANES, LANES), 0) % per == iota((LANES, LANES), 1) // pad).astype(F32).astype(BF16)
    row_len = dot(wide, spread)
    return row_len, (lane % pad).astype(F32) < row_len


def along(ref):
    return jnp.concatenate([ref[k : k + 1, :] for k in range(ref.shape[0])], axis=1)


def sums_kernel(pad, cap, *refs):
    (probes, lengths_in, ids_in, firms_in), sends, slots_out = refs[:4], refs[4 : 4 + NEAR], refs[4 + NEAR]
    refs = refs[5 + NEAR :]
    x1, mask_ids, weight, valid, x, sums, lengths, ids, firms, bands_sem, small = refs
    bands = [pl.ds(at, 8) for at in range(0, x.shape[0], 8)]
    copies = [pltpu.make_async_copy(probes.at[at], x.at[at], bands_sem.at[b]) for b, at in enumerate(bands)]
    first = [
        pltpu.make_async_copy(source, target, small.at[k])
        for k, (source, target) in enumerate(((lengths_in, lengths), (ids_in, ids), (firms_in, firms)))
    ]
    start_all(first)
    start_all(copies)
    columns, slots = sums.shape
    part = columns // NEAR
    me = lax.axis_index("rows") % NEAR
    wait_all(first)
    row_len, inside = row_lengths(lengths[...], pad)
    valid[...] = jnp.where(inside, 1.0, 0.0)
    weight[...] = jnp.where(inside, 1.0 / row_len, 0.0)
    masked = jnp.where(inside, ids[...], -1)
    mask_ids[...] = masked
    turned = jnp.concatenate([masked.astype(F32)] * (LANES // masked.shape[0]), axis=0).T
    keys = (iota((1, slots), 1) // cap * FIRMS_PER_SHARD + along(firms)).astype(F32)
    across = slots // LANES
    rows = ids.shape[0] // across
    masked = jnp.concatenate([masked[k * rows : (k + 1) * rows] for k in range(across)], axis=1).astype(F32)
    sends[1][part + 8 :] = masked
    slots_out[8:] = masked

    table = jnp.concatenate([same_worker(pad, 256)] * 2, axis=0)
    wait_all(copies)
    total = None
    for b in range(x.shape[1] // BLOCK):
        ok = row(valid, b, BLOCK)
        x0 = x[:, b * BLOCK : (b + 1) * BLOCK] * ok
        rest = x0 - by_worker(x0, table) * row(weight, b, BLOCK)
        x1[:, b * BLOCK : (b + 1) * BLOCK] = rest
        counted = jnp.broadcast_to(ok, (16, BLOCK)).astype(BF16)
        data = jnp.concatenate([*split(rest), counted], axis=0)
        per = BLOCK // LANES
        block = dot(data, one_hot_down(turned[:, b * per : (b + 1) * per], slots))
        total = block if total is None else total + block
    sums[...] = total[:columns] + total[columns : 2 * columns]
    about = jnp.where(iota((8, slots), 0) == 0, keys, total[2 * columns : 2 * columns + 1])
    for step, send in zip(NEAR_STEPS, sends):
        send[:part] = sums[pl.ds(pl.multiple_of((me ^ step) * part, part), part), :]
        send[part : part + 8] = about
    slots_out[:8] = about


def join_kernel(part, *refs):
    parts, out = refs[:NEAR], refs[-1]
    for k, one in enumerate(parts):
        out[part * k : part * (k + 1)] = one[:part]
        out[part * NEAR + 2 * k : part * NEAR + 2 * k + 2] = one[part : part + 2]


def pairs_kernel(pad, several, *refs):
    parts, (out, *copy, ids, size, counts) = refs[:several], refs[several:]
    for ref in copy:
        ref[...] = parts[0][...]
    slots = out.shape[1]
    kind = BF16 if slots <= 256 else F32
    per = LANES // pad
    total_rows = ids.shape[1]
    across = slots // LANES
    rows = total_rows // across
    for k, part in enumerate(parts):
        start = part.shape[0] - rows
        size[k] = jnp.broadcast_to(part[start - 7 : start - 6], (8, slots))
        for at in range(across):
            ids[k, at * rows : (at + 1) * rows] = part[start:, at * LANES : (at + 1) * LANES]
    at = iota((LANES, pad * LANES), 1)
    deal = (iota((LANES, pad * LANES), 0) == at % per * pad + at // LANES).astype(F32).astype(BF16)
    mine = iota((total_rows, pad * LANES), 1) % LANES // per == iota((total_rows, pad * LANES), 0) % pad
    slot = iota((slots, LANES), 0).astype(F32).astype(kind)
    one, zero = jnp.ones((slots, LANES), kind), jnp.zeros((slots, LANES), kind)
    diagonal = iota((slots, slots), 1) == iota((slots, slots), 0)

    def device(k, carry):
        dealt = dot(jnp.concatenate(split(ids[k]), axis=0), deal)
        dealt = jnp.where(mine, dealt[:total_rows] + dealt[total_rows:], 0.0)
        dealt = jnp.sum(dealt.reshape(total_rows // pad, pad, pad * LANES), axis=1)
        spells = dealt.astype(kind)
        for g in range(total_rows // pad):
            total = zero
            for j in range(pad):
                total += jnp.where(slot == spells[g : g + 1, j * LANES : (j + 1) * LANES], one, zero)
            counts[k, :, g * LANES : (g + 1) * LANES] = total.astype(BF16)
        valid = jnp.where(dealt >= 0.0, 1.0, 0.0)
        length = valid[:, :LANES]
        for j in range(1, pad):
            length += valid[:, j * LANES : (j + 1) * LANES]
        inverse = 1.0 / length
        inverse = jnp.concatenate([inverse[g : g + 1] for g in range(total_rows // pad)], axis=1)
        here = counts[k]
        total = dot(jnp.concatenate(split(here.astype(F32) * inverse), axis=0), here, NT)
        total = total[:slots] + total[slots:] - jnp.where(diagonal, size[k, :1], 0.0)
        hi, lo = split(total)
        out[k, :, :slots] = hi
        out[k, :, slots:] = lo
        return carry

    lax.fori_loop(0, len(parts), device, 0, unroll=len(parts) if slots <= 256 else 1)


def same_firm(own, one, part, at):
    mine, keys = ([ref[part * NEAR + 2 * k : part * NEAR + 2 * k + 1, at] for k in range(NEAR)] for ref in (own, one))
    mine = jnp.concatenate(mine, axis=1)
    down = jnp.concatenate([jnp.broadcast_to(key, (8, LANES)) for key in keys], axis=0).T
    found = [(down[:, 8 * k : 8 * k + 1] == mine).astype(F32).astype(BF16) for k in range(NEAR)]
    return jnp.concatenate(found, axis=0)


def each_tile(slots, do):
    tiles = slots // LANES
    if tiles <= 2:
        for t in range(tiles):
            do(t, slice(t * LANES, (t + 1) * LANES))
    else:
        lax.fori_loop(0, tiles, lambda t, c: (do(t, pl.ds(pl.multiple_of(t * LANES, LANES), LANES)), c)[1], 0)


def firms_kernel(part, own, one, passed, out, *copy):
    for ref in copy:
        ref[...] = passed[...]
    each_tile(own.shape[1], lambda t, at: out.__setitem__(t, same_firm(own, one, part, at)))


def gathered(parts, part, at):
    data = [one[part * k : part * (k + 1), at] for one in parts for k in range(NEAR)]
    return jnp.concatenate(split(jnp.concatenate(data, axis=1)), axis=0)


def spread_out(means, out, part, at):
    for k in range(NEAR):
        out[part * k : part * (k + 1), at] = means[:, k * LANES : (k + 1) * LANES]


def change_kernel(far, part, ready, *refs):
    parts, tables, refs = refs[:far], refs[far : far + ready], refs[far + ready :]
    pairs = [(group, k) for group in refs[:3] for k in range(group.shape[0])]
    (mean, sums, scale), made = refs[3:6], refs[6:]
    slots = mean.shape[1]

    def tile(t, at):
        if tables:
            between = [same_firm(parts[0], one, part, at) for one in parts[1:-1]]
            for ref, one in zip(made, between):
                ref[t] = one
            same = [tables[0][t], *between, tables[1][t]]
        else:
            same = [same_firm(parts[0], one, part, at) for one in parts]
        same = jnp.concatenate(same, axis=0)
        count = [one[part * NEAR + 2 * k + 1 : part * NEAR + 2 * k + 2, at] for one in parts for k in range(NEAR)]
        count = jnp.concatenate(count, axis=1)
        high = count.astype(BF16).astype(F32)
        counts = jnp.where(iota((16, count.shape[1]), 0) < 8, high, count - high).astype(BF16)
        found = dot(jnp.concatenate([gathered(parts, part, at), counts], axis=0), same)
        size = found[2 * part : 2 * part + 1] + found[2 * part + 8 : 2 * part + 9]
        inverse = 1.0 / jnp.maximum(size, 1.0)
        scale[t] = jnp.broadcast_to(inverse, scale.shape[1:])
        spread_out((found[:part] + found[part : 2 * part]) * inverse, mean, part, at)

    each_tile(slots, tile)
    for k in range(NEAR):
        cut = slice(part * k, part * (k + 1))
        both = jnp.concatenate(split(mean[cut]), axis=0)
        change = dot(both, pairs[k][0][pairs[k][1]])
        change = change[:part] + change[part:]
        sums[cut] = parts[0][cut] + (change[:, :slots] + change[:, slots:])


def tables_kernel(pad, mask_ids, mean, spread, workers, *sends):
    part = mean.shape[0] // NEAR
    for k, send in enumerate(sends):
        send[...] = mean[part * k : part * (k + 1)]
    slots, width = spread.shape
    table = jnp.concatenate([same_worker(pad, 256)] * 2, axis=0)
    for b in range(width // BLOCK):
        found = one_hot(row(mask_ids, b, BLOCK), slots)
        spread[:, b * BLOCK : (b + 1) * BLOCK] = found
        for at in range(0, BLOCK, 256):
            count = dot(found[:, at : at + 256], table[:256])
            workers[:, b * BLOCK + at : b * BLOCK + at + 256] = count.astype(BF16)


def means_kernel(far, part, kept, *refs):
    parts, source, scale, sends, mean = refs[:far], refs[far:-7], refs[-7], refs[-5:-1], refs[-1]

    def tile(t, at):
        same = [table[t] if kept else same_firm(source[0], table, part, at) for table in source]
        same = jnp.concatenate(same, axis=0)
        found = dot(gathered(parts, part, at), same)
        spread_out((found[:part] + found[part:]) * scale[t][:1], mean, part, at)

    each_tile(mean.shape[1], tile)
    for k, send in enumerate(sends):
        send[...] = mean[part * k : part * (k + 1)]


def own_means(parts, means):
    me = lax.axis_index("rows") % NEAR
    part = parts[0].shape[0]
    for step, one in zip(NEAR_STEPS, parts):
        means[pl.ds(pl.multiple_of((me ^ step) * part, part), part), :] = one[...]
    return jnp.concatenate(split(means[...]), axis=0)


def first_kernel(pad, *refs):
    parts, (x1, mask_ids, weight), tables, (y, means) = refs[:NEAR], refs[NEAR : NEAR + 3], refs[NEAR + 3 : -2], refs[-2:]
    columns, slots = means.shape
    first = own_means(parts, means)
    table = jnp.concatenate([same_worker(pad, 256)] * 2, axis=0)
    for b in range(y.shape[1] // BLOCK):
        at = slice(b * BLOCK, (b + 1) * BLOCK)
        found = tables[0][:, at] if tables else one_hot(row(mask_ids, b, BLOCK), slots)
        spread = dot(first, found)
        spread = spread[:columns] + spread[columns:]
        if tables:
            worker = dot(first, tables[1][:, at])
            worker = worker[:columns] + worker[columns:]
        else:
            worker = by_worker(spread, table)
        y[:, at] = x1[:, at] - spread + worker * row(weight, b, BLOCK)


def last_kernel(*refs):
    parts, (before, mask_ids), tables, (out, means, y, sems) = refs[:NEAR], refs[NEAR : NEAR + 2], refs[NEAR + 2 : -4], refs[-4:]
    outs = column_copies(y, out, sems)
    columns, slots = means.shape
    second = own_means(parts, means)
    for b in range(len(outs)):
        at = slice(b * BLOCK, (b + 1) * BLOCK)
        found = tables[0][:, at] if tables else one_hot(row(mask_ids, b, BLOCK), slots)
        spread = dot(second, found)
        y[:, at] = before[:, at] - (spread[:columns] + spread[columns:])
        outs[b].start()
    wait_all(outs)


def near_exchange(parts, n):
    steps = [[(i, i ^ step) for i in range(n)] for step in NEAR_STEPS[1:]]
    return [parts[0]] + [lax.ppermute(one, "rows", step) for one, step in zip(parts[1:], steps)]


def far_share(one, n):
    steps = [[(i, i ^ (k * NEAR)) for i in range(n)] for k in range(1, n // NEAR)]
    return [one] + [lax.ppermute(one, "rows", step) for step in steps]


def in_hbm(x):
    return pltpu.with_memory_space_constraint(x, pltpu.HBM)


def call(kernel, out_shape, in_specs, out_specs, scratch, flops, moved):
    return pl.pallas_call(
        kernel,
        out_shape=out_shape,
        in_specs=in_specs,
        out_specs=out_specs,
        scratch_shapes=scratch,
        compiler_params=pltpu.CompilerParams(vmem_limit_bytes=VMEM_BYTES),
        cost_estimate=pl.CostEstimate(flops=flops, bytes_accessed=moved, transcendentals=0),
    )


def body(probes, worker_len, spell_to_slot, slot_to_firm, *, n):
    columns, rows_dev = probes.shape
    workers = worker_len.shape[0]
    pad = rows_dev // workers
    slots = slot_to_firm.shape[0]
    tiles = slots // LANES
    part = columns // NEAR
    far = n // NEAR
    keep = tiles * NEAR * n * LANES * LANES * 2 <= 8 * 1024 * 1024
    blocks = rows_dev // BLOCK
    vmem, hbm = pl.BlockSpec(memory_space=pltpu.VMEM), pl.BlockSpec(memory_space=pltpu.HBM)
    lengths = worker_len.reshape(workers // LANES, LANES)
    ids = spell_to_slot.reshape(rows_dev // LANES, LANES)
    firms = slot_to_firm.reshape(tiles, LANES)
    array = jax.ShapeDtypeStruct
    of_rows = (rows_dev // LANES, LANES)
    work = 2 * rows_dev * slots * 2 * columns
    sems = pltpu.SemaphoreType.DMA((blocks,))
    whole = (columns, rows_dev)
    about = part + 8
    message = array((about + rows_dev // slots, slots), F32)
    short = array((about, slots), F32)
    slots_message = array((message.shape[0] - part, slots), F32)
    of_near = array((columns, slots), F32)

    *sends, own_slots, x1, mask_ids, weight = call(
        functools.partial(sums_kernel, pad, slots // n),
        [short, message, short, short, slots_message, array(whole, F32), array(of_rows, jnp.int32), array(of_rows, F32)],
        [hbm] * 4,
        [vmem] * (NEAR + 4),
        [
            pltpu.VMEM(of_rows, F32),
            pltpu.VMEM(whole, F32),
            pltpu.VMEM((columns, slots), F32),
            pltpu.VMEM(lengths.shape, jnp.int32),
            pltpu.VMEM(ids.shape, jnp.int32),
            pltpu.VMEM(firms.shape, jnp.int32),
            pltpu.SemaphoreType.DMA((columns // 8,)),
            pltpu.SemaphoreType.DMA((3,)),
        ],
        2 * work,
        4 * columns * rows_dev,
    )(in_hbm(probes), in_hbm(lengths), in_hbm(ids), in_hbm(firms))

    def pair_counts(parts, copy=()):
        count = len(parts)
        return call(
            functools.partial(pairs_kernel, pad, count),
            [array((count, slots, 2 * slots), BF16), *copy],
            [vmem] * count,
            [vmem] * (1 + len(copy)),
            [
                pltpu.VMEM((count, *of_rows), F32),
                pltpu.VMEM((count, 8, slots), F32),
                pltpu.VMEM((count, slots, workers), BF16),
            ],
            work * count // 4,
            4 * slots * slots,
        )(*parts)

    def near_step(one, step):
        return lax.ppermute(one, "rows", [(i, i ^ step) for i in range(n)])

    arrived = near_exchange(sends, n)
    own_pairs, own_slots = pair_counts([own_slots], [slots_message])
    passed = near_step(own_slots, 2)
    pairs = [own_pairs]
    joined = call(
        functools.partial(join_kernel, part),
        array((columns + 2 * NEAR, slots), F32),
        [vmem] * (NEAR + 1),
        vmem,
        [],
        0,
        message.size * 8,
    )(*arrived, *pairs)
    shared = far_share(joined, n)
    tables, beside = [], passed
    table = array((tiles, NEAR * LANES, NEAR * LANES), BF16)

    def firm_table(one, passed, out):
        return call(
            functools.partial(firms_kernel, part),
            out,
            [vmem] * 3,
            [vmem] * len(out),
            [],
            work // 64,
            tiles * (NEAR * LANES) ** 2 * 2,
        )(joined, one, passed)

    if keep:
        first_table, beside = firm_table(joined, passed, [table, slots_message])
        tables = [first_table, *firm_table(shared[-1], first_table, [table])]
    pairs += pair_counts([arrived[1], passed]) + pair_counts([near_step(beside, 1)])
    scale = array((tiles, 8, NEAR * LANES), F32)
    made = [table] * (far - 2) * keep
    mean, sums, scales, *made = call(
        functools.partial(change_kernel, far, part, len(tables)),
        [of_near, of_near, scale, *made],
        [vmem] * (far + len(tables) + len(pairs)),
        [vmem] * (3 + len(made)),
        [],
        work // 4,
        slots * slots * 4,
    )(*shared, *tables, *pairs)
    again = far_share(sums, n)
    source = [tables[0], *made, tables[1]] if keep else shared
    spreads = []
    sends = [mean[part * k : part * (k + 1)] for k in range(NEAR)]
    if keep:
        *spreads, a, b, c, d = call(
            functools.partial(tables_kernel, pad),
            [array((slots, rows_dev), BF16)] * 2 + [array((part, slots), F32)] * NEAR,
            [vmem] * 2,
            [vmem] * (2 + NEAR),
            [],
            work,
            4 * slots * rows_dev,
        )(mask_ids, mean)
        sends = [a, b, c, d]
    first = near_exchange(sends, n)
    sends = call(
        functools.partial(means_kernel, far, part, keep),
        [array((part, slots), F32)] * NEAR,
        [vmem] * (far + len(source) + 2),
        [vmem] * NEAR,
        [pltpu.VMEM((columns, slots), F32)],
        work // 4,
        slots * slots * 4,
    )(*again, *source, scales, spreads[1] if keep else scales)
    arrived = near_exchange(sends, n)
    before = call(
        functools.partial(first_kernel, pad),
        array(whole, F32),
        [vmem] * (NEAR + 3 + len(spreads)),
        vmem,
        [pltpu.VMEM((columns, slots), F32)],
        work,
        8 * columns * rows_dev,
    )(*first, x1, mask_ids, weight, *spreads)
    return call(
        last_kernel,
        array(whole, F32),
        [vmem] * (NEAR + 2 + len(spreads[:1])),
        hbm,
        [pltpu.VMEM((columns, slots), F32), pltpu.VMEM(whole, F32), sems],
        work,
        8 * columns * rows_dev,
    )(*arrived, before, mask_ids, *spreads[:1])


def solution(mesh):
    placed = (P(None, ("grp", "rows")), P(("grp", "rows")), P(("grp", "rows")), P(("grp", "rows")))
    return jax.shard_map(
        functools.partial(body, n=mesh.shape["rows"]),
        mesh=mesh,
        in_specs=placed,
        out_specs=P(None, ("grp", "rows")),
        check_vma=False,
    )
```

```python
import functools

import jax
import jax.numpy as jnp
from jax import lax
from jax.experimental import pallas as pl
from jax.experimental.pallas import tpu as pltpu
from jax.sharding import PartitionSpec as P

FIRMS_PER_SHARD = 1024
LANES = 128
BLOCK = 1024
VMEM_BYTES = 32 * 1024 * 1024
NEAR = 4
NEAR_STEPS = (0, 1, 2, 3)
F32, BF16 = jnp.float32, jnp.bfloat16
NT = (((1,), (1,)), ((), ()))
NN = (((1,), (0,)), ((), ()))


def dot(a, b, dims=NN):
    return lax.dot_general(a, b, dims, preferred_element_type=F32)


def iota(shape, dim):
    return lax.broadcasted_iota(jnp.int32, shape, dim)


def split(x):
    hi = x.astype(BF16)
    return hi, (x - hi.astype(F32)).astype(BF16)


def row(ref, block, size):
    per = size // LANES
    return jnp.concatenate([ref[block * per + k : block * per + k + 1, :] for k in range(per)], axis=1)


def one_hot(ids, slots):
    kind = BF16 if slots <= 256 else F32
    slot = iota((slots, LANES), 0).astype(F32).astype(kind)
    ids = ids.astype(F32).astype(kind)
    one, zero = jnp.ones((slots, LANES), kind), jnp.zeros((slots, LANES), kind)
    parts = [jnp.where(slot == ids[:, k : k + LANES], one, zero) for k in range(0, ids.shape[1], LANES)]
    return jnp.concatenate(parts, axis=1).astype(BF16)


def one_hot_down(columns, slots):
    kind = BF16 if slots <= 256 else F32
    one, zero = jnp.ones((LANES, LANES), kind), jnp.zeros((LANES, LANES), kind)
    along_slots = [(iota((LANES, LANES), 1) + at).astype(F32).astype(kind) for at in range(0, slots, LANES)]
    parts, columns = [], columns.astype(kind)
    for k in range(columns.shape[1]):
        ids = jnp.broadcast_to(columns[:, k : k + 1], (LANES, LANES))
        parts.append(jnp.concatenate([jnp.where(slot == ids, one, zero) for slot in along_slots], axis=1))
    return jnp.concatenate(parts, axis=0).astype(BF16)


def same_worker(pad, width):
    return (iota((width, width), 0) // pad == iota((width, width), 1) // pad).astype(F32).astype(BF16)


def by_worker(x, table):
    rows, width = x.shape
    step = table.shape[1]
    both = [
        jnp.concatenate([one[:, k : k + step] for k in range(0, width, step)], axis=0) for one in split(x)
    ]
    total = dot(jnp.concatenate(both, axis=1), table)
    return jnp.concatenate([total[k : k + rows] for k in range(0, total.shape[0], rows)], axis=1)


def start_all(copies):
    for copy in copies:
        copy.start()


def wait_all(copies):
    for copy in copies:
        copy.wait()


def column_copies(source, target, sems, size=BLOCK):
    width = source.shape[1]
    cuts = [pl.ds(start, size) for start in range(0, width, size)]
    return [pltpu.make_async_copy(source.at[:, cut], target.at[:, cut], sems.at[b]) for b, cut in enumerate(cuts)]


def row_lengths(lengths, pad):
    total_rows = lengths.shape[0] * pad
    here = iota((total_rows, LANES), 0)
    lane = iota((total_rows, LANES), 1)
    wide = jnp.broadcast_to(lengths.astype(F32)[:, None, :], (lengths.shape[0], pad, LANES)).reshape(total_rows, LANES)
    per = LANES // pad
    wide = jnp.where(lane // per == here % pad, wide, 0.0).astype(BF16)
    spread = (iota((LANES, LANES), 0) % per == iota((LANES, LANES), 1) // pad).astype(F32).astype(BF16)
    row_len = dot(wide, spread)
    return row_len, (lane % pad).astype(F32) < row_len


def along(ref):
    return jnp.concatenate([ref[k : k + 1, :] for k in range(ref.shape[0])], axis=1)


def sums_kernel(pad, cap, *refs):
    (probes, lengths_in, ids_in, firms_in), sends, slots_out = refs[:4], refs[4 : 4 + NEAR], refs[4 + NEAR]
    refs = refs[5 + NEAR :]
    x1, mask_ids, weight, valid, x, sums, lengths, ids, firms, bands_sem, small = refs
    bands = [pl.ds(at, 8) for at in range(0, x.shape[0], 8)]
    copies = [pltpu.make_async_copy(probes.at[at], x.at[at], bands_sem.at[b]) for b, at in enumerate(bands)]
    first = [
        pltpu.make_async_copy(source, target, small.at[k])
        for k, (source, target) in enumerate(((lengths_in, lengths), (ids_in, ids), (firms_in, firms)))
    ]
    start_all(first)
    start_all(copies)
    columns, slots = sums.shape
    part = columns // NEAR
    me = lax.axis_index("rows") % NEAR
    wait_all(first)
    row_len, inside = row_lengths(lengths[...], pad)
    valid[...] = jnp.where(inside, 1.0, 0.0)
    weight[...] = jnp.where(inside, 1.0 / row_len, 0.0)
    masked = jnp.where(inside, ids[...], -1)
    mask_ids[...] = masked
    turned = jnp.concatenate([masked.astype(F32)] * (LANES // masked.shape[0]), axis=0).T
    keys = (iota((1, slots), 1) // cap * FIRMS_PER_SHARD + along(firms)).astype(F32)
    across = slots // LANES
    rows = ids.shape[0] // across
    masked = jnp.concatenate([masked[k * rows : (k + 1) * rows] for k in range(across)], axis=1).astype(F32)
    sends[1][part + 8 :] = masked
    slots_out[8:] = masked

    table = jnp.concatenate([same_worker(pad, 256)] * 2, axis=0)
    wait_all(copies)
    total = None
    for b in range(x.shape[1] // BLOCK):
        ok = row(valid, b, BLOCK)
        x0 = x[:, b * BLOCK : (b + 1) * BLOCK] * ok
        rest = x0 - by_worker(x0, table) * row(weight, b, BLOCK)
        x1[:, b * BLOCK : (b + 1) * BLOCK] = rest
        counted = jnp.broadcast_to(ok, (16, BLOCK)).astype(BF16)
        data = jnp.concatenate([*split(rest), counted], axis=0)
        per = BLOCK // LANES
        block = dot(data, one_hot_down(turned[:, b * per : (b + 1) * per], slots))
        total = block if total is None else total + block
    sums[...] = total[:columns] + total[columns : 2 * columns]
    about = jnp.where(iota((8, slots), 0) == 0, keys, total[2 * columns : 2 * columns + 1])
    for step, send in zip(NEAR_STEPS, sends):
        send[:part] = sums[pl.ds(pl.multiple_of((me ^ step) * part, part), part), :]
        send[part : part + 8] = about
    slots_out[:8] = about


def join_kernel(part, *refs):
    parts, out = refs[:NEAR], refs[-1]
    for k, one in enumerate(parts):
        out[part * k : part * (k + 1)] = one[:part]
        out[part * NEAR + 2 * k : part * NEAR + 2 * k + 2] = one[part : part + 2]


def pairs_kernel(pad, several, *refs):
    parts, (out, *copy, ids, size, counts) = refs[:several], refs[several:]
    for ref in copy:
        ref[...] = parts[0][...]
    slots = out.shape[1]
    kind = BF16 if slots <= 256 else F32
    per = LANES // pad
    total_rows = ids.shape[1]
    across = slots // LANES
    rows = total_rows // across
    for k, part in enumerate(parts):
        start = part.shape[0] - rows
        size[k] = jnp.broadcast_to(part[start - 7 : start - 6], (8, slots))
        for at in range(across):
            ids[k, at * rows : (at + 1) * rows] = part[start:, at * LANES : (at + 1) * LANES]
    at = iota((LANES, pad * LANES), 1)
    deal = (iota((LANES, pad * LANES), 0) == at % per * pad + at // LANES).astype(F32).astype(BF16)
    mine = iota((total_rows, pad * LANES), 1) % LANES // per == iota((total_rows, pad * LANES), 0) % pad
    slot = iota((slots, LANES), 0).astype(F32).astype(kind)
    one, zero = jnp.ones((slots, LANES), kind), jnp.zeros((slots, LANES), kind)
    diagonal = iota((slots, slots), 1) == iota((slots, slots), 0)

    def device(k, carry):
        dealt = dot(jnp.concatenate(split(ids[k]), axis=0), deal)
        dealt = jnp.where(mine, dealt[:total_rows] + dealt[total_rows:], 0.0)
        dealt = jnp.sum(dealt.reshape(total_rows // pad, pad, pad * LANES), axis=1)
        spells = dealt.astype(kind)
        for g in range(total_rows // pad):
            total = zero
            for j in range(pad):
                total += jnp.where(slot == spells[g : g + 1, j * LANES : (j + 1) * LANES], one, zero)
            counts[k, :, g * LANES : (g + 1) * LANES] = total.astype(BF16)
        valid = jnp.where(dealt >= 0.0, 1.0, 0.0)
        length = valid[:, :LANES]
        for j in range(1, pad):
            length += valid[:, j * LANES : (j + 1) * LANES]
        inverse = 1.0 / length
        inverse = jnp.concatenate([inverse[g : g + 1] for g in range(total_rows // pad)], axis=1)
        here = counts[k]
        total = dot(jnp.concatenate(split(here.astype(F32) * inverse), axis=0), here, NT)
        total = total[:slots] + total[slots:] - jnp.where(diagonal, size[k, :1], 0.0)
        hi, lo = split(total)
        out[k, :, :slots] = hi
        out[k, :, slots:] = lo
        return carry

    lax.fori_loop(0, len(parts), device, 0, unroll=len(parts) if slots <= 256 else 1)


def same_firm(own, one, part, at):
    mine, keys = ([ref[part * NEAR + 2 * k : part * NEAR + 2 * k + 1, at] for k in range(NEAR)] for ref in (own, one))
    mine = jnp.concatenate(mine, axis=1)
    down = jnp.concatenate([jnp.broadcast_to(key, (8, LANES)) for key in keys], axis=0).T
    found = [(down[:, 8 * k : 8 * k + 1] == mine).astype(F32).astype(BF16) for k in range(NEAR)]
    return jnp.concatenate(found, axis=0)


def each_tile(slots, do):
    tiles = slots // LANES
    if tiles <= 2:
        for t in range(tiles):
            do(t, slice(t * LANES, (t + 1) * LANES))
    else:
        lax.fori_loop(0, tiles, lambda t, c: (do(t, pl.ds(pl.multiple_of(t * LANES, LANES), LANES)), c)[1], 0)


def firms_kernel(part, own, one, passed, out, *copy):
    for ref in copy:
        ref[...] = passed[...]
    each_tile(own.shape[1], lambda t, at: out.__setitem__(t, same_firm(own, one, part, at)))


def gathered(parts, part, at):
    data = [one[part * k : part * (k + 1), at] for one in parts for k in range(NEAR)]
    return jnp.concatenate(split(jnp.concatenate(data, axis=1)), axis=0)


def spread_out(means, out, part, at):
    for k in range(NEAR):
        out[part * k : part * (k + 1), at] = means[:, k * LANES : (k + 1) * LANES]


def change_kernel(far, part, ready, *refs):
    parts, tables, refs = refs[:far], refs[far : far + ready], refs[far + ready :]
    pairs = [(group, k) for group in refs[:3] for k in range(group.shape[0])]
    (mean, sums, scale), made = refs[3:6], refs[6:]
    slots = mean.shape[1]

    def tile(t, at):
        if tables:
            between = [same_firm(parts[0], one, part, at) for one in parts[1:-1]]
            for ref, one in zip(made, between):
                ref[t] = one
            same = [tables[0][t], *between, tables[1][t]]
        else:
            same = [same_firm(parts[0], one, part, at) for one in parts]
        same = jnp.concatenate(same, axis=0)
        count = [one[part * NEAR + 2 * k + 1 : part * NEAR + 2 * k + 2, at] for one in parts for k in range(NEAR)]
        count = jnp.concatenate(count, axis=1)
        high = count.astype(BF16).astype(F32)
        counts = jnp.where(iota((16, count.shape[1]), 0) < 8, high, count - high).astype(BF16)
        found = dot(jnp.concatenate([gathered(parts, part, at), counts], axis=0), same)
        size = found[2 * part : 2 * part + 1] + found[2 * part + 8 : 2 * part + 9]
        inverse = 1.0 / jnp.maximum(size, 1.0)
        scale[t] = jnp.broadcast_to(inverse, scale.shape[1:])
        spread_out((found[:part] + found[part : 2 * part]) * inverse, mean, part, at)

    each_tile(slots, tile)
    for k in range(NEAR):
        cut = slice(part * k, part * (k + 1))
        both = jnp.concatenate(split(mean[cut]), axis=0)
        change = dot(both, pairs[k][0][pairs[k][1]])
        change = change[:part] + change[part:]
        sums[cut] = parts[0][cut] + (change[:, :slots] + change[:, slots:])


def tables_kernel(pad, mask_ids, mean, spread, workers, *sends):
    part = mean.shape[0] // NEAR
    for k, send in enumerate(sends):
        send[...] = mean[part * k : part * (k + 1)]
    slots, width = spread.shape
    table = jnp.concatenate([same_worker(pad, 256)] * 2, axis=0)
    for b in range(width // BLOCK):
        found = one_hot(row(mask_ids, b, BLOCK), slots)
        spread[:, b * BLOCK : (b + 1) * BLOCK] = found
        for at in range(0, BLOCK, 256):
            count = dot(found[:, at : at + 256], table[:256])
            workers[:, b * BLOCK + at : b * BLOCK + at + 256] = count.astype(BF16)


def means_kernel(far, part, kept, *refs):
    parts, source, scale, sends, mean = refs[:far], refs[far:-7], refs[-7], refs[-5:-1], refs[-1]

    def tile(t, at):
        same = [table[t] if kept else same_firm(source[0], table, part, at) for table in source]
        same = jnp.concatenate(same, axis=0)
        found = dot(gathered(parts, part, at), same)
        spread_out((found[:part] + found[part:]) * scale[t][:1], mean, part, at)

    each_tile(mean.shape[1], tile)
    for k, send in enumerate(sends):
        send[...] = mean[part * k : part * (k + 1)]


def own_means(parts, means):
    me = lax.axis_index("rows") % NEAR
    part = parts[0].shape[0]
    for step, one in zip(NEAR_STEPS, parts):
        means[pl.ds(pl.multiple_of((me ^ step) * part, part), part), :] = one[...]
    return jnp.concatenate(split(means[...]), axis=0)


def first_kernel(pad, *refs):
    parts, (x1, mask_ids, weight), tables, (y, means) = refs[:NEAR], refs[NEAR : NEAR + 3], refs[NEAR + 3 : -2], refs[-2:]
    columns, slots = means.shape
    first = own_means(parts, means)
    table = jnp.concatenate([same_worker(pad, 256)] * 2, axis=0)
    for b in range(y.shape[1] // BLOCK):
        at = slice(b * BLOCK, (b + 1) * BLOCK)
        found = tables[0][:, at] if tables else one_hot(row(mask_ids, b, BLOCK), slots)
        spread = dot(first, found)
        spread = spread[:columns] + spread[columns:]
        if tables:
            worker = dot(first, tables[1][:, at])
            worker = worker[:columns] + worker[columns:]
        else:
            worker = by_worker(spread, table)
        y[:, at] = x1[:, at] - spread + worker * row(weight, b, BLOCK)


def last_kernel(*refs):
    parts, (before, mask_ids), tables, (out, means, y, sems) = refs[:NEAR], refs[NEAR : NEAR + 2], refs[NEAR + 2 : -4], refs[-4:]
    outs = column_copies(y, out, sems, BLOCK // 2)
    columns, slots = means.shape
    second = own_means(parts, means)
    for b, copy in enumerate(outs):
        at = slice(b * BLOCK // 2, (b + 1) * BLOCK // 2)
        found = tables[0][:, at] if tables else one_hot(row(mask_ids, b, BLOCK // 2), slots)
        spread = dot(second, found)
        y[:, at] = before[:, at] - (spread[:columns] + spread[columns:])
        copy.start()
    wait_all(outs)


def near_exchange(parts, n):
    steps = [[(i, i ^ step) for i in range(n)] for step in NEAR_STEPS[1:]]
    return [parts[0]] + [lax.ppermute(one, "rows", step) for one, step in zip(parts[1:], steps)]


def far_share(one, n):
    steps = [[(i, i ^ (k * NEAR)) for i in range(n)] for k in range(1, n // NEAR)]
    return [one] + [lax.ppermute(one, "rows", step) for step in steps]


def in_hbm(x):
    return pltpu.with_memory_space_constraint(x, pltpu.HBM)


def call(kernel, out_shape, in_specs, out_specs, scratch, flops, moved):
    return pl.pallas_call(
        kernel,
        out_shape=out_shape,
        in_specs=in_specs,
        out_specs=out_specs,
        scratch_shapes=scratch,
        compiler_params=pltpu.CompilerParams(vmem_limit_bytes=VMEM_BYTES),
        cost_estimate=pl.CostEstimate(flops=flops, bytes_accessed=moved, transcendentals=0),
    )


def body(probes, worker_len, spell_to_slot, slot_to_firm, *, n):
    columns, rows_dev = probes.shape
    workers = worker_len.shape[0]
    pad = rows_dev // workers
    slots = slot_to_firm.shape[0]
    tiles = slots // LANES
    part = columns // NEAR
    far = n // NEAR
    keep = tiles * NEAR * n * LANES * LANES * 2 <= 8 * 1024 * 1024
    blocks = rows_dev // BLOCK
    vmem, hbm = pl.BlockSpec(memory_space=pltpu.VMEM), pl.BlockSpec(memory_space=pltpu.HBM)
    lengths = worker_len.reshape(workers // LANES, LANES)
    ids = spell_to_slot.reshape(rows_dev // LANES, LANES)
    firms = slot_to_firm.reshape(tiles, LANES)
    array = jax.ShapeDtypeStruct
    of_rows = (rows_dev // LANES, LANES)
    work = 2 * rows_dev * slots * 2 * columns
    sems = pltpu.SemaphoreType.DMA((blocks,))
    whole = (columns, rows_dev)
    about = part + 8
    message = array((about + rows_dev // slots, slots), F32)
    short = array((about, slots), F32)
    slots_message = array((message.shape[0] - part, slots), F32)
    of_near = array((columns, slots), F32)

    *sends, own_slots, x1, mask_ids, weight = call(
        functools.partial(sums_kernel, pad, slots // n),
        [short, message, short, short, slots_message, array(whole, F32), array(of_rows, jnp.int32), array(of_rows, F32)],
        [hbm] * 4,
        [vmem] * (NEAR + 4),
        [
            pltpu.VMEM(of_rows, F32),
            pltpu.VMEM(whole, F32),
            pltpu.VMEM((columns, slots), F32),
            pltpu.VMEM(lengths.shape, jnp.int32),
            pltpu.VMEM(ids.shape, jnp.int32),
            pltpu.VMEM(firms.shape, jnp.int32),
            pltpu.SemaphoreType.DMA((columns // 8,)),
            pltpu.SemaphoreType.DMA((3,)),
        ],
        2 * work,
        4 * columns * rows_dev,
    )(in_hbm(probes), in_hbm(lengths), in_hbm(ids), in_hbm(firms))

    def pair_counts(parts, copy=()):
        count = len(parts)
        return call(
            functools.partial(pairs_kernel, pad, count),
            [array((count, slots, 2 * slots), BF16), *copy],
            [vmem] * count,
            [vmem] * (1 + len(copy)),
            [
                pltpu.VMEM((count, *of_rows), F32),
                pltpu.VMEM((count, 8, slots), F32),
                pltpu.VMEM((count, slots, workers), BF16),
            ],
            work * count // 4,
            4 * slots * slots,
        )(*parts)

    def near_step(one, step):
        return lax.ppermute(one, "rows", [(i, i ^ step) for i in range(n)])

    arrived = near_exchange(sends, n)
    own_pairs, own_slots = pair_counts([own_slots], [slots_message])
    passed = near_step(own_slots, 2)
    pairs = [own_pairs]
    joined = call(
        functools.partial(join_kernel, part),
        array((columns + 2 * NEAR, slots), F32),
        [vmem] * (NEAR + 1),
        vmem,
        [],
        0,
        message.size * 8,
    )(*arrived, *pairs)
    shared = far_share(joined, n)
    tables, beside = [], passed
    table = array((tiles, NEAR * LANES, NEAR * LANES), BF16)

    def firm_table(one, passed, out):
        return call(
            functools.partial(firms_kernel, part),
            out,
            [vmem] * 3,
            [vmem] * len(out),
            [],
            work // 64,
            tiles * (NEAR * LANES) ** 2 * 2,
        )(joined, one, passed)

    if keep:
        first_table, beside = firm_table(joined, passed, [table, slots_message])
        tables = [first_table, *firm_table(shared[-1], first_table, [table])]
    pairs += pair_counts([arrived[1], passed]) + pair_counts([near_step(beside, 1)])
    scale = array((tiles, 8, NEAR * LANES), F32)
    made = [table] * (far - 2) * keep
    mean, sums, scales, *made = call(
        functools.partial(change_kernel, far, part, len(tables)),
        [of_near, of_near, scale, *made],
        [vmem] * (far + len(tables) + len(pairs)),
        [vmem] * (3 + len(made)),
        [],
        work // 4,
        slots * slots * 4,
    )(*shared, *tables, *pairs)
    again = far_share(sums, n)
    source = [tables[0], *made, tables[1]] if keep else shared
    spreads = []
    sends = [mean[part * k : part * (k + 1)] for k in range(NEAR)]
    if keep:
        *spreads, a, b, c, d = call(
            functools.partial(tables_kernel, pad),
            [array((slots, rows_dev), BF16)] * 2 + [array((part, slots), F32)] * NEAR,
            [vmem] * 2,
            [vmem] * (2 + NEAR),
            [],
            work,
            4 * slots * rows_dev,
        )(mask_ids, mean)
        sends = [a, b, c, d]
    first = near_exchange(sends, n)
    sends = call(
        functools.partial(means_kernel, far, part, keep),
        [array((part, slots), F32)] * NEAR,
        [vmem] * (far + len(source) + 2),
        [vmem] * NEAR,
        [pltpu.VMEM((columns, slots), F32)],
        work // 4,
        slots * slots * 4,
    )(*again, *source, scales, spreads[1] if keep else scales)
    arrived = near_exchange(sends, n)
    before = call(
        functools.partial(first_kernel, pad),
        array(whole, F32),
        [vmem] * (NEAR + 3 + len(spreads)),
        vmem,
        [pltpu.VMEM((columns, slots), F32)],
        work,
        8 * columns * rows_dev,
    )(*first, x1, mask_ids, weight, *spreads)
    return call(
        last_kernel,
        array(whole, F32),
        [vmem] * (NEAR + 2 + len(spreads[:1])),
        hbm,
        [pltpu.VMEM((columns, slots), F32), pltpu.VMEM(whole, F32), pltpu.SemaphoreType.DMA((2 * blocks,))],
        work,
        8 * columns * rows_dev,
    )(*arrived, before, mask_ids, *spreads[:1])


def solution(mesh):
    placed = (P(None, ("grp", "rows")), P(("grp", "rows")), P(("grp", "rows")), P(("grp", "rows")))
    return jax.shard_map(
        functools.partial(body, n=mesh.shape["rows"]),
        mesh=mesh,
        in_specs=placed,
        out_specs=P(None, ("grp", "rows")),
        check_vma=False,
    )
```

```python
import functools

import jax
import jax.numpy as jnp
from jax import lax
from jax.experimental import pallas as pl
from jax.experimental.pallas import tpu as pltpu
from jax.sharding import PartitionSpec as P

FIRMS_PER_SHARD = 1024
LANES = 128
BLOCK = 1024
WIDE = 2048
VMEM_BYTES = 32 * 1024 * 1024
NEAR = 4
NEAR_STEPS = (0, 1, 2, 3)
F32, BF16 = jnp.float32, jnp.bfloat16
NT = (((1,), (1,)), ((), ()))
NN = (((1,), (0,)), ((), ()))


def dot(a, b, dims=NN):
    return lax.dot_general(a, b, dims, preferred_element_type=F32)


def iota(shape, dim):
    return lax.broadcasted_iota(jnp.int32, shape, dim)


def split(x):
    hi = x.astype(BF16)
    return hi, (x - hi.astype(F32)).astype(BF16)


def row(ref, block, size):
    per = size // LANES
    return jnp.concatenate([ref[block * per + k : block * per + k + 1, :] for k in range(per)], axis=1)


def one_hot(ids, slots):
    kind = BF16 if slots <= 256 else F32
    slot = iota((slots, LANES), 0).astype(F32).astype(kind)
    ids = ids.astype(F32).astype(kind)
    one, zero = jnp.ones((slots, LANES), kind), jnp.zeros((slots, LANES), kind)
    parts = [jnp.where(slot == ids[:, k : k + LANES], one, zero) for k in range(0, ids.shape[1], LANES)]
    return jnp.concatenate(parts, axis=1).astype(BF16)


def one_hot_down(columns, slots):
    kind = BF16 if slots <= 256 else F32
    one, zero = jnp.ones((LANES, LANES), kind), jnp.zeros((LANES, LANES), kind)
    along_slots = [(iota((LANES, LANES), 1) + at).astype(F32).astype(kind) for at in range(0, slots, LANES)]
    parts, columns = [], columns.astype(kind)
    for k in range(columns.shape[1]):
        ids = jnp.broadcast_to(columns[:, k : k + 1], (LANES, LANES))
        parts.append(jnp.concatenate([jnp.where(slot == ids, one, zero) for slot in along_slots], axis=1))
    return jnp.concatenate(parts, axis=0).astype(BF16)


def same_worker(pad, width):
    return (iota((width, width), 0) // pad == iota((width, width), 1) // pad).astype(F32).astype(BF16)


def by_worker(x, table):
    rows, width = x.shape
    step = table.shape[1]
    both = [
        jnp.concatenate([one[:, k : k + step] for k in range(0, width, step)], axis=0) for one in split(x)
    ]
    total = dot(jnp.concatenate(both, axis=1), table)
    return jnp.concatenate([total[k : k + rows] for k in range(0, total.shape[0], rows)], axis=1)


def start_all(copies):
    for copy in copies:
        copy.start()


def wait_all(copies):
    for copy in copies:
        copy.wait()


def column_copies(source, target, sems, size=BLOCK):
    width = source.shape[1]
    cuts = [pl.ds(start, size) for start in range(0, width, size)]
    return [pltpu.make_async_copy(source.at[:, cut], target.at[:, cut], sems.at[b]) for b, cut in enumerate(cuts)]


def row_lengths(lengths, pad):
    total_rows = lengths.shape[0] * pad
    here = iota((total_rows, LANES), 0)
    lane = iota((total_rows, LANES), 1)
    wide = jnp.broadcast_to(lengths.astype(F32)[:, None, :], (lengths.shape[0], pad, LANES)).reshape(total_rows, LANES)
    per = LANES // pad
    wide = jnp.where(lane // per == here % pad, wide, 0.0).astype(BF16)
    spread = (iota((LANES, LANES), 0) % per == iota((LANES, LANES), 1) // pad).astype(F32).astype(BF16)
    row_len = dot(wide, spread)
    return row_len, (lane % pad).astype(F32) < row_len


def along(ref):
    return jnp.concatenate([ref[k : k + 1, :] for k in range(ref.shape[0])], axis=1)


def sums_kernel(pad, cap, *refs):
    (probes, lengths_in, ids_in, firms_in), sends, slots_out = refs[:4], refs[4 : 4 + NEAR], refs[4 + NEAR]
    refs = refs[5 + NEAR :]
    x1, mask_ids, weight, valid, x, sums, lengths, ids, firms, bands_sem, small = refs
    bands = [pl.ds(at, 8) for at in range(0, x.shape[0], 8)]
    copies = [pltpu.make_async_copy(probes.at[at], x.at[at], bands_sem.at[b]) for b, at in enumerate(bands)]
    first = [
        pltpu.make_async_copy(source, target, small.at[k])
        for k, (source, target) in enumerate(((lengths_in, lengths), (ids_in, ids), (firms_in, firms)))
    ]
    start_all(first)
    start_all(copies)
    columns, slots = sums.shape
    part = columns // NEAR
    me = lax.axis_index("rows") % NEAR
    wait_all(first)
    row_len, inside = row_lengths(lengths[...], pad)
    valid[...] = jnp.where(inside, 1.0, 0.0)
    weight[...] = jnp.where(inside, 1.0 / row_len, 0.0)
    masked = jnp.where(inside, ids[...], -1)
    mask_ids[...] = masked
    turned = jnp.concatenate([masked.astype(F32)] * (LANES // masked.shape[0]), axis=0).T
    keys = (iota((1, slots), 1) // cap * FIRMS_PER_SHARD + along(firms)).astype(F32)
    across = slots // LANES
    rows = ids.shape[0] // across
    masked = jnp.concatenate([masked[k * rows : (k + 1) * rows] for k in range(across)], axis=1).astype(F32)
    sends[1][part + 8 :] = masked
    slots_out[8:] = masked

    table = jnp.concatenate([same_worker(pad, 256)] * 2, axis=0)
    wait_all(copies)
    total = None
    for b in range(x.shape[1] // WIDE):
        ok = row(valid, b, WIDE)
        x0 = x[:, b * WIDE : (b + 1) * WIDE] * ok
        rest = x0 - by_worker(x0, table) * row(weight, b, WIDE)
        x1[:, b * WIDE : (b + 1) * WIDE] = rest
        counted = jnp.broadcast_to(ok, (16, WIDE)).astype(BF16)
        data = jnp.concatenate([*split(rest), counted], axis=0)
        per = WIDE // LANES
        block = dot(data, one_hot_down(turned[:, b * per : (b + 1) * per], slots))
        total = block if total is None else total + block
    sums[...] = total[:columns] + total[columns : 2 * columns]
    about = jnp.where(iota((8, slots), 0) == 0, keys, total[2 * columns : 2 * columns + 1])
    for step, send in zip(NEAR_STEPS, sends):
        send[:part] = sums[pl.ds(pl.multiple_of((me ^ step) * part, part), part), :]
        send[part : part + 8] = about
    slots_out[:8] = about


def join_kernel(part, *refs):
    parts, out = refs[:NEAR], refs[-1]
    for k, one in enumerate(parts):
        out[part * k : part * (k + 1)] = one[:part]
        out[part * NEAR + 2 * k : part * NEAR + 2 * k + 2] = one[part : part + 2]


def pairs_kernel(pad, start, several, *refs):
    parts, (out, *copy, ids, size, counts) = refs[:several], refs[several:]
    for ref in copy:
        ref[...] = parts[0][...]
    slots = out.shape[1]
    kind = BF16 if slots <= 256 else F32
    per = LANES // pad
    total_rows = ids.shape[1]
    across = slots // LANES
    rows = total_rows // across
    for k, part in enumerate(parts):
        size[k] = jnp.broadcast_to(part[start - 7 : start - 6], (8, slots))
        for at in range(across):
            ids[k, at * rows : (at + 1) * rows] = part[start:, at * LANES : (at + 1) * LANES]
    at = iota((LANES, pad * LANES), 1)
    deal = (iota((LANES, pad * LANES), 0) == at % per * pad + at // LANES).astype(F32).astype(BF16)
    mine = iota((total_rows, pad * LANES), 1) % LANES // per == iota((total_rows, pad * LANES), 0) % pad
    slot = iota((slots, LANES), 0).astype(F32).astype(kind)
    one, zero = jnp.ones((slots, LANES), kind), jnp.zeros((slots, LANES), kind)
    diagonal = iota((slots, slots), 1) == iota((slots, slots), 0)

    def device(k, carry):
        dealt = dot(jnp.concatenate(split(ids[k]), axis=0), deal)
        dealt = jnp.where(mine, dealt[:total_rows] + dealt[total_rows:], 0.0)
        dealt = jnp.sum(dealt.reshape(total_rows // pad, pad, pad * LANES), axis=1)
        spells = dealt.astype(kind)
        for g in range(total_rows // pad):
            total = zero
            for j in range(pad):
                total += jnp.where(slot == spells[g : g + 1, j * LANES : (j + 1) * LANES], one, zero)
            counts[k, :, g * LANES : (g + 1) * LANES] = total.astype(BF16)
        valid = jnp.where(dealt >= 0.0, 1.0, 0.0)
        length = valid[:, :LANES]
        for j in range(1, pad):
            length += valid[:, j * LANES : (j + 1) * LANES]
        inverse = 1.0 / length
        inverse = jnp.concatenate([inverse[g : g + 1] for g in range(total_rows // pad)], axis=1)
        here = counts[k]
        total = dot(jnp.concatenate(split(here.astype(F32) * inverse), axis=0), here, NT)
        total = total[:slots] + total[slots:] - jnp.where(diagonal, size[k, :1], 0.0)
        hi, lo = split(total)
        out[k, :, :slots] = hi
        out[k, :, slots:] = lo
        return carry

    lax.fori_loop(0, len(parts), device, 0, unroll=len(parts) if slots <= 256 else 1)


def same_firm(own, one, part, at):
    mine, keys = ([ref[part * NEAR + 2 * k : part * NEAR + 2 * k + 1, at] for k in range(NEAR)] for ref in (own, one))
    mine = jnp.concatenate(mine, axis=1)
    down = jnp.concatenate([jnp.broadcast_to(key, (8, LANES)) for key in keys], axis=0).T
    found = [(down[:, 8 * k : 8 * k + 1] == mine).astype(F32).astype(BF16) for k in range(NEAR)]
    return jnp.concatenate(found, axis=0)


def each_tile(slots, do):
    tiles = slots // LANES
    if tiles <= 2:
        for t in range(tiles):
            do(t, slice(t * LANES, (t + 1) * LANES))
    else:
        lax.fori_loop(0, tiles, lambda t, c: (do(t, pl.ds(pl.multiple_of(t * LANES, LANES), LANES)), c)[1], 0)


def firms_kernel(part, own, one, passed, out, *copy):
    for ref in copy:
        ref[...] = passed[...]
    each_tile(own.shape[1], lambda t, at: out.__setitem__(t, same_firm(own, one, part, at)))


def gathered(parts, part, at):
    data = [one[part * k : part * (k + 1), at] for one in parts for k in range(NEAR)]
    return jnp.concatenate(split(jnp.concatenate(data, axis=1)), axis=0)


def spread_out(means, out, part, at):
    for k in range(NEAR):
        out[part * k : part * (k + 1), at] = means[:, k * LANES : (k + 1) * LANES]


def change_kernel(far, part, ready, *refs):
    tables, pairs, refs = refs[far : far + ready], refs[far + ready : far + ready + NEAR], refs
    parts, (mean, sums, scale), made = refs[:far], refs[far + ready + NEAR :][:3], refs[far + ready + NEAR + 3 :]
    slots = mean.shape[1]

    def tile(t, at):
        if tables:
            between = [same_firm(parts[0], one, part, at) for one in parts[1:-1]]
            for ref, one in zip(made, between):
                ref[t] = one
            same = [tables[0][t], *between, tables[1][t]]
        else:
            same = [same_firm(parts[0], one, part, at) for one in parts]
        same = jnp.concatenate(same, axis=0)
        count = [one[part * NEAR + 2 * k + 1 : part * NEAR + 2 * k + 2, at] for one in parts for k in range(NEAR)]
        count = jnp.concatenate(count, axis=1)
        high = count.astype(BF16).astype(F32)
        counts = jnp.where(iota((16, count.shape[1]), 0) < 8, high, count - high).astype(BF16)
        found = dot(jnp.concatenate([gathered(parts, part, at), counts], axis=0), same)
        size = found[2 * part : 2 * part + 1] + found[2 * part + 8 : 2 * part + 9]
        inverse = 1.0 / jnp.maximum(size, 1.0)
        scale[t] = jnp.broadcast_to(inverse, scale.shape[1:])
        spread_out((found[:part] + found[part : 2 * part]) * inverse, mean, part, at)

    each_tile(slots, tile)
    for k in range(NEAR):
        cut = slice(part * k, part * (k + 1))
        both = jnp.concatenate(split(mean[cut]), axis=0)
        change = dot(both, pairs[k][0])
        change = change[:part] + change[part:]
        sums[cut] = parts[0][cut] + (change[:, :slots] + change[:, slots:])


def tables_kernel(pad, mask_ids, mean, spread, workers, *sends):
    part = mean.shape[0] // NEAR
    for k, send in enumerate(sends):
        send[...] = mean[part * k : part * (k + 1)]
    slots, width = spread.shape
    table = jnp.concatenate([same_worker(pad, 256)] * 2, axis=0)
    for b in range(width // BLOCK):
        found = one_hot(row(mask_ids, b, BLOCK), slots)
        spread[:, b * BLOCK : (b + 1) * BLOCK] = found
        for at in range(0, BLOCK, 256):
            count = dot(found[:, at : at + 256], table[:256])
            workers[:, b * BLOCK + at : b * BLOCK + at + 256] = count.astype(BF16)


def means_kernel(far, part, kept, *refs):
    parts, source, scale, sends, mean = refs[:far], refs[far:-7], refs[-7], refs[-5:-1], refs[-1]

    def tile(t, at):
        same = [table[t] if kept else same_firm(source[0], table, part, at) for table in source]
        same = jnp.concatenate(same, axis=0)
        found = dot(gathered(parts, part, at), same)
        spread_out((found[:part] + found[part:]) * scale[t][:1], mean, part, at)

    each_tile(mean.shape[1], tile)
    for k, send in enumerate(sends):
        send[...] = mean[part * k : part * (k + 1)]


def own_means(parts, means):
    me = lax.axis_index("rows") % NEAR
    part = parts[0].shape[0]
    for step, one in zip(NEAR_STEPS, parts):
        means[pl.ds(pl.multiple_of((me ^ step) * part, part), part), :] = one[...]
    return jnp.concatenate(split(means[...]), axis=0)


def first_kernel(pad, *refs):
    parts, (x1, mask_ids, weight), tables, (y, means) = refs[:NEAR], refs[NEAR : NEAR + 3], refs[NEAR + 3 : -2], refs[-2:]
    columns, slots = means.shape
    first = own_means(parts, means)
    table = jnp.concatenate([same_worker(pad, 256)] * 2, axis=0)
    for b in range(y.shape[1] // BLOCK):
        at = slice(b * BLOCK, (b + 1) * BLOCK)
        found = tables[0][:, at] if tables else one_hot(row(mask_ids, b, BLOCK), slots)
        spread = dot(first, found)
        spread = spread[:columns] + spread[columns:]
        if tables:
            worker = dot(first, tables[1][:, at])
            worker = worker[:columns] + worker[columns:]
        else:
            worker = by_worker(spread, table)
        y[:, at] = x1[:, at] - spread + worker * row(weight, b, BLOCK)


def last_kernel(*refs):
    parts, (before, mask_ids), tables, (out, means, y, sems) = refs[:NEAR], refs[NEAR : NEAR + 2], refs[NEAR + 2 : -4], refs[-4:]
    outs = column_copies(y, out, sems)
    columns, slots = means.shape
    second = own_means(parts, means)
    for b in range(len(outs)):
        at = slice(b * BLOCK, (b + 1) * BLOCK)
        found = tables[0][:, at] if tables else one_hot(row(mask_ids, b, BLOCK), slots)
        spread = dot(second, found)
        y[:, at] = before[:, at] - (spread[:columns] + spread[columns:])
        outs[b].start()
    wait_all(outs)


def near_exchange(parts, n):
    steps = [[(i, i ^ step) for i in range(n)] for step in NEAR_STEPS[1:]]
    return [parts[0]] + [lax.ppermute(one, "rows", step) for one, step in zip(parts[1:], steps)]


def far_share(one, n):
    steps = [[(i, i ^ (k * NEAR)) for i in range(n)] for k in range(1, n // NEAR)]
    return [one] + [lax.ppermute(one, "rows", step) for step in steps]


def in_hbm(x):
    return pltpu.with_memory_space_constraint(x, pltpu.HBM)


def call(kernel, out_shape, in_specs, out_specs, scratch, flops, moved):
    return pl.pallas_call(
        kernel,
        out_shape=out_shape,
        in_specs=in_specs,
        out_specs=out_specs,
        scratch_shapes=scratch,
        compiler_params=pltpu.CompilerParams(vmem_limit_bytes=VMEM_BYTES),
        cost_estimate=pl.CostEstimate(flops=flops, bytes_accessed=moved, transcendentals=0),
    )


def body(probes, worker_len, spell_to_slot, slot_to_firm, *, n):
    columns, rows_dev = probes.shape
    workers = worker_len.shape[0]
    pad = rows_dev // workers
    slots = slot_to_firm.shape[0]
    tiles = slots // LANES
    part = columns // NEAR
    far = n // NEAR
    keep = tiles * NEAR * n * LANES * LANES * 2 <= 8 * 1024 * 1024
    blocks = rows_dev // BLOCK
    vmem, hbm = pl.BlockSpec(memory_space=pltpu.VMEM), pl.BlockSpec(memory_space=pltpu.HBM)
    lengths = worker_len.reshape(workers // LANES, LANES)
    ids = spell_to_slot.reshape(rows_dev // LANES, LANES)
    firms = slot_to_firm.reshape(tiles, LANES)
    array = jax.ShapeDtypeStruct
    of_rows = (rows_dev // LANES, LANES)
    work = 2 * rows_dev * slots * 2 * columns
    sems = pltpu.SemaphoreType.DMA((blocks,))
    whole = (columns, rows_dev)
    about = part + 8
    message = array((about + rows_dev // slots, slots), F32)
    short = array((about, slots), F32)
    slots_message = array((message.shape[0] - part, slots), F32)
    of_near = array((columns, slots), F32)

    *sends, own_slots, x1, mask_ids, weight = call(
        functools.partial(sums_kernel, pad, slots // n),
        [short, message, short, short, slots_message, array(whole, F32), array(of_rows, jnp.int32), array(of_rows, F32)],
        [hbm] * 4,
        [vmem] * (NEAR + 4),
        [
            pltpu.VMEM(of_rows, F32),
            pltpu.VMEM(whole, F32),
            pltpu.VMEM((columns, slots), F32),
            pltpu.VMEM(lengths.shape, jnp.int32),
            pltpu.VMEM(ids.shape, jnp.int32),
            pltpu.VMEM(firms.shape, jnp.int32),
            pltpu.SemaphoreType.DMA((columns // 8,)),
            pltpu.SemaphoreType.DMA((3,)),
        ],
        2 * work,
        4 * columns * rows_dev,
    )(in_hbm(probes), in_hbm(lengths), in_hbm(ids), in_hbm(firms))

    def pair_counts(one, start, copy=()):
        return call(
            functools.partial(pairs_kernel, pad, start, 1),
            [array((1, slots, 2 * slots), BF16), *copy],
            [vmem],
            [vmem] * (1 + len(copy)),
            [
                pltpu.VMEM((1, *of_rows), F32),
                pltpu.VMEM((1, 8, slots), F32),
                pltpu.VMEM((1, slots, workers), BF16),
            ],
            work // 4,
            4 * slots * slots,
        )(one)

    def near_step(one, step):
        return lax.ppermute(one, "rows", [(i, i ^ step) for i in range(n)])

    arrived = near_exchange(sends, n)
    own_pairs, own_slots = pair_counts(own_slots, 8, [slots_message])
    passed = near_step(own_slots, 2)
    pairs = [own_pairs]
    joined = call(
        functools.partial(join_kernel, part),
        array((columns + 2 * NEAR, slots), F32),
        [vmem] * (NEAR + 1),
        vmem,
        [],
        0,
        message.size * 8,
    )(*arrived, *pairs)
    shared = far_share(joined, n)
    tables, beside = [], passed
    table = array((tiles, NEAR * LANES, NEAR * LANES), BF16)

    def firm_table(one, passed, out):
        return call(
            functools.partial(firms_kernel, part),
            out,
            [vmem] * 3,
            [vmem] * len(out),
            [],
            work // 64,
            tiles * (NEAR * LANES) ** 2 * 2,
        )(joined, one, passed)

    if keep:
        first_table, beside = firm_table(joined, passed, [table, slots_message])
        tables = [first_table, *firm_table(shared[-1], first_table, [table])]
    pairs += pair_counts(arrived[1], about) + pair_counts(passed, 8) + pair_counts(near_step(beside, 1), 8)
    scale = array((tiles, 8, NEAR * LANES), F32)
    made = [table] * (far - 2) * keep
    mean, sums, scales, *made = call(
        functools.partial(change_kernel, far, part, len(tables)),
        [of_near, of_near, scale, *made],
        [vmem] * (far + len(tables) + len(pairs)),
        [vmem] * (3 + len(made)),
        [],
        work // 4,
        slots * slots * 4,
    )(*shared, *tables, *pairs)
    again = far_share(sums, n)
    source = [tables[0], *made, tables[1]] if keep else shared
    spreads = []
    sends = [mean[part * k : part * (k + 1)] for k in range(NEAR)]
    if keep:
        *spreads, a, b, c, d = call(
            functools.partial(tables_kernel, pad),
            [array((slots, rows_dev), BF16)] * 2 + [array((part, slots), F32)] * NEAR,
            [vmem] * 2,
            [vmem] * (2 + NEAR),
            [],
            work,
            4 * slots * rows_dev,
        )(mask_ids, mean)
        sends = [a, b, c, d]
    first = near_exchange(sends, n)
    sends = call(
        functools.partial(means_kernel, far, part, keep),
        [array((part, slots), F32)] * NEAR,
        [vmem] * (far + len(source) + 2),
        [vmem] * NEAR,
        [pltpu.VMEM((columns, slots), F32)],
        work // 4,
        slots * slots * 4,
    )(*again, *source, scales, spreads[1] if keep else scales)
    arrived = near_exchange(sends, n)
    before = call(
        functools.partial(first_kernel, pad),
        array(whole, F32),
        [vmem] * (NEAR + 3 + len(spreads)),
        vmem,
        [pltpu.VMEM((columns, slots), F32)],
        work,
        8 * columns * rows_dev,
    )(*first, x1, mask_ids, weight, *spreads)
    return call(
        last_kernel,
        array(whole, F32),
        [vmem] * (NEAR + 2 + len(spreads[:1])),
        hbm,
        [pltpu.VMEM((columns, slots), F32), pltpu.VMEM(whole, F32), sems],
        work,
        8 * columns * rows_dev,
    )(*arrived, before, mask_ids, *spreads[:1])


def solution(mesh):
    placed = (P(None, ("grp", "rows")), P(("grp", "rows")), P(("grp", "rows")), P(("grp", "rows")))
    return jax.shard_map(
        functools.partial(body, n=mesh.shape["rows"]),
        mesh=mesh,
        in_specs=placed,
        out_specs=P(None, ("grp", "rows")),
        check_vma=False,
    )
```

```python
import functools

import jax
import jax.numpy as jnp
from jax import lax
from jax.experimental import pallas as pl
from jax.experimental.pallas import tpu as pltpu
from jax.sharding import PartitionSpec as P

FIRMS_PER_SHARD = 1024
LANES = 128
BLOCK = 1024
VMEM_BYTES = 32 * 1024 * 1024
NEAR = 4
NEAR_STEPS = (0, 1, 2, 3)
F32, BF16 = jnp.float32, jnp.bfloat16
NT = (((1,), (1,)), ((), ()))
NN = (((1,), (0,)), ((), ()))


def dot(a, b, dims=NN):
    return lax.dot_general(a, b, dims, preferred_element_type=F32)


def iota(shape, dim):
    return lax.broadcasted_iota(jnp.int32, shape, dim)


def split(x):
    hi = x.astype(BF16)
    return hi, (x - hi.astype(F32)).astype(BF16)


def row(ref, block, size):
    per = size // LANES
    return jnp.concatenate([ref[block * per + k : block * per + k + 1, :] for k in range(per)], axis=1)


def one_hot(ids, slots):
    kind = BF16 if slots <= 256 else F32
    slot = iota((slots, LANES), 0).astype(F32).astype(kind)
    ids = ids.astype(F32).astype(kind)
    one, zero = jnp.ones((slots, LANES), kind), jnp.zeros((slots, LANES), kind)
    parts = [jnp.where(slot == ids[:, k : k + LANES], one, zero) for k in range(0, ids.shape[1], LANES)]
    return jnp.concatenate(parts, axis=1).astype(BF16)


def one_hot_down(columns, slots):
    kind = BF16 if slots <= 256 else F32
    one, zero = jnp.ones((LANES, LANES), kind), jnp.zeros((LANES, LANES), kind)
    along_slots = [(iota((LANES, LANES), 1) + at).astype(F32).astype(kind) for at in range(0, slots, LANES)]
    parts, columns = [], columns.astype(kind)
    for k in range(columns.shape[1]):
        ids = jnp.broadcast_to(columns[:, k : k + 1], (LANES, LANES))
        parts.append(jnp.concatenate([jnp.where(slot == ids, one, zero) for slot in along_slots], axis=1))
    return jnp.concatenate(parts, axis=0).astype(BF16)


def same_worker(pad, width):
    return (iota((width, width), 0) // pad == iota((width, width), 1) // pad).astype(F32).astype(BF16)


def by_worker(x, table):
    rows, width = x.shape
    step = table.shape[1]
    both = [
        jnp.concatenate([one[:, k : k + step] for k in range(0, width, step)], axis=0) for one in split(x)
    ]
    total = dot(jnp.concatenate(both, axis=1), table)
    return jnp.concatenate([total[k : k + rows] for k in range(0, total.shape[0], rows)], axis=1)


def start_all(copies):
    for copy in copies:
        copy.start()


def wait_all(copies):
    for copy in copies:
        copy.wait()


def column_copies(source, target, sems, size=BLOCK):
    width = source.shape[1]
    cuts = [pl.ds(start, size) for start in range(0, width, size)]
    return [pltpu.make_async_copy(source.at[:, cut], target.at[:, cut], sems.at[b]) for b, cut in enumerate(cuts)]


def row_lengths(lengths, pad):
    total_rows = lengths.shape[0] * pad
    here = iota((total_rows, LANES), 0)
    lane = iota((total_rows, LANES), 1)
    wide = jnp.broadcast_to(lengths.astype(F32)[:, None, :], (lengths.shape[0], pad, LANES)).reshape(total_rows, LANES)
    per = LANES // pad
    wide = jnp.where(lane // per == here % pad, wide, 0.0).astype(BF16)
    spread = (iota((LANES, LANES), 0) % per == iota((LANES, LANES), 1) // pad).astype(F32).astype(BF16)
    row_len = dot(wide, spread)
    return row_len, (lane % pad).astype(F32) < row_len


def along(ref):
    return jnp.concatenate([ref[k : k + 1, :] for k in range(ref.shape[0])], axis=1)


def sums_kernel(pad, cap, *refs):
    (probes, lengths_in, ids_in, firms_in), sends, slots_out = refs[:4], refs[4 : 4 + NEAR], refs[4 + NEAR]
    refs = refs[5 + NEAR :]
    x1, mask_ids, weight, valid, x, sums, lengths, ids, firms, bands_sem, small = refs
    bands = [pl.ds(at, 8) for at in range(0, x.shape[0], 8)]
    copies = [pltpu.make_async_copy(probes.at[at], x.at[at], bands_sem.at[b]) for b, at in enumerate(bands)]
    first = [
        pltpu.make_async_copy(source, target, small.at[k])
        for k, (source, target) in enumerate(((lengths_in, lengths), (ids_in, ids), (firms_in, firms)))
    ]
    start_all(first)
    start_all(copies)
    columns, slots = sums.shape
    part = columns // NEAR
    me = lax.axis_index("rows") % NEAR
    wait_all(first)
    row_len, inside = row_lengths(lengths[...], pad)
    valid[...] = jnp.where(inside, 1.0, 0.0)
    weight[...] = jnp.where(inside, 1.0 / row_len, 0.0)
    masked = jnp.where(inside, ids[...], -1)
    mask_ids[...] = masked
    turned = jnp.concatenate([masked.astype(F32)] * (LANES // masked.shape[0]), axis=0).T
    keys = (iota((1, slots), 1) // cap * FIRMS_PER_SHARD + along(firms)).astype(F32)
    across = slots // LANES
    rows = ids.shape[0] // across
    masked = jnp.concatenate([masked[k * rows : (k + 1) * rows] for k in range(across)], axis=1).astype(F32)
    sends[1][part + 8 :] = masked
    slots_out[8:] = masked

    table = jnp.concatenate([same_worker(pad, 256)] * 2, axis=0)
    wait_all(copies)
    total = None
    for b in range(x.shape[1] // BLOCK):
        ok = row(valid, b, BLOCK)
        x0 = x[:, b * BLOCK : (b + 1) * BLOCK] * ok
        rest = x0 - by_worker(x0, table) * row(weight, b, BLOCK)
        x1[:, b * BLOCK : (b + 1) * BLOCK] = rest
        counted = jnp.broadcast_to(ok, (16, BLOCK)).astype(BF16)
        data = jnp.concatenate([*split(rest), counted], axis=0)
        per = BLOCK // LANES
        block = dot(data, one_hot_down(turned[:, b * per : (b + 1) * per], slots))
        total = block if total is None else total + block
    sums[...] = total[:columns] + total[columns : 2 * columns]
    about = jnp.where(iota((8, slots), 0) == 0, keys, total[2 * columns : 2 * columns + 1])
    for step, send in zip(NEAR_STEPS, sends):
        send[:part] = sums[pl.ds(pl.multiple_of((me ^ step) * part, part), part), :]
        send[part : part + 8] = about
    slots_out[:8] = about


def join_copy(one, out):
    out[...] = one[...]


def join_kernel(part, *refs):
    parts, out = refs[:NEAR], refs[-1]
    for k, one in enumerate(parts):
        out[part * k : part * (k + 1)] = one[:part]
        out[part * NEAR + 2 * k : part * NEAR + 2 * k + 2] = one[part : part + 2]


def pairs_kernel(pad, several, *refs):
    parts, (out, *copy, ids, size, counts) = refs[:several], refs[several:]
    for ref in copy:
        ref[...] = parts[0][...]
    slots = out.shape[1]
    kind = BF16 if slots <= 256 else F32
    per = LANES // pad
    total_rows = ids.shape[1]
    across = slots // LANES
    rows = total_rows // across
    for k, part in enumerate(parts):
        start = part.shape[0] - rows
        size[k] = jnp.broadcast_to(part[start - 7 : start - 6], (8, slots))
        for at in range(across):
            ids[k, at * rows : (at + 1) * rows] = part[start:, at * LANES : (at + 1) * LANES]
    at = iota((LANES, pad * LANES), 1)
    deal = (iota((LANES, pad * LANES), 0) == at % per * pad + at // LANES).astype(F32).astype(BF16)
    mine = iota((total_rows, pad * LANES), 1) % LANES // per == iota((total_rows, pad * LANES), 0) % pad
    slot = iota((slots, LANES), 0).astype(F32).astype(kind)
    one, zero = jnp.ones((slots, LANES), kind), jnp.zeros((slots, LANES), kind)
    diagonal = iota((slots, slots), 1) == iota((slots, slots), 0)

    def device(k, carry):
        dealt = dot(jnp.concatenate(split(ids[k]), axis=0), deal)
        dealt = jnp.where(mine, dealt[:total_rows] + dealt[total_rows:], 0.0)
        dealt = jnp.sum(dealt.reshape(total_rows // pad, pad, pad * LANES), axis=1)
        spells = dealt.astype(kind)
        for g in range(total_rows // pad):
            total = zero
            for j in range(pad):
                total += jnp.where(slot == spells[g : g + 1, j * LANES : (j + 1) * LANES], one, zero)
            counts[k, :, g * LANES : (g + 1) * LANES] = total.astype(BF16)
        valid = jnp.where(dealt >= 0.0, 1.0, 0.0)
        length = valid[:, :LANES]
        for j in range(1, pad):
            length += valid[:, j * LANES : (j + 1) * LANES]
        inverse = 1.0 / length
        inverse = jnp.concatenate([inverse[g : g + 1] for g in range(total_rows // pad)], axis=1)
        here = counts[k]
        total = dot(jnp.concatenate(split(here.astype(F32) * inverse), axis=0), here, NT)
        total = total[:slots] + total[slots:] - jnp.where(diagonal, size[k, :1], 0.0)
        hi, lo = split(total)
        out[k, :, :slots] = hi
        out[k, :, slots:] = lo
        return carry

    lax.fori_loop(0, len(parts), device, 0, unroll=len(parts) if slots <= 256 else 1)


def same_firm(own, one, part, at):
    mine, keys = ([ref[part * NEAR + 2 * k : part * NEAR + 2 * k + 1, at] for k in range(NEAR)] for ref in (own, one))
    mine = jnp.concatenate(mine, axis=1)
    down = jnp.concatenate([jnp.broadcast_to(key, (8, LANES)) for key in keys], axis=0).T
    found = [(down[:, 8 * k : 8 * k + 1] == mine).astype(F32).astype(BF16) for k in range(NEAR)]
    return jnp.concatenate(found, axis=0)


def each_tile(slots, do):
    tiles = slots // LANES
    if tiles <= 2:
        for t in range(tiles):
            do(t, slice(t * LANES, (t + 1) * LANES))
    else:
        lax.fori_loop(0, tiles, lambda t, c: (do(t, pl.ds(pl.multiple_of(t * LANES, LANES), LANES)), c)[1], 0)


def firms_kernel(part, own, one, passed, out, *copy):
    for ref in copy:
        ref[...] = passed[...]
    each_tile(own.shape[1], lambda t, at: out.__setitem__(t, same_firm(own, one, part, at)))


def gathered(parts, part, at):
    data = [one[part * k : part * (k + 1), at] for one in parts for k in range(NEAR)]
    return jnp.concatenate(split(jnp.concatenate(data, axis=1)), axis=0)


def spread_out(means, out, part, at):
    for k in range(NEAR):
        out[part * k : part * (k + 1), at] = means[:, k * LANES : (k + 1) * LANES]


def change_kernel(far, part, ready, *refs):
    parts, tables, refs = refs[:far], refs[far : far + ready], refs[far + ready :]
    pairs = [(group, k) for group in refs[:2] for k in range(group.shape[0])]
    (mean, sums, scale), made = refs[2:5], refs[5:]
    slots = mean.shape[1]

    def tile(t, at):
        if tables:
            between = [same_firm(parts[0], one, part, at) for one in parts[1:-1]]
            for ref, one in zip(made, between):
                ref[t] = one
            same = [tables[0][t], *between, tables[1][t]]
        else:
            same = [same_firm(parts[0], one, part, at) for one in parts]
        same = jnp.concatenate(same, axis=0)
        count = [one[part * NEAR + 2 * k + 1 : part * NEAR + 2 * k + 2, at] for one in parts for k in range(NEAR)]
        count = jnp.concatenate(count, axis=1)
        high = count.astype(BF16).astype(F32)
        counts = jnp.where(iota((16, count.shape[1]), 0) < 8, high, count - high).astype(BF16)
        found = dot(jnp.concatenate([gathered(parts, part, at), counts], axis=0), same)
        size = found[2 * part : 2 * part + 1] + found[2 * part + 8 : 2 * part + 9]
        inverse = 1.0 / jnp.maximum(size, 1.0)
        scale[t] = jnp.broadcast_to(inverse, scale.shape[1:])
        spread_out((found[:part] + found[part : 2 * part]) * inverse, mean, part, at)

    each_tile(slots, tile)
    for k in range(NEAR):
        cut = slice(part * k, part * (k + 1))
        both = jnp.concatenate(split(mean[cut]), axis=0)
        change = dot(both, pairs[k][0][pairs[k][1]])
        change = change[:part] + change[part:]
        sums[cut] = parts[0][cut] + (change[:, :slots] + change[:, slots:])


def tables_kernel(pad, mask_ids, mean, spread, workers, *sends):
    part = mean.shape[0] // NEAR
    for k, send in enumerate(sends):
        send[...] = mean[part * k : part * (k + 1)]
    slots, width = spread.shape
    table = jnp.concatenate([same_worker(pad, 256)] * 2, axis=0)
    for b in range(width // BLOCK):
        found = one_hot(row(mask_ids, b, BLOCK), slots)
        spread[:, b * BLOCK : (b + 1) * BLOCK] = found
        for at in range(0, BLOCK, 256):
            count = dot(found[:, at : at + 256], table[:256])
            workers[:, b * BLOCK + at : b * BLOCK + at + 256] = count.astype(BF16)


def means_kernel(far, part, kept, *refs):
    parts, source, scale, sends, mean = refs[:far], refs[far:-7], refs[-7], refs[-5:-1], refs[-1]

    def tile(t, at):
        same = [table[t] if kept else same_firm(source[0], table, part, at) for table in source]
        same = jnp.concatenate(same, axis=0)
        found = dot(gathered(parts, part, at), same)
        spread_out((found[:part] + found[part:]) * scale[t][:1], mean, part, at)

    each_tile(mean.shape[1], tile)
    for k, send in enumerate(sends):
        send[...] = mean[part * k : part * (k + 1)]


def own_means(parts, means):
    me = lax.axis_index("rows") % NEAR
    part = parts[0].shape[0]
    for step, one in zip(NEAR_STEPS, parts):
        means[pl.ds(pl.multiple_of((me ^ step) * part, part), part), :] = one[...]
    return jnp.concatenate(split(means[...]), axis=0)


def first_kernel(pad, *refs):
    parts, (x1, mask_ids, weight), tables, (y, means) = refs[:NEAR], refs[NEAR : NEAR + 3], refs[NEAR + 3 : -2], refs[-2:]
    columns, slots = means.shape
    first = own_means(parts, means)
    table = jnp.concatenate([same_worker(pad, 256)] * 2, axis=0)
    for b in range(y.shape[1] // BLOCK):
        at = slice(b * BLOCK, (b + 1) * BLOCK)
        found = tables[0][:, at] if tables else one_hot(row(mask_ids, b, BLOCK), slots)
        spread = dot(first, found)
        spread = spread[:columns] + spread[columns:]
        if tables:
            worker = dot(first, tables[1][:, at])
            worker = worker[:columns] + worker[columns:]
        else:
            worker = by_worker(spread, table)
        y[:, at] = x1[:, at] - spread + worker * row(weight, b, BLOCK)


def last_kernel(*refs):
    parts, (before, mask_ids), tables, (out, means, y, sems) = refs[:NEAR], refs[NEAR : NEAR + 2], refs[NEAR + 2 : -4], refs[-4:]
    outs = column_copies(y, out, sems)
    columns, slots = means.shape
    second = own_means(parts, means)
    for b in range(len(outs)):
        at = slice(b * BLOCK, (b + 1) * BLOCK)
        found = tables[0][:, at] if tables else one_hot(row(mask_ids, b, BLOCK), slots)
        spread = dot(second, found)
        y[:, at] = before[:, at] - (spread[:columns] + spread[columns:])
        outs[b].start()
    wait_all(outs)


def near_exchange(parts, n):
    steps = [[(i, i ^ step) for i in range(n)] for step in NEAR_STEPS[1:]]
    return [parts[0]] + [lax.ppermute(one, "rows", step) for one, step in zip(parts[1:], steps)]


def far_share(one, n):
    steps = [[(i, i ^ (k * NEAR)) for i in range(n)] for k in range(1, n // NEAR)]
    return [one] + [lax.ppermute(one, "rows", step) for step in steps]


def in_hbm(x):
    return pltpu.with_memory_space_constraint(x, pltpu.HBM)


def call(kernel, out_shape, in_specs, out_specs, scratch, flops, moved):
    return pl.pallas_call(
        kernel,
        out_shape=out_shape,
        in_specs=in_specs,
        out_specs=out_specs,
        scratch_shapes=scratch,
        compiler_params=pltpu.CompilerParams(vmem_limit_bytes=VMEM_BYTES),
        cost_estimate=pl.CostEstimate(flops=flops, bytes_accessed=moved, transcendentals=0),
    )


def body(probes, worker_len, spell_to_slot, slot_to_firm, *, n):
    columns, rows_dev = probes.shape
    workers = worker_len.shape[0]
    pad = rows_dev // workers
    slots = slot_to_firm.shape[0]
    tiles = slots // LANES
    part = columns // NEAR
    far = n // NEAR
    keep = tiles * NEAR * n * LANES * LANES * 2 <= 8 * 1024 * 1024
    blocks = rows_dev // BLOCK
    vmem, hbm = pl.BlockSpec(memory_space=pltpu.VMEM), pl.BlockSpec(memory_space=pltpu.HBM)
    lengths = worker_len.reshape(workers // LANES, LANES)
    ids = spell_to_slot.reshape(rows_dev // LANES, LANES)
    firms = slot_to_firm.reshape(tiles, LANES)
    array = jax.ShapeDtypeStruct
    of_rows = (rows_dev // LANES, LANES)
    work = 2 * rows_dev * slots * 2 * columns
    sems = pltpu.SemaphoreType.DMA((blocks,))
    whole = (columns, rows_dev)
    about = part + 8
    message = array((about + rows_dev // slots, slots), F32)
    short = array((about, slots), F32)
    slots_message = array((message.shape[0] - part, slots), F32)
    of_near = array((columns, slots), F32)

    *sends, own_slots, x1, mask_ids, weight = call(
        functools.partial(sums_kernel, pad, slots // n),
        [short, message, short, short, slots_message, array(whole, F32), array(of_rows, jnp.int32), array(of_rows, F32)],
        [hbm] * 4,
        [vmem] * (NEAR + 4),
        [
            pltpu.VMEM(of_rows, F32),
            pltpu.VMEM(whole, F32),
            pltpu.VMEM((columns, slots), F32),
            pltpu.VMEM(lengths.shape, jnp.int32),
            pltpu.VMEM(ids.shape, jnp.int32),
            pltpu.VMEM(firms.shape, jnp.int32),
            pltpu.SemaphoreType.DMA((columns // 8,)),
            pltpu.SemaphoreType.DMA((3,)),
        ],
        2 * work,
        4 * columns * rows_dev,
    )(in_hbm(probes), in_hbm(lengths), in_hbm(ids), in_hbm(firms))

    def pair_counts(parts, copy=()):
        count = len(parts)
        return call(
            functools.partial(pairs_kernel, pad, count),
            [array((count, slots, 2 * slots), BF16), *copy],
            [vmem] * count,
            [vmem] * (1 + len(copy)),
            [
                pltpu.VMEM((count, *of_rows), F32),
                pltpu.VMEM((count, 8, slots), F32),
                pltpu.VMEM((count, slots, workers), BF16),
            ],
            work * count // 4,
            4 * slots * slots,
        )(*parts)

    def near_step(one, step):
        return lax.ppermute(one, "rows", [(i, i ^ step) for i in range(n)])

    arrived = near_exchange(sends, n)
    ready = call(join_copy, slots_message, [vmem], vmem, [], 0, slots_message.size * 8)(own_slots)
    passed = near_step(ready, 2)
    joined = call(
        functools.partial(join_kernel, part),
        array((columns + 2 * NEAR, slots), F32),
        [vmem] * NEAR,
        vmem,
        [],
        0,
        message.size * 8,
    )(*arrived)
    shared = far_share(joined, n)
    tables, beside = [], passed
    table = array((tiles, NEAR * LANES, NEAR * LANES), BF16)

    def firm_table(one, passed, out):
        return call(
            functools.partial(firms_kernel, part),
            out,
            [vmem] * 3,
            [vmem] * len(out),
            [],
            work // 64,
            tiles * (NEAR * LANES) ** 2 * 2,
        )(joined, one, passed)

    if keep:
        first_table, beside = firm_table(joined, passed, [table, slots_message])
        tables = [first_table, *firm_table(shared[-1], first_table, [table])]
    pairs = pair_counts([own_slots, arrived[1], passed]) + pair_counts([near_step(beside, 1)])
    scale = array((tiles, 8, NEAR * LANES), F32)
    made = [table] * (far - 2) * keep
    mean, sums, scales, *made = call(
        functools.partial(change_kernel, far, part, len(tables)),
        [of_near, of_near, scale, *made],
        [vmem] * (far + len(tables) + len(pairs)),
        [vmem] * (3 + len(made)),
        [],
        work // 4,
        slots * slots * 4,
    )(*shared, *tables, *pairs)
    again = far_share(sums, n)
    source = [tables[0], *made, tables[1]] if keep else shared
    spreads = []
    sends = [mean[part * k : part * (k + 1)] for k in range(NEAR)]
    if keep:
        *spreads, a, b, c, d = call(
            functools.partial(tables_kernel, pad),
            [array((slots, rows_dev), BF16)] * 2 + [array((part, slots), F32)] * NEAR,
            [vmem] * 2,
            [vmem] * (2 + NEAR),
            [],
            work,
            4 * slots * rows_dev,
        )(mask_ids, mean)
        sends = [a, b, c, d]
    first = near_exchange(sends, n)
    sends = call(
        functools.partial(means_kernel, far, part, keep),
        [array((part, slots), F32)] * NEAR,
        [vmem] * (far + len(source) + 2),
        [vmem] * NEAR,
        [pltpu.VMEM((columns, slots), F32)],
        work // 4,
        slots * slots * 4,
    )(*again, *source, scales, spreads[1] if keep else scales)
    arrived = near_exchange(sends, n)
    before = call(
        functools.partial(first_kernel, pad),
        array(whole, F32),
        [vmem] * (NEAR + 3 + len(spreads)),
        vmem,
        [pltpu.VMEM((columns, slots), F32)],
        work,
        8 * columns * rows_dev,
    )(*first, x1, mask_ids, weight, *spreads)
    return call(
        last_kernel,
        array(whole, F32),
        [vmem] * (NEAR + 2 + len(spreads[:1])),
        hbm,
        [pltpu.VMEM((columns, slots), F32), pltpu.VMEM(whole, F32), sems],
        work,
        8 * columns * rows_dev,
    )(*arrived, before, mask_ids, *spreads[:1])


def solution(mesh):
    placed = (P(None, ("grp", "rows")), P(("grp", "rows")), P(("grp", "rows")), P(("grp", "rows")))
    return jax.shard_map(
        functools.partial(body, n=mesh.shape["rows"]),
        mesh=mesh,
        in_specs=placed,
        out_specs=P(None, ("grp", "rows")),
        check_vma=False,
    )
```

```python
import functools

import jax
import jax.numpy as jnp
from jax import lax
from jax.experimental import pallas as pl
from jax.experimental.pallas import tpu as pltpu
from jax.sharding import PartitionSpec as P

FIRMS_PER_SHARD = 1024
LANES = 128
BLOCK = 1024
VMEM_BYTES = 32 * 1024 * 1024
NEAR = 4
NEAR_STEPS = (0, 1, 2, 3)
F32, BF16 = jnp.float32, jnp.bfloat16
NT = (((1,), (1,)), ((), ()))
NN = (((1,), (0,)), ((), ()))


def dot(a, b, dims=NN):
    return lax.dot_general(a, b, dims, preferred_element_type=F32)


def iota(shape, dim):
    return lax.broadcasted_iota(jnp.int32, shape, dim)


def split(x):
    hi = x.astype(BF16)
    return hi, (x - hi.astype(F32)).astype(BF16)


def row(ref, block, size):
    per = size // LANES
    return jnp.concatenate([ref[block * per + k : block * per + k + 1, :] for k in range(per)], axis=1)


def one_hot(ids, slots):
    kind = BF16 if slots <= 256 else F32
    slot = iota((slots, LANES), 0).astype(F32).astype(kind)
    ids = ids.astype(F32).astype(kind)
    one, zero = jnp.ones((slots, LANES), kind), jnp.zeros((slots, LANES), kind)
    parts = [jnp.where(slot == ids[:, k : k + LANES], one, zero) for k in range(0, ids.shape[1], LANES)]
    return jnp.concatenate(parts, axis=1).astype(BF16)


def one_hot_down(columns, slots):
    kind = BF16 if slots <= 256 else F32
    one, zero = jnp.ones((LANES, LANES), kind), jnp.zeros((LANES, LANES), kind)
    along_slots = [(iota((LANES, LANES), 1) + at).astype(F32).astype(kind) for at in range(0, slots, LANES)]
    parts, columns = [], columns.astype(kind)
    for k in range(columns.shape[1]):
        ids = jnp.broadcast_to(columns[:, k : k + 1], (LANES, LANES))
        parts.append(jnp.concatenate([jnp.where(slot == ids, one, zero) for slot in along_slots], axis=1))
    return jnp.concatenate(parts, axis=0).astype(BF16)


def same_worker(pad, width):
    return (iota((width, width), 0) // pad == iota((width, width), 1) // pad).astype(F32).astype(BF16)


def by_worker(x, table):
    rows, width = x.shape
    step = table.shape[1]
    both = [
        jnp.concatenate([one[:, k : k + step] for k in range(0, width, step)], axis=0) for one in split(x)
    ]
    total = dot(jnp.concatenate(both, axis=1), table)
    return jnp.concatenate([total[k : k + rows] for k in range(0, total.shape[0], rows)], axis=1)


def start_all(copies):
    for copy in copies:
        copy.start()


def wait_all(copies):
    for copy in copies:
        copy.wait()


def column_copies(source, target, sems, size=BLOCK):
    width = source.shape[1]
    cuts = [pl.ds(start, size) for start in range(0, width, size)]
    return [pltpu.make_async_copy(source.at[:, cut], target.at[:, cut], sems.at[b]) for b, cut in enumerate(cuts)]


def row_lengths(lengths, pad):
    total_rows = lengths.shape[0] * pad
    here = iota((total_rows, LANES), 0)
    lane = iota((total_rows, LANES), 1)
    wide = jnp.broadcast_to(lengths.astype(F32)[:, None, :], (lengths.shape[0], pad, LANES)).reshape(total_rows, LANES)
    per = LANES // pad
    wide = jnp.where(lane // per == here % pad, wide, 0.0).astype(BF16)
    spread = (iota((LANES, LANES), 0) % per == iota((LANES, LANES), 1) // pad).astype(F32).astype(BF16)
    row_len = dot(wide, spread)
    return row_len, (lane % pad).astype(F32) < row_len


def along(ref):
    return jnp.concatenate([ref[k : k + 1, :] for k in range(ref.shape[0])], axis=1)


def sums_kernel(pad, cap, *refs):
    (probes, lengths_in, ids_in, firms_in), sends, slots_out = refs[:4], refs[4 : 4 + NEAR], refs[4 + NEAR]
    refs = refs[5 + NEAR :]
    x1, mask_ids, weight, valid, x, sums, lengths, ids, firms, bands_sem, small = refs
    bands = [pl.ds(at, 8) for at in range(0, x.shape[0], 8)]
    copies = [pltpu.make_async_copy(probes.at[at], x.at[at], bands_sem.at[b]) for b, at in enumerate(bands)]
    first = [
        pltpu.make_async_copy(source, target, small.at[k])
        for k, (source, target) in enumerate(((lengths_in, lengths), (ids_in, ids), (firms_in, firms)))
    ]
    start_all(first)
    start_all(copies)
    columns, slots = sums.shape
    part = columns // NEAR
    me = lax.axis_index("rows") % NEAR
    wait_all(first)
    row_len, inside = row_lengths(lengths[...], pad)
    valid[...] = jnp.where(inside, 1.0, 0.0)
    weight[...] = jnp.where(inside, 1.0 / row_len, 0.0)
    masked = jnp.where(inside, ids[...], -1)
    mask_ids[...] = masked
    turned = jnp.concatenate([masked.astype(F32)] * (LANES // masked.shape[0]), axis=0).T
    keys = (iota((1, slots), 1) // cap * FIRMS_PER_SHARD + along(firms)).astype(F32)
    across = slots // LANES
    rows = ids.shape[0] // across
    masked = jnp.concatenate([masked[k * rows : (k + 1) * rows] for k in range(across)], axis=1).astype(F32)
    sends[1][part + 8 :] = masked
    slots_out[8:] = masked

    table = jnp.concatenate([same_worker(pad, 256)] * 2, axis=0)
    wait_all(copies)
    total = None
    for b in range(x.shape[1] // BLOCK):
        ok = row(valid, b, BLOCK)
        x0 = x[:, b * BLOCK : (b + 1) * BLOCK] * ok
        rest = x0 - by_worker(x0, table) * row(weight, b, BLOCK)
        x1[:, b * BLOCK : (b + 1) * BLOCK] = rest
        counted = jnp.broadcast_to(ok, (16, BLOCK)).astype(BF16)
        data = jnp.concatenate([*split(rest), counted], axis=0)
        per = BLOCK // LANES
        block = dot(data, one_hot_down(turned[:, b * per : (b + 1) * per], slots))
        total = block if total is None else total + block
    sums[...] = total[:columns] + total[columns : 2 * columns]
    about = jnp.where(iota((8, slots), 0) == 0, keys, total[2 * columns : 2 * columns + 1])
    for step, send in zip(NEAR_STEPS, sends):
        send[:part] = sums[pl.ds(pl.multiple_of((me ^ step) * part, part), part), :]
        send[part : part + 8] = about
    slots_out[:8] = about


def join_kernel(part, *refs):
    parts, out = refs[:NEAR], refs[-1]
    for k, one in enumerate(parts):
        out[part * k : part * (k + 1)] = one[:part]
        out[part * NEAR + 2 * k : part * NEAR + 2 * k + 2] = one[part : part + 2]


def pairs_kernel(pad, start, several, *refs):
    parts, (out, *copy, ids, size, counts) = refs[:several], refs[several:]
    for ref in copy:
        ref[...] = parts[0][...]
    slots = out.shape[1]
    kind = BF16 if slots <= 256 else F32
    per = LANES // pad
    total_rows = ids.shape[1]
    across = slots // LANES
    rows = total_rows // across
    for k, part in enumerate(parts):
        size[k] = jnp.broadcast_to(part[start - 7 : start - 6], (8, slots))
        for at in range(across):
            ids[k, at * rows : (at + 1) * rows] = part[start:, at * LANES : (at + 1) * LANES]
    at = iota((LANES, pad * LANES), 1)
    deal = (iota((LANES, pad * LANES), 0) == at % per * pad + at // LANES).astype(F32).astype(BF16)
    mine = iota((total_rows, pad * LANES), 1) % LANES // per == iota((total_rows, pad * LANES), 0) % pad
    slot = iota((slots, LANES), 0).astype(F32).astype(kind)
    one, zero = jnp.ones((slots, LANES), kind), jnp.zeros((slots, LANES), kind)
    diagonal = iota((slots, slots), 1) == iota((slots, slots), 0)

    def device(k, carry):
        dealt = dot(jnp.concatenate(split(ids[k]), axis=0), deal)
        dealt = jnp.where(mine, dealt[:total_rows] + dealt[total_rows:], 0.0)
        dealt = jnp.sum(dealt.reshape(total_rows // pad, pad, pad * LANES), axis=1)
        spells = dealt.astype(kind)
        for g in range(total_rows // pad):
            total = zero
            for j in range(pad):
                total += jnp.where(slot == spells[g : g + 1, j * LANES : (j + 1) * LANES], one, zero)
            counts[k, :, g * LANES : (g + 1) * LANES] = total.astype(BF16)
        valid = jnp.where(dealt >= 0.0, 1.0, 0.0)
        length = valid[:, :LANES]
        for j in range(1, pad):
            length += valid[:, j * LANES : (j + 1) * LANES]
        inverse = 1.0 / length
        inverse = jnp.concatenate([inverse[g : g + 1] for g in range(total_rows // pad)], axis=1)
        here = counts[k]
        total = dot(jnp.concatenate(split(here.astype(F32) * inverse), axis=0), here, NT)
        total = total[:slots] + total[slots:] - jnp.where(diagonal, size[k, :1], 0.0)
        hi, lo = split(total)
        out[k, :, :slots] = hi
        out[k, :, slots:] = lo
        return carry

    lax.fori_loop(0, len(parts), device, 0, unroll=len(parts) if slots <= 256 else 1)


def same_firm(own, one, part, at):
    mine, keys = ([ref[part * NEAR + 2 * k : part * NEAR + 2 * k + 1, at] for k in range(NEAR)] for ref in (own, one))
    mine = jnp.concatenate(mine, axis=1)
    down = jnp.concatenate([jnp.broadcast_to(key, (8, LANES)) for key in keys], axis=0).T
    found = [(down[:, 8 * k : 8 * k + 1] == mine).astype(F32).astype(BF16) for k in range(NEAR)]
    return jnp.concatenate(found, axis=0)


def each_tile(slots, do):
    tiles = slots // LANES
    if tiles <= 2:
        for t in range(tiles):
            do(t, slice(t * LANES, (t + 1) * LANES))
    else:
        lax.fori_loop(0, tiles, lambda t, c: (do(t, pl.ds(pl.multiple_of(t * LANES, LANES), LANES)), c)[1], 0)


def firms_kernel(part, own, one, passed, out, *copy):
    for ref in copy:
        ref[...] = passed[...]
    each_tile(own.shape[1], lambda t, at: out.__setitem__(t, same_firm(own, one, part, at)))


def gathered(parts, part, at):
    data = [one[part * k : part * (k + 1), at] for one in parts for k in range(NEAR)]
    return jnp.concatenate(split(jnp.concatenate(data, axis=1)), axis=0)


def spread_out(means, out, part, at):
    for k in range(NEAR):
        out[part * k : part * (k + 1), at] = means[:, k * LANES : (k + 1) * LANES]


def change_kernel(far, part, ready, *refs):
    tables, pairs, refs = refs[far : far + ready], refs[far + ready : far + ready + NEAR], refs
    parts, (mean, sums, scale), made = refs[:far], refs[far + ready + NEAR :][:3], refs[far + ready + NEAR + 3 :]
    slots = mean.shape[1]

    def tile(t, at):
        if tables:
            between = [same_firm(parts[0], one, part, at) for one in parts[1:-1]]
            for ref, one in zip(made, between):
                ref[t] = one
            same = [tables[0][t], *between, tables[1][t]]
        else:
            same = [same_firm(parts[0], one, part, at) for one in parts]
        same = jnp.concatenate(same, axis=0)
        count = [one[part * NEAR + 2 * k + 1 : part * NEAR + 2 * k + 2, at] for one in parts for k in range(NEAR)]
        count = jnp.concatenate(count, axis=1)
        high = count.astype(BF16).astype(F32)
        counts = jnp.where(iota((16, count.shape[1]), 0) < 8, high, count - high).astype(BF16)
        found = dot(jnp.concatenate([gathered(parts, part, at), counts], axis=0), same)
        size = found[2 * part : 2 * part + 1] + found[2 * part + 8 : 2 * part + 9]
        inverse = 1.0 / jnp.maximum(size, 1.0)
        scale[t] = jnp.broadcast_to(inverse, scale.shape[1:])
        spread_out((found[:part] + found[part : 2 * part]) * inverse, mean, part, at)

    each_tile(slots, tile)
    for k in range(NEAR):
        cut = slice(part * k, part * (k + 1))
        both = jnp.concatenate(split(mean[cut]), axis=0)
        change = dot(both, pairs[k][0])
        change = change[:part] + change[part:]
        sums[cut] = parts[0][cut] + (change[:, :slots] + change[:, slots:])


def tables_kernel(pad, mask_ids, mean, spread, workers, *sends):
    part = mean.shape[0] // NEAR
    for k, send in enumerate(sends):
        send[...] = mean[part * k : part * (k + 1)]
    slots, width = spread.shape
    table = jnp.concatenate([same_worker(pad, 256)] * 2, axis=0)
    for b in range(width // BLOCK):
        found = one_hot(row(mask_ids, b, BLOCK), slots)
        spread[:, b * BLOCK : (b + 1) * BLOCK] = found
        for at in range(0, BLOCK, 256):
            count = dot(found[:, at : at + 256], table[:256])
            workers[:, b * BLOCK + at : b * BLOCK + at + 256] = count.astype(BF16)


def means_kernel(far, part, kept, *refs):
    parts, source, scale, sends, mean = refs[:far], refs[far:-7], refs[-7], refs[-5:-1], refs[-1]

    def tile(t, at):
        same = [table[t] if kept else same_firm(source[0], table, part, at) for table in source]
        same = jnp.concatenate(same, axis=0)
        found = dot(gathered(parts, part, at), same)
        spread_out((found[:part] + found[part:]) * scale[t][:1], mean, part, at)

    each_tile(mean.shape[1], tile)
    for k, send in enumerate(sends):
        send[...] = mean[part * k : part * (k + 1)]


def own_means(parts, means):
    me = lax.axis_index("rows") % NEAR
    part = parts[0].shape[0]
    for step, one in zip(NEAR_STEPS, parts):
        means[pl.ds(pl.multiple_of((me ^ step) * part, part), part), :] = one[...]
    return jnp.concatenate(split(means[...]), axis=0)


def first_kernel(pad, *refs):
    parts, (x1, mask_ids, weight), tables, (y, means) = refs[:NEAR], refs[NEAR : NEAR + 3], refs[NEAR + 3 : -2], refs[-2:]
    columns, slots = means.shape
    first = own_means(parts, means)
    table = jnp.concatenate([same_worker(pad, 256)] * 2, axis=0)
    for b in range(y.shape[1] // BLOCK):
        at = slice(b * BLOCK, (b + 1) * BLOCK)
        found = tables[0][:, at] if tables else one_hot(row(mask_ids, b, BLOCK), slots)
        spread = dot(first, found)
        spread = spread[:columns] + spread[columns:]
        if tables:
            worker = dot(first, tables[1][:, at])
            worker = worker[:columns] + worker[columns:]
        else:
            worker = by_worker(spread, table)
        y[:, at] = x1[:, at] - spread + worker * row(weight, b, BLOCK)


def last_kernel(*refs):
    parts, (before, mask_ids), tables, (out, means, y, sems) = refs[:NEAR], refs[NEAR : NEAR + 2], refs[NEAR + 2 : -4], refs[-4:]
    outs = column_copies(y, out, sems)
    columns, slots = means.shape
    second = own_means([*parts[:2], parts[3], parts[2]], means)
    for b in range(len(outs)):
        at = slice(b * BLOCK, (b + 1) * BLOCK)
        found = tables[0][:, at] if tables else one_hot(row(mask_ids, b, BLOCK), slots)
        spread = dot(second, found)
        y[:, at] = before[:, at] - (spread[:columns] + spread[columns:])
        outs[b].start()
    wait_all(outs)


def near_exchange(parts, n):
    steps = [[(i, i ^ step) for i in range(n)] for step in NEAR_STEPS[1:]]
    return [parts[0]] + [lax.ppermute(one, "rows", step) for one, step in zip(parts[1:], steps)]


def far_share(one, n):
    steps = [[(i, i ^ (k * NEAR)) for i in range(n)] for k in range(1, n // NEAR)]
    return [one] + [lax.ppermute(one, "rows", step) for step in steps]


def in_hbm(x):
    return pltpu.with_memory_space_constraint(x, pltpu.HBM)


def call(kernel, out_shape, in_specs, out_specs, scratch, flops, moved):
    return pl.pallas_call(
        kernel,
        out_shape=out_shape,
        in_specs=in_specs,
        out_specs=out_specs,
        scratch_shapes=scratch,
        compiler_params=pltpu.CompilerParams(vmem_limit_bytes=VMEM_BYTES),
        cost_estimate=pl.CostEstimate(flops=flops, bytes_accessed=moved, transcendentals=0),
    )


def body(probes, worker_len, spell_to_slot, slot_to_firm, *, n):
    columns, rows_dev = probes.shape
    workers = worker_len.shape[0]
    pad = rows_dev // workers
    slots = slot_to_firm.shape[0]
    tiles = slots // LANES
    part = columns // NEAR
    far = n // NEAR
    keep = tiles * NEAR * n * LANES * LANES * 2 <= 8 * 1024 * 1024
    blocks = rows_dev // BLOCK
    vmem, hbm = pl.BlockSpec(memory_space=pltpu.VMEM), pl.BlockSpec(memory_space=pltpu.HBM)
    lengths = worker_len.reshape(workers // LANES, LANES)
    ids = spell_to_slot.reshape(rows_dev // LANES, LANES)
    firms = slot_to_firm.reshape(tiles, LANES)
    array = jax.ShapeDtypeStruct
    of_rows = (rows_dev // LANES, LANES)
    work = 2 * rows_dev * slots * 2 * columns
    sems = pltpu.SemaphoreType.DMA((blocks,))
    whole = (columns, rows_dev)
    about = part + 8
    message = array((about + rows_dev // slots, slots), F32)
    short = array((about, slots), F32)
    slots_message = array((message.shape[0] - part, slots), F32)
    of_near = array((columns, slots), F32)

    *sends, own_slots, x1, mask_ids, weight = call(
        functools.partial(sums_kernel, pad, slots // n),
        [short, message, short, short, slots_message, array(whole, F32), array(of_rows, jnp.int32), array(of_rows, F32)],
        [hbm] * 4,
        [vmem] * (NEAR + 4),
        [
            pltpu.VMEM(of_rows, F32),
            pltpu.VMEM(whole, F32),
            pltpu.VMEM((columns, slots), F32),
            pltpu.VMEM(lengths.shape, jnp.int32),
            pltpu.VMEM(ids.shape, jnp.int32),
            pltpu.VMEM(firms.shape, jnp.int32),
            pltpu.SemaphoreType.DMA((columns // 8,)),
            pltpu.SemaphoreType.DMA((3,)),
        ],
        2 * work,
        4 * columns * rows_dev,
    )(in_hbm(probes), in_hbm(lengths), in_hbm(ids), in_hbm(firms))

    def pair_counts(one, start, copy=()):
        return call(
            functools.partial(pairs_kernel, pad, start, 1),
            [array((1, slots, 2 * slots), BF16), *copy],
            [vmem],
            [vmem] * (1 + len(copy)),
            [
                pltpu.VMEM((1, *of_rows), F32),
                pltpu.VMEM((1, 8, slots), F32),
                pltpu.VMEM((1, slots, workers), BF16),
            ],
            work // 4,
            4 * slots * slots,
        )(one)

    def near_step(one, step):
        return lax.ppermute(one, "rows", [(i, i ^ step) for i in range(n)])

    arrived = near_exchange(sends, n)
    own_pairs, own_slots = pair_counts(own_slots, 8, [slots_message])
    passed = near_step(own_slots, 2)
    pairs = [own_pairs]
    joined = call(
        functools.partial(join_kernel, part),
        array((columns + 2 * NEAR, slots), F32),
        [vmem] * (NEAR + 1),
        vmem,
        [],
        0,
        message.size * 8,
    )(*arrived, *pairs)
    shared = far_share(joined, n)
    tables, beside = [], passed
    table = array((tiles, NEAR * LANES, NEAR * LANES), BF16)

    def firm_table(one, passed, out):
        return call(
            functools.partial(firms_kernel, part),
            out,
            [vmem] * 3,
            [vmem] * len(out),
            [],
            work // 64,
            tiles * (NEAR * LANES) ** 2 * 2,
        )(joined, one, passed)

    if keep:
        first_table, beside = firm_table(joined, passed, [table, slots_message])
        tables = [first_table, *firm_table(shared[-1], first_table, [table])]
    pairs += pair_counts(arrived[1], about) + pair_counts(passed, 8) + pair_counts(near_step(beside, 1), 8)
    scale = array((tiles, 8, NEAR * LANES), F32)
    made = [table] * (far - 2) * keep
    mean, sums, scales, *made = call(
        functools.partial(change_kernel, far, part, len(tables)),
        [of_near, of_near, scale, *made],
        [vmem] * (far + len(tables) + len(pairs)),
        [vmem] * (3 + len(made)),
        [],
        work // 4,
        slots * slots * 4,
    )(*shared, *tables, *pairs)
    again = far_share(sums, n)
    source = [tables[0], *made, tables[1]] if keep else shared
    spreads = []
    sends = [mean[part * k : part * (k + 1)] for k in range(NEAR)]
    if keep:
        *spreads, a, b, c, d = call(
            functools.partial(tables_kernel, pad),
            [array((slots, rows_dev), BF16)] * 2 + [array((part, slots), F32)] * NEAR,
            [vmem] * 2,
            [vmem] * (2 + NEAR),
            [],
            work,
            4 * slots * rows_dev,
        )(mask_ids, mean)
        sends = [a, b, c, d]
    first = near_exchange(sends, n)
    sends = call(
        functools.partial(means_kernel, far, part, keep),
        [array((part, slots), F32)] * NEAR,
        [vmem] * (far + len(source) + 2),
        [vmem] * NEAR,
        [pltpu.VMEM((columns, slots), F32)],
        work // 4,
        slots * slots * 4,
    )(*again, *source, scales, spreads[1] if keep else scales)
    arrived = near_exchange(sends, n)
    before = call(
        functools.partial(first_kernel, pad),
        array(whole, F32),
        [vmem] * (NEAR + 3 + len(spreads)),
        vmem,
        [pltpu.VMEM((columns, slots), F32)],
        work,
        8 * columns * rows_dev,
    )(*first, x1, mask_ids, weight, *spreads)
    return call(
        last_kernel,
        array(whole, F32),
        [vmem] * (NEAR + 2 + len(spreads[:1])),
        hbm,
        [pltpu.VMEM((columns, slots), F32), pltpu.VMEM(whole, F32), sems],
        work,
        8 * columns * rows_dev,
    )(*arrived[:2], arrived[3], arrived[2], before, mask_ids, *spreads[:1])


def solution(mesh):
    placed = (P(None, ("grp", "rows")), P(("grp", "rows")), P(("grp", "rows")), P(("grp", "rows")))
    return jax.shard_map(
        functools.partial(body, n=mesh.shape["rows"]),
        mesh=mesh,
        in_specs=placed,
        out_specs=P(None, ("grp", "rows")),
        check_vma=False,
    )
```

```python
import functools

import jax
import jax.numpy as jnp
from jax import lax
from jax.experimental import pallas as pl
from jax.experimental.pallas import tpu as pltpu
from jax.sharding import PartitionSpec as P

FIRMS_PER_SHARD = 1024
LANES = 128
BLOCK = 1024
VMEM_BYTES = 32 * 1024 * 1024
NEAR = 4
NEAR_STEPS = (0, 1, 2, 3)
F32, BF16 = jnp.float32, jnp.bfloat16
NT = (((1,), (1,)), ((), ()))
NN = (((1,), (0,)), ((), ()))


def dot(a, b, dims=NN):
    return lax.dot_general(a, b, dims, preferred_element_type=F32)


def iota(shape, dim):
    return lax.broadcasted_iota(jnp.int32, shape, dim)


def split(x):
    hi = x.astype(BF16)
    return hi, (x - hi.astype(F32)).astype(BF16)


def row(ref, block, size):
    per = size // LANES
    return jnp.concatenate([ref[block * per + k : block * per + k + 1, :] for k in range(per)], axis=1)


def one_hot(ids, slots):
    kind = BF16 if slots <= 256 else F32
    slot = iota((slots, LANES), 0).astype(F32).astype(kind)
    ids = ids.astype(F32).astype(kind)
    one, zero = jnp.ones((slots, LANES), kind), jnp.zeros((slots, LANES), kind)
    parts = [jnp.where(slot == ids[:, k : k + LANES], one, zero) for k in range(0, ids.shape[1], LANES)]
    return jnp.concatenate(parts, axis=1).astype(BF16)


def one_hot_down(columns, slots):
    kind = BF16 if slots <= 256 else F32
    one, zero = jnp.ones((LANES, LANES), kind), jnp.zeros((LANES, LANES), kind)
    along_slots = [(iota((LANES, LANES), 1) + at).astype(F32).astype(kind) for at in range(0, slots, LANES)]
    parts, columns = [], columns.astype(kind)
    for k in range(columns.shape[1]):
        ids = jnp.broadcast_to(columns[:, k : k + 1], (LANES, LANES))
        parts.append(jnp.concatenate([jnp.where(slot == ids, one, zero) for slot in along_slots], axis=1))
    return jnp.concatenate(parts, axis=0).astype(BF16)


def same_worker(pad, width):
    return (iota((width, width), 0) // pad == iota((width, width), 1) // pad).astype(F32).astype(BF16)


def by_worker(x, table):
    rows, width = x.shape
    step = table.shape[1]
    both = [
        jnp.concatenate([one[:, k : k + step] for k in range(0, width, step)], axis=0) for one in split(x)
    ]
    total = dot(jnp.concatenate(both, axis=1), table)
    return jnp.concatenate([total[k : k + rows] for k in range(0, total.shape[0], rows)], axis=1)


def start_all(copies):
    for copy in copies:
        copy.start()


def wait_all(copies):
    for copy in copies:
        copy.wait()


def column_copies(source, target, sems, size=BLOCK):
    width = source.shape[1]
    cuts = [pl.ds(start, size) for start in range(0, width, size)]
    return [pltpu.make_async_copy(source.at[:, cut], target.at[:, cut], sems.at[b]) for b, cut in enumerate(cuts)]


def row_lengths(lengths, pad):
    total_rows = lengths.shape[0] * pad
    here = iota((total_rows, LANES), 0)
    lane = iota((total_rows, LANES), 1)
    wide = jnp.broadcast_to(lengths.astype(F32)[:, None, :], (lengths.shape[0], pad, LANES)).reshape(total_rows, LANES)
    per = LANES // pad
    wide = jnp.where(lane // per == here % pad, wide, 0.0).astype(BF16)
    spread = (iota((LANES, LANES), 0) % per == iota((LANES, LANES), 1) // pad).astype(F32).astype(BF16)
    row_len = dot(wide, spread)
    return row_len, (lane % pad).astype(F32) < row_len


def along(ref):
    return jnp.concatenate([ref[k : k + 1, :] for k in range(ref.shape[0])], axis=1)


def sums_kernel(pad, cap, *refs):
    (probes, lengths_in, ids_in, firms_in), sends, slots_out = refs[:4], refs[4 : 4 + NEAR], refs[4 + NEAR]
    refs = refs[5 + NEAR :]
    x1, mask_ids, weight, valid, x, sums, lengths, ids, firms, bands_sem, small = refs
    bands = [pl.ds(at, 8) for at in range(0, x.shape[0], 8)]
    copies = [pltpu.make_async_copy(probes.at[at], x.at[at], bands_sem.at[b]) for b, at in enumerate(bands)]
    first = [
        pltpu.make_async_copy(source, target, small.at[k])
        for k, (source, target) in enumerate(((lengths_in, lengths), (ids_in, ids), (firms_in, firms)))
    ]
    start_all(first)
    start_all(copies)
    columns, slots = sums.shape
    part = columns // NEAR
    me = lax.axis_index("rows") % NEAR
    wait_all(first)
    row_len, inside = row_lengths(lengths[...], pad)
    valid[...] = jnp.where(inside, 1.0, 0.0)
    weight[...] = jnp.where(inside, 1.0 / row_len, 0.0)
    masked = jnp.where(inside, ids[...], -1)
    mask_ids[...] = masked
    turned = jnp.concatenate([masked.astype(F32)] * (LANES // masked.shape[0]), axis=0).T
    keys = (iota((1, slots), 1) // cap * FIRMS_PER_SHARD + along(firms)).astype(F32)
    across = slots // LANES
    rows = ids.shape[0] // across
    masked = jnp.concatenate([masked[k * rows : (k + 1) * rows] for k in range(across)], axis=1).astype(F32)
    sends[1][part + 8 :] = masked
    slots_out[8:] = masked

    table = jnp.concatenate([same_worker(pad, 256)] * 2, axis=0)
    wait_all(copies)
    total = None
    for b in range(x.shape[1] // BLOCK):
        ok = row(valid, b, BLOCK)
        x0 = x[:, b * BLOCK : (b + 1) * BLOCK] * ok
        rest = x0 - by_worker(x0, table) * row(weight, b, BLOCK)
        x1[:, b * BLOCK : (b + 1) * BLOCK] = rest
        counted = jnp.broadcast_to(ok, (16, BLOCK)).astype(BF16)
        data = jnp.concatenate([*split(rest), counted], axis=0)
        per = BLOCK // LANES
        block = dot(data, one_hot_down(turned[:, b * per : (b + 1) * per], slots))
        total = block if total is None else total + block
    sums[...] = total[:columns] + total[columns : 2 * columns]
    about = jnp.where(iota((8, slots), 0) == 0, keys, total[2 * columns : 2 * columns + 1])
    for step, send in zip(NEAR_STEPS, sends):
        send[:part] = sums[pl.ds(pl.multiple_of((me ^ step) * part, part), part), :]
        send[part : part + 8] = about
    slots_out[:8] = about


def join_kernel(part, *refs):
    parts, out = refs[:NEAR], refs[-1]
    for k, one in enumerate(parts):
        out[part * k : part * (k + 1)] = one[:part]
        out[part * NEAR + 2 * k : part * NEAR + 2 * k + 2] = one[part : part + 2]


def pairs_kernel(pad, start, several, *refs):
    parts, (out, *copy, ids, size, counts) = refs[:several], refs[several:]
    for ref in copy:
        ref[...] = parts[0][...]
    slots = out.shape[1]
    kind = BF16 if slots <= 256 else F32
    per = LANES // pad
    total_rows = ids.shape[1]
    across = slots // LANES
    rows = total_rows // across
    for k, part in enumerate(parts):
        size[k] = jnp.broadcast_to(part[start - 7 : start - 6], (8, slots))
        for at in range(across):
            ids[k, at * rows : (at + 1) * rows] = part[start:, at * LANES : (at + 1) * LANES]
    at = iota((LANES, pad * LANES), 1)
    deal = (iota((LANES, pad * LANES), 0) == at % per * pad + at // LANES).astype(F32).astype(BF16)
    mine = iota((total_rows, pad * LANES), 1) % LANES // per == iota((total_rows, pad * LANES), 0) % pad
    slot = iota((slots, LANES), 0).astype(F32).astype(kind)
    one, zero = jnp.ones((slots, LANES), kind), jnp.zeros((slots, LANES), kind)
    diagonal = iota((slots, slots), 1) == iota((slots, slots), 0)

    def device(k, carry):
        dealt = dot(jnp.concatenate(split(ids[k]), axis=0), deal)
        dealt = jnp.where(mine, dealt[:total_rows] + dealt[total_rows:], 0.0)
        dealt = jnp.sum(dealt.reshape(total_rows // pad, pad, pad * LANES), axis=1)
        spells = dealt.astype(kind)
        for g in range(total_rows // pad):
            total = zero
            for j in range(pad):
                total += jnp.where(slot == spells[g : g + 1, j * LANES : (j + 1) * LANES], one, zero)
            counts[k, :, g * LANES : (g + 1) * LANES] = total.astype(BF16)
        valid = jnp.where(dealt >= 0.0, 1.0, 0.0)
        length = valid[:, :LANES]
        for j in range(1, pad):
            length += valid[:, j * LANES : (j + 1) * LANES]
        inverse = 1.0 / length
        inverse = jnp.concatenate([inverse[g : g + 1] for g in range(total_rows // pad)], axis=1)
        here = counts[k]
        total = dot(jnp.concatenate(split(here.astype(F32) * inverse), axis=0), here, NT)
        total = total[:slots] + total[slots:] - jnp.where(diagonal, size[k, :1], 0.0)
        hi, lo = split(total)
        out[k, :, :slots] = hi
        out[k, :, slots:] = lo
        return carry

    lax.fori_loop(0, len(parts), device, 0, unroll=len(parts) if slots <= 256 else 1)


def same_firm(own, one, part, at):
    mine, keys = ([ref[part * NEAR + 2 * k : part * NEAR + 2 * k + 1, at] for k in range(NEAR)] for ref in (own, one))
    mine = jnp.concatenate(mine, axis=1)
    down = jnp.concatenate([jnp.broadcast_to(key, (8, LANES)) for key in keys], axis=0).T
    found = [(down[:, 8 * k : 8 * k + 1] == mine).astype(F32).astype(BF16) for k in range(NEAR)]
    return jnp.concatenate(found, axis=0)


def each_tile(slots, do):
    tiles = slots // LANES
    if tiles <= 2:
        for t in range(tiles):
            do(t, slice(t * LANES, (t + 1) * LANES))
    else:
        lax.fori_loop(0, tiles, lambda t, c: (do(t, pl.ds(pl.multiple_of(t * LANES, LANES), LANES)), c)[1], 0)


def firms_kernel(part, own, one, passed, out, *copy):
    for ref in copy:
        ref[...] = passed[...]
    each_tile(own.shape[1], lambda t, at: out.__setitem__(t, same_firm(own, one, part, at)))


def gathered(parts, part, at):
    data = [one[part * k : part * (k + 1), at] for one in parts for k in range(NEAR)]
    return jnp.concatenate(split(jnp.concatenate(data, axis=1)), axis=0)


def spread_out(means, out, part, at):
    for k in range(NEAR):
        out[part * k : part * (k + 1), at] = means[:, k * LANES : (k + 1) * LANES]


def change_kernel(far, part, ready, *refs):
    tables, pairs, refs = refs[far : far + ready], refs[far + ready : far + ready + NEAR], refs
    parts, (mean, sums, scale), made = refs[:far], refs[far + ready + NEAR :][:3], refs[far + ready + NEAR + 3 :]
    slots = mean.shape[1]

    def tile(t, at):
        if tables:
            between = [same_firm(parts[0], one, part, at) for one in parts[1:-1]]
            for ref, one in zip(made, between):
                ref[t] = one
            same = [tables[0][t], *between, tables[1][t]]
        else:
            same = [same_firm(parts[0], one, part, at) for one in parts]
        same = jnp.concatenate(same, axis=0)
        count = [one[part * NEAR + 2 * k + 1 : part * NEAR + 2 * k + 2, at] for one in parts for k in range(NEAR)]
        count = jnp.concatenate(count, axis=1)
        high = count.astype(BF16).astype(F32)
        counts = jnp.where(iota((16, count.shape[1]), 0) < 8, high, count - high).astype(BF16)
        found = dot(jnp.concatenate([gathered(parts, part, at), counts], axis=0), same)
        size = found[2 * part : 2 * part + 1] + found[2 * part + 8 : 2 * part + 9]
        inverse = 1.0 / jnp.maximum(size, 1.0)
        scale[t] = jnp.broadcast_to(inverse, scale.shape[1:])
        spread_out((found[:part] + found[part : 2 * part]) * inverse, mean, part, at)

    each_tile(slots, tile)
    for k in range(NEAR):
        cut = slice(part * k, part * (k + 1))
        both = jnp.concatenate(split(mean[cut]), axis=0)
        change = dot(both, pairs[k][0])
        change = change[:part] + change[part:]
        sums[cut] = parts[0][cut] + (change[:, :slots] + change[:, slots:])


def tables_kernel(pad, mask_ids, mean, spread, workers, *sends):
    part = mean.shape[0] // NEAR
    for k, send in enumerate(sends):
        send[...] = mean[part * k : part * (k + 1)]
    slots, width = spread.shape
    table = jnp.concatenate([same_worker(pad, 256)] * 2, axis=0)
    for b in range(width // BLOCK):
        found = one_hot(row(mask_ids, b, BLOCK), slots)
        spread[:, b * BLOCK : (b + 1) * BLOCK] = found
        for at in range(0, BLOCK, 256):
            count = dot(found[:, at : at + 256], table[:256])
            workers[:, b * BLOCK + at : b * BLOCK + at + 256] = count.astype(BF16)


def means_kernel(far, part, kept, *refs):
    parts, source, scale, sends, mean = refs[:far], refs[far:-7], refs[-7], refs[-5:-1], refs[-1]

    def tile(t, at):
        same = [table[t] if kept else same_firm(source[0], table, part, at) for table in source]
        same = jnp.concatenate(same, axis=0)
        found = dot(gathered(parts, part, at), same)
        spread_out((found[:part] + found[part:]) * scale[t][:1], mean, part, at)

    each_tile(mean.shape[1], tile)
    for k, send in enumerate(sends):
        send[...] = mean[part * k : part * (k + 1)]


def own_means(parts, means):
    me = lax.axis_index("rows") % NEAR
    part = parts[0].shape[0]
    for step, one in zip(NEAR_STEPS, parts):
        means[pl.ds(pl.multiple_of((me ^ step) * part, part), part), :] = one[...]
    return jnp.concatenate(split(means[...]), axis=0)


def first_kernel(pad, *refs):
    parts, (x1, mask_ids, weight), tables, (y, means) = refs[:NEAR], refs[NEAR : NEAR + 3], refs[NEAR + 3 : -2], refs[-2:]
    columns, slots = means.shape
    first = own_means(parts, means)
    table = jnp.concatenate([same_worker(pad, 256)] * 2, axis=0)
    for b in range(y.shape[1] // BLOCK):
        at = slice(b * BLOCK, (b + 1) * BLOCK)
        found = tables[0][:, at] if tables else one_hot(row(mask_ids, b, BLOCK), slots)
        spread = dot(first, found)
        spread = spread[:columns] + spread[columns:]
        if tables:
            worker = dot(first, tables[1][:, at])
            worker = worker[:columns] + worker[columns:]
        else:
            worker = by_worker(spread, table)
        y[:, at] = x1[:, at] - spread + worker * row(weight, b, BLOCK)


def last_kernel(*refs):
    parts, (before, mask_ids), tables, (out, means, y, sems) = refs[:NEAR], refs[NEAR : NEAR + 2], refs[NEAR + 2 : -4], refs[-4:]
    outs = column_copies(y, out, sems)
    columns, slots = means.shape
    second = own_means(parts, means)
    piece = BLOCK // 2
    for b in range(2 * len(outs)):
        at = slice(b * piece, (b + 1) * piece)
        found = tables[0][:, at] if tables else one_hot(row(mask_ids, b, piece), slots)
        spread = dot(second, found)
        y[:, at] = before[:, at] - (spread[:columns] + spread[columns:])
        if b % 2:
            outs[b // 2].start()
    wait_all(outs)


def near_exchange(parts, n):
    steps = [[(i, i ^ step) for i in range(n)] for step in NEAR_STEPS[1:]]
    return [parts[0]] + [lax.ppermute(one, "rows", step) for one, step in zip(parts[1:], steps)]


def far_share(one, n):
    steps = [[(i, i ^ (k * NEAR)) for i in range(n)] for k in range(1, n // NEAR)]
    return [one] + [lax.ppermute(one, "rows", step) for step in steps]


def in_hbm(x):
    return pltpu.with_memory_space_constraint(x, pltpu.HBM)


def call(kernel, out_shape, in_specs, out_specs, scratch, flops, moved):
    return pl.pallas_call(
        kernel,
        out_shape=out_shape,
        in_specs=in_specs,
        out_specs=out_specs,
        scratch_shapes=scratch,
        compiler_params=pltpu.CompilerParams(vmem_limit_bytes=VMEM_BYTES),
        cost_estimate=pl.CostEstimate(flops=flops, bytes_accessed=moved, transcendentals=0),
    )


def body(probes, worker_len, spell_to_slot, slot_to_firm, *, n):
    columns, rows_dev = probes.shape
    workers = worker_len.shape[0]
    pad = rows_dev // workers
    slots = slot_to_firm.shape[0]
    tiles = slots // LANES
    part = columns // NEAR
    far = n // NEAR
    keep = tiles * NEAR * n * LANES * LANES * 2 <= 8 * 1024 * 1024
    blocks = rows_dev // BLOCK
    vmem, hbm = pl.BlockSpec(memory_space=pltpu.VMEM), pl.BlockSpec(memory_space=pltpu.HBM)
    lengths = worker_len.reshape(workers // LANES, LANES)
    ids = spell_to_slot.reshape(rows_dev // LANES, LANES)
    firms = slot_to_firm.reshape(tiles, LANES)
    array = jax.ShapeDtypeStruct
    of_rows = (rows_dev // LANES, LANES)
    work = 2 * rows_dev * slots * 2 * columns
    sems = pltpu.SemaphoreType.DMA((blocks,))
    whole = (columns, rows_dev)
    about = part + 8
    message = array((about + rows_dev // slots, slots), F32)
    short = array((about, slots), F32)
    slots_message = array((message.shape[0] - part, slots), F32)
    of_near = array((columns, slots), F32)

    *sends, own_slots, x1, mask_ids, weight = call(
        functools.partial(sums_kernel, pad, slots // n),
        [short, message, short, short, slots_message, array(whole, F32), array(of_rows, jnp.int32), array(of_rows, F32)],
        [hbm] * 4,
        [vmem] * (NEAR + 4),
        [
            pltpu.VMEM(of_rows, F32),
            pltpu.VMEM(whole, F32),
            pltpu.VMEM((columns, slots), F32),
            pltpu.VMEM(lengths.shape, jnp.int32),
            pltpu.VMEM(ids.shape, jnp.int32),
            pltpu.VMEM(firms.shape, jnp.int32),
            pltpu.SemaphoreType.DMA((columns // 8,)),
            pltpu.SemaphoreType.DMA((3,)),
        ],
        2 * work,
        4 * columns * rows_dev,
    )(in_hbm(probes), in_hbm(lengths), in_hbm(ids), in_hbm(firms))

    def pair_counts(one, start, copy=()):
        return call(
            functools.partial(pairs_kernel, pad, start, 1),
            [array((1, slots, 2 * slots), BF16), *copy],
            [vmem],
            [vmem] * (1 + len(copy)),
            [
                pltpu.VMEM((1, *of_rows), F32),
                pltpu.VMEM((1, 8, slots), F32),
                pltpu.VMEM((1, slots, workers), BF16),
            ],
            work // 4,
            4 * slots * slots,
        )(one)

    def near_step(one, step):
        return lax.ppermute(one, "rows", [(i, i ^ step) for i in range(n)])

    arrived = near_exchange(sends, n)
    own_pairs, own_slots = pair_counts(own_slots, 8, [slots_message])
    passed = near_step(own_slots, 2)
    pairs = [own_pairs]
    joined = call(
        functools.partial(join_kernel, part),
        array((columns + 2 * NEAR, slots), F32),
        [vmem] * (NEAR + 1),
        vmem,
        [],
        0,
        message.size * 8,
    )(*arrived, *pairs)
    shared = far_share(joined, n)
    tables, beside = [], passed
    table = array((tiles, NEAR * LANES, NEAR * LANES), BF16)

    def firm_table(one, passed, out):
        return call(
            functools.partial(firms_kernel, part),
            out,
            [vmem] * 3,
            [vmem] * len(out),
            [],
            work // 64,
            tiles * (NEAR * LANES) ** 2 * 2,
        )(joined, one, passed)

    if keep:
        first_table, beside = firm_table(joined, passed, [table, slots_message])
        tables = [first_table, *firm_table(shared[-1], first_table, [table])]
    pairs += pair_counts(arrived[1], about) + pair_counts(passed, 8) + pair_counts(near_step(beside, 1), 8)
    scale = array((tiles, 8, NEAR * LANES), F32)
    made = [table] * (far - 2) * keep
    mean, sums, scales, *made = call(
        functools.partial(change_kernel, far, part, len(tables)),
        [of_near, of_near, scale, *made],
        [vmem] * (far + len(tables) + len(pairs)),
        [vmem] * (3 + len(made)),
        [],
        work // 4,
        slots * slots * 4,
    )(*shared, *tables, *pairs)
    again = far_share(sums, n)
    source = [tables[0], *made, tables[1]] if keep else shared
    spreads = []
    sends = [mean[part * k : part * (k + 1)] for k in range(NEAR)]
    if keep:
        *spreads, a, b, c, d = call(
            functools.partial(tables_kernel, pad),
            [array((slots, rows_dev), BF16)] * 2 + [array((part, slots), F32)] * NEAR,
            [vmem] * 2,
            [vmem] * (2 + NEAR),
            [],
            work,
            4 * slots * rows_dev,
        )(mask_ids, mean)
        sends = [a, b, c, d]
    first = near_exchange(sends, n)
    sends = call(
        functools.partial(means_kernel, far, part, keep),
        [array((part, slots), F32)] * NEAR,
        [vmem] * (far + len(source) + 2),
        [vmem] * NEAR,
        [pltpu.VMEM((columns, slots), F32)],
        work // 4,
        slots * slots * 4,
    )(*again, *source, scales, spreads[1] if keep else scales)
    arrived = near_exchange(sends, n)
    before = call(
        functools.partial(first_kernel, pad),
        array(whole, F32),
        [vmem] * (NEAR + 3 + len(spreads)),
        vmem,
        [pltpu.VMEM((columns, slots), F32)],
        work,
        8 * columns * rows_dev,
    )(*first, x1, mask_ids, weight, *spreads)
    return call(
        last_kernel,
        array(whole, F32),
        [vmem] * (NEAR + 2 + len(spreads[:1])),
        hbm,
        [pltpu.VMEM((columns, slots), F32), pltpu.VMEM(whole, F32), sems],
        work,
        8 * columns * rows_dev,
    )(*arrived, before, mask_ids, *spreads[:1])


def solution(mesh):
    placed = (P(None, ("grp", "rows")), P(("grp", "rows")), P(("grp", "rows")), P(("grp", "rows")))
    return jax.shard_map(
        functools.partial(body, n=mesh.shape["rows"]),
        mesh=mesh,
        in_specs=placed,
        out_specs=P(None, ("grp", "rows")),
        check_vma=False,
    )
```
